32 devices in a mesh: pipe: 2 (over x), dp: 4 (over z), tensor: 4 (over y, core).
Axes of the slice: x: 2, y: 2, z: 4, core: 2. Of those that a mesh axis runs over, the one named last changes fastest.
Arguments:
- inputs: bfloat16 [8, 512, 768], P('dp'), may hold values from -6 to 6
- out_grad: bfloat16 [8, 512, 768], P('dp'), may hold values from -6 to 6
- doc_lengths: int32 [8, 4], P('dp'), may hold values from 1 to 256, 512 in all within a row
- w_qkv: bfloat16 [2, 3, 768, 768], P('pipe', None, None, 'tensor'), may hold values from -0.21875 to 0.21875
- b_qv: bfloat16 [2, 2, 768], P('pipe', None, 'tensor'), may hold values from -3 to 3
- w_out: bfloat16 [2, 768, 768], P('pipe', 'tensor'), may hold values from -0.875 to 0.875
- b_out: float32 [2, 768], P('pipe'), may hold values from -3 to 3
- norm1_gain: float32 [2, 768], P('pipe'), may hold values from 0.25 to 1.75
- norm1_bias: float32 [2, 768], P('pipe'), may hold values from -3 to 3
- w_in: bfloat16 [2, 768, 3072], P('pipe', None, 'tensor'), may hold values from -0.21875 to 0.21875
- b_in: bfloat16 [2, 3072], P('pipe', 'tensor'), may hold values from -3 to 3
- w_back: bfloat16 [2, 3072, 768], P('pipe', 'tensor'), may hold values from -0.21875 to 0.21875
- b_back: float32 [2, 768], P('pipe'), may hold values from -3 to 3
- norm2_gain: float32 [2, 768], P('pipe'), may hold values from 0.25 to 1.75
- norm2_bias: float32 [2, 768], P('pipe'), may hold values from -3 to 3
- mask_logits: float32 [2, 512, 512], P('pipe'), may hold values from -5 to 5
- mask_noise: float32 [2, 512, 512], P('pipe'), may hold values from -5 to 5
Outputs:
- activations: bfloat16 [2, 8, 512, 768], P('pipe', 'dp', 'tensor')
- input_grads: float32 [2, 8, 512, 768], P('pipe', 'dp', 'tensor')
- grad_w_qkv: float32 [2, 3, 768, 768], P('pipe', None, None, 'tensor')
- grad_b_qv: float32 [2, 2, 768], P('pipe', None, 'tensor')
- grad_w_out: float32 [2, 768, 768], P('pipe', 'tensor')
- grad_b_out: float32 [2, 768], P('pipe')
- grad_norm1_gain: float32 [2, 768], P('pipe')
- grad_norm1_bias: float32 [2, 768], P('pipe')
- grad_w_in: float32 [2, 768, 3072], P('pipe', None, 'tensor')
- grad_b_in: float32 [2, 3072], P('pipe', 'tensor')
- grad_w_back: float32 [2, 3072, 768], P('pipe', 'tensor')
- grad_b_back: float32 [2, 768], P('pipe')
- grad_norm2_gain: float32 [2, 768], P('pipe')
- grad_norm2_bias: float32 [2, 768], P('pipe')
- grad_mask_logits: float32 [2, 512, 512], P('pipe')
The draws below stay inside these ranges and needn't reach their ends.
Inputs may be any that keep to these rules, and one draw needn't show every extreme that they name: `doc_lengths`: each row of 4 lengths sums to 512, and its largest is exactly 256.
All inputs are finite; a program needn't handle non-finite values.
Results may differ from the reference program's by a relative error of at most 0.039.
Values may be sent and summed in bfloat16 or wider, within the bound.
No kernel may reach another device: no remote copies, remote signals or barrier semaphores. Data moves between devices by JAX's collectives and lax.ppermute only.
A program may use at most 128 MiB of HBM per device.

```python
import functools
import math
import jax
import jax.numpy as jnp
import numpy as np
from jax import lax

D = 768
FF = 3072
HEAD_DIM = 64
HEADS = 12
SEQ = 512
DOCS = 4
LAYERS = 2
SEQS = 8


def level_of(key, shape, cuts, least, top_value):
    gain = 1.0
    for axis_at, blocks in cuts:
        steps = jax.random.uniform(jax.random.fold_in(jax.random.fold_in(key, 6), axis_at), (blocks,), jnp.float32, least / len(cuts), top_value / len(cuts))
        gain = gain * jnp.repeat(jnp.exp(steps), shape[axis_at] // blocks).reshape((-1,) + (1,) * (len(shape) - 1 - axis_at))
    return gain


def profile(count, total, limit, skew):
    weights = [(1 << 20) // math.isqrt(grade ** skew) + 1 for grade in range(2, count + 1)]
    surplus, given = total - limit - (count - 1), [1] * (count - 1)
    while surplus > 0:
        candidates = [i for i in range(count - 1) if given[i] < limit]
        whole, remaining = sum([weights[i] for i in candidates]), surplus
        for i in candidates:
            extra = min(limit - given[i], max(1, remaining * weights[i] // whole), surplus)
            given[i] = given[i] + extra
            surplus = surplus - extra
    return np.array([limit] + given)


def ragged(stream_key, amount, total, bound, slope):
    if amount == 2:
        one = jax.random.randint(stream_key, (), max(1, total - bound), min(bound, total - 1) + 1)
        return jnp.stack([one, total - one])
    sizes = jnp.asarray(profile(amount, total, bound, slope), jnp.int32)
    twos = (amount - 1) // 2
    donor, sink = sizes[1:1 + 2 * twos:2], sizes[2:2 + 2 * twos:2]
    room = jnp.minimum(donor - 1, bound - sink)
    moved = jax.random.randint(jax.random.fold_in(stream_key, 1), (twos,), 0, 1 << 20) % (room + 1)
    sizes = sizes.at[1:1 + 2 * twos:2].set(donor - moved).at[2:2 + 2 * twos:2].set(sink + moved)
    return sizes[jax.random.permutation(jax.random.fold_in(stream_key, 2), amount)]


def scatter_about(rng, extent, spread, limit, cuts=(), held_as=jnp.bfloat16):
    array = spread * jax.random.normal(rng, extent, jnp.float32)
    if cuts:
        array = array * level_of(rng, extent, cuts, -0.22, 0.18)
    return jnp.clip(array, -limit, limit).astype(held_as)


def setup_inputs(seed: int = 0) -> dict:
    streams_of = jax.random.split(jax.random.key(seed), 18)
    return {
        "inputs": scatter_about(streams_of[0], (SEQS, SEQ, D), 1.0, 6.0, ((0, 4),)),
        "out_grad": scatter_about(streams_of[1], (SEQS, SEQ, D), 1.0, 6.0, ((0, 4),)),
        "doc_lengths": jax.vmap(lambda own: ragged(own, DOCS, SEQ, SEQ // 2, 1))(jax.random.split(streams_of[2], SEQS)).reshape((SEQS, DOCS)).astype(jnp.int32),
        "w_qkv": scatter_about(streams_of[3], (LAYERS, 3, D, D), D ** -0.5, 0.21875, ((0, 2), (3, 4))),
        "b_qv": scatter_about(streams_of[4], (LAYERS, 2, D), 0.5, 3.0, ((0, 2), (2, 4))),
        "w_out": scatter_about(streams_of[5], (LAYERS, D, D), (D // 16) ** -0.5, 0.875, ((0, 2), (1, 4))),
        "b_out": scatter_about(streams_of[6], (LAYERS, D), 0.5, 3.0, ((0, 2),), jnp.float32),
        "norm1_gain": jnp.clip(1.0 + 0.15 * jax.random.normal(streams_of[7], (LAYERS, D), jnp.float32), 0.25, 1.75),
        "norm1_bias": scatter_about(streams_of[8], (LAYERS, D), 0.5, 3.0, ((0, 2),), jnp.float32),
        "w_in": scatter_about(streams_of[9], (LAYERS, D, FF), D ** -0.5, 0.21875, ((0, 2), (2, 4))),
        "b_in": scatter_about(streams_of[10], (LAYERS, FF), 0.5, 3.0, ((0, 2), (1, 4))),
        "w_back": scatter_about(streams_of[11], (LAYERS, FF, D), (FF // 4) ** -0.5, 0.21875, ((0, 2), (1, 4))),
        "b_back": scatter_about(streams_of[12], (LAYERS, D), 0.5, 3.0, ((0, 2),), jnp.float32),
        "norm2_gain": jnp.clip(1.0 + 0.15 * jax.random.normal(streams_of[13], (LAYERS, D), jnp.float32), 0.25, 1.75),
        "norm2_bias": scatter_about(streams_of[14], (LAYERS, D), 0.5, 3.0, ((0, 2),), jnp.float32),
        "mask_logits": scatter_about(streams_of[15], (LAYERS, SEQ, SEQ), 1.0, 5.0, ((0, 2),), jnp.float32),
        "mask_noise": scatter_about(streams_of[16], (LAYERS, SEQ, SEQ), 1.0, 5.0, ((0, 2),), jnp.float32),
    }


@jax.custom_vjp
def low(v):
    return lax.optimization_barrier(v.astype(jnp.bfloat16)).astype(jnp.float32)

@jax.custom_vjp
def low_back(v):
    return v

def low_keep(v):
    return (low(v), None)

def low_pass(kept, grad):
    return (grad,)

def back_keep(v):
    return (v, None)

def back_low(kept, grad):
    return (low(grad),)
low.defvjp(low_keep, low_pass)
low_back.defvjp(back_keep, back_low)
HIGHEST = lax.Precision.HIGHEST
EPSILON = 1e-12
MASKED = -1e+30

def product(left, right):
    return jnp.dot(left, right, precision=HIGHEST)

def normalize(values, gain_vector, offset_vector):
    average = lax.optimization_barrier(jnp.mean(values, axis=-1, keepdims=True))
    centred = values - average
    variance = lax.optimization_barrier(jnp.mean(centred * centred, axis=-1, keepdims=True))
    return centred * lax.rsqrt(variance + EPSILON) * gain_vector + offset_vector

def document_mask(lengths, seq_length):
    bounds = jnp.cumsum(lengths.astype(jnp.int32))
    places = jnp.arange(seq_length, dtype=jnp.int32)
    owners = lax.optimization_barrier(jnp.sum((places[:, None] >= bounds[None, :]).astype(jnp.int32), axis=1))
    return owners[:, None] == owners[None, :]

def attend(mask_term, pieces):
    queries, key_rows, values, same_doc = pieces
    scores = jnp.einsum('qhd,khd->hqk', queries, key_rows, precision=HIGHEST) / math.sqrt(HEAD_DIM) + mask_term[None]
    scores = low_back(scores)
    scores = jnp.where(same_doc[None], scores, MASKED)
    row_peak = lax.optimization_barrier(jnp.max(scores, axis=-1, keepdims=True))
    exponent = jnp.exp(scores - row_peak)
    probabilities = low(exponent / lax.optimization_barrier(jnp.sum(exponent, axis=-1, keepdims=True)))
    return jnp.einsum('hqk,khd->qhd', probabilities, values, precision=HIGHEST)

def layer(tokens, params, same_docs):
    w_qkv, b_qv, w_out, b_out, gain_one, offset_one, w_in, b_in, w_back, b_back, gain_two, offset_two, mask_logits, mask_noise = params
    mask_term = jax.nn.log_sigmoid(mask_logits + mask_noise)
    queries = low_back(low(product(tokens, w_qkv[0]) + b_qv[0]))
    key_rows = low_back(low(product(tokens, w_qkv[1])))
    values = low_back(low(product(tokens, w_qkv[2]) + b_qv[1]))
    shaped = (same_docs.shape[0], same_docs.shape[1], HEADS, HEAD_DIM)
    checkpointed = jax.checkpoint(attend)

    def attend_one(pieces):
        return checkpointed(mask_term, pieces)
    attended = lax.map(attend_one, (queries.reshape(shaped), key_rows.reshape(shaped), values.reshape(shaped), same_docs))
    attended = low_back(low(attended.reshape(tokens.shape)))
    branch = low_back(product(attended, w_out)) + b_out
    first_out = normalize(tokens + branch, gain_one, offset_one)
    pre_act = low_back(product(low(first_out), w_in) + b_in)
    hidden = low(jax.nn.gelu(pre_act, approximate=False))
    second_in = first_out + low_back(product(hidden, w_back)) + b_back
    return normalize(second_in, gain_two, offset_two)

def reference(inputs, out_grad, doc_lengths, w_qkv, b_qv, w_out, b_out, norm1_gain, norm1_bias, w_in, b_in, w_back, b_back, norm2_gain, norm2_bias, mask_logits, mask_noise):
    seq_length = inputs.shape[1]
    same_docs = jax.vmap(functools.partial(document_mask, seq_length=seq_length))(doc_lengths)
    stacked = tuple((item.astype(jnp.float32) for item in (w_qkv, b_qv, w_out, b_out, norm1_gain, norm1_bias, w_in, b_in, w_back, b_back, norm2_gain, norm2_bias, mask_logits, mask_noise)))
    layer_call = functools.partial(layer, same_docs=same_docs)
    tokens = inputs.reshape(-1, D).astype(jnp.float32)
    pullbacks = []
    outputs = []
    for layer_index in range(LAYERS):
        params = tuple((item[layer_index] for item in stacked))
        result, pullback = jax.vjp(layer_call, tokens, params)
        outputs.append(result.astype(jnp.bfloat16).reshape(inputs.shape))
        pullbacks.append(pullback)
        tokens = low(result)
    cotangent = out_grad.reshape(-1, D).astype(jnp.float32)
    input_list = [None] * LAYERS
    param_list = [None] * LAYERS
    for layer_index in reversed(range(LAYERS)):
        token_grad, params_grad = pullbacks[layer_index](cotangent)
        input_list[layer_index] = token_grad.reshape(inputs.shape)
        param_list[layer_index] = params_grad
        cotangent = low(token_grad)
    gathered = [jnp.stack([param_list[layer_index][slot_index] for layer_index in range(LAYERS)]) for slot_index in range(13)]
    return (jnp.stack(outputs), jnp.stack(input_list), gathered[0], gathered[1], gathered[2], gathered[3], gathered[4], gathered[5], gathered[6], gathered[7], gathered[8], gathered[9], gathered[10], gathered[11], gathered[12])
```

```python
import math

import jax
import jax.numpy as jnp
from jax import lax
from jax.sharding import PartitionSpec as P

HEAD_DIM = 64
EPSILON = 1e-12
MASKED = -1e30
BF = jnp.bfloat16
F32 = jnp.float32


def dot(left, right, dims=((1,), (0,))):
    return lax.dot_general(left, right, (dims, ((), ())), preferred_element_type=F32)


def swap(block, distance):
    size = lax.axis_size("tensor")
    return lax.ppermute(block, "tensor", [(i, i ^ distance) for i in range(size)])


def pair_sum(partial):
    low = partial.astype(BF)
    return low.astype(F32) + swap(low, 1).astype(F32)


def dp_sum(block):
    size = lax.axis_size("dp")
    if size != 4:
        return lax.psum(block, "dp").astype(F32)
    place = lax.axis_index("dp")
    middle = (place == 1) | (place == 2)
    near = lax.ppermute(block, "dp", [(0, 1), (3, 2)])
    half = (block.astype(F32) + near.astype(F32)).astype(BF)
    far = lax.ppermute(half, "dp", [(1, 2), (2, 1)])
    whole = (half.astype(F32) + far.astype(F32)).astype(BF)
    back = lax.ppermute(whole, "dp", [(1, 0), (2, 3)])
    return jnp.where(middle, whole, back).astype(F32)


def norm_forward(values, gain, offset):
    average = jnp.mean(values, axis=-1, keepdims=True)
    centred = values - average
    variance = jnp.mean(centred * centred, axis=-1, keepdims=True)
    scale = lax.rsqrt(variance + EPSILON)
    unit = centred * scale
    return unit * gain + offset, (unit, scale)


def norm_backward(grad, kept, gain):
    unit, scale = kept
    direct = grad * gain
    return scale * (
        direct
        - jnp.mean(direct, axis=-1, keepdims=True)
        - unit * jnp.mean(direct * unit, axis=-1, keepdims=True)
    )


def gelu_pair(values):
    cdf = 0.5 * (1.0 + lax.erf(values * math.sqrt(0.5)))
    density = jnp.exp(-0.5 * values * values) * (1.0 / math.sqrt(2.0 * math.pi))
    return values * cdf, cdf + values * density


def forward(tokens, weights, bias_table):
    w_q, w_k, w_v, b_q, b_v, w_out, b_out, gain_one, offset_one = weights[:9]
    w_in, b_in, w_back, b_back, gain_two, offset_two = weights[9:]
    seq = tokens.shape[0]
    shaped = (seq, -1, HEAD_DIM)
    queries = (dot(tokens, w_q) + b_q).astype(BF)
    keys = dot(tokens, w_k).astype(BF)
    values = (dot(tokens, w_v) + b_v).astype(BF)
    scores = jnp.einsum(
        "qhd,khd->hqk", queries.reshape(shaped), keys.reshape(shaped), preferred_element_type=F32
    ) / math.sqrt(HEAD_DIM) + bias_table
    peak = jnp.max(scores, axis=-1, keepdims=True)
    exponent = jnp.exp(scores - peak)
    total = jnp.sum(exponent, axis=-1, keepdims=True)
    attended = jnp.einsum(
        "hqk,khd->qhd",
        (exponent / total).astype(BF),
        values.reshape(shaped),
        preferred_element_type=F32,
    ).reshape(seq, -1).astype(BF)
    log_norm = peak + jnp.log(total)
    first_in = tokens.astype(F32) + pair_sum(dot(attended, w_out)) + b_out
    first, kept_one = norm_forward(first_in, gain_one, offset_one)
    first_low = first.astype(BF)
    pre_act = dot(first_low, w_in) + b_in
    hidden, slope = gelu_pair(pre_act)
    hidden = hidden.astype(BF)
    second_in = first + pair_sum(dot(hidden, w_back)) + b_back
    second, kept_two = norm_forward(second_in, gain_two, offset_two)
    stored = (
        tokens, queries, keys, values, log_norm, attended, kept_one, first_low, slope, hidden, kept_two,
    )
    return second.astype(BF), stored


def backward(top, stored, weights, bias_table):
    w_q, w_k, w_v, b_q, b_v, w_out, b_out, gain_one, offset_one = weights[:9]
    w_in, b_in, w_back, b_back, gain_two, offset_two = weights[9:]
    tokens, queries, keys, values, log_norm, attended, kept_one, first_low, slope, hidden, kept_two = stored
    seq = tokens.shape[0]
    shaped = (seq, -1, HEAD_DIM)
    root = math.sqrt(HEAD_DIM)
    last = ((1,), (1,))
    first_dims = ((0,), (0,))
    top = top.astype(F32)
    sum_grad = norm_backward(top, kept_two, gain_two)
    ffn_low = sum_grad.astype(BF)
    pre_low = (dot(ffn_low, w_back, last) * slope).astype(BF)
    first_grad = sum_grad + pair_sum(dot(pre_low, w_in, last))
    branch_grad = norm_backward(first_grad, kept_one, gain_one)
    branch_low = branch_grad.astype(BF)
    attended_grad = dot(branch_low, w_out, last).astype(BF).reshape(shaped)
    query_heads, key_heads, value_heads = (v.reshape(shaped) for v in (queries, keys, values))
    scores = jnp.einsum(
        "qhd,khd->hqk", query_heads, key_heads, preferred_element_type=F32
    ) / root + bias_table
    chance = jnp.exp(scores - log_norm)
    values_grad = jnp.einsum("hqk,qhd->khd", chance.astype(BF), attended_grad, preferred_element_type=F32)
    chance_grad = jnp.einsum("qhd,khd->hqk", attended_grad, value_heads, preferred_element_type=F32)
    score_low = (
        chance * (chance_grad - jnp.sum(chance * chance_grad, axis=-1, keepdims=True))
    ).astype(BF)
    queries_grad = jnp.einsum("hqk,khd->qhd", score_low, key_heads, preferred_element_type=F32) / root
    keys_grad = jnp.einsum("hqk,qhd->khd", score_low, query_heads, preferred_element_type=F32) / root
    queries_grad, keys_grad, values_grad = (
        v.astype(BF).reshape(seq, -1) for v in (queries_grad, keys_grad, values_grad)
    )
    rows_partial = (
        dot(queries_grad, w_q, last) + dot(keys_grad, w_k, last) + dot(values_grad, w_v, last)
    )
    in_grad = branch_grad + pair_sum(rows_partial)

    def parameter_grads():
        vectors = jnp.stack(
            [
                jnp.sum(branch_grad, axis=0),
                jnp.sum(first_grad * kept_one[0], axis=0),
                jnp.sum(first_grad, axis=0),
                jnp.sum(sum_grad, axis=0),
                jnp.sum(top * kept_two[0], axis=0),
                jnp.sum(top, axis=0),
            ]
        )
        return dict(
            w_back=dot(hidden, ffn_low, first_dims),
            w_in=dot(first_low, pre_low, first_dims),
            w_out=dot(attended, branch_low, first_dims),
            w_qkv=[dot(tokens, v, first_dims) for v in (queries_grad, keys_grad, values_grad)],
            b_qv=[jnp.sum(v.astype(F32), axis=0) for v in (queries_grad, values_grad)],
            b_in=jnp.sum(pre_low.astype(F32), axis=0),
            vectors=vectors,
            mask=jnp.sum(score_low.astype(F32), axis=0),
        )

    return in_grad, parameter_grads


def document_mask(lengths, seq_length):
    bounds = jnp.cumsum(lengths)
    places = jnp.arange(seq_length, dtype=jnp.int32)
    owners = jnp.sum((places[:, None] >= bounds[None, :]).astype(jnp.int32), axis=1)
    return owners[:, None] == owners[None, :]


def shards(
    inputs, out_grad, doc_lengths, w_qkv, b_qv, w_out, b_out, norm1_gain, norm1_bias,
    w_in, b_in, w_back, b_back, norm2_gain, norm2_bias, mask_logits, mask_noise,
):
    count, seq, width = inputs.shape
    tensor = lax.axis_size("tensor")
    assert lax.axis_size("pipe") == 2 and tensor == 4 and count == 2
    part = lax.axis_index("tensor")
    core, chip = part % 2, part // 2
    section = lax.axis_index("pipe")
    rows = seq // tensor
    half = seq // 2

    def mine(stack):
        return lax.dynamic_index_in_dim(stack, chip, 0, keepdims=False)

    own = [w_qkv[0], w_out[0], w_in[0], w_back[0]]
    fetched = []
    behind = None
    for block in own:
        if len(fetched) >= 2:
            block, fetched[-2] = lax.optimization_barrier((block, fetched[-2]))
        fetched.append(swap(block, 2))
    other_b_qv, other_b_in = swap(b_qv[0], 2), swap(b_in[0], 2)
    both_qkv = jnp.concatenate([own[0], fetched[0]], axis=2)
    both_b_qv = jnp.concatenate([b_qv[0], other_b_qv], axis=1).astype(F32)
    weights = (
        both_qkv[0], both_qkv[1], both_qkv[2], both_b_qv[0], both_b_qv[1],
        jnp.concatenate([own[1], fetched[1]], axis=0), b_out[0], norm1_gain[0], norm1_bias[0],
        jnp.concatenate([own[2], fetched[2]], axis=1),
        jnp.concatenate([b_in[0], other_b_in]).astype(F32),
        jnp.concatenate([own[3], fetched[3]], axis=0), b_back[0], norm2_gain[0], norm2_bias[0],
    )
    mask_input = mask_logits[0] + mask_noise[0]
    mask_term = jax.nn.log_sigmoid(mask_input)
    same_doc = document_mask(mine(doc_lengths), seq)
    bias_table = jnp.where(same_doc, mask_term, MASKED)

    def rows_across(full, route):
        part_rows = lax.dynamic_slice_in_dim(full, core * half, half, 0)
        got = lax.ppermute(part_rows, "pipe", route)
        also = swap(got, 1)
        return jnp.where(
            core == 0, jnp.concatenate([got, also]), jnp.concatenate([also, got])
        )

    first_tokens = mine(inputs)
    second, unused = forward(first_tokens, weights, bias_table)
    passed = rows_across(second, [(0, 1)])
    tokens = jnp.where(section == 0, first_tokens, passed)
    second, stored = forward(tokens, weights, bias_table)

    top_grad = mine(out_grad)
    in_grad, unused = backward(top_grad, stored, weights, bias_table)
    passed = rows_across(in_grad.astype(BF), [(1, 0)])
    top = jnp.where(section == 1, top_grad, passed)
    in_grad, parameter_grads = backward(top, stored, weights, bias_table)
    grads = parameter_grads()

    def both_sequences(full):
        keep = lax.dynamic_slice_in_dim(full, part * rows, rows, 0)
        give = lax.dynamic_slice_in_dim(full, (part ^ 2) * rows, rows, 0)
        got = swap(give, 2)
        return jnp.where(chip == 0, jnp.stack([keep, got]), jnp.stack([got, keep]))

    def owned(grad, axis):
        size = grad.shape[axis] // 2
        keep = lax.slice_in_dim(grad, 0, size, axis=axis)
        give = lax.slice_in_dim(grad, size, 2 * size, axis=axis).astype(BF)
        return dp_sum((keep + swap(give, 2).astype(F32)).astype(BF))

    grad_w_back = owned(grads["w_back"], 0)
    grad_w_in = owned(grads["w_in"], 1)
    grad_w_out = owned(grads["w_out"], 0)
    grad_w_qkv = jnp.stack([owned(v, 1) for v in grads["w_qkv"]])
    biases = jnp.stack(
        [jnp.concatenate([v.reshape(2, -1)[i] for v in grads["b_qv"]] + [grads["b_in"].reshape(2, -1)[i]]) for i in range(2)]
    )
    grad_biases = owned(biases, 0)[0]
    wide = grads["b_qv"][0].shape[0] // 2
    vectors = grads["vectors"].astype(BF)
    vectors = dp_sum((vectors.astype(F32) + swap(vectors, 2).astype(F32)).astype(BF))
    mask = grads["mask"].astype(BF)
    keep = lax.dynamic_slice_in_dim(mask, core * half, half, 0)
    give = lax.dynamic_slice_in_dim(mask, (1 - core) * half, half, 0)
    mask = (keep.astype(F32) + swap(give, 1).astype(F32)).astype(BF)
    mask = dp_sum((mask.astype(F32) + swap(mask, 2).astype(F32)).astype(BF)).astype(BF)
    also = swap(mask, 1)
    mask = jnp.where(core == 0, jnp.concatenate([mask, also]), jnp.concatenate([also, mask]))
    grad_mask = mask.astype(F32) * jax.nn.sigmoid(-mask_input)
    results = (
        both_sequences(second),
        both_sequences(in_grad.astype(BF)).astype(F32),
        grad_w_qkv,
        grad_biases[: 2 * wide].reshape(2, wide),
        grad_w_out,
        vectors[0], vectors[1], vectors[2],
        grad_w_in,
        grad_biases[2 * wide :],
        grad_w_back,
        vectors[3], vectors[4], vectors[5],
        grad_mask,
    )
    return tuple(item[None] for item in results)


def solution(mesh):
    placed = (
        P("dp", None, None),
        P("dp", None, None),
        P("dp", None),
        P("pipe", None, None, "tensor"),
        P("pipe", None, "tensor"),
        P("pipe", "tensor", None),
        P("pipe", None),
        P("pipe", None),
        P("pipe", None),
        P("pipe", None, "tensor"),
        P("pipe", "tensor"),
        P("pipe", "tensor", None),
        P("pipe", None),
        P("pipe", None),
        P("pipe", None),
        P("pipe", None, None),
        P("pipe", None, None),
    )
    return jax.shard_map(
        shards,
        mesh=mesh,
        in_specs=placed,
        out_specs=(
            P("pipe", "dp", "tensor", None),
            P("pipe", "dp", "tensor", None),
            P("pipe", None, None, "tensor"),
            P("pipe", None, "tensor"),
            P("pipe", "tensor", None),
            P("pipe", None),
            P("pipe", None),
            P("pipe", None),
            P("pipe", None, "tensor"),
            P("pipe", "tensor"),
            P("pipe", "tensor", None),
            P("pipe", None),
            P("pipe", None),
            P("pipe", None),
            P("pipe", None, None),
        ),
        check_vma=False,
    )
```

```python
import functools
import math

import jax
import jax.numpy as jnp
from jax import lax
from jax.experimental import pallas as pl
from jax.experimental.pallas import tpu as pltpu
from jax.sharding import Mesh
from jax.sharding import PartitionSpec as P

HEAD_DIM = 64
EPSILON = 1e-12
MASKED = -1e30
BF = jnp.bfloat16
F32 = jnp.float32
NT = ((1,), (1,))
TN = ((0,), (0,))
NN = ((1,), (0,))
PARTS = 4
PAD = 16
TENSOR = ("chip", "core")


def dot(left, right, dims=NN):
    return lax.dot_general(left, right, (dims, ((), ())), preferred_element_type=F32)


def swap(block, axis):
    return lax.ppermute(block, axis, [(i, i ^ 1) for i in range(lax.axis_size(axis))])


SMEM = pl.BlockSpec(memory_space=pltpu.SMEM)
VMEM = pl.BlockSpec(memory_space=pltpu.VMEM)
ANY = pl.BlockSpec(memory_space=pl.ANY)


def shape(*dims, dtype=BF):
    return jax.ShapeDtypeStruct(dims, dtype)


def call(kernel, out, ins, args, scratch=(), flops=0, moved=0):
    return pl.pallas_call(
        kernel,
        out_shape=out,
        in_specs=ins,
        out_specs=jax.tree.map(lambda _: VMEM, out),
        scratch_shapes=list(scratch),
        compiler_params=pltpu.CompilerParams(vmem_limit_bytes=52 << 20),
        cost_estimate=pl.CostEstimate(flops=flops, bytes_accessed=moved, transcendentals=0),
    )(*args)


def longest_start(info, lengths, docs):
    chip = info[1]
    sizes = [lengths[chip, i] for i in range(docs)]
    bounds, start, total = [], jnp.int32(0), jnp.int32(0)
    longest = sizes[0]
    for size in sizes[1:]:
        longest = jnp.maximum(longest, size)
    for size in sizes:
        start = jnp.where(size == longest, total, start)
        total = total + size
        bounds.append(total)
    return start, bounds


def prepare_kernel(docs, info, lengths, inputs, grads, logits, noise, tokens_out, top_out, bias_out):
    seq = logits.shape[0]
    half = seq // 2
    start, bounds = longest_start(info, lengths, docs)
    begin = lax.rem(start + half * info[0], seq)
    shift = lax.rem(seq - begin, seq)
    tokens_out[...] = pltpu.roll(inputs[info[1]].astype(F32), shift, 0)[:half].astype(BF)
    top_out[...] = pltpu.roll(grads[info[1]].astype(F32), shift, 0)[:half].astype(BF)
    table = logits[...] + noise[...]
    table = pltpu.roll(table, shift, 0)[:half]
    table = pltpu.roll(table, shift, 1)[:, :half]
    term = jnp.minimum(table, 0.0) - jnp.log1p(jnp.exp(-jnp.abs(table)))

    def owners(axis):
        place = begin + lax.broadcasted_iota(jnp.int32, (half, half), axis)
        place = jnp.where(place >= seq, place - seq, place)
        owner = jnp.zeros((half, half), jnp.int32)
        for bound in bounds:
            owner = owner + jnp.where(place >= bound, 1, 0)
        return owner

    bias_out[...] = jnp.where(owners(0) == owners(1), term, MASKED).T


def norm(values):
    average = jnp.mean(values, axis=-1, keepdims=True)
    centred = values - average
    variance = jnp.mean(centred * centred, axis=-1, keepdims=True)
    scale = lax.rsqrt(variance + EPSILON)
    return centred * scale, scale


def norm_back(grad, unit, scale, gain):
    direct = grad * gain
    return scale * (
        direct
        - jnp.mean(direct, axis=-1, keepdims=True)
        - unit * jnp.mean(direct * unit, axis=-1, keepdims=True)
    )


class Copies:
    def __init__(self, sems):
        self.sems, self.used, self.waits = sems, 0, {}

    def start(self, name, src, dst):
        copy = pltpu.make_async_copy(src, dst, self.sems.at[self.used])
        self.used += 1
        copy.start()
        self.waits.setdefault(name, []).append(copy)

    def pick(self, name, flag, zero, one, dst):
        sem = self.sems.at[self.used]
        self.used += 1

        @pl.when(flag == 0)
        def _():
            pltpu.make_async_copy(zero, dst, sem).start()

        @pl.when(flag != 0)
        def _():
            pltpu.make_async_copy(one, dst, sem).start()

        self.waits.setdefault(name, []).append(pltpu.make_async_copy(zero, dst, sem))

    def wait(self, name):
        for copy in self.waits.pop(name):
            copy.wait()


def load_qkv(copies, odd, pieces, w_scr, b_in_scr, b_qv_scr):
    head = w_scr.shape[1] // PARTS
    plan = [(0, 0, 0, head), (0, head, 1, head), (0, 2 * head, None, PAD)]
    plan += [(1, 0, 2, head), (1, head, 3, head), (1, 2 * head, None, PAD)]
    step = 2 * head + PAD
    for part in range(PARTS):
        for which, row, to, count in plan:
            if to is None:
                dst = (b_in_scr if which == 0 else b_qv_scr).at[part]
            else:
                dst = w_scr.at[to, pl.ds(part * head, count)]
            name = "qkv" if to != 3 else "out"
            if part < 2:
                copies.start(name, pieces[part].at[pl.ds(which * step + row, count)], dst)
            else:
                got, also = pieces[2 * part - 2], pieces[2 * part - 1]
                zero, one = (got, also) if which == 0 else (also, got)
                src = [v.at[pl.ds(row, count)] for v in (zero, one)]
                copies.pick(name, odd, src[0], src[1], dst)


def load_halves(copies, name, odd, got, also, dst):
    size = got.shape[0]
    copies.pick(name, odd, got, also, dst.at[pl.ds(0, size)])
    copies.pick(name, odd, also, got, dst.at[pl.ds(size, size)])


def load_in(copies, odd, pieces, w_scr, parts):
    for part in parts:
        if part < 2:
            copies.start(f"in{part}", pieces[part], w_scr.at[part])
        else:
            load_halves(copies, f"in{part}", odd, pieces[2 * part - 2], pieces[2 * part - 1], w_scr.at[part])


def load_back(copies, pieces, w_scr, parts):
    for part in parts:
        copies.start(f"back{part}", pieces[part], w_scr.at[part])


def attention_forward(tokens, bias, w_scr, b_qv_scr, out_parts):
    width = tokens.shape[1]
    head = width // PARTS
    b_q = jnp.concatenate([b_qv_scr[p, 0:1, :head] for p in range(PARTS)], axis=1).astype(F32)
    b_v = jnp.concatenate([b_qv_scr[p, 0:1, head : 2 * head] for p in range(PARTS)], axis=1).astype(F32)
    queries = (dot(tokens, w_scr[0], NT) + b_q).astype(BF)
    keys = dot(tokens, w_scr[1], NT).astype(BF)
    values = (dot(tokens, w_scr[2], NT) + b_v).astype(BF)
    values_t = values.T
    if out_parts is not None:
        q_out, k_out, v_out, kt_out, p_out = out_parts
        q_out[...], k_out[...], v_out[...] = queries, keys, values
        kt_out[...] = keys.T
    scaled = queries * jnp.asarray(1.0 / math.sqrt(HEAD_DIM), BF)
    pair = 2 * HEAD_DIM
    lane = lax.broadcasted_iota(jnp.int32, (tokens.shape[0], pair), 1)
    attended = []
    for j in range(width // pair):
        q_pair = scaled[:, j * pair : (j + 1) * pair]
        k_pair = keys[:, j * pair : (j + 1) * pair]
        for s in range(2):
            mine = (lane >= HEAD_DIM) if s else (lane < HEAD_DIM)
            scores = dot(jnp.where(mine, k_pair, jnp.zeros_like(k_pair)), q_pair, NT) + bias
            exponent = jnp.exp(scores - jnp.max(scores, axis=0, keepdims=True))
            chance = (exponent * (1.0 / jnp.sum(exponent, axis=0, keepdims=True))).astype(BF)
            h = 2 * j + s
            if out_parts is not None:
                p_out[h] = chance
            attended.append(dot(values_t[h * HEAD_DIM : (h + 1) * HEAD_DIM], chance).astype(BF))
    return jnp.concatenate(attended, axis=0).T


def gelu(values):
    cdf = 0.5 * (1.0 + lax.erf(values * math.sqrt(0.5)))
    return values * cdf, cdf


def ffn_forward(first_low, total, parts, copies, w_in, w_back, b_in, hidden_out, slope_out):
    width = first_low.shape[1]
    units = w_in.shape[2]
    for part in parts:
        copies.wait(f"in{part}")
        pre = dot(first_low, w_in[part]) + b_in[part, 0:1, :].astype(F32)
        value, cdf = gelu(pre)
        hidden = value.astype(BF)
        if hidden_out is not None:
            hidden_out[:, part * units : (part + 1) * units] = hidden
            density = jnp.exp(-0.5 * pre * pre) * (1.0 / math.sqrt(2.0 * math.pi))
            slope_out[:, part * units : (part + 1) * units] = (cdf + pre * density).astype(BF)
        copies.wait(f"back{part}")
        total = total + dot(hidden, w_back[part])
    return total


def attention_kernel(info, tokens, bias, b_out, gain, offset, *rest):
    pieces, (first_out, w_scr, b_in_scr, b_qv_scr, sems) = rest[:6], rest[6:]
    copies = Copies(sems)
    load_qkv(copies, info[2], pieces, w_scr, b_in_scr, b_qv_scr)
    copies.wait("qkv")
    attended = attention_forward(tokens[...], bias[...], w_scr, b_qv_scr, None)
    copies.wait("out")
    unit, _ = norm(tokens[...].astype(F32) + dot(attended, w_scr[3]) + b_out[...])
    first_out[...] = unit * gain[...] + offset[...]


def ffn_kernel(parts, finish, info, first, total, vec_back, gain, offset, *rest):
    count = len(parts)
    if finish:
        p1, w_ins, w_backs, tail = rest[:4], rest[4:8], rest[8:10], rest[10:]
    else:
        p1, w_ins, w_backs, tail = rest[:2], rest[2:4], rest[4:6], rest[6:]
    out, w_in, w_back, b_in, sems = tail
    copies = Copies(sems)
    step = p1[0].shape[0] // (1 if finish else 2)
    for i in range(count):
        if finish:
            src = [v.at[pl.ds(step - PAD, PAD)] for v in (p1[2 * i], p1[2 * i + 1])]
            copies.pick("bias", info[2], src[0], src[1], b_in.at[i])
            load_halves(copies, f"in{i}", info[2], w_ins[2 * i], w_ins[2 * i + 1], w_in.at[i])
        else:
            copies.start("bias", p1[i].at[pl.ds(step - PAD, PAD)], b_in.at[i])
            copies.start(f"in{i}", w_ins[i], w_in.at[i])
        copies.start(f"back{i}", w_backs[i], w_back.at[i])
    copies.wait("bias")
    first_low = first[...].astype(BF)
    start = total[...] if finish else first[...] + vec_back[...]
    result = ffn_forward(first_low, start, range(count), copies, w_in, w_back, b_in, None, None)
    if finish:
        unit, _ = norm(result)
        out[...] = (unit * gain[...] + offset[...]).astype(BF)
    else:
        out[...] = result


def layer_kernel(info, first_tokens, passed, bias, b_out, gain_one, offset_one, b_back, gain_two, offset_two, *rest):
    p1, w_ins, w_backs, rest = rest[:6], rest[6:12], rest[12:16], rest[16:]
    (second_out, tokens_out, q_out, k_out, v_out, kt_out, p_out, att_out, unit1_out, scale1_out, first_out,
     hidden_out, slope_out, unit2_out, scale2_out, w_scr, w_in, w_back, b_in, b_qv, sems) = rest
    copies = Copies(sems)
    load_qkv(copies, info[2], p1, w_scr, b_in, b_qv)
    for part in range(PARTS):
        load_in(copies, info[2], w_ins, w_in, [part])
        load_back(copies, w_backs, w_back, [part])
    tokens = jnp.where(info[3] == 0, first_tokens[...], passed[...])
    tokens_out[...] = tokens
    copies.wait("qkv")
    attended = attention_forward(tokens, bias[...], w_scr, b_qv, (q_out, k_out, v_out, kt_out, p_out))
    att_out[...] = attended
    copies.wait("out")
    unit, scale = norm(tokens.astype(F32) + dot(attended, w_scr[3]) + b_out[...])
    unit1_out[...] = unit
    scale1_out[...] = jnp.broadcast_to(scale, scale1_out.shape)
    first = unit * gain_one[...] + offset_one[...]
    first_low = first.astype(BF)
    first_out[...] = first_low
    total = ffn_forward(
        first_low, first + b_back[...], range(PARTS), copies, w_in, w_back, b_in, hidden_out, slope_out
    )
    unit, scale = norm(total)
    unit2_out[...] = unit
    scale2_out[...] = jnp.broadcast_to(scale, scale2_out.shape)
    second_out[...] = (unit * gain_two[...] + offset_two[...]).astype(BF)


def rows_sum(values):
    return jnp.sum(values, axis=0, keepdims=True)


def ffn_backward(top, unit, scale, gain, slope, copies, w_in, w_back, pre_out, ffn_out):
    units = w_in.shape[2]
    sum_grad = norm_back(top, unit, scale, gain)
    ffn_low = sum_grad.astype(BF)
    if ffn_out is not None:
        ffn_out[...] = ffn_low
    first_grad = sum_grad
    for part in range(PARTS):
        copies.wait(f"back{part}")
        pre = dot(ffn_low, w_back[part], NT) * slope[:, part * units : (part + 1) * units].astype(F32)
        pre = pre.astype(BF)
        if pre_out is not None:
            pre_out[:, part * units : (part + 1) * units] = pre
        copies.wait(f"in{part}")
        first_grad = first_grad + dot(pre, w_in[part], NT)
    return sum_grad, first_grad


def attention_backward(first_grad, unit, scale, gain, refs, w_scr, copies, dqt_scr, outs):
    q_ref, k_ref, v_ref, kt_ref, p_ref = refs
    width = first_grad.shape[1]
    branch = norm_back(first_grad, unit, scale, gain)
    branch_low = branch.astype(BF)
    copies.wait("out")
    att_grad = dot(branch_low, w_scr[3], NT).astype(BF)
    pair = 2 * HEAD_DIM
    rows = first_grad.shape[0]
    lane = lax.broadcasted_iota(jnp.int32, (rows, pair), 1)
    term = jnp.zeros((rows, rows), F32)
    root = 1.0 / math.sqrt(HEAD_DIM)
    keys_grad, values_grad = [], []
    for j in range(width // pair):
        here = slice(j * pair, (j + 1) * pair)
        q_pair, v_pair, o_pair = q_ref[:, here], v_ref[:, here], att_grad[:, here]
        dk, dv = [], []
        for s in range(2):
            h = 2 * j + s
            mine = (lane >= HEAD_DIM) if s else (lane < HEAD_DIM)
            chance_low = p_ref[h]
            chance = chance_low.astype(F32)
            chance_grad = dot(jnp.where(mine, v_pair, jnp.zeros_like(v_pair)), o_pair, NT)
            inner = jnp.sum(chance * chance_grad, axis=0, keepdims=True)
            score = chance * (chance_grad - inner)
            term = term + score
            low = score.astype(BF)
            dv.append(dot(chance_low, o_pair))
            dk.append(dot(low, q_pair))
            dqt_scr[h * HEAD_DIM : (h + 1) * HEAD_DIM] = dot(kt_ref[h * HEAD_DIM : (h + 1) * HEAD_DIM], low) * root
        keys_grad.append((jnp.where(lane < HEAD_DIM, dk[0], dk[1]) * root).astype(BF))
        values_grad.append(jnp.where(lane < HEAD_DIM, dv[0], dv[1]).astype(BF))
    dq = dqt_scr[...].T.astype(BF)
    dk = jnp.concatenate(keys_grad, axis=1)
    dv = jnp.concatenate(values_grad, axis=1)
    copies.wait("qkv")
    in_grad = branch + dot(dq, w_scr[0]) + dot(dk, w_scr[1]) + dot(dv, w_scr[2])
    if outs is not None:
        branch_out, dq_out, dk_out, dv_out, term_out = outs
        branch_out[...] = branch_low
        dq_out[...], dk_out[...], dv_out[...] = dq, dk, dv
        term_out[...] = term
    return branch, in_grad


def down_kernel(info, top, unit1, scale1, gain_one, unit2, scale2, gain_two, slope, q_ref, k_ref, v_ref, kt_ref, p_ref, *rest):
    p1, w_ins, w_backs, rest = rest[:6], rest[6:12], rest[12:16], rest[16:]
    grad_out, w_scr, w_in, w_back, b_in, b_qv, dqt_scr, sems = rest
    copies = Copies(sems)
    for part in range(PARTS):
        load_back(copies, w_backs, w_back, [part])
        load_in(copies, info[2], w_ins, w_in, [part])
    load_qkv(copies, info[2], p1, w_scr, b_in, b_qv)
    sum_grad, first_grad = ffn_backward(
        top[...].astype(F32), unit2[...], scale2[:, :1], gain_two[...], slope, copies, w_in, w_back, None, None
    )
    branch, in_grad = attention_backward(
        first_grad, unit1[...], scale1[:, :1], gain_one[...], (q_ref, k_ref, v_ref, kt_ref, p_ref),
        w_scr, copies, dqt_scr, None,
    )
    grad_out[...] = in_grad.astype(BF)


def down_ffn_kernel(info, own_top, passed, unit2, scale2, gain_two, slope, *rest):
    w_ins, w_backs, rest = rest[:6], rest[6:10], rest[10:]
    ffn_out, pre_out, first_grad_out, sums_out, w_in, w_back, sems = rest
    copies = Copies(sems)
    for part in range(PARTS):
        load_back(copies, w_backs, w_back, [part])
        load_in(copies, info[2], w_ins, w_in, [part])
    top = jnp.where(info[3] == 0, passed[...], own_top[...]).astype(F32)
    unit = unit2[...]
    sum_grad, first_grad = ffn_backward(
        top, unit, scale2[:, :1], gain_two[...], slope, copies, w_in, w_back, pre_out, ffn_out
    )
    first_grad_out[...] = first_grad
    sums_out[...] = jnp.zeros_like(sums_out)
    sums_out[3:4] = rows_sum(sum_grad)
    sums_out[4:5] = rows_sum(top * unit)
    sums_out[5:6] = rows_sum(top)
    units = w_in.shape[2]
    place = 2 * info[1] + info[0]
    for part in range(PARTS):
        sums = rows_sum(pre_out[:, part * units : (part + 1) * units].astype(F32))
        sums_out[pl.ds(6 + jnp.bitwise_xor(place, part), 1)] = sums


def down_attention_kernel(info, first_grad, sums, unit1, scale1, gain_one, q_ref, k_ref, v_ref, kt_ref, p_ref, *rest):
    p1, rest = rest[:6], rest[6:]
    (grad_out, branch_out, dq_out, dk_out, dv_out, term_out, sums_out,
     w_scr, b_in, b_qv, dqt_scr, sems) = rest
    copies = Copies(sems)
    load_qkv(copies, info[2], p1, w_scr, b_in, b_qv)
    unit = unit1[...]
    grad = first_grad[...]
    branch, in_grad = attention_backward(
        grad, unit, scale1[:, :1], gain_one[...], (q_ref, k_ref, v_ref, kt_ref, p_ref),
        w_scr, copies, dqt_scr, (branch_out, dq_out, dk_out, dv_out, term_out),
    )
    grad_out[...] = in_grad.astype(BF)
    sums_out[...] = sums[...]
    sums_out[0:1] = rows_sum(branch)
    sums_out[1:2] = rows_sum(grad * unit)
    sums_out[2:3] = rows_sum(grad)
    width = grad.shape[1]
    head = width // PARTS
    place = 2 * info[1] + info[0]
    dq_sum, dv_sum = rows_sum(dq_out[...].astype(F32)), rows_sum(dv_out[...].astype(F32))
    for part in range(PARTS):
        here = slice(part * head, (part + 1) * head)
        row = jnp.concatenate(
            [dq_sum[:, here], dv_sum[:, here], jnp.zeros((1, width - 2 * head), F32)], axis=1
        )
        sums_out[pl.ds(10 + jnp.bitwise_xor(place, part), 1)] = row


def mask_kernel(docs, info, lengths, own, other, out, scr):
    half = own.shape[0]
    seq = 2 * half
    start, _ = longest_start(info, lengths, docs)
    mine, theirs = own[...].astype(F32).T, other[...].astype(F32).T
    zero = jnp.zeros_like(mine)
    low = info[0] == 0
    scr[:half, :half] = jnp.where(low, mine, theirs)
    scr[half:, half:] = jnp.where(low, theirs, mine)
    scr[:half, half:] = zero
    scr[half:, :half] = zero
    full = pltpu.roll(scr[...], lax.rem(start + half * (1 - info[0]) + half, seq), 0)[:half]
    full = pltpu.roll(full, start, 1).astype(BF)
    out[...] = jnp.zeros_like(out)
    for row, column, source_row, source_column, count in packing(half):
        out[row : row + count, column : column + half] = full[
            source_row : source_row + count, source_column : source_column + half
        ]


def packing(half):
    rows = packed_rows(half)
    moves = []
    for piece in range(2):
        done = 0
        while done < half:
            place = piece * half + done
            count = min(half - done, rows - place % rows)
            moves.append((place % rows, place // rows * half, done, piece * half, count))
            done += count
    return moves


def packed_rows(half):
    return -(-2 * half // (3 * PAD)) * PAD


def mask_out_kernel(info, own, other, logits, noise, out):
    half = logits.shape[0] // 2
    low = info[0] == 0
    first = jnp.where(low, own[...], other[...])
    second = jnp.where(low, other[...], own[...])
    for base, block in ((0, first), (half, second)):
        for row, column, to_row, to_column, count in packing(half):
            here = (slice(base + to_row, base + to_row + count), slice(to_column, to_column + half))
            slope = 1.0 / (1.0 + jnp.exp(logits[here] + noise[here]))
            out[here] = block[row : row + count, column : column + half].astype(F32) * slope


def rows_kernel(docs, info, lengths, own, other, keep_out, give_out, scr):
    half = own.shape[0]
    seq = 2 * half
    rows = seq // PARTS
    start, _ = longest_start(info, lengths, docs)
    low = info[0] == 0
    mine, theirs = own[...].astype(F32), other[...].astype(F32)
    scr[:half] = jnp.where(low, mine, theirs)
    scr[half:] = jnp.where(low, theirs, mine)
    place = 2 * info[1] + info[0]
    far = 2 * (1 - info[1]) + info[0]
    keep_out[...] = pltpu.roll(scr[...], lax.rem(start + seq - place * rows, seq), 0)[:rows].astype(BF)
    give_out[...] = pltpu.roll(scr[...], lax.rem(start + seq - far * rows, seq), 0)[:rows].astype(BF)


class Order:
    def __init__(self):
        self.last = None

    def run(self, step, *inputs):
        if self.last is not None:
            *inputs, _ = lax.optimization_barrier((*inputs, self.last))
        result = step(*inputs)
        self.last = jax.tree.leaves(result)[0]
        return result


def added(left, right):
    return (left.astype(F32) + right.astype(F32)).astype(BF)


class Reduction:
    def __init__(self, order):
        self.order = order
        self.line = lax.axis_size("dp") == 4
        place = lax.axis_index("dp")
        self.middle = (place == 1) | (place == 2)
        self.stage, self.sent, self.kept, self.done = {}, {}, {}, {}

    def put(self, name, give, keep):
        self.stage[name], self.sent[name], self.kept[name] = 0, swap(give, "chip"), keep

    def step(self, name):
        stage = self.stage[name]
        self.stage[name] = stage + 1
        if stage < 3:
            self.kept[name] = self.order.run(added, self.kept[name], self.sent[name])
            if not self.line:
                self.sent[name] = lax.psum(self.kept[name], "dp") if stage == 0 else None
                if stage == 0:
                    self.done[name] = self.sent[name]
                    self.stage[name] = 4
                return
            routes = ([(0, 1), (3, 2)], [(1, 2), (2, 1)], [(1, 0), (2, 3)])
            self.sent[name] = lax.ppermute(self.kept[name], "dp", routes[stage])
        elif stage == 3:
            self.done[name] = jnp.where(self.middle, self.kept[name], self.sent[name])

    def finish(self):
        names = list(self.stage)
        while any(self.stage[n] < 4 for n in names):
            waiting = [n for n in names if self.stage[n] < 4]
            front = waiting[0]
            group = [n for n in waiting if self.stage[n] > 0] + [n for n in waiting if self.stage[n] == 0][:1]
            for n in reversed(group):
                self.step(n)
        return self.done


def shards(
    inputs, out_grad, doc_lengths, w_qkv, b_qv, w_out, b_out, norm1_gain, norm1_bias,
    w_in, b_in, w_back, b_back, norm2_gain, norm2_bias, mask_logits, mask_noise,
):
    count, seq, width = inputs.shape
    docs = doc_lengths.shape[1]
    core, chip = lax.axis_index("core"), lax.axis_index("chip")
    odd = lax.axis_index("dp") % 2
    part = 2 * chip + core
    half = seq // 2
    head = w_out.shape[1]
    units = w_in.shape[2]
    assert lax.axis_size("pipe") == 2 and lax.axis_size("chip") == 2 and count == 2
    assert lax.axis_size("dp") % 2 == 0 and PARTS * head == width and seq % (2 * PARTS) == 0
    info = jnp.stack([core, chip, odd, lax.axis_index("pipe")]).astype(jnp.int32)

    qkv = jnp.swapaxes(w_qkv[0], 1, 2).reshape(3 * head, width)
    bias_one = jnp.pad(b_in, ((0, PAD - 1), (0, width - units)))
    bias_two = jnp.pad(b_qv[0].reshape(1, 2 * head), ((0, PAD - 1), (0, width - 2 * head)))
    pack = jnp.concatenate([qkv[: 2 * head], bias_one, qkv[2 * head :], w_out[0], bias_two])
    own = [pack, w_in[0], w_back[0]]

    def halved(block):
        size = block.shape[0] // 2
        return lax.dynamic_slice_in_dim(block, odd * size, size, 0)

    got_pack = swap(halved(pack), "chip")
    got_in = swap(halved(w_in[0]), "chip")
    also_pack = swap(got_pack, "dp")
    w_back_own, got_pack = lax.optimization_barrier((w_back[0], got_pack))
    got_back = swap(w_back_own, "chip")
    also_in = swap(got_in, "dp")
    near = [swap(v, "core") for v in own]
    p1 = (pack, near[0], got_pack, also_pack, swap(got_pack, "core"), swap(also_pack, "core"))
    w_ins = (w_in[0], near[1], got_in, also_in, swap(got_in, "core"), swap(also_in, "core"))
    w_backs = (w_back[0], near[2], got_back, swap(got_back, "core"))

    tokens0, top0, bias = call(
        functools.partial(prepare_kernel, docs),
        [shape(half, width), shape(half, width), shape(half, half, dtype=F32)],
        [SMEM, SMEM, VMEM, VMEM, VMEM, VMEM],
        (info, doc_lengths, inputs, out_grad, mask_logits[0], mask_noise[0]),
    )
    w4 = pltpu.VMEM((4, width, width), BF)
    w_in_scr = pltpu.VMEM((PARTS, width, units), BF)
    w_back_scr = pltpu.VMEM((PARTS, units, width), BF)
    b_scr = pltpu.VMEM((PARTS, PAD, width), BF)
    layer_flops = 2 * half * width * (4 * width + 2 * PARTS * units)
    layer_bytes = 2 * (4 * width * width + 2 * PARTS * units * width)

    def sems(n):
        return pltpu.SemaphoreType.DMA((n,))

    first = call(
        attention_kernel,
        shape(half, width, dtype=F32),
        [SMEM] + [VMEM] * 5 + [ANY] * 6,
        (info, tokens0, bias, b_out, norm1_gain, norm1_bias) + p1,
        [w4, b_scr, b_scr, sems(24)],
        layer_flops // 3, layer_bytes // 3,
    )

    def ffn(parts, finish, total, p1_part, in_part, back_part):
        n = len(parts)
        return call(
            functools.partial(ffn_kernel, parts, finish),
            shape(half, width, dtype=BF if finish else F32),
            [SMEM] + [VMEM] * 5 + [ANY] * (len(p1_part) + len(in_part) + len(back_part)),
            (info, first, total, b_back, norm2_gain, norm2_bias) + p1_part + in_part + back_part,
            [pltpu.VMEM((n, width, units), BF), pltpu.VMEM((n, units, width), BF),
             pltpu.VMEM((n, PAD, width), BF), sems(4 * n)],
            layer_flops // 3, layer_bytes // 3,
        )

    total = ffn((0, 1), False, first, p1[:2], w_ins[:2], w_backs[:2])
    second = ffn((2, 3), True, total, p1[2:], w_ins[2:], w_backs[2:])
    passed = lax.ppermute(second, "pipe", [(0, 1)])
    (second, tokens, q, k, v, kt, chance, attended, unit1, scale1, first_low, hidden, slope, unit2, scale2) = call(
        layer_kernel,
        [
            shape(half, width), shape(half, width), shape(half, width), shape(half, width), shape(half, width),
            shape(width, half), shape(width // HEAD_DIM, half, half), shape(half, width),
            shape(half, width, dtype=F32), shape(half, 128, dtype=F32), shape(half, width),
            shape(half, PARTS * units), shape(half, PARTS * units),
            shape(half, width, dtype=F32), shape(half, 128, dtype=F32),
        ],
        [SMEM] + [VMEM] * 9 + [ANY] * 16,
        (info, tokens0, passed, bias, b_out, norm1_gain, norm1_bias, b_back, norm2_gain, norm2_bias)
        + p1 + w_ins + w_backs,
        [w4, w_in_scr, w_back_scr, b_scr, b_scr, sems(36)],
        layer_flops, layer_bytes,
    )
    dqt = pltpu.VMEM((width, half), F32)
    down = call(
        down_kernel,
        shape(half, width),
        [SMEM] + [VMEM] * 13 + [ANY] * 16,
        (info, top0, unit1, scale1, norm1_gain, unit2, scale2, norm2_gain, slope, q, k, v, kt, chance)
        + p1 + w_ins + w_backs,
        [w4, w_in_scr, w_back_scr, b_scr, b_scr, dqt, sems(36)],
        layer_flops, layer_bytes,
    )
    passed = lax.ppermute(down, "pipe", [(1, 0)])
    ffn_low, pre_low, first_grad, sums = call(
        down_ffn_kernel,
        [shape(half, width), shape(half, PARTS * units), shape(half, width, dtype=F32),
         shape(PAD, width, dtype=F32)],
        [SMEM] + [VMEM] * 6 + [ANY] * 10,
        (info, top0, passed, unit2, scale2, norm2_gain, slope) + w_ins + w_backs,
        [w_in_scr, w_back_scr, sems(12)],
        layer_flops * 2 // 3, layer_bytes * 2 // 3,
    )

    def down_attention(first_grad, sums):
        return call(
            down_attention_kernel,
            [shape(half, width), shape(half, width), shape(half, width), shape(half, width), shape(half, width),
             shape(half, half, dtype=F32), shape(PAD, width, dtype=F32)],
            [SMEM] + [VMEM] * 10 + [ANY] * 6,
            (info, first_grad, sums, unit1, scale1, norm1_gain, q, k, v, kt, chance) + p1,
            [w4, b_scr, b_scr, dqt, sems(24)],
            layer_flops // 2, layer_bytes // 3,
        )


    def whole_rows(own_rows, got):
        return jnp.concatenate([own_rows, got])

    def odd_parts(arrays, size):
        return jnp.concatenate([a[:, i * size : (i + 1) * size] for i in (1, 3) for a in arrays], axis=1)

    def owned_parts(arrays, got, size):
        middle = got.shape[1] // 2
        return [
            jnp.concatenate(
                [
                    jnp.concatenate([a[:, i * size : (i + 1) * size] for a in arrays], axis=1),
                    got[:, (i // 2) * middle : (i // 2 + 1) * middle],
                ]
            )
            for i in (0, 2)
        ]

    tokens_all, first_all = (whole_rows(v, swap(v, "core")) for v in (tokens, first_low))
    hidden_mine, hidden_far = owned_parts([hidden], swap(odd_parts([hidden], units), "core"), units)
    attended_mine, attended_far = owned_parts([attended], swap(odd_parts([attended], head), "core"), head)

    order = Order()
    red = Reduction(order)
    rows_cut = width // 2

    def grads(left, right):
        return dot(left, right, TN)

    def grads_low(left, right):
        return dot(left, right, TN).astype(BF)

    def put(name, give, keep, pieces):
        size = give.shape[0] // pieces
        for i in range(pieces):
            red.put(f"{name}{i}", give[i * size : (i + 1) * size], keep[i * size : (i + 1) * size])

    got_ffn = swap(ffn_low, "core")
    got_pre = swap(odd_parts([pre_low], units), "core")
    ffn_all = whole_rows(ffn_low, got_ffn)
    pre_mine, pre_far = owned_parts([pre_low], got_pre, units)
    give = order.run(grads_low, hidden_far, ffn_all)
    keep = order.run(grads, hidden_mine, ffn_all)
    put("back", give, keep, 2)
    give = order.run(grads_low, first_all, pre_far)
    keep = order.run(grads, first_all, pre_mine)
    put("in", give, keep, 2)
    in_grad, branch_low, dq, dk, dv, term, sums = order.run(down_attention, first_grad, sums)
    red.step("back0")
    got_branch = swap(branch_low, "core")
    got_projected = swap(odd_parts([dq, dk, dv], head), "core")
    term = term.astype(BF)
    mask = call(
        functools.partial(mask_kernel, docs),
        shape(packed_rows(half), 3 * half),
        [SMEM, SMEM, VMEM, VMEM],
        (info, doc_lengths, term, swap(term, "core")),
        [pltpu.VMEM((seq, seq), F32)],
    )
    branch_all = whole_rows(branch_low, got_branch)
    projected_mine, projected_far = owned_parts([dq, dk, dv], got_projected, head)
    give_out = order.run(grads_low, attended_far, branch_all)
    give_qkv = order.run(grads_low, projected_far, tokens_all)
    red.step("back1")
    red.step("back0")
    keep_out = order.run(grads, attended_mine, branch_all)
    keep_qkv = order.run(grads, projected_mine, tokens_all)
    put("rest", jnp.concatenate([give_out, give_qkv]), jnp.concatenate([keep_out, keep_qkv]), 2)
    small = (sums + swap(sums, "core")).astype(BF)
    last = jnp.concatenate([mask, small])
    put("last", last, last, 1)
    summed = red.finish()
    grad_w_back = jnp.concatenate([summed["back0"], summed["back1"]]).astype(F32)
    grad_w_in = jnp.concatenate([summed["in0"], summed["in1"]]).astype(F32)
    rest = jnp.concatenate([summed["rest0"], summed["rest1"]]).astype(F32)
    grad_w_out = rest[:head]
    grad_w_qkv = jnp.swapaxes(rest[head:].reshape(3, head, width), 1, 2)
    sums = summed["last0"][packed_rows(half) :].astype(F32)
    mask = summed["last0"][: packed_rows(half)]
    grad_mask = call(
        mask_out_kernel,
        shape(seq, seq, dtype=F32),
        [SMEM] + [VMEM] * 4,
        (info, mask, swap(mask, "core"), mask_logits[0], mask_noise[0]),
    )

    def both_sequences(own_rows):
        keep, give = call(
            functools.partial(rows_kernel, docs),
            [shape(seq // PARTS, width)] * 2,
            [SMEM, SMEM, VMEM, VMEM],
            (info, doc_lengths, own_rows, swap(own_rows, "core")),
            [pltpu.VMEM((seq, width), F32)],
        )
        got = swap(give, "chip")
        return jnp.where(chip == 0, jnp.stack([keep, got]), jnp.stack([got, keep]))

    def row(i):
        return lax.dynamic_index_in_dim(sums, i, 0, keepdims=False)

    results = (
        both_sequences(second),
        both_sequences(in_grad).astype(F32),
        grad_w_qkv,
        row(10 + part)[: 2 * head].reshape(2, head),
        grad_w_out,
        sums[0], sums[1], sums[2],
        grad_w_in,
        row(6 + part)[:units],
        grad_w_back,
        sums[3], sums[4], sums[5],
        grad_mask,
    )
    return tuple(item[None] for item in results)


def solution(mesh):
    pipe, dp, tensor = (mesh.shape[name] for name in ("pipe", "dp", "tensor"))
    split = Mesh(mesh.devices.reshape(pipe, dp, tensor // 2, 2), ("pipe", "dp", "chip", "core"))
    placed = (
        P("dp", None, None),
        P("dp", None, None),
        P("dp", None),
        P("pipe", None, None, TENSOR),
        P("pipe", None, TENSOR),
        P("pipe", TENSOR, None),
        P("pipe", None),
        P("pipe", None),
        P("pipe", None),
        P("pipe", None, TENSOR),
        P("pipe", TENSOR),
        P("pipe", TENSOR, None),
        P("pipe", None),
        P("pipe", None),
        P("pipe", None),
        P("pipe", None, None),
        P("pipe", None, None),
    )
    return jax.shard_map(
        shards,
        mesh=split,
        in_specs=placed,
        out_specs=(
            P("pipe", "dp", TENSOR, None),
            P("pipe", "dp", TENSOR, None),
            P("pipe", None, None, TENSOR),
            P("pipe", None, TENSOR),
            P("pipe", TENSOR, None),
            P("pipe", None),
            P("pipe", None),
            P("pipe", None),
            P("pipe", None, TENSOR),
            P("pipe", TENSOR),
            P("pipe", TENSOR, None),
            P("pipe", None),
            P("pipe", None),
            P("pipe", None),
            P("pipe", None, None),
        ),
        check_vma=False,
    )
```

```python
import functools
import math

import jax
import jax.numpy as jnp
from jax import lax
from jax.experimental import pallas as pl
from jax.experimental.pallas import tpu as pltpu
from jax.sharding import Mesh
from jax.sharding import PartitionSpec as P

HEAD_DIM = 64
EPSILON = 1e-12
MASKED = -1e30
BF = jnp.bfloat16
F32 = jnp.float32
NT = ((1,), (1,))
TN = ((0,), (0,))
NN = ((1,), (0,))
PARTS = 4
PAD = 16
TENSOR = ("chip", "core")


def dot(left, right, dims=NN):
    return lax.dot_general(left, right, (dims, ((), ())), preferred_element_type=F32)


def swap(block, axis):
    return lax.ppermute(block, axis, [(i, i ^ 1) for i in range(lax.axis_size(axis))])


SMEM = pl.BlockSpec(memory_space=pltpu.SMEM)
VMEM = pl.BlockSpec(memory_space=pltpu.VMEM)
ANY = pl.BlockSpec(memory_space=pl.ANY)


def shape(*dims, dtype=BF):
    return jax.ShapeDtypeStruct(dims, dtype)


def call(kernel, out, ins, args, scratch=()):
    return pl.pallas_call(
        kernel,
        out_shape=out,
        in_specs=ins,
        out_specs=jax.tree.map(lambda _: VMEM, out),
        scratch_shapes=list(scratch),
        compiler_params=pltpu.CompilerParams(vmem_limit_bytes=52 << 20),
        cost_estimate=pl.CostEstimate(flops=0, bytes_accessed=0, transcendentals=0),
    )(*args)


def longest_start(info, lengths, docs):
    chip = info[1]
    sizes = [lengths[chip, i] for i in range(docs)]
    bounds, start, total = [], jnp.int32(0), jnp.int32(0)
    longest = sizes[0]
    for size in sizes[1:]:
        longest = jnp.maximum(longest, size)
    for size in sizes:
        start = jnp.where(size == longest, total, start)
        total = total + size
        bounds.append(total)
    return start, bounds


def prepare_kernel(docs, info, lengths, inputs, grads, logits, noise, tokens_out, top_out, bias_out):
    seq = logits.shape[0]
    half = seq // 2
    start, bounds = longest_start(info, lengths, docs)
    begin = lax.rem(start + half * info[0], seq)
    shift = lax.rem(seq - begin, seq)
    tokens_out[...] = pltpu.roll(inputs[info[1]].astype(F32), shift, 0)[:half].astype(BF)
    top_out[...] = pltpu.roll(grads[info[1]].astype(F32), shift, 0)[:half].astype(BF)
    table = logits[...] + noise[...]
    table = pltpu.roll(table, shift, 0)[:half]
    table = pltpu.roll(table, shift, 1)[:, :half]
    term = jnp.minimum(table, 0.0) - jnp.log1p(jnp.exp(-jnp.abs(table)))

    def owners(axis):
        place = begin + lax.broadcasted_iota(jnp.int32, (half, half), axis)
        place = jnp.where(place >= seq, place - seq, place)
        owner = jnp.zeros((half, half), jnp.int32)
        for bound in bounds:
            owner = owner + jnp.where(place >= bound, 1, 0)
        return owner

    bias_out[...] = jnp.where(owners(0) == owners(1), term, MASKED).T


def split_kernel(info, qkv, w_out, w_in, b_in, b_qv, pack, half_pack, half_in):
    head = w_out.shape[0]
    step = 2 * head + PAD
    pack[: 2 * head] = qkv[: 2 * head]
    pack[2 * head : step] = jnp.zeros((PAD, pack.shape[1]), BF)
    pack[2 * head : 2 * head + 1, : b_in.shape[1]] = b_in[...]
    pack[step : step + head] = qkv[2 * head :]
    pack[step + head : step + 2 * head] = w_out[...]
    pack[step + 2 * head :] = jnp.zeros((PAD, pack.shape[1]), BF)
    pack[step + 2 * head : step + 2 * head + 1, :head] = b_qv[0:1]
    pack[step + 2 * head : step + 2 * head + 1, head : 2 * head] = b_qv[1:2]
    half_pack[...] = pack[pl.ds(pl.multiple_of(info[2] * step, PAD), step)]
    size = half_in.shape[0]
    half_in[...] = w_in[pl.ds(pl.multiple_of(info[2] * size, size), size)]


def norm(values):
    average = jnp.mean(values, axis=-1, keepdims=True)
    centred = values - average
    variance = jnp.mean(centred * centred, axis=-1, keepdims=True)
    scale = lax.rsqrt(variance + EPSILON)
    return centred * scale, scale


def norm_back(grad, unit, scale, gain):
    direct = grad * gain
    return scale * (
        direct
        - jnp.mean(direct, axis=-1, keepdims=True)
        - unit * jnp.mean(direct * unit, axis=-1, keepdims=True)
    )


class Copies:
    def __init__(self, sems):
        self.sems, self.used, self.waits = sems, 0, {}

    def start(self, name, src, dst):
        copy = pltpu.make_async_copy(src, dst, self.sems.at[self.used])
        self.used += 1
        copy.start()
        self.waits.setdefault(name, []).append(copy)

    def pick(self, name, flag, zero, one, dst):
        sem = self.sems.at[self.used]
        self.used += 1

        @pl.when(flag == 0)
        def _():
            pltpu.make_async_copy(zero, dst, sem).start()

        @pl.when(flag != 0)
        def _():
            pltpu.make_async_copy(one, dst, sem).start()

        self.waits.setdefault(name, []).append(pltpu.make_async_copy(zero, dst, sem))

    def wait(self, name):
        for copy in self.waits.pop(name):
            copy.wait()


def load_qkv(copies, odd, pieces, w_scr, b_in_scr, b_qv_scr):
    head = w_scr.shape[1] // PARTS
    plan = [(0, 0, 0, head), (0, head, 1, head), (0, 2 * head, None, PAD)]
    plan += [(1, 0, 2, head), (1, head, 3, head), (1, 2 * head, None, PAD)]
    step = 2 * head + PAD
    for part in range(PARTS):
        for which, row, to, count in plan:
            if to is None:
                dst = (b_in_scr if which == 0 else b_qv_scr).at[part]
            else:
                dst = w_scr.at[to, pl.ds(part * head, count)]
            name = "qkv" if to != 3 else "out"
            if part < 2:
                copies.start(name, pieces[part].at[pl.ds(which * step + row, count)], dst)
            else:
                got, also = pieces[2 * part - 2], pieces[2 * part - 1]
                zero, one = (got, also) if which == 0 else (also, got)
                src = [v.at[pl.ds(row, count)] for v in (zero, one)]
                copies.pick(name, odd, src[0], src[1], dst)


def load_halves(copies, name, odd, got, also, dst):
    size = got.shape[0]
    copies.pick(name, odd, got, also, dst.at[pl.ds(0, size)])
    copies.pick(name, odd, also, got, dst.at[pl.ds(size, size)])


def load_in(copies, odd, pieces, w_scr, parts):
    for part in parts:
        if part < 2:
            copies.start(f"in{part}", pieces[part], w_scr.at[part])
        else:
            load_halves(copies, f"in{part}", odd, pieces[2 * part - 2], pieces[2 * part - 1], w_scr.at[part])


def load_back(copies, pieces, w_scr, parts):
    for part in parts:
        copies.start(f"back{part}", pieces[part], w_scr.at[part])


def attention_forward(tokens, bias, w_scr, b_qv_scr, out_parts):
    width = tokens.shape[1]
    head = width // PARTS
    b_q = jnp.concatenate([b_qv_scr[p, 0:1, :head] for p in range(PARTS)], axis=1).astype(F32)
    b_v = jnp.concatenate([b_qv_scr[p, 0:1, head : 2 * head] for p in range(PARTS)], axis=1).astype(F32)
    queries = (dot(tokens, w_scr[0], NT) + b_q).astype(BF)
    keys = dot(tokens, w_scr[1], NT).astype(BF)
    values = (dot(tokens, w_scr[2], NT) + b_v).astype(BF)
    values_t = values.T
    if out_parts is not None:
        q_out, k_out, v_out, kt_out, p_out = out_parts
        q_out[...], k_out[...], v_out[...] = queries, keys, values
        kt_out[...] = keys.T
    scaled = queries * jnp.asarray(1.0 / math.sqrt(HEAD_DIM), BF)
    pair = 2 * HEAD_DIM
    lane = lax.broadcasted_iota(jnp.int32, (tokens.shape[0], pair), 1)
    attended = []
    for j in range(width // pair):
        q_pair = scaled[:, j * pair : (j + 1) * pair]
        k_pair = keys[:, j * pair : (j + 1) * pair]
        for s in range(2):
            mine = (lane >= HEAD_DIM) if s else (lane < HEAD_DIM)
            scores = dot(jnp.where(mine, k_pair, jnp.zeros_like(k_pair)), q_pair, NT) + bias
            exponent = jnp.exp(scores - jnp.max(scores, axis=0, keepdims=True))
            chance = (exponent * (1.0 / jnp.sum(exponent, axis=0, keepdims=True))).astype(BF)
            h = 2 * j + s
            if out_parts is not None:
                p_out[h] = chance
            attended.append(dot(values_t[h * HEAD_DIM : (h + 1) * HEAD_DIM], chance).astype(BF))
    return jnp.concatenate(attended, axis=0).T


def gelu(values):
    cdf = 0.5 * (1.0 + lax.erf(values * math.sqrt(0.5)))
    return values * cdf, cdf


def ffn_forward(first_low, total, parts, copies, w_in, w_back, b_in, keep_outs, slope_out):
    width = first_low.shape[1]
    units = w_in.shape[2]
    for part in parts:
        copies.wait(f"in{part}")
        pre = dot(first_low, w_in[part]) + b_in[part, 0:1, :units].astype(F32)
        value, cdf = gelu(pre)
        hidden = value.astype(BF)
        if keep_outs is not None:
            keep_outs[part][:, :units] = hidden
            density = jnp.exp(-0.5 * pre * pre) * (1.0 / math.sqrt(2.0 * math.pi))
            slope_out[:, part * units : (part + 1) * units] = (cdf + pre * density).astype(BF)
        copies.wait(f"back{part}")
        total = total + dot(hidden, w_back[part])
    return total


def attention_kernel(info, tokens, bias, b_out, gain, offset, *rest):
    pieces, (first_out, w_scr, b_in_scr, b_qv_scr, sems) = rest[:6], rest[6:]
    copies = Copies(sems)
    load_qkv(copies, info[2], pieces, w_scr, b_in_scr, b_qv_scr)
    copies.wait("qkv")
    attended = attention_forward(tokens[...], bias[...], w_scr, b_qv_scr, None)
    copies.wait("out")
    unit, _ = norm(tokens[...].astype(F32) + dot(attended, w_scr[3]) + b_out[...])
    first_out[...] = unit * gain[...] + offset[...]


def ffn_kernel(parts, finish, info, first, total, vec_back, gain, offset, *rest):
    count = len(parts)
    if finish:
        p1, w_ins, w_backs, tail = rest[:4], rest[4:8], rest[8:10], rest[10:]
    else:
        p1, w_ins, w_backs, tail = rest[:2], rest[2:4], rest[4:6], rest[6:]
    out, w_in, w_back, b_in, sems = tail
    copies = Copies(sems)
    step = p1[0].shape[0] // (1 if finish else 2)
    for i in range(count):
        if finish:
            src = [v.at[pl.ds(step - PAD, PAD)] for v in (p1[2 * i], p1[2 * i + 1])]
            copies.pick("bias", info[2], src[0], src[1], b_in.at[i])
            load_halves(copies, f"in{i}", info[2], w_ins[2 * i], w_ins[2 * i + 1], w_in.at[i])
        else:
            copies.start("bias", p1[i].at[pl.ds(step - PAD, PAD)], b_in.at[i])
            copies.start(f"in{i}", w_ins[i], w_in.at[i])
        copies.start(f"back{i}", w_backs[i], w_back.at[i])
    copies.wait("bias")
    first_low = first[...].astype(BF)
    start = total[...] if finish else first[...] + vec_back[...]
    result = ffn_forward(first_low, start, range(count), copies, w_in, w_back, b_in, None, None)
    if finish:
        unit, _ = norm(result)
        out[...] = (unit * gain[...] + offset[...]).astype(BF)
    else:
        out[...] = result


def layer_kernel(info, first_tokens, passed, bias, b_out, gain_one, offset_one, b_back, gain_two, offset_two, *rest):
    p1, w_ins, w_backs, rest = rest[:6], rest[6:12], rest[12:16], rest[16:]
    (second_out, pair_out, *keep_outs, q_out, k_out, v_out, kt_out, p_out, unit1_out, scale1_out,
     slope_out, unit2_out, scale2_out, w_scr, w_in, w_back, b_in, b_qv, sems) = rest
    copies = Copies(sems)
    load_qkv(copies, info[2], p1, w_scr, b_in, b_qv)
    for part in range(PARTS):
        load_in(copies, info[2], w_ins, w_in, [part])
        load_back(copies, w_backs, w_back, [part])
    tokens = jnp.where(info[3] == 0, first_tokens[...], passed[...])
    width = tokens.shape[1]
    pair_out[:, width:] = tokens
    copies.wait("qkv")
    attended = attention_forward(tokens, bias[...], w_scr, b_qv, (q_out, k_out, v_out, kt_out, p_out))
    units, head = w_in.shape[2], width // PARTS
    for part in range(PARTS):
        keep_outs[part][:, units:] = attended[:, part * head : (part + 1) * head]
    copies.wait("out")
    unit, scale = norm(tokens.astype(F32) + dot(attended, w_scr[3]) + b_out[...])
    unit1_out[...] = unit
    scale1_out[...] = jnp.broadcast_to(scale, scale1_out.shape)
    first = unit * gain_one[...] + offset_one[...]
    first_low = first.astype(BF)
    pair_out[:, :width] = first_low
    total = ffn_forward(
        first_low, first + b_back[...], range(PARTS), copies, w_in, w_back, b_in, keep_outs, slope_out
    )
    unit, scale = norm(total)
    unit2_out[...] = unit
    scale2_out[...] = jnp.broadcast_to(scale, scale2_out.shape)
    second_out[...] = (unit * gain_two[...] + offset_two[...]).astype(BF)


def rows_sum(values):
    return jnp.sum(values, axis=0, keepdims=True)


def ffn_backward(sum_grad, slope, copies, w_in, w_back, pre_outs):
    units = w_in.shape[2]
    ffn_low = sum_grad.astype(BF)
    first_grad = sum_grad
    for part in range(PARTS):
        copies.wait(f"back{part}")
        pre = dot(ffn_low, w_back[part], NT) * slope[:, part * units : (part + 1) * units].astype(F32)
        pre = pre.astype(BF)
        if pre_outs is not None:
            pre_outs[part][...] = pre
        copies.wait(f"in{part}")
        first_grad = first_grad + dot(pre, w_in[part], NT)
    return first_grad


def attention_backward(first_grad, unit, scale, gain, refs, w_scr, copies, dqt_scr, outs):
    q_ref, k_ref, v_ref, kt_ref, p_ref = refs
    width = first_grad.shape[1]
    branch = norm_back(first_grad, unit, scale, gain)
    branch_low = branch.astype(BF)
    copies.wait("out")
    att_grad = dot(branch_low, w_scr[3], NT).astype(BF)
    pair = 2 * HEAD_DIM
    rows = first_grad.shape[0]
    lane = lax.broadcasted_iota(jnp.int32, (rows, pair), 1)
    term = jnp.zeros((rows, rows), F32)
    root = 1.0 / math.sqrt(HEAD_DIM)
    keys_grad, values_grad = [], []
    for j in range(width // pair):
        here = slice(j * pair, (j + 1) * pair)
        q_pair, v_pair, o_pair = q_ref[:, here], v_ref[:, here], att_grad[:, here]
        dk, dv = [], []
        for s in range(2):
            h = 2 * j + s
            mine = (lane >= HEAD_DIM) if s else (lane < HEAD_DIM)
            chance_low = p_ref[h]
            chance = chance_low.astype(F32)
            chance_grad = dot(jnp.where(mine, v_pair, jnp.zeros_like(v_pair)), o_pair, NT)
            inner = jnp.sum(chance * chance_grad, axis=0, keepdims=True)
            score = chance * (chance_grad - inner)
            term = term + score
            low = score.astype(BF)
            dv.append(dot(chance_low, o_pair))
            dk.append(dot(low, q_pair))
            dqt_scr[h * HEAD_DIM : (h + 1) * HEAD_DIM] = dot(kt_ref[h * HEAD_DIM : (h + 1) * HEAD_DIM], low) * root
        keys_grad.append((jnp.where(lane < HEAD_DIM, dk[0], dk[1]) * root).astype(BF))
        values_grad.append(jnp.where(lane < HEAD_DIM, dv[0], dv[1]).astype(BF))
    dq = dqt_scr[...].T.astype(BF)
    dk = jnp.concatenate(keys_grad, axis=1)
    dv = jnp.concatenate(values_grad, axis=1)
    copies.wait("qkv")
    in_grad = branch + dot(dq, w_scr[0]) + dot(dk, w_scr[1]) + dot(dv, w_scr[2])
    if outs is not None:
        branch_out, projected_outs, term_out = outs
        branch_out[...] = branch_low
        head = width // PARTS
        for part in range(PARTS):
            for i, grad in enumerate((dq, dk, dv)):
                projected_outs[part][:, i * head : (i + 1) * head] = grad[:, part * head : (part + 1) * head]
        term_out[...] = term
    return branch, in_grad, dq, dv


def down_kernel(info, top, unit1, scale1, gain_one, unit2, scale2, gain_two, slope, q_ref, k_ref, v_ref, kt_ref, p_ref, *rest):
    p1, w_ins, w_backs, rest = rest[:6], rest[6:12], rest[12:16], rest[16:]
    grad_out, w_scr, w_in, w_back, b_in, b_qv, dqt_scr, sems = rest
    copies = Copies(sems)
    for part in range(PARTS):
        load_back(copies, w_backs, w_back, [part])
        load_in(copies, info[2], w_ins, w_in, [part])
    load_qkv(copies, info[2], p1, w_scr, b_in, b_qv)
    sum_grad = norm_back(top[...].astype(F32), unit2[...], scale2[:, :1], gain_two[...])
    first_grad = ffn_backward(sum_grad, slope, copies, w_in, w_back, None)
    _, in_grad, _, _ = attention_backward(
        first_grad, unit1[...], scale1[:, :1], gain_one[...], (q_ref, k_ref, v_ref, kt_ref, p_ref),
        w_scr, copies, dqt_scr, None,
    )
    grad_out[...] = in_grad.astype(BF)


def down_norm_kernel(info, own_top, passed, unit2, scale2, gain_two, ffn_out, sum_grad_out, sums_out):
    top = jnp.where(info[3] == 0, passed[...], own_top[...]).astype(F32)
    unit = unit2[...]
    sum_grad = norm_back(top, unit, scale2[:, :1], gain_two[...])
    sum_grad_out[...] = sum_grad
    ffn_out[...] = sum_grad.astype(BF)
    sums_out[...] = jnp.zeros_like(sums_out)
    sums_out[3:4] = rows_sum(sum_grad)
    sums_out[4:5] = rows_sum(top * unit)
    sums_out[5:6] = rows_sum(top)


def down_ffn_kernel(info, sum_grad, slope, *rest):
    w_ins, w_backs, rest = rest[:6], rest[6:10], rest[10:]
    *pre_outs, first_grad_out, w_in, w_back, sems = rest
    copies = Copies(sems)
    for part in range(PARTS):
        load_back(copies, w_backs, w_back, [part])
        load_in(copies, info[2], w_ins, w_in, [part])
    first_grad_out[...] = ffn_backward(sum_grad[...], slope, copies, w_in, w_back, pre_outs)


def down_attention_kernel(info, first_grad, sums, unit1, scale1, gain_one, q_ref, k_ref, v_ref, kt_ref, p_ref, *rest):
    pres, p1, rest = rest[:PARTS], rest[PARTS : PARTS + 6], rest[PARTS + 6 :]
    (grad_out, branch_out, *projected_outs, term_out, sums_out, w_scr, b_in, b_qv, dqt_scr, sems) = rest
    copies = Copies(sems)
    load_qkv(copies, info[2], p1, w_scr, b_in, b_qv)
    unit = unit1[...]
    grad = first_grad[...]
    branch, in_grad, dq, dv = attention_backward(
        grad, unit, scale1[:, :1], gain_one[...], (q_ref, k_ref, v_ref, kt_ref, p_ref),
        w_scr, copies, dqt_scr, (branch_out, projected_outs, term_out),
    )
    grad_out[...] = in_grad.astype(BF)
    sums_out[...] = sums[...]
    sums_out[0:1] = rows_sum(branch)
    sums_out[1:2] = rows_sum(grad * unit)
    sums_out[2:3] = rows_sum(grad)
    width = grad.shape[1]
    head = width // PARTS
    place = 2 * info[1] + info[0]
    dq_sum, dv_sum = rows_sum(dq.astype(F32)), rows_sum(dv.astype(F32))
    for part in range(PARTS):
        sums_out[pl.ds(6 + jnp.bitwise_xor(place, part), 1), : pres[part].shape[1]] = rows_sum(
            pres[part][...].astype(F32)
        )
        here = slice(part * head, (part + 1) * head)
        row = jnp.concatenate(
            [dq_sum[:, here], dv_sum[:, here], jnp.zeros((1, width - 2 * head), F32)], axis=1
        )
        sums_out[pl.ds(10 + jnp.bitwise_xor(place, part), 1)] = row


def products(lefts, left_columns, rights, right_columns):
    total = None
    for left, right in zip(lefts, rights):
        value = dot(left[:, left_columns], right[:, right_columns], TN)
        total = value if total is None else total + value
    return total


def back_products_kernel(*refs):
    keeps, ffns, outs = refs[:PARTS], refs[PARTS : 2 * PARTS], refs[2 * PARTS :]
    size, width = outs[0].shape
    for i, out in enumerate(outs):
        out[...] = products(keeps, slice(i * size, (i + 1) * size), ffns, slice(0, width)).astype(BF)


def in_products_kernel(*refs):
    pairs, pres, outs = refs[:PARTS], refs[PARTS : 2 * PARTS], refs[2 * PARTS :]
    size, units = outs[0].shape
    for i, out in enumerate(outs):
        out[...] = products(pairs, slice(i * size, (i + 1) * size), pres, slice(0, units)).astype(BF)


def rest_products_kernel(*refs):
    keeps, branches, pairs, projected = (refs[i * PARTS : (i + 1) * PARTS] for i in range(4))
    one, two = refs[4 * PARTS :]
    width = one.shape[1]
    head = width // PARTS
    units = keeps[0].shape[1] - head
    one[:head] = products(keeps, slice(units, units + head), branches, slice(0, width)).astype(BF)
    for i, out in enumerate((one.at[pl.ds(head, head)], two.at[pl.ds(0, head)], two.at[pl.ds(head, head)])):
        out[...] = products(
            projected, slice(i * head, (i + 1) * head), pairs, slice(width, 2 * width)
        ).astype(BF)


def add_kernel(left, right, out):
    out[...] = (left[...].astype(F32) + right[...].astype(F32)).astype(BF)


def whole_kernel(info, *refs):
    *sources, out = refs
    row = 0
    for kept, got in zip(sources[::2], sources[1::2]):
        size = kept.shape[0]
        out[row : row + size] = jnp.where(info[4] == 1, kept[...], got[...]).astype(F32)
        row += size


def rest_out_kernel(info, one_kept, one_got, two_kept, two_got, w_out, w_qkv):
    middle = info[4] == 1
    one = jnp.where(middle, one_kept[...], one_got[...]).astype(F32)
    two = jnp.where(middle, two_kept[...], two_got[...]).astype(F32)
    head = w_out.shape[0]
    w_out[...] = one[:head]
    w_qkv[0] = one[head:]
    w_qkv[1] = two[:head]
    w_qkv[2] = two[head:]


def choose_kernel(info, kept, got, out):
    out[...] = jnp.where(info[4] == 1, kept[...], got[...])


def stack_kernel(info, keep, got, out):
    out[info[1]] = keep[...].astype(out.dtype)
    out[1 - info[1]] = got[...].astype(out.dtype)


def last_kernel(docs, info, lengths, own, other, own_sums, other_sums, out, scr):
    half = own.shape[0]
    seq = 2 * half
    start, _ = longest_start(info, lengths, docs)
    mine, theirs = own[...].astype(F32).T, other[...].astype(F32).T
    zero = jnp.zeros_like(mine)
    low = info[0] == 0
    scr[:half, :half] = jnp.where(low, mine, theirs)
    scr[half:, half:] = jnp.where(low, theirs, mine)
    scr[:half, half:] = zero
    scr[half:, :half] = zero
    full = pltpu.roll(scr[...], lax.rem(start + half * (1 - info[0]) + half, seq), 0)[:half]
    full = pltpu.roll(full, start, 1).astype(BF)
    rows = packed_rows(half)
    out[:rows] = jnp.zeros((rows, out.shape[1]), BF)
    out[rows:] = (own_sums[...] + other_sums[...]).astype(BF)
    for row, column, source_row, source_column, count in packing(half):
        out[row : row + count, column : column + half] = full[
            source_row : source_row + count, source_column : source_column + half
        ]


def packing(half):
    rows = packed_rows(half)
    moves = []
    for piece in range(2):
        done = 0
        while done < half:
            place = piece * half + done
            count = min(half - done, rows - place % rows)
            moves.append((place % rows, place // rows * half, done, piece * half, count))
            done += count
    return moves


def packed_rows(half):
    return -(-2 * half // (3 * PAD)) * PAD


def last_out_kernel(info, own, other, logits, noise, mask_out, *outs):
    half = logits.shape[0] // 2
    low = info[0] == 0
    first = jnp.where(low, own[...], other[...])
    second = jnp.where(low, other[...], own[...])
    for base, block in ((0, first), (half, second)):
        for row, column, to_row, to_column, count in packing(half):
            here = (slice(base + to_row, base + to_row + count), slice(to_column, to_column + half))
            slope = 1.0 / (1.0 + jnp.exp(logits[here] + noise[here]))
            mask_out[here] = block[row : row + count, column : column + half].astype(F32) * slope
    sums = own[packed_rows(half) :].astype(F32)
    *vectors, b_in, b_qv = outs
    for i, out in enumerate(vectors):
        out[...] = sums[i : i + 1]
    place = 2 * info[1] + info[0]
    for part in range(PARTS):

        @pl.when(place == part)
        def _():
            b_in[...] = sums[6 + part : 7 + part, : b_in.shape[1]]
            head = b_qv.shape[1]
            b_qv[0:1] = sums[10 + part : 11 + part, :head]
            b_qv[1:2] = sums[10 + part : 11 + part, head : 2 * head]


def rows_kernel(docs, info, lengths, own, other, keep_out, give_out, scr):
    half = own.shape[0]
    seq = 2 * half
    rows = seq // PARTS
    start, _ = longest_start(info, lengths, docs)
    low = info[0] == 0
    mine, theirs = own[...].astype(F32), other[...].astype(F32)
    scr[:half] = jnp.where(low, mine, theirs)
    scr[half:] = jnp.where(low, theirs, mine)
    place = 2 * info[1] + info[0]
    far = 2 * (1 - info[1]) + info[0]
    keep_out[...] = pltpu.roll(scr[...], lax.rem(start + seq - place * rows, seq), 0)[:rows].astype(BF)
    give_out[...] = pltpu.roll(scr[...], lax.rem(start + seq - far * rows, seq), 0)[:rows].astype(BF)


class Order:
    def __init__(self):
        self.last = None

    def after(self, *values):
        if self.last is None:
            return values
        return lax.optimization_barrier((*values, self.last))[:-1]

    def run(self, step, *inputs):
        result = step(*self.after(*inputs))
        self.last = jax.tree.leaves(result)[0]
        return result


def shards(
    inputs, out_grad, doc_lengths, w_qkv, b_qv, w_out, b_out, norm1_gain, norm1_bias,
    w_in, b_in, w_back, b_back, norm2_gain, norm2_bias, mask_logits, mask_noise,
):
    count, seq, width = inputs.shape
    docs = doc_lengths.shape[1]
    core, chip = lax.axis_index("core"), lax.axis_index("chip")
    odd = lax.axis_index("dp") % 2
    part = 2 * chip + core
    half = seq // 2
    head = w_out.shape[1]
    units = w_in.shape[2]
    assert lax.axis_size("pipe") == 2 and lax.axis_size("chip") == 2 and count == 2
    assert lax.axis_size("dp") % 2 == 0 and PARTS * head == width and seq % (2 * PARTS) == 0
    place = lax.axis_index("dp")
    line = lax.axis_size("dp") == 4
    middle = ((place == 1) | (place == 2)) if line else place >= 0
    info = jnp.stack([core, chip, odd, lax.axis_index("pipe"), middle]).astype(jnp.int32)
    order = Order()
    everyone = ("chip", "core")

    def diagonal(block):
        return lax.ppermute(block, everyone, [(i, i ^ 3) for i in range(PARTS)])

    def sems(n):
        return pltpu.SemaphoreType.DMA((n,))

    w4 = pltpu.VMEM((4, width, width), BF)
    w_in_scr = pltpu.VMEM((PARTS, width, units), BF)
    w_back_scr = pltpu.VMEM((PARTS, units, width), BF)
    b_scr = pltpu.VMEM((PARTS, PAD, width), BF)
    dqt = pltpu.VMEM((width, half), F32)
    flat = shape(half, width)
    flat32 = shape(half, width, dtype=F32)

    pack, half_pack, half_in = call(
        split_kernel,
        [shape(4 * head + 2 * PAD, width), shape(2 * head + PAD, width), shape(width // 2, units)],
        [SMEM] + [VMEM] * 5,
        (info, jnp.swapaxes(w_qkv[0], 1, 2).reshape(3 * head, width), w_out[0], w_in[0], b_in, b_qv[0]),
    )
    got_pack = swap(half_pack, "chip")
    got_in = swap(half_in, "chip")
    near = [swap(v, "core") for v in (pack, w_in[0], w_back[0])]

    def prepare(*args):
        return call(
            functools.partial(prepare_kernel, docs),
            [flat, flat, shape(half, half, dtype=F32)],
            [SMEM, SMEM, VMEM, VMEM, VMEM, VMEM],
            args,
        )

    tokens0, top0, bias = order.run(prepare, info, doc_lengths, inputs, out_grad, mask_logits[0], mask_noise[0])
    (got_pack,) = order.after(got_pack)
    also_pack = swap(got_pack, "dp")
    w_back_own, got_pack = lax.optimization_barrier((w_back[0], got_pack))
    got_back = swap(w_back_own, "chip")
    cross_got_pack = swap(got_pack, "core")
    got_in, got_pack = lax.optimization_barrier((got_in, got_pack))
    also_in = swap(got_in, "dp")
    cross_got_in = swap(got_in, "core")
    also_pack, got_in = lax.optimization_barrier((also_pack, got_in))
    p1 = (pack, near[0], got_pack, also_pack, cross_got_pack, swap(also_pack, "core"))

    def attention(tokens, *p1):
        return call(
            attention_kernel, flat32, [SMEM] + [VMEM] * 5 + [ANY] * 6,
            (info, tokens, bias, b_out, norm1_gain, norm1_bias) + p1,
            [w4, b_scr, b_scr, sems(24)],
        )

    def ffn(parts, finish, first, total, *pieces):
        n = len(parts)
        return call(
            functools.partial(ffn_kernel, parts, finish),
            shape(half, width, dtype=BF if finish else F32),
            [SMEM] + [VMEM] * 5 + [ANY] * len(pieces),
            (info, first, total, b_back, norm2_gain, norm2_bias) + pieces,
            [pltpu.VMEM((n, width, units), BF), pltpu.VMEM((n, units, width), BF),
             pltpu.VMEM((n, PAD, width), BF), sems(4 * n)],
        )

    first = order.run(attention, tokens0, *p1)
    total = order.run(
        functools.partial(ffn, (0, 1), False), first, first, pack, near[0], w_in[0], near[1], w_back[0], near[2]
    )
    also_in, got_back = order.after(also_in, got_back)
    w_ins = (w_in[0], near[1], got_in, also_in, cross_got_in, swap(also_in, "core"))
    w_backs = (w_back[0], near[2], got_back, swap(got_back, "core"))
    second = order.run(functools.partial(ffn, (2, 3), True), first, total, *p1[2:], *w_ins[2:], *w_backs[2:])
    passed = lax.ppermute(second, "pipe", [(0, 1)])

    def layer(tokens, passed):
        return call(
            layer_kernel,
            [flat, shape(half, 2 * width)] + [shape(half, units + head)] * PARTS
            + [flat, flat, flat, shape(width, half), shape(width // HEAD_DIM, half, half),
               flat32, shape(half, 128, dtype=F32), shape(half, PARTS * units),
               flat32, shape(half, 128, dtype=F32)],
            [SMEM] + [VMEM] * 9 + [ANY] * 16,
            (info, tokens, passed, bias, b_out, norm1_gain, norm1_bias, b_back, norm2_gain, norm2_bias)
            + p1 + w_ins + w_backs,
            [w4, w_in_scr, w_back_scr, b_scr, b_scr, sems(36)],
        )

    second, pair, *kept = order.run(layer, tokens0, passed)
    keeps, kept = kept[:PARTS], kept[PARTS:]
    q, k, v, kt, chance, unit1, scale1, slope, unit2, scale2 = kept
    keeps = [keeps[0], swap(keeps[1], "core"), swap(keeps[2], "chip"), diagonal(keeps[3])]
    pair_chip = swap(pair, "chip")
    pair_core = swap(pair, "core")
    second_other = swap(second, "core")

    def down(top):
        return call(
            down_kernel, flat, [SMEM] + [VMEM] * 13 + [ANY] * 16,
            (info, top, unit1, scale1, norm1_gain, unit2, scale2, norm2_gain, slope, q, k, v, kt, chance)
            + p1 + w_ins + w_backs,
            [w4, w_in_scr, w_back_scr, b_scr, b_scr, dqt, sems(36)],
        )

    down_grad = order.run(down, top0)
    passed = lax.ppermute(down_grad, "pipe", [(1, 0)])

    def rows_of(own_rows, other_rows):
        return call(
            functools.partial(rows_kernel, docs),
            [shape(seq // PARTS, width)] * 2,
            [SMEM, SMEM, VMEM, VMEM],
            (info, doc_lengths, own_rows, other_rows),
            [pltpu.VMEM((seq, width), F32)],
        )

    act_keep, act_give = order.run(rows_of, second, second_other)
    act_got = swap(act_give, "chip")
    (pair_chip,) = order.after(pair_chip)
    pairs = [pair, pair_core, pair_chip, swap(pair_chip, "core")]

    def down_norm(top, passed):
        return call(
            down_norm_kernel, [flat, flat32, shape(PAD, width, dtype=F32)], [SMEM] + [VMEM] * 5,
            (info, top, passed, unit2, scale2, norm2_gain),
        )

    ffn_low, sum_grad, sums = order.run(down_norm, top0, passed)
    ffn_chip = swap(ffn_low, "chip")
    ffn_core = swap(ffn_low, "core")

    def down_ffn(sum_grad):
        return call(
            down_ffn_kernel, [shape(half, units)] * PARTS + [flat32], [SMEM] + [VMEM] * 2 + [ANY] * 10,
            (info, sum_grad, slope) + w_ins + w_backs,
            [w_in_scr, w_back_scr, sems(12)],
        )

    *pres, first_grad = order.run(down_ffn, sum_grad)
    pre_all = [pres[0], swap(pres[1], "core"), swap(pres[2], "chip"), diagonal(pres[3])]
    (ffn_chip,) = order.after(ffn_chip)
    ffns = [ffn_low, ffn_core, ffn_chip, swap(ffn_chip, "core")]

    def matmuls(kernel, outs, *operands):
        return call(kernel, outs, [VMEM] * len(operands), operands)

    sent, chunk = {}, {}

    def travel(name, stage):
        routes = ([(0, 1), (3, 2)], [(1, 2), (2, 1)], [(1, 0), (2, 3)])
        if line:
            sent[name] = lax.ppermute(chunk[name], "dp", routes[stage])
        elif stage == 0:
            chunk[name] = sent[name] = lax.psum(chunk[name], "dp")

    def step(stage, *names):
        for name in names:
            if line:
                chunk[name] = order.run(
                    lambda a, b: call(add_kernel, shape(*a.shape), [VMEM] * 2, (a, b)), chunk[name], sent[name]
                )
            travel(name, stage)

    def matrix(*names):
        sources = [v for name in names for v in (chunk[name], sent[name])]
        rows = sum(chunk[name].shape[0] for name in names)
        return order.run(
            lambda *a: call(
                whole_kernel, shape(rows, a[0].shape[1], dtype=F32), [SMEM] + [VMEM] * len(a), (info,) + a
            ),
            *sources,
        )

    two = [shape(units // 2, width)] * 2
    chunk["b0"], chunk["b1"] = order.run(functools.partial(matmuls, back_products_kernel, two), *keeps, *ffns)
    travel("b0", 0)
    travel("b1", 0)

    def down_attention(first_grad, sums, *pres):
        return call(
            down_attention_kernel,
            [flat, flat] + [shape(half, 3 * head)] * PARTS + [shape(half, half, dtype=F32), shape(PAD, width, dtype=F32)],
            [SMEM] + [VMEM] * (10 + PARTS) + [ANY] * 6,
            (info, first_grad, sums, unit1, scale1, norm1_gain, q, k, v, kt, chance) + pres + p1,
            [w4, b_scr, b_scr, dqt, sems(24)],
        )

    in_grad, branch_low, *projected, term, sums = order.run(down_attention, first_grad, sums, *pres)
    branch_chip = swap(branch_low, "chip")
    projected = [projected[0], swap(projected[1], "core"), swap(projected[2], "chip"), diagonal(projected[3])]
    branch_core = swap(branch_low, "core")
    term_other, sums_other = swap(term, "core"), swap(sums, "core")
    in_grad_other = swap(in_grad, "core")
    two = [shape(width // 2, units)] * 2
    chunk["i0"], chunk["i1"] = order.run(functools.partial(matmuls, in_products_kernel, two), *pairs, *pre_all)
    travel("i0", 0)
    travel("i1", 0)
    step(1, "b0", "b1")

    def last_chunk(*args):
        return call(
            functools.partial(last_kernel, docs),
            shape(packed_rows(half) + PAD, width),
            [SMEM, SMEM] + [VMEM] * 4,
            (info, doc_lengths) + args,
            [pltpu.VMEM((seq, seq), F32)],
        )

    chunk["l"] = order.run(last_chunk, term, term_other, sums, sums_other)
    last_got = swap(chunk["l"], "chip")
    grad_keep, grad_give = order.run(rows_of, in_grad, in_grad_other)
    grad_got = swap(grad_give, "chip")
    (branch_chip,) = order.after(branch_chip)
    branches = [branch_low, branch_core, branch_chip, swap(branch_chip, "core")]
    step(2, "b0")
    two = [shape(2 * head, width)] * 2
    chunk["r0"], chunk["r1"] = order.run(
        functools.partial(matmuls, rest_products_kernel, two), *keeps, *branches, *pairs, *projected
    )
    travel("r0", 0)
    travel("r1", 0)
    step(1, "i0")
    step(2, "b1")
    chunk["l"] = order.run(
        lambda a, b: call(add_kernel, shape(*a.shape), [VMEM] * 2, (a, b)), chunk["l"], last_got
    )
    travel("l", 0)
    step(1, "i1")
    step(2, "i0")
    grad_w_back = matrix("b0", "b1")
    activations = order.run(
        lambda a, b: call(stack_kernel, shape(2, seq // PARTS, width), [SMEM, VMEM, VMEM], (info, a, b)),
        act_keep, act_got,
    )
    step(1, "r0")
    step(2, "i1")
    step(1, "r1")
    input_grads = order.run(
        lambda a, b: call(stack_kernel, shape(2, seq // PARTS, width, dtype=F32), [SMEM, VMEM, VMEM], (info, a, b)),
        grad_keep, grad_got,
    )
    step(2, "r0")
    step(1, "l")
    grad_w_in = matrix("i0", "i1")
    step(2, "r1")
    step(2, "l")
    grad_w_out, grad_w_qkv = order.run(
        lambda *a: call(
            rest_out_kernel,
            [shape(head, width, dtype=F32), shape(3, head, width, dtype=F32)],
            [SMEM] + [VMEM] * 4, (info,) + a,
        ),
        chunk["r0"], sent["r0"], chunk["r1"], sent["r1"],
    )
    last = order.run(
        lambda a, b: call(choose_kernel, shape(*a.shape), [SMEM, VMEM, VMEM], (info, a, b)), chunk["l"], sent["l"]
    )
    grad_mask, *vectors, grad_b_in, grad_b_qv = call(
        last_out_kernel,
        [shape(seq, seq, dtype=F32)] + [shape(1, width, dtype=F32)] * 6
        + [shape(1, units, dtype=F32), shape(2, head, dtype=F32)],
        [SMEM] + [VMEM] * 4,
        (info, last, swap(last, "core"), mask_logits[0], mask_noise[0]),
    )
    results = (
        activations, input_grads, jnp.swapaxes(grad_w_qkv, 1, 2), grad_b_qv, grad_w_out,
        vectors[0][0], vectors[1][0], vectors[2][0],
        grad_w_in, grad_b_in[0], grad_w_back,
        vectors[3][0], vectors[4][0], vectors[5][0],
        grad_mask,
    )
    return tuple(item[None] for item in results)


def solution(mesh):
    pipe, dp, tensor = (mesh.shape[name] for name in ("pipe", "dp", "tensor"))
    split = Mesh(mesh.devices.reshape(pipe, dp, tensor // 2, 2), ("pipe", "dp", "chip", "core"))
    placed = (
        P("dp", None, None),
        P("dp", None, None),
        P("dp", None),
        P("pipe", None, None, TENSOR),
        P("pipe", None, TENSOR),
        P("pipe", TENSOR, None),
        P("pipe", None),
        P("pipe", None),
        P("pipe", None),
        P("pipe", None, TENSOR),
        P("pipe", TENSOR),
        P("pipe", TENSOR, None),
        P("pipe", None),
        P("pipe", None),
        P("pipe", None),
        P("pipe", None, None),
        P("pipe", None, None),
    )
    return jax.shard_map(
        shards,
        mesh=split,
        in_specs=placed,
        out_specs=(
            P("pipe", "dp", TENSOR, None),
            P("pipe", "dp", TENSOR, None),
            P("pipe", None, None, TENSOR),
            P("pipe", None, TENSOR),
            P("pipe", TENSOR, None),
            P("pipe", None),
            P("pipe", None),
            P("pipe", None),
            P("pipe", None, TENSOR),
            P("pipe", TENSOR),
            P("pipe", TENSOR, None),
            P("pipe", None),
            P("pipe", None),
            P("pipe", None),
            P("pipe", None, None),
        ),
        check_vma=False,
    )
```

```python
import functools
import math

import jax
import jax.numpy as jnp
from jax import lax
from jax.experimental import pallas as pl
from jax.experimental.pallas import tpu as pltpu
from jax.sharding import Mesh
from jax.sharding import PartitionSpec as P

HEAD_DIM = 64
EPSILON = 1e-12
MASKED = -1e30
BF = jnp.bfloat16
F32 = jnp.float32
NT = ((1,), (1,))
TN = ((0,), (0,))
NN = ((1,), (0,))
PARTS = 4
PAD = 16
TENSOR = ("chip", "core")
LIMIT = 8 << 20


def dot(left, right, dims=NN):
    return lax.dot_general(left, right, (dims, ((), ())), preferred_element_type=F32)


def swap(block, axis):
    return lax.ppermute(block, axis, [(i, i ^ 1) for i in range(lax.axis_size(axis))])


SMEM = pl.BlockSpec(memory_space=pltpu.SMEM)
VMEM = pl.BlockSpec(memory_space=pltpu.VMEM)
HBM = pl.BlockSpec(memory_space=pltpu.HBM)


def shape(*dims, dtype=BF):
    return jax.ShapeDtypeStruct(dims, dtype)


def call(kernel, out, ins, args, scratch=(), limit=LIMIT):
    return pl.pallas_call(
        kernel,
        out_shape=out,
        in_specs=ins,
        out_specs=jax.tree.map(lambda _: VMEM, out),
        scratch_shapes=list(scratch),
        compiler_params=pltpu.CompilerParams(vmem_limit_bytes=limit),
        cost_estimate=pl.CostEstimate(flops=0, bytes_accessed=0, transcendentals=0),
    )(*args)


def longest_start(info, lengths, docs):
    chip = info[1]
    sizes = [lengths[chip, i] for i in range(docs)]
    bounds, start, total = [], jnp.int32(0), jnp.int32(0)
    longest = sizes[0]
    for size in sizes[1:]:
        longest = jnp.maximum(longest, size)
    for size in sizes:
        start = jnp.where(size == longest, total, start)
        total = total + size
        bounds.append(total)
    return start, bounds


def prepare_kernel(docs, info, lengths, inputs, grads, logits, noise, tokens_out, top_out, bias_out):
    seq = logits.shape[0]
    half = seq // 2
    start, bounds = longest_start(info, lengths, docs)
    begin = lax.rem(start + half * info[0], seq)
    shift = lax.rem(seq - begin, seq)
    tokens_out[...] = pltpu.roll(inputs[info[1]].astype(F32), shift, 0)[:half].astype(BF)
    top_out[...] = pltpu.roll(grads[info[1]].astype(F32), shift, 0)[:half].astype(BF)
    table = logits[...] + noise[...]
    table = pltpu.roll(table, shift, 0)[:half]
    table = pltpu.roll(table, shift, 1)[:, :half]
    term = jnp.minimum(table, 0.0) - jnp.log1p(jnp.exp(-jnp.abs(table)))

    def owners(axis):
        place = begin + lax.broadcasted_iota(jnp.int32, (half, half), axis)
        place = jnp.where(place >= seq, place - seq, place)
        owner = jnp.zeros((half, half), jnp.int32)
        for bound in bounds:
            owner = owner + jnp.where(place >= bound, 1, 0)
        return owner

    bias_out[...] = jnp.where(owners(0) == owners(1), term, MASKED).T


def split_kernel(info, qkv, w_out, w_in, b_in, b_qv, pack, half_pack, half_in, qkv_scr, out_scr, in_scr, b_in_scr, b_qv_scr, sems):
    size = w_in.shape[0] // 2
    pairs = (
        (qkv, qkv_scr), (w_out, out_scr), (b_in, b_in_scr), (b_qv, b_qv_scr),
        (w_in.at[pl.ds(pl.multiple_of(info[2] * size, size), size)], in_scr),
    )
    copies = [pltpu.make_async_copy(src, dst, sems.at[i]) for i, (src, dst) in enumerate(pairs)]
    for copy in copies:
        copy.start()
    for copy in copies:
        copy.wait()
    head = out_scr.shape[0]
    step = 2 * head + PAD
    pack[: 2 * head] = qkv_scr[: 2 * head]
    pack[2 * head : step] = jnp.zeros((PAD, pack.shape[1]), BF)
    pack[2 * head : 2 * head + 1, : b_in.shape[1]] = b_in_scr[...]
    pack[step : step + head] = qkv_scr[2 * head :]
    pack[step + head : step + 2 * head] = out_scr[...]
    pack[step + 2 * head :] = jnp.zeros((PAD, pack.shape[1]), BF)
    pack[step + 2 * head : step + 2 * head + 1, :head] = b_qv_scr[0:1]
    pack[step + 2 * head : step + 2 * head + 1, head : 2 * head] = b_qv_scr[1:2]
    half_pack[...] = pack[pl.ds(pl.multiple_of(info[2] * step, PAD), step)]
    half_in[:size] = in_scr[...]
    half_in[size:] = jnp.zeros((half_in.shape[0] - size, half_in.shape[1]), BF)


def norm(values):
    average = jnp.mean(values, axis=-1, keepdims=True)
    centred = values - average
    variance = jnp.mean(centred * centred, axis=-1, keepdims=True)
    scale = lax.rsqrt(variance + EPSILON)
    return centred * scale, scale


def norm_back(grad, unit, scale, gain):
    direct = grad * gain
    return scale * (
        direct
        - jnp.mean(direct, axis=-1, keepdims=True)
        - unit * jnp.mean(direct * unit, axis=-1, keepdims=True)
    )


def assemble(info, pieces, w4, b_qv, b_in):
    head = w4.shape[1] // PARTS
    step = 2 * head + PAD
    even = info[2] == 0
    for part in range(PARTS):
        here = slice(part * head, (part + 1) * head)
        for which in range(2):
            if part < 2:
                block = pieces[part][which * step : (which + 1) * step]
            else:
                got, also = pieces[2 * part - 2], pieces[2 * part - 1]
                block = jnp.where(even, got[...], also[...]) if which == 0 else jnp.where(even, also[...], got[...])
            w4[2 * which, here] = block[:head]
            w4[2 * which + 1, here] = block[head : 2 * head]
            if which == 0:
                b_in[part : part + 1] = block[2 * head : 2 * head + 1, : b_in.shape[1]].astype(F32)
            else:
                row = block[2 * head : 2 * head + 1].astype(F32)
                b_qv[0:1, here] = row[:, :head]
                b_qv[1:2, here] = row[:, head : 2 * head]


class Weights:
    def __init__(self, refs):
        self.w4, self.b_qv, self.b_in, self.in_near, self.in_far, self.backs = (
            refs[0], refs[1], refs[2], refs[3:5], refs[5], refs[6:10]
        )
        self.units = self.in_far.shape[2]

    def w_in(self, part):
        return self.in_near[part][...] if part < 2 else self.in_far[part - 2]

    def w_back(self, part):
        return self.backs[part][...]


WEIGHTS = 10


def attention_forward(tokens, bias_ref, w4, b_qv, out_parts, scratch):
    width = tokens.shape[1]
    q_scr, k_scr, vt_scr, at_scr = scratch
    queries = (dot(tokens, w4[0], NT) + b_qv[0:1]).astype(BF)
    keys = dot(tokens, w4[1], NT).astype(BF)
    values = (dot(tokens, w4[2], NT) + b_qv[1:2]).astype(BF)
    values_t = values.T
    if out_parts is not None:
        q_out, k_out, v_out, kt_out, p_out = out_parts
        q_out[...], k_out[...], v_out[...] = queries, keys, values
        kt_out[...] = keys.T
    q_scr[...] = queries * jnp.asarray(1.0 / math.sqrt(HEAD_DIM), BF)
    k_scr[...] = keys
    vt_scr[...] = values_t
    pair = 2 * HEAD_DIM
    lane = lax.broadcasted_iota(jnp.int32, (tokens.shape[0], pair), 1)

    def heads(j):
        here = pl.ds(j * pair, pair)
        q_pair, k_pair = q_scr[:, here], k_scr[:, here]
        for s in range(2):
            mine = (lane >= HEAD_DIM) if s else (lane < HEAD_DIM)
            scores = dot(jnp.where(mine, k_pair, jnp.zeros_like(k_pair)), q_pair, NT) + bias_ref[...]
            exponent = jnp.exp(scores - jnp.max(scores, axis=0, keepdims=True))
            chance = (exponent * (1.0 / jnp.sum(exponent, axis=0, keepdims=True))).astype(BF)
            if out_parts is not None:
                p_out[2 * j + s] = chance
            rows = pl.ds(j * pair + s * HEAD_DIM, HEAD_DIM)
            at_scr[rows, :] = dot(vt_scr[rows, :], chance).astype(BF)

    for j in range(width // pair):
        heads(j)
    return at_scr[...].T


def gelu(values):
    cdf = 0.5 * (1.0 + lax.erf(values * math.sqrt(0.5)))
    return values * cdf, cdf


def attention_kernel(info, tokens, bias, b_out, gain, offset, *rest):
    pieces, (first_out, w4, b_qv, b_in, *scratch) = rest[:6], rest[6:]
    assemble(info, pieces, w4, b_qv, b_in)
    attended = attention_forward(tokens[...], bias, w4, b_qv, None, scratch)
    unit, _ = norm(tokens[...].astype(F32) + dot(attended, w4[3]) + b_out[...])
    first_out[...] = unit * gain[...] + offset[...]


def ffn_near_kernel(first, b_back, b_in, *rest):
    w_ins, w_backs, out = rest[:2], rest[2:4], rest[4]
    first_low = first[...].astype(BF)
    total = first[...] + b_back[...]
    for part in range(2):
        hidden, _ = gelu(dot(first_low, w_ins[part][...]) + b_in[part : part + 1])
        total = total + dot(hidden.astype(BF), w_backs[part][...])
    out[...] = total


def ffn_far_kernel(info, first, b_in, far_got, far_also, cross_got, cross_also, hidden_out, in_out):
    even = info[2] == 0
    units = in_out.shape[2]
    half = in_out.shape[1] // 2
    first_low = first[...].astype(BF)
    for part, (got, also) in enumerate(((far_got, far_also), (cross_got, cross_also))):
        in_out[part, :half] = jnp.where(even, got[:half], also[:half])
        in_out[part, half:] = jnp.where(even, also[:half], got[:half])
        hidden, _ = gelu(dot(first_low, in_out[part]) + b_in[part + 2 : part + 3])
        hidden_out[:, part * units : (part + 1) * units] = hidden.astype(BF)


def ffn_end_kernel(total, hidden, gain, offset, far, cross, out):
    units = far.shape[0]
    result = total[...] + dot(hidden[:, :units], far[...]) + dot(hidden[:, units:], cross[...])
    unit, _ = norm(result)
    out[...] = (unit * gain[...] + offset[...]).astype(BF)


def choose_tokens_kernel(info, first_tokens, passed, out):
    out[...] = jnp.where(info[3] == 0, first_tokens[...], passed[...])


def layer_kernel(tokens_ref, bias, b_out, gain_one, offset_one, b_back, gain_two, offset_two, *rest):
    weights, rest = Weights(rest[:WEIGHTS]), rest[WEIGHTS:]
    second_out, first_out, *rest = rest
    keep_outs, rest = rest[:PARTS], rest[PARTS:]
    (q_out, k_out, v_out, kt_out, p_out, unit1_out, scale1_out, slope_out, unit2_out, scale2_out, *scratch) = rest
    tokens = tokens_ref[...]
    width = tokens.shape[1]
    attended = attention_forward(
        tokens, bias, weights.w4, weights.b_qv, (q_out, k_out, v_out, kt_out, p_out), scratch
    )
    units, head = weights.units, width // PARTS
    for part in range(PARTS):
        keep_outs[part][:, units:] = attended[:, part * head : (part + 1) * head]
    unit, scale = norm(tokens.astype(F32) + dot(attended, weights.w4[3]) + b_out[...])
    unit1_out[...] = unit
    scale1_out[...] = jnp.broadcast_to(scale, scale1_out.shape)
    first = unit * gain_one[...] + offset_one[...]
    first_low = first.astype(BF)
    first_out[...] = first_low
    total = first + b_back[...]
    for part in range(PARTS):
        pre = dot(first_low, weights.w_in(part)) + weights.b_in[part : part + 1]
        value, cdf = gelu(pre)
        hidden = value.astype(BF)
        keep_outs[part][:, :units] = hidden
        density = jnp.exp(-0.5 * pre * pre) * (1.0 / math.sqrt(2.0 * math.pi))
        slope_out[:, part * units : (part + 1) * units] = (cdf + pre * density).astype(BF)
        total = total + dot(hidden, weights.w_back(part))
    unit, scale = norm(total)
    unit2_out[...] = unit
    scale2_out[...] = jnp.broadcast_to(scale, scale2_out.shape)
    second_out[...] = (unit * gain_two[...] + offset_two[...]).astype(BF)


def rows_sum(values):
    return jnp.sum(values, axis=0, keepdims=True)


def ffn_backward(sum_grad, slope, weights, pre_outs):
    units = weights.units
    ffn_low = sum_grad.astype(BF)
    first_grad = sum_grad
    for part in range(PARTS):
        pre = dot(ffn_low, weights.w_back(part), NT) * slope[:, part * units : (part + 1) * units].astype(F32)
        pre = pre.astype(BF)
        if pre_outs is not None:
            pre_outs[part][...] = pre
        first_grad = first_grad + dot(pre, weights.w_in(part), NT)
    return first_grad


def attention_backward(first_grad, unit, scale, gain, refs, w_scr, scratch, outs):
    q_ref, k_ref, v_ref, kt_ref, p_ref = refs
    width = first_grad.shape[1]
    branch = norm_back(first_grad, unit, scale, gain)
    branch_low = branch.astype(BF)
    att_grad = dot(branch_low, w_scr[3], NT).astype(BF)
    pair = 2 * HEAD_DIM
    rows = first_grad.shape[0]
    lane = lax.broadcasted_iota(jnp.int32, (rows, pair), 1)
    root = 1.0 / math.sqrt(HEAD_DIM)
    dqt_scr, dk_scr, dv_scr, o_scr, term_scr = scratch
    o_scr[...] = att_grad
    term_scr[...] = jnp.zeros((rows, rows), F32)

    def heads(j, carry):
        here = pl.ds(pl.multiple_of(j * pair, pair), pair)
        q_pair, v_pair, o_pair = q_ref[:, here], v_ref[:, here], o_scr[:, here]
        dk, dv = [], []
        for s in range(2):
            mine = (lane >= HEAD_DIM) if s else (lane < HEAD_DIM)
            chance_low = p_ref[2 * j + s]
            chance = chance_low.astype(F32)
            chance_grad = dot(jnp.where(mine, v_pair, jnp.zeros_like(v_pair)), o_pair, NT)
            inner = jnp.sum(chance * chance_grad, axis=0, keepdims=True)
            score = chance * (chance_grad - inner)
            term_scr[...] += score
            low = score.astype(BF)
            dv.append(dot(chance_low, o_pair))
            dk.append(dot(low, q_pair))
            part = pl.ds(pl.multiple_of(j * pair + s * HEAD_DIM, HEAD_DIM), HEAD_DIM)
            dqt_scr[part, :] = dot(kt_ref[part, :], low) * root
        dk_scr[:, here] = (jnp.where(lane < HEAD_DIM, dk[0], dk[1]) * root).astype(BF)
        dv_scr[:, here] = jnp.where(lane < HEAD_DIM, dv[0], dv[1]).astype(BF)
        return carry

    lax.fori_loop(0, width // pair, heads, 0)
    dq = dqt_scr[...].T.astype(BF)
    dk, dv = dk_scr[...], dv_scr[...]
    term = term_scr[...]
    in_grad = branch + dot(dq, w_scr[0]) + dot(dk, w_scr[1]) + dot(dv, w_scr[2])
    if outs is not None:
        chip_out, core_out, projected_outs = outs
        chip_out[:, :width] = branch_low
        core_out[:rows, :width] = branch_low
        core_out[:rows, width : 2 * width] = in_grad.astype(BF)
        core_out[:rows, 2 * width : 2 * width + rows] = term.astype(BF)
        head = width // PARTS
        end = 2 * width + rows + 3 * head
        core_out[:rows, end:] = jnp.zeros((rows, core_out.shape[1] - end), BF)
        end = width + 6 * head
        if end < chip_out.shape[1]:
            chip_out[:, end:] = jnp.zeros((rows, chip_out.shape[1] - end), BF)
        for part in range(PARTS):
            out, base = (core_out, 2 * width + rows) if part == 1 else (projected_outs[0], 0)
            out, base = (chip_out, width + (part - 2) * 3 * head) if part > 1 else (out, base)
            for i, grad in enumerate((dq, dk, dv)):
                out[:rows, base + i * head : base + (i + 1) * head] = grad[:, part * head : (part + 1) * head]
    return branch, in_grad, dq, dv


def down_kernel(top, unit1, scale1, gain_one, unit2, scale2, gain_two, slope, q_ref, k_ref, v_ref, kt_ref, p_ref, *rest):
    weights, (grad_out, *scratch) = Weights(rest[:WEIGHTS]), rest[WEIGHTS:]
    sum_grad = norm_back(top[...].astype(F32), unit2[...], scale2[:, :1], gain_two[...])
    first_grad = ffn_backward(sum_grad, slope, weights, None)
    _, in_grad, _, _ = attention_backward(
        first_grad, unit1[...], scale1[:, :1], gain_one[...], (q_ref, k_ref, v_ref, kt_ref, p_ref),
        weights.w4, scratch, None,
    )
    grad_out[...] = in_grad.astype(BF)


def down_norm_kernel(info, own_top, passed, unit2, scale2, gain_two, first, ffn_out, core_out, sum_grad_out, sums_out):
    top = jnp.where(info[3] == 0, passed[...], own_top[...]).astype(F32)
    unit = unit2[...]
    sum_grad = norm_back(top, unit, scale2[:, :1], gain_two[...])
    sum_grad_out[...] = sum_grad
    width = first.shape[1]
    ffn_out[...] = sum_grad.astype(BF)
    core_out[:, :width] = sum_grad.astype(BF)
    core_out[:, width:] = first[...]
    sums_out[...] = jnp.zeros_like(sums_out)
    sums_out[3:4] = rows_sum(sum_grad)
    sums_out[4:5] = rows_sum(top * unit)
    sums_out[5:6] = rows_sum(top)


def down_ffn_kernel(sum_grad, slope, first, *rest):
    weights, (zero, one, chip_out, first_grad_out) = Weights(rest[:WEIGHTS]), rest[WEIGHTS:]
    width, units = first.shape[1], weights.units
    chip_out[:, :width] = first[...]
    pre_outs = (zero, one, chip_out.at[:, pl.ds(width, units)], chip_out.at[:, pl.ds(width + units, units)])
    first_grad_out[...] = ffn_backward(sum_grad[...], slope, weights, pre_outs)


def down_attention_kernel(info, first_grad, sums, unit1, scale1, gain_one, q_ref, k_ref, v_ref, kt_ref, p_ref, *rest):
    pres, w4, rest = rest[: PARTS - 1], rest[PARTS - 1], rest[PARTS:]
    chip_out, core_out, zero, sums_scr, *scratch = rest
    unit = unit1[...]
    grad = first_grad[...]
    rows, width = grad.shape
    branch, in_grad, dq, dv = attention_backward(
        grad, unit, scale1[:, :1], gain_one[...], (q_ref, k_ref, v_ref, kt_ref, p_ref),
        w4, scratch, (chip_out, core_out, (zero,)),
    )
    sums_scr[...] = sums[...]
    sums_scr[0:1] = rows_sum(branch)
    sums_scr[1:2] = rows_sum(grad * unit)
    sums_scr[2:3] = rows_sum(grad)
    head = width // PARTS
    place = 2 * info[1] + info[0]
    dq_sum, dv_sum = rows_sum(dq.astype(F32)), rows_sum(dv.astype(F32))
    for part in range(PARTS):
        units = pres[0].shape[1]
        pre = pres[part][...] if part < 2 else pres[2][:, width + (part - 2) * units : width + (part - 1) * units]
        sums_scr[pl.ds(6 + jnp.bitwise_xor(place, part), 1), :units] = rows_sum(pre.astype(F32))
        here = slice(part * head, (part + 1) * head)
        row = jnp.concatenate(
            [dq_sum[:, here], dv_sum[:, here], jnp.zeros((1, width - 2 * head), F32)], axis=1
        )
        sums_scr[pl.ds(10 + jnp.bitwise_xor(place, part), 1)] = row
    core_out[rows:, :width] = sums_scr[...].astype(BF)
    core_out[rows:, width:] = jnp.zeros((PAD, core_out.shape[1] - width), BF)


def products(lefts, rights):
    total = None
    for left, right in zip(lefts, rights):
        value = dot(left, right, TN)
        total = value if total is None else total + value
    return total.astype(BF)


def products_kernel(rows, left_starts, left_first, right_starts, right_size, *refs):
    lefts, rights, outs = refs[:PARTS], refs[PARTS : 2 * PARTS], refs[2 * PARTS :]
    done = left_first
    for out in outs:
        size = out.shape[0]
        out[...] = products(
            [ref[:rows, start + done : start + done + size] for ref, start in zip(lefts, left_starts)],
            [ref[:rows, start : start + right_size] for ref, start in zip(rights, right_starts)],
        )
        done += size


def add_kernel(left, right, out):
    out[...] = (left[...].astype(F32) + right[...].astype(F32)).astype(BF)


def whole_kernel(info, *refs):
    *sources, out = refs
    row = 0
    for kept, got in zip(sources[::2], sources[1::2]):
        size = kept.shape[0]
        out[row : row + size] = jnp.where(info[4] == 1, kept[...], got[...]).astype(F32)
        row += size


def rest_products_kernel(rows, head_start, keep_starts, projected_starts, token_starts, *refs):
    keeps, branches, projected, tokens = (refs[i * PARTS : (i + 1) * PARTS] for i in range(4))
    one, two, three = refs[4 * PARTS :]
    width = one.shape[1]
    head = width // PARTS

    def from_projected(first, size):
        return products(
            [ref[:rows, start + first : start + first + size] for ref, start in zip(projected, projected_starts)],
            [ref[:rows, start : start + width] for ref, start in zip(tokens, token_starts)],
        )

    one[:head] = products(
        [ref[:rows, start + head_start : start + head_start + head] for ref, start in zip(keeps, keep_starts)],
        [ref[:rows, :width] for ref in branches]
    )
    rest = one.shape[0] - head
    one[head:] = from_projected(0, rest)
    two[...] = from_projected(rest, two.shape[0])
    three[...] = from_projected(rest + two.shape[0], three.shape[0])


def last_join_kernel(part, own, other, out):
    size = part.shape[0]
    out[:size] = part[...]
    out[size:] = (own[...].astype(F32) + other[...].astype(F32)).astype(BF)


def split_columns_kernel(starts, ref, *outs):
    for start, out in zip(starts, outs):
        out[...] = ref[:, start : start + out.shape[1]]


def rest_out_kernel(info, *refs):
    *sources, w_out, w_qkv, last = refs
    one, two, three = (
        jnp.where(info[4] == 1, kept[...], got[...]) for kept, got in zip(sources[::2], sources[1::2])
    )
    head = w_out.shape[0]
    rest = one.shape[0] - head
    end = three.shape[0] - last.shape[0]
    w_out[...] = one[:head].astype(F32)
    w_qkv[:rest] = one[head:].astype(F32)
    w_qkv[rest : rest + two.shape[0]] = two[...].astype(F32)
    w_qkv[rest + two.shape[0] :] = three[:end].astype(F32)
    last[...] = three[end:]


def stack_kernel(info, keep, got, out):
    out[info[1]] = keep[...].astype(out.dtype)
    out[1 - info[1]] = got[...].astype(out.dtype)


def last_kernel(docs, info, lengths, own_core, other_core, out, scr):
    seq = scr.shape[0]
    half = seq // 2
    width = out.shape[1]
    start, _ = longest_start(info, lengths, docs)
    here = slice(2 * width, 2 * width + half)
    mine, theirs = own_core[:half, here].astype(F32).T, other_core[:half, here].astype(F32).T
    zero = jnp.zeros_like(mine)
    low = info[0] == 0
    scr[:half, :half] = jnp.where(low, mine, theirs)
    scr[half:, half:] = jnp.where(low, theirs, mine)
    scr[:half, half:] = zero
    scr[half:, :half] = zero
    full = pltpu.roll(scr[...], lax.rem(start + half * (1 - info[0]) + half, seq), 0)[:half]
    full = pltpu.roll(full, start, 1).astype(BF)
    rows = packed_rows(half)
    out[:rows] = jnp.zeros((rows, out.shape[1]), BF)
    out[rows:] = (own_core[half:, :width].astype(F32) + other_core[half:, :width].astype(F32)).astype(BF)
    for row, column, source_row, source_column, count in packing(half):
        out[row : row + count, column : column + half] = full[
            source_row : source_row + count, source_column : source_column + half
        ]


def packing(half):
    rows = packed_rows(half)
    moves = []
    for piece in range(2):
        done = 0
        while done < half:
            place = piece * half + done
            count = min(half - done, rows - place % rows)
            moves.append((place % rows, place // rows * half, done, piece * half, count))
            done += count
    return moves


def packed_rows(half):
    return -(-2 * half // (3 * PAD)) * PAD


def last_out_kernel(info, own, other, logits, noise, mask_out, *outs):
    half = logits.shape[0] // 2
    low = info[0] == 0
    first = jnp.where(low, own[...], other[...])
    second = jnp.where(low, other[...], own[...])
    for base, block in ((0, first), (half, second)):
        for row, column, to_row, to_column, count in packing(half):
            here = (slice(base + to_row, base + to_row + count), slice(to_column, to_column + half))
            slope = 1.0 / (1.0 + jnp.exp(logits[here] + noise[here]))
            mask_out[here] = block[row : row + count, column : column + half].astype(F32) * slope
    sums = own[packed_rows(half) :].astype(F32)
    *vectors, b_in, b_qv = outs
    for i, out in enumerate(vectors):
        out[...] = sums[i : i + 1]
    place = 2 * info[1] + info[0]
    for part in range(PARTS):

        @pl.when(place == part)
        def _():
            b_in[...] = sums[6 + part : 7 + part, : b_in.shape[1]]
            head = b_qv.shape[1]
            b_qv[0:1] = sums[10 + part : 11 + part, :head]
            b_qv[1:2] = sums[10 + part : 11 + part, head : 2 * head]


def rows_kernel(docs, column, info, lengths, own, other, keep_out, give_out, scr):
    seq, width = scr.shape
    half = seq // 2
    rows = seq // PARTS
    start, _ = longest_start(info, lengths, docs)
    low = info[0] == 0
    here = slice(column, column + width)
    mine, theirs = own[:half, here].astype(F32), other[:half, here].astype(F32)
    scr[:half] = jnp.where(low, mine, theirs)
    scr[half:] = jnp.where(low, theirs, mine)
    place = 2 * info[1] + info[0]
    far = 2 * (1 - info[1]) + info[0]
    keep_out[...] = pltpu.roll(scr[...], lax.rem(start + seq - place * rows, seq), 0)[:rows].astype(BF)
    give_out[...] = pltpu.roll(scr[...], lax.rem(start + seq - far * rows, seq), 0)[:rows].astype(BF)


class Order:
    def __init__(self):
        self.last = None

    def after(self, *values):
        if self.last is None:
            return values
        return lax.optimization_barrier((*values, self.last))[:-1]

    def run(self, step, *inputs):
        return self.run_with((), step, *inputs)[0]

    def run_with(self, arrivals, step, *inputs):
        values = self.after(*inputs, *arrivals)
        result = step(*values[: len(inputs)])
        self.last = jax.tree.leaves(result)[0]
        return result, values[len(inputs) :]


def shards(
    inputs, out_grad, doc_lengths, w_qkv, b_qv, w_out, b_out, norm1_gain, norm1_bias,
    w_in, b_in, w_back, b_back, norm2_gain, norm2_bias, mask_logits, mask_noise,
):
    count, seq, width = inputs.shape
    docs = doc_lengths.shape[1]
    core, chip = lax.axis_index("core"), lax.axis_index("chip")
    odd = lax.axis_index("dp") % 2
    part = 2 * chip + core
    half = seq // 2
    head = w_out.shape[1]
    units = w_in.shape[2]
    assert lax.axis_size("pipe") == 2 and lax.axis_size("chip") == 2 and count == 2
    assert lax.axis_size("dp") % 2 == 0 and PARTS * head == width and seq % (2 * PARTS) == 0
    place = lax.axis_index("dp")
    line = lax.axis_size("dp") == 4
    middle = ((place == 1) | (place == 2)) if line else place >= 0
    info = jnp.stack([core, chip, odd, lax.axis_index("pipe"), middle]).astype(jnp.int32)
    order = Order()
    everyone = ("chip", "core")

    def diagonal(block):
        return lax.ppermute(block, everyone, [(i, i ^ 3) for i in range(PARTS)])

    low_rows = pltpu.VMEM((half, width), BF)
    low_columns = pltpu.VMEM((width, half), BF)
    up_scratch = [low_rows, low_rows, low_columns, low_columns]
    down_scratch = [pltpu.VMEM((width, half), F32), low_rows, low_rows, low_rows, pltpu.VMEM((half, half), F32)]
    flat = shape(half, width)
    flat32 = shape(half, width, dtype=F32)

    pack, half_pack, half_in = call(
        split_kernel,
        [shape(4 * head + 2 * PAD, width), shape(2 * head + PAD, width), shape(width // 2 + 2 * PAD, units)],
        [SMEM] + [HBM] * 5,
        (info, jnp.swapaxes(w_qkv[0], 1, 2).reshape(3 * head, width), w_out[0], w_in[0], b_in, b_qv[0]),
        [pltpu.VMEM((3 * head, width), BF), pltpu.VMEM((head, width), BF), pltpu.VMEM((width // 2, units), BF),
         pltpu.VMEM((1, units), BF), pltpu.VMEM((2, head), BF), pltpu.SemaphoreType.DMA((5,))],
        56 << 20,
    )
    got_pack = swap(half_pack, "chip")
    got_in = swap(half_in, "chip")
    near = [swap(v, "core") for v in (pack, w_in[0], w_back[0])]

    def prepare(*args):
        return call(
            functools.partial(prepare_kernel, docs),
            [flat, flat, shape(half, half, dtype=F32)],
            [SMEM, SMEM, VMEM, VMEM, VMEM, VMEM],
            args,
        )

    tokens0, top0, bias = order.run(prepare, info, doc_lengths, inputs, out_grad, mask_logits[0], mask_noise[0])
    (got_pack,) = order.after(got_pack)
    also_pack = swap(got_pack, "dp")
    w_back_own, got_pack = lax.optimization_barrier((w_back[0], got_pack))
    got_back = swap(w_back_own, "chip")
    cross_got_pack = swap(got_pack, "core")
    got_in, got_pack = lax.optimization_barrier((got_in, got_pack))
    also_in = swap(got_in, "dp")
    cross_got_in = swap(got_in, "core")
    also_pack, got_in = lax.optimization_barrier((also_pack, got_in))
    p1 = (pack, near[0], got_pack, also_pack, cross_got_pack, swap(also_pack, "core"))

    def attention(tokens, *p1):
        return call(
            attention_kernel,
            [flat32, shape(4, width, width), shape(2, width, dtype=F32), shape(PARTS, units, dtype=F32)],
            [SMEM] + [VMEM] * 11,
            (info, tokens, bias, b_out, norm1_gain, norm1_bias) + p1,
            up_scratch,
        )

    first, w4, both_b_qv, full_b_in = order.run(attention, tokens0, *p1)
    total = order.run(
        lambda *a: call(ffn_near_kernel, flat32, [VMEM] * 7, a),
        first, b_back, full_b_in, w_in[0], near[1], w_back[0], near[2],
    )
    (also_in,) = order.after(also_in)
    hidden_far, in_far = order.run(
        lambda *a: call(
            ffn_far_kernel, [shape(half, 2 * units), shape(2, width, units)], [SMEM] + [VMEM] * 6, (info,) + a
        ),
        first, full_b_in, got_in, also_in, cross_got_in, swap(also_in, "core"),
    )
    (got_back,) = order.after(got_back)
    backs = (w_back[0], near[2], got_back, swap(got_back, "core"))
    second = order.run(
        lambda *a: call(ffn_end_kernel, flat, [VMEM] * 6, a),
        total, hidden_far, norm2_gain, norm2_bias, backs[2], backs[3],
    )
    weights = (w4, both_b_qv, full_b_in, w_in[0], near[1], in_far) + backs
    passed = lax.ppermute(second, "pipe", [(0, 1)])

    tokens = order.run(
        lambda *a: call(choose_tokens_kernel, flat, [SMEM, VMEM, VMEM], (info,) + a), tokens0, passed
    )
    tokens_chip = swap(tokens, "chip")
    tokens_core = swap(tokens, "core")

    keep_width = units + head

    def layer(tokens):
        return call(
            layer_kernel,
            [flat, flat] + [shape(half, keep_width)] * PARTS
            + [flat, flat, flat, shape(width, half), shape(width // HEAD_DIM, half, half),
               flat32, shape(half, 128, dtype=F32), shape(half, PARTS * units),
               flat32, shape(half, 128, dtype=F32)],
            [VMEM] * (8 + WEIGHTS),
            (tokens, bias, b_out, norm1_gain, norm1_bias, b_back, norm2_gain, norm2_bias) + weights,
            up_scratch,
        )

    second, first_low, *kept = order.run(layer, tokens)
    keeps, kept = kept[:PARTS], kept[PARTS:]
    q, k, v, kt, chance, unit1, scale1, slope, unit2, scale2 = kept
    keeps = [keeps[0], swap(keeps[1], "core"), swap(keeps[2], "chip"), diagonal(keeps[3])]
    second_other = swap(second, "core")

    def down(top):
        return call(
            down_kernel, flat, [VMEM] * (13 + WEIGHTS),
            (top, unit1, scale1, norm1_gain, unit2, scale2, norm2_gain, slope, q, k, v, kt, chance) + weights,
            down_scratch,
        )

    down_grad, (tokens_chip, tokens_core) = order.run_with((tokens_chip, tokens_core), down, top0)
    passed = lax.ppermute(down_grad, "pipe", [(1, 0)])
    tokens_all = [tokens, tokens_core, tokens_chip, swap(tokens_chip, "core")]

    def rows_of(column, own_rows, other_rows):
        return call(
            functools.partial(rows_kernel, docs, column),
            [shape(seq // PARTS, width)] * 2,
            [SMEM, SMEM, VMEM, VMEM],
            (info, doc_lengths, own_rows, other_rows),
            [pltpu.VMEM((seq, width), F32)],
        )

    (act_keep, act_give), keeps[1:] = order.run_with(
        keeps[1:], functools.partial(rows_of, 0), second, second_other
    )

    def down_norm(top, passed):
        return call(
            down_norm_kernel, [flat, shape(half, 2 * width), flat32, shape(PAD, width, dtype=F32)], [SMEM] + [VMEM] * 6,
            (info, top, passed, unit2, scale2, norm2_gain, first_low),
        )

    ffn_low, ffn_pack, sum_grad, sums = order.run(down_norm, top0, passed)
    ffn_chip = swap(ffn_low, "chip")
    ffn_core = swap(ffn_pack, "core")

    def down_ffn(sum_grad):
        return call(
            down_ffn_kernel,
            [shape(half, units), shape(half, units), shape(half, width + 2 * units), flat32],
            [VMEM] * (3 + WEIGHTS),
            (sum_grad, slope, first_low) + weights,
        )

    *pres, first_grad = order.run(down_ffn, sum_grad)
    pre_chip = swap(pres[2], "chip")
    pre_core = swap(pres[1], "core")

    sent, chunk = {}, {}

    def travel(name, stage):
        routes = ([(0, 1), (3, 2)], [(1, 2), (2, 1)], [(1, 0), (2, 3)])
        if line:
            sent[name] = lax.ppermute(chunk[name], "dp", routes[stage])
        elif stage == 0:
            chunk[name] = sent[name] = lax.psum(chunk[name], "dp")

    def step(stage, *names):
        for name in names:
            if line:
                chunk[name] = order.run(
                    lambda a, b: call(add_kernel, shape(*a.shape), [VMEM] * 2, (a, b)), chunk[name], sent[name]
                )
            travel(name, stage)

    def products_of(outs, lefts, left_starts, left_first, rights, right_starts, right_size):
        return order.run(
            lambda *a: call(
                functools.partial(products_kernel, half, left_starts, left_first, right_starts, right_size),
                [shape(n, right_size) for n in outs], [VMEM] * (2 * PARTS), a,
            ),
            *lefts, *rights,
        )

    chip_width = -(-(width + 6 * head) // 128) * 128

    def down_attention(first_grad, sums, *pres):
        return call(
            down_attention_kernel,
            [shape(half, chip_width), shape(half + PAD, -(-(2 * width + half + 3 * head) // 128) * 128)]
            + [shape(half, 3 * head)],
            [SMEM] + [VMEM] * (10 + PARTS),
            (info, first_grad, sums, unit1, scale1, norm1_gain, q, k, v, kt, chance) + pres + (w4,),
            [pltpu.VMEM((PAD, width), F32)] + down_scratch,
        )

    down_core_projected = 2 * width + half
    down_chip, down_pack, projected_zero = order.run(down_attention, first_grad, sums, *pres)
    (ffn_chip,) = order.after(ffn_chip)
    ffns = [ffn_low, ffn_core, ffn_chip, swap(ffn_chip, "core")]
    down_other = swap(down_pack, "core")
    none = (0, 0, 0, 0)
    chunk["b0"], chunk["b1"] = products_of((units // 2, units // 2), keeps, none, 0, ffns, none, width)
    travel("b0", 0)
    travel("b1", 0)
    step(1, "b0")

    def split_columns(starts, sizes, packed):
        return order.run(
            lambda a: call(
                functools.partial(split_columns_kernel, starts), [shape(half, n) for n in sizes], [VMEM], (a,)
            ),
            packed,
        )

    far_first, far_pre = split_columns((0, width + units), (width, units), pre_chip)
    far_first, far_pre = swap(far_first, "core"), swap(far_pre, "core")
    branch_chip = swap(down_chip, "chip")
    chunk["i0"], chunk["i1"] = products_of(
        (width // 2, width // 2), [first_low, ffn_core, pre_chip, far_first], (0, width, 0, 0), 0,
        [pres[0], pre_core, pre_chip, far_pre], (0, 0, width, 0), units,
    )
    travel("i0", 0)
    travel("i1", 0)

    def last_chunk(*args):
        return call(
            functools.partial(last_kernel, docs),
            shape(packed_rows(half) + PAD, width),
            [SMEM, SMEM] + [VMEM] * 2,
            (info, doc_lengths) + args,
            [pltpu.VMEM((seq, seq), F32)],
        )

    last = order.run(last_chunk, down_pack, down_other)
    last_got = swap(last, "chip")
    step(1, "b1")
    step(2, "b0")
    grad_keep, grad_give = order.run(functools.partial(rows_of, width), down_pack, down_other)
    step(1, "i0")
    far_branch, far_projected = split_columns((0, width + 3 * head), (width, 3 * head), branch_chip)
    far_branch, far_projected = swap(far_branch, "core"), swap(far_projected, "core")
    size = (4 * head + last.shape[0]) // 3
    chunk["r0"], chunk["r1"], part = order.run(
        lambda *a: call(
            functools.partial(
                rest_products_kernel, half, units, none, (0, down_core_projected, width, 0), none
            ),
            [shape(size, width), shape(size, width), shape(4 * head - 2 * size, width)], [VMEM] * (4 * PARTS), a,
        ),
        *keeps, down_chip, down_other, branch_chip, far_branch,
        projected_zero, down_other, branch_chip, far_projected, *tokens_all,
    )
    travel("r0", 0)
    travel("r1", 0)
    step(2, "b1")
    chunk["r2"] = order.run(
        lambda *a: call(last_join_kernel, shape(size, width), [VMEM] * 3, a), part, last, last_got
    )
    travel("r2", 0)
    act_give, grad_give = order.after(act_give, grad_give)
    act_got, grad_got = swap(act_give, "chip"), swap(grad_give, "chip")
    step(1, "i1")
    step(2, "i0")
    step(1, "r0")
    grad_w_back = order.run(
        lambda *a: call(whole_kernel, shape(units, width, dtype=F32), [SMEM] + [VMEM] * 4, (info,) + a),
        *[v for name in ("b0", "b1") for v in (chunk[name], sent[name])],
    )
    step(2, "i1")
    step(1, "r1")
    activations = order.run(
        lambda a, b: call(stack_kernel, shape(2, seq // PARTS, width), [SMEM, VMEM, VMEM], (info, a, b)),
        act_keep, act_got,
    )
    step(2, "r0")
    input_grads = order.run(
        lambda a, b: call(stack_kernel, shape(2, seq // PARTS, width, dtype=F32), [SMEM, VMEM, VMEM], (info, a, b)),
        grad_keep, grad_got,
    )
    step(1, "r2")
    grad_w_in = order.run(
        lambda *a: call(whole_kernel, shape(width, units, dtype=F32), [SMEM] + [VMEM] * 4, (info,) + a),
        *[v for name in ("i0", "i1") for v in (chunk[name], sent[name])],
    )
    step(2, "r1")
    step(2, "r2")
    grad_w_out, grad_w_qkv, last = order.run(
        lambda *a: call(
            rest_out_kernel,
            [shape(head, width, dtype=F32), shape(3 * head, width, dtype=F32), shape(*last.shape)],
            [SMEM] + [VMEM] * 6, (info,) + a,
        ),
        *[v for name in ("r0", "r1", "r2") for v in (chunk[name], sent[name])],
    )
    grad_w_qkv = grad_w_qkv.reshape(3, head, width)
    grad_mask, *vectors, grad_b_in, grad_b_qv = call(
        last_out_kernel,
        [shape(seq, seq, dtype=F32)] + [shape(1, width, dtype=F32)] * 6
        + [shape(1, units, dtype=F32), shape(2, head, dtype=F32)],
        [SMEM] + [VMEM] * 4,
        (info, last, swap(last, "core"), mask_logits[0], mask_noise[0]),
    )
    results = (
        activations, input_grads, jnp.swapaxes(grad_w_qkv, 1, 2), grad_b_qv, grad_w_out,
        vectors[0][0], vectors[1][0], vectors[2][0],
        grad_w_in, grad_b_in[0], grad_w_back,
        vectors[3][0], vectors[4][0], vectors[5][0],
        grad_mask,
    )
    return tuple(item[None] for item in results)


def solution(mesh):
    pipe, dp, tensor = (mesh.shape[name] for name in ("pipe", "dp", "tensor"))
    split = Mesh(mesh.devices.reshape(pipe, dp, tensor // 2, 2), ("pipe", "dp", "chip", "core"))
    placed = (
        P("dp", None, None),
        P("dp", None, None),
        P("dp", None),
        P("pipe", None, None, TENSOR),
        P("pipe", None, TENSOR),
        P("pipe", TENSOR, None),
        P("pipe", None),
        P("pipe", None),
        P("pipe", None),
        P("pipe", None, TENSOR),
        P("pipe", TENSOR),
        P("pipe", TENSOR, None),
        P("pipe", None),
        P("pipe", None),
        P("pipe", None),
        P("pipe", None, None),
        P("pipe", None, None),
    )
    return jax.shard_map(
        shards,
        mesh=split,
        in_specs=placed,
        out_specs=(
            P("pipe", "dp", TENSOR, None),
            P("pipe", "dp", TENSOR, None),
            P("pipe", None, None, TENSOR),
            P("pipe", None, TENSOR),
            P("pipe", TENSOR, None),
            P("pipe", None),
            P("pipe", None),
            P("pipe", None),
            P("pipe", None, TENSOR),
            P("pipe", TENSOR),
            P("pipe", TENSOR, None),
            P("pipe", None),
            P("pipe", None),
            P("pipe", None),
            P("pipe", None, None),
        ),
        check_vma=False,
    )
```

```python
import functools
import math

import jax
import jax.numpy as jnp
from jax import lax
from jax.experimental import pallas as pl
from jax.experimental.pallas import tpu as pltpu
from jax.sharding import Mesh
from jax.sharding import PartitionSpec as P

HEAD_DIM = 64
EPSILON = 1e-12
MASKED = -1e30
BF = jnp.bfloat16
F32 = jnp.float32
NT = ((1,), (1,))
TN = ((0,), (0,))
NN = ((1,), (0,))
PARTS = 4
PAD = 16
TENSOR = ("chip", "core")
LIMIT = 8 << 20


def dot(left, right, dims=NN):
    return lax.dot_general(left, right, (dims, ((), ())), preferred_element_type=F32)


def swap(block, axis):
    return lax.ppermute(block, axis, [(i, i ^ 1) for i in range(lax.axis_size(axis))])


SMEM = pl.BlockSpec(memory_space=pltpu.SMEM)
VMEM = pl.BlockSpec(memory_space=pltpu.VMEM)
HBM = pl.BlockSpec(memory_space=pltpu.HBM)


def shape(*dims, dtype=BF):
    return jax.ShapeDtypeStruct(dims, dtype)


def call(kernel, out, ins, args, scratch=(), limit=LIMIT):
    return pl.pallas_call(
        kernel,
        out_shape=out,
        in_specs=ins,
        out_specs=jax.tree.map(lambda _: VMEM, out),
        scratch_shapes=list(scratch),
        compiler_params=pltpu.CompilerParams(vmem_limit_bytes=limit),
        cost_estimate=pl.CostEstimate(flops=0, bytes_accessed=0, transcendentals=0),
    )(*args)


def longest_start(info, lengths, docs):
    chip = info[1]
    sizes = [lengths[chip, i] for i in range(docs)]
    bounds, start, total = [], jnp.int32(0), jnp.int32(0)
    longest = sizes[0]
    for size in sizes[1:]:
        longest = jnp.maximum(longest, size)
    for size in sizes:
        start = jnp.where(size == longest, total, start)
        total = total + size
        bounds.append(total)
    return start, bounds


def prepare_kernel(docs, info, lengths, inputs, grads, logits, noise, tokens_out, top_out, bias_out):
    seq = logits.shape[0]
    half = seq // 2
    start, bounds = longest_start(info, lengths, docs)
    begin = lax.rem(start + half * info[0], seq)
    shift = lax.rem(seq - begin, seq)
    tokens_out[...] = pltpu.roll(inputs[info[1]].astype(F32), shift, 0)[:half].astype(BF)
    top_out[...] = pltpu.roll(grads[info[1]].astype(F32), shift, 0)[:half].astype(BF)
    table = logits[...] + noise[...]
    table = pltpu.roll(table, shift, 0)[:half]
    table = pltpu.roll(table, shift, 1)[:, :half]
    term = jnp.minimum(table, 0.0) - jnp.log1p(jnp.exp(-jnp.abs(table)))

    def owners(axis):
        place = begin + lax.broadcasted_iota(jnp.int32, (half, half), axis)
        place = jnp.where(place >= seq, place - seq, place)
        owner = jnp.zeros((half, half), jnp.int32)
        for bound in bounds:
            owner = owner + jnp.where(place >= bound, 1, 0)
        return owner

    bias_out[...] = jnp.where(owners(0) == owners(1), term, MASKED).T


def split_kernel(info, qkv, w_out, w_in, b_in, b_qv, pack, half_pack, half_in, qkv_scr, out_scr, in_scr, b_in_scr, b_qv_scr, sems):
    size = w_in.shape[0] // 2
    pairs = (
        (qkv, qkv_scr), (w_out, out_scr), (b_in, b_in_scr), (b_qv, b_qv_scr),
        (w_in.at[pl.ds(pl.multiple_of(info[2] * size, size), size)], in_scr),
    )
    copies = [pltpu.make_async_copy(src, dst, sems.at[i]) for i, (src, dst) in enumerate(pairs)]
    for copy in copies:
        copy.start()
    for copy in copies:
        copy.wait()
    head = out_scr.shape[0]
    step = 2 * head + PAD
    pack[: 2 * head] = qkv_scr[: 2 * head]
    pack[2 * head : step] = jnp.zeros((PAD, pack.shape[1]), BF)
    pack[2 * head : 2 * head + 1, : b_in.shape[1]] = b_in_scr[...]
    pack[step : step + head] = qkv_scr[2 * head :]
    pack[step + head : step + 2 * head] = out_scr[...]
    pack[step + 2 * head :] = jnp.zeros((PAD, pack.shape[1]), BF)
    pack[step + 2 * head : step + 2 * head + 1, :head] = b_qv_scr[0:1]
    pack[step + 2 * head : step + 2 * head + 1, head : 2 * head] = b_qv_scr[1:2]
    half_pack[...] = pack[pl.ds(pl.multiple_of(info[2] * step, PAD), step)]
    half_in[:size] = in_scr[...]
    half_in[size:] = jnp.zeros((half_in.shape[0] - size, half_in.shape[1]), BF)


def norm(values):
    average = jnp.mean(values, axis=-1, keepdims=True)
    centred = values - average
    variance = jnp.mean(centred * centred, axis=-1, keepdims=True)
    scale = lax.rsqrt(variance + EPSILON)
    return centred * scale, scale


def norm_back(grad, unit, scale, gain):
    direct = grad * gain
    return scale * (
        direct
        - jnp.mean(direct, axis=-1, keepdims=True)
        - unit * jnp.mean(direct * unit, axis=-1, keepdims=True)
    )


def assemble(info, pieces, w4, b_qv, b_in):
    head = w4.shape[1] // PARTS
    step = 2 * head + PAD
    even = info[2] == 0
    for part in range(PARTS):
        here = slice(part * head, (part + 1) * head)
        for which in range(2):
            if part < 2:
                block = pieces[part][which * step : (which + 1) * step]
            else:
                got, also = pieces[2 * part - 2], pieces[2 * part - 1]
                block = jnp.where(even, got[...], also[...]) if which == 0 else jnp.where(even, also[...], got[...])
            w4[2 * which, here] = block[:head]
            w4[2 * which + 1, here] = block[head : 2 * head]
            if which == 0:
                b_in[part : part + 1] = block[2 * head : 2 * head + 1, : b_in.shape[1]].astype(F32)
            else:
                row = block[2 * head : 2 * head + 1].astype(F32)
                b_qv[0:1, here] = row[:, :head]
                b_qv[1:2, here] = row[:, head : 2 * head]


class Weights:
    def __init__(self, refs):
        self.w4, self.b_qv, self.b_in, self.in_near, self.in_far, self.backs = (
            refs[0], refs[1], refs[2], refs[3:5], refs[5], refs[6:10]
        )
        self.units = self.in_far.shape[2]

    def w_in(self, part):
        return self.in_near[part][...] if part < 2 else self.in_far[part - 2]

    def w_back(self, part):
        return self.backs[part][...]


WEIGHTS = 10


def attention_forward(tokens, bias_ref, w4, b_qv, out_parts, scratch):
    width = tokens.shape[1]
    q_scr, k_scr, vt_scr, at_scr = scratch
    queries = (dot(tokens, w4[0], NT) + b_qv[0:1]).astype(BF)
    keys = dot(tokens, w4[1], NT).astype(BF)
    values = (dot(tokens, w4[2], NT) + b_qv[1:2]).astype(BF)
    values_t = values.T
    if out_parts is not None:
        q_out, k_out, v_out, kt_out, p_out = out_parts
        q_out[...], k_out[...], v_out[...] = queries, keys, values
        kt_out[...] = keys.T
    q_scr[...] = queries * jnp.asarray(1.0 / math.sqrt(HEAD_DIM), BF)
    k_scr[...] = keys
    vt_scr[...] = values_t
    pair = 2 * HEAD_DIM
    lane = lax.broadcasted_iota(jnp.int32, (tokens.shape[0], pair), 1)

    def heads(j):
        here = pl.ds(j * pair, pair)
        q_pair, k_pair = q_scr[:, here], k_scr[:, here]
        for s in range(2):
            mine = (lane >= HEAD_DIM) if s else (lane < HEAD_DIM)
            scores = dot(jnp.where(mine, k_pair, jnp.zeros_like(k_pair)), q_pair, NT) + bias_ref[...]
            exponent = jnp.exp(scores - jnp.max(scores, axis=0, keepdims=True))
            chance = (exponent * (1.0 / jnp.sum(exponent, axis=0, keepdims=True))).astype(BF)
            if out_parts is not None:
                p_out[2 * j + s] = chance
            rows = pl.ds(j * pair + s * HEAD_DIM, HEAD_DIM)
            at_scr[rows, :] = dot(vt_scr[rows, :], chance).astype(BF)

    for j in range(width // pair):
        heads(j)
    return at_scr[...].T


def gelu(values):
    cdf = 0.5 * (1.0 + lax.erf(values * math.sqrt(0.5)))
    return values * cdf, cdf


def attention_kernel(info, tokens, bias, b_out, gain, offset, *rest):
    pieces, (first_out, w4, b_qv, b_in, *scratch) = rest[:6], rest[6:]
    assemble(info, pieces, w4, b_qv, b_in)
    attended = attention_forward(tokens[...], bias, w4, b_qv, None, scratch)
    unit, _ = norm(tokens[...].astype(F32) + dot(attended, w4[3]) + b_out[...])
    first_out[...] = unit * gain[...] + offset[...]


def ffn_near_kernel(first, b_back, b_in, *rest):
    w_ins, w_backs, out = rest[:2], rest[2:4], rest[4]
    first_low = first[...].astype(BF)
    total = first[...] + b_back[...]
    for part in range(2):
        hidden, _ = gelu(dot(first_low, w_ins[part][...]) + b_in[part : part + 1])
        total = total + dot(hidden.astype(BF), w_backs[part][...])
    out[...] = total


def ffn_far_kernel(info, first, b_in, far_got, far_also, cross_got, cross_also, hidden_out, in_out):
    even = info[2] == 0
    units = in_out.shape[2]
    half = in_out.shape[1] // 2
    first_low = first[...].astype(BF)
    for part, (got, also) in enumerate(((far_got, far_also), (cross_got, cross_also))):
        in_out[part, :half] = jnp.where(even, got[:half], also[:half])
        in_out[part, half:] = jnp.where(even, also[:half], got[:half])
        hidden, _ = gelu(dot(first_low, in_out[part]) + b_in[part + 2 : part + 3])
        hidden_out[:, part * units : (part + 1) * units] = hidden.astype(BF)


def ffn_end_kernel(total, hidden, gain, offset, far, cross, out):
    units = far.shape[0]
    result = total[...] + dot(hidden[:, :units], far[...]) + dot(hidden[:, units:], cross[...])
    unit, _ = norm(result)
    out[...] = (unit * gain[...] + offset[...]).astype(BF)


def choose_tokens_kernel(info, first_tokens, passed, out):
    out[...] = jnp.where(info[3] == 0, first_tokens[...], passed[...])


def layer_kernel(tokens_ref, bias, b_out, gain_one, offset_one, b_back, gain_two, offset_two, *rest):
    weights, rest = Weights(rest[:WEIGHTS]), rest[WEIGHTS:]
    second_out, first_out, att_out, *rest = rest
    keep_outs, rest = rest[:PARTS], rest[PARTS:]
    (q_out, k_out, v_out, kt_out, p_out, unit1_out, scale1_out, slope_out, unit2_out, scale2_out, *scratch) = rest
    tokens = tokens_ref[...]
    width = tokens.shape[1]
    attended = attention_forward(
        tokens, bias, weights.w4, weights.b_qv, (q_out, k_out, v_out, kt_out, p_out), scratch
    )
    units, head = weights.units, width // PARTS
    for part in range(PARTS):
        out, base = (keep_outs[part], units) if part < 2 else (att_out, (part - 2) * head)
        out[:, base : base + head] = attended[:, part * head : (part + 1) * head]
    unit, scale = norm(tokens.astype(F32) + dot(attended, weights.w4[3]) + b_out[...])
    unit1_out[...] = unit
    scale1_out[...] = jnp.broadcast_to(scale, scale1_out.shape)
    first = unit * gain_one[...] + offset_one[...]
    first_low = first.astype(BF)
    first_out[...] = first_low
    total = first + b_back[...]
    for part in range(PARTS):
        pre = dot(first_low, weights.w_in(part)) + weights.b_in[part : part + 1]
        value, cdf = gelu(pre)
        hidden = value.astype(BF)
        keep_outs[part][:, :units] = hidden
        density = jnp.exp(-0.5 * pre * pre) * (1.0 / math.sqrt(2.0 * math.pi))
        slope_out[:, part * units : (part + 1) * units] = (cdf + pre * density).astype(BF)
        total = total + dot(hidden, weights.w_back(part))
    unit, scale = norm(total)
    unit2_out[...] = unit
    scale2_out[...] = jnp.broadcast_to(scale, scale2_out.shape)
    second_out[...] = (unit * gain_two[...] + offset_two[...]).astype(BF)


def rows_sum(values):
    return jnp.sum(values, axis=0, keepdims=True)


def ffn_backward(sum_grad, slope, weights, pre_outs):
    units = weights.units
    ffn_low = sum_grad.astype(BF)
    first_grad = sum_grad
    for part in range(PARTS):
        pre = dot(ffn_low, weights.w_back(part), NT) * slope[:, part * units : (part + 1) * units].astype(F32)
        pre = pre.astype(BF)
        if pre_outs is not None:
            pre_outs[part][...] = pre
        first_grad = first_grad + dot(pre, weights.w_in(part), NT)
    return first_grad


def attention_backward(first_grad, unit, scale, gain, refs, w_scr, scratch, outs):
    q_ref, k_ref, v_ref, kt_ref, p_ref = refs
    width = first_grad.shape[1]
    branch = norm_back(first_grad, unit, scale, gain)
    branch_low = branch.astype(BF)
    att_grad = dot(branch_low, w_scr[3], NT).astype(BF)
    pair = 2 * HEAD_DIM
    rows = first_grad.shape[0]
    lane = lax.broadcasted_iota(jnp.int32, (rows, pair), 1)
    root = 1.0 / math.sqrt(HEAD_DIM)
    dqt_scr, dk_scr, dv_scr, o_scr, term_scr = scratch
    o_scr[...] = att_grad
    term_scr[...] = jnp.zeros((rows, rows), F32)

    def heads(j, carry):
        here = pl.ds(pl.multiple_of(j * pair, pair), pair)
        q_pair, v_pair, o_pair = q_ref[:, here], v_ref[:, here], o_scr[:, here]
        dk, dv = [], []
        for s in range(2):
            mine = (lane >= HEAD_DIM) if s else (lane < HEAD_DIM)
            chance_low = p_ref[2 * j + s]
            chance = chance_low.astype(F32)
            chance_grad = dot(jnp.where(mine, v_pair, jnp.zeros_like(v_pair)), o_pair, NT)
            inner = jnp.sum(chance * chance_grad, axis=0, keepdims=True)
            score = chance * (chance_grad - inner)
            term_scr[...] += score
            low = score.astype(BF)
            dv.append(dot(chance_low, o_pair))
            dk.append(dot(low, q_pair))
            part = pl.ds(pl.multiple_of(j * pair + s * HEAD_DIM, HEAD_DIM), HEAD_DIM)
            dqt_scr[part, :] = dot(kt_ref[part, :], low) * root
        dk_scr[:, here] = (jnp.where(lane < HEAD_DIM, dk[0], dk[1]) * root).astype(BF)
        dv_scr[:, here] = jnp.where(lane < HEAD_DIM, dv[0], dv[1]).astype(BF)
        return carry

    lax.fori_loop(0, width // pair, heads, 0)
    dq = dqt_scr[...].T.astype(BF)
    dk, dv = dk_scr[...], dv_scr[...]
    term = term_scr[...]
    in_grad = branch + dot(dq, w_scr[0]) + dot(dk, w_scr[1]) + dot(dv, w_scr[2])
    if outs is not None:
        chip_out, core_out, projected_outs = outs
        chip_out[:, :width] = branch_low
        core_out[:rows, :width] = branch_low
        core_out[:rows, width : 2 * width] = in_grad.astype(BF)
        core_out[:rows, 2 * width : 2 * width + rows] = term.astype(BF)
        head = width // PARTS
        end = 2 * width + rows + 3 * head
        core_out[:rows, end:] = jnp.zeros((rows, core_out.shape[1] - end), BF)
        for part in range(PARTS):
            out, base = (core_out, 2 * width + rows) if part == 1 else (projected_outs[0], 0)
            out, base = (chip_out, width + (part - 2) * 4 * head) if part > 1 else (out, base)
            for i, grad in enumerate((dq, dk, dv)):
                out[:rows, base + i * head : base + (i + 1) * head] = grad[:, part * head : (part + 1) * head]
    return branch, in_grad, dq, dv


def down_kernel(top, unit1, scale1, gain_one, unit2, scale2, gain_two, slope, q_ref, k_ref, v_ref, kt_ref, p_ref, *rest):
    weights, (grad_out, *scratch) = Weights(rest[:WEIGHTS]), rest[WEIGHTS:]
    sum_grad = norm_back(top[...].astype(F32), unit2[...], scale2[:, :1], gain_two[...])
    first_grad = ffn_backward(sum_grad, slope, weights, None)
    _, in_grad, _, _ = attention_backward(
        first_grad, unit1[...], scale1[:, :1], gain_one[...], (q_ref, k_ref, v_ref, kt_ref, p_ref),
        weights.w4, scratch, None,
    )
    grad_out[...] = in_grad.astype(BF)


def down_norm_kernel(info, own_top, passed, unit2, scale2, gain_two, first, ffn_out, core_out, sum_grad_out, sums_out):
    top = jnp.where(info[3] == 0, passed[...], own_top[...]).astype(F32)
    unit = unit2[...]
    sum_grad = norm_back(top, unit, scale2[:, :1], gain_two[...])
    sum_grad_out[...] = sum_grad
    width = first.shape[1]
    ffn_out[...] = sum_grad.astype(BF)
    core_out[:, :width] = sum_grad.astype(BF)
    core_out[:, width:] = first[...]
    sums_out[...] = jnp.zeros_like(sums_out)
    sums_out[3:4] = rows_sum(sum_grad)
    sums_out[4:5] = rows_sum(top * unit)
    sums_out[5:6] = rows_sum(top)


def down_ffn_kernel(sum_grad, slope, *rest):
    weights, (zero, one, chip_out, first_grad_out) = Weights(rest[:WEIGHTS]), rest[WEIGHTS:]
    units = weights.units
    pre_outs = (zero, one, chip_out.at[:, pl.ds(0, units)], chip_out.at[:, pl.ds(units, units)])
    first_grad_out[...] = ffn_backward(sum_grad[...], slope, weights, pre_outs)


def down_attention_kernel(info, first_grad, sums, unit1, scale1, gain_one, q_ref, k_ref, v_ref, kt_ref, p_ref, *rest):
    pres, attended, w4, rest = rest[: PARTS - 1], rest[PARTS - 1], rest[PARTS], rest[PARTS + 1 :]
    chip_out, core_out, zero, sums_scr, *scratch = rest
    unit = unit1[...]
    grad = first_grad[...]
    rows, width = grad.shape
    branch, in_grad, dq, dv = attention_backward(
        grad, unit, scale1[:, :1], gain_one[...], (q_ref, k_ref, v_ref, kt_ref, p_ref),
        w4, scratch, (chip_out, core_out, (zero,)),
    )
    head = width // PARTS
    for i in range(2):
        end = width + (i + 1) * 4 * head
        chip_out[:, end - head : end] = attended[:, i * head : (i + 1) * head]
    sums_scr[...] = sums[...]
    sums_scr[0:1] = rows_sum(branch)
    sums_scr[1:2] = rows_sum(grad * unit)
    sums_scr[2:3] = rows_sum(grad)
    head = width // PARTS
    place = 2 * info[1] + info[0]
    dq_sum, dv_sum = rows_sum(dq.astype(F32)), rows_sum(dv.astype(F32))
    for part in range(PARTS):
        units = pres[0].shape[1]
        pre = pres[part][...] if part < 2 else pres[2][:, (part - 2) * units : (part - 1) * units]
        sums_scr[pl.ds(6 + jnp.bitwise_xor(place, part), 1), :units] = rows_sum(pre.astype(F32))
        here = slice(part * head, (part + 1) * head)
        row = jnp.concatenate(
            [dq_sum[:, here], dv_sum[:, here], jnp.zeros((1, width - 2 * head), F32)], axis=1
        )
        sums_scr[pl.ds(10 + jnp.bitwise_xor(place, part), 1)] = row
    core_out[rows:, :width] = sums_scr[...].astype(BF)
    core_out[rows:, width:] = jnp.zeros((PAD, core_out.shape[1] - width), BF)


def products(lefts, rights):
    total = None
    for left, right in zip(lefts, rights):
        value = dot(left, right, TN)
        total = value if total is None else total + value
    return total.astype(BF)


def products_kernel(rows, left_starts, left_first, right_starts, right_size, *refs):
    lefts, rights, outs = refs[:PARTS], refs[PARTS : 2 * PARTS], refs[2 * PARTS :]
    done = left_first
    for out in outs:
        size = out.shape[0]
        out[...] = products(
            [ref[:rows, start + done : start + done + size] for ref, start in zip(lefts, left_starts)],
            [ref[:rows, start : start + right_size] for ref, start in zip(rights, right_starts)],
        )
        done += size


def add_kernel(left, right, out):
    out[...] = (left[...].astype(F32) + right[...].astype(F32)).astype(BF)


def whole_kernel(info, *refs):
    *sources, out = refs
    row = 0
    for kept, got in zip(sources[::2], sources[1::2]):
        size = kept.shape[0]
        out[row : row + size] = jnp.where(info[4] == 1, kept[...], got[...]).astype(F32)
        row += size


def slot_kernel(with_half, with_whole, with_new, info, *refs):
    refs = list(refs)
    ins = refs[: 2 * with_half + 2 * with_whole + (with_new and with_whole)]
    outs = refs[len(ins) :]

    def add():
        left, right = ins.pop(0), ins.pop(0)
        return (left[...].astype(F32) + right[...].astype(F32)).astype(BF)

    if with_half:
        outs.pop(0)[...] = add()
    if with_whole:
        whole = add()
        outs.pop(0)[...] = whole
        if with_new:
            outs.pop(0)[...] = jnp.where(info[4] == 1, whole, ins.pop(0)[...])


def split_columns_kernel(starts, ref, *outs):
    for start, out in zip(starts, outs):
        out[...] = ref[:, start : start + out.shape[1]]


def float_kernel(out, query, key, value, w_out, w_qkv):
    w_out[...] = out[...].astype(F32)
    for i, low in enumerate((query, key, value)):
        w_qkv[i] = low[...].astype(F32)


def choose_kernel(info, kept, got, out):
    out[...] = jnp.where(info[4] == 1, kept[...], got[...])


def stack_kernel(info, keep, got, out):
    out[info[1]] = keep[...].astype(out.dtype)
    out[1 - info[1]] = got[...].astype(out.dtype)


def last_kernel(docs, info, lengths, own_core, other_core, out, scr):
    seq = scr.shape[0]
    half = seq // 2
    width = out.shape[1]
    start, _ = longest_start(info, lengths, docs)
    here = slice(2 * width, 2 * width + half)
    mine, theirs = own_core[:half, here].astype(F32).T, other_core[:half, here].astype(F32).T
    zero = jnp.zeros_like(mine)
    low = info[0] == 0
    scr[:half, :half] = jnp.where(low, mine, theirs)
    scr[half:, half:] = jnp.where(low, theirs, mine)
    scr[:half, half:] = zero
    scr[half:, :half] = zero
    full = pltpu.roll(scr[...], lax.rem(start + half * (1 - info[0]) + half, seq), 0)[:half]
    full = pltpu.roll(full, start, 1).astype(BF)
    rows = packed_rows(half)
    out[:rows] = jnp.zeros((rows, out.shape[1]), BF)
    out[rows:] = (own_core[half:, :width].astype(F32) + other_core[half:, :width].astype(F32)).astype(BF)
    for row, column, source_row, source_column, count in packing(half):
        out[row : row + count, column : column + half] = full[
            source_row : source_row + count, source_column : source_column + half
        ]


def packing(half):
    rows = packed_rows(half)
    moves = []
    for piece in range(2):
        done = 0
        while done < half:
            place = piece * half + done
            count = min(half - done, rows - place % rows)
            moves.append((place % rows, place // rows * half, done, piece * half, count))
            done += count
    return moves


def packed_rows(half):
    return -(-2 * half // (3 * PAD)) * PAD


def last_out_kernel(info, own, other, logits, noise, mask_out, *outs):
    half = logits.shape[0] // 2
    low = info[0] == 0
    first = jnp.where(low, own[...], other[...])
    second = jnp.where(low, other[...], own[...])
    for base, block in ((0, first), (half, second)):
        for row, column, to_row, to_column, count in packing(half):
            here = (slice(base + to_row, base + to_row + count), slice(to_column, to_column + half))
            slope = 1.0 / (1.0 + jnp.exp(logits[here] + noise[here]))
            mask_out[here] = block[row : row + count, column : column + half].astype(F32) * slope
    sums = own[packed_rows(half) :].astype(F32)
    *vectors, b_in, b_qv = outs
    for i, out in enumerate(vectors):
        out[...] = sums[i : i + 1]
    place = 2 * info[1] + info[0]
    for part in range(PARTS):

        @pl.when(place == part)
        def _():
            b_in[...] = sums[6 + part : 7 + part, : b_in.shape[1]]
            head = b_qv.shape[1]
            b_qv[0:1] = sums[10 + part : 11 + part, :head]
            b_qv[1:2] = sums[10 + part : 11 + part, head : 2 * head]


def rows_kernel(docs, column, info, lengths, own, other, keep_out, give_out, scr):
    seq, width = scr.shape
    half = seq // 2
    rows = seq // PARTS
    start, _ = longest_start(info, lengths, docs)
    low = info[0] == 0
    here = slice(column, column + width)
    mine, theirs = own[:half, here].astype(F32), other[:half, here].astype(F32)
    scr[:half] = jnp.where(low, mine, theirs)
    scr[half:] = jnp.where(low, theirs, mine)
    place = 2 * info[1] + info[0]
    far = 2 * (1 - info[1]) + info[0]
    keep_out[...] = pltpu.roll(scr[...], lax.rem(start + seq - place * rows, seq), 0)[:rows].astype(BF)
    give_out[...] = pltpu.roll(scr[...], lax.rem(start + seq - far * rows, seq), 0)[:rows].astype(BF)


class Order:
    def __init__(self):
        self.last = None
        self.due = []

    def after(self, *values):
        if self.last is None:
            return values
        return lax.optimization_barrier((*values, self.last))[: len(values)]

    def arrived(self, *values):
        self.due += values

    def run(self, step, *inputs):
        return self.run_with((), step, *inputs)[0]

    def run_with(self, arrivals, step, *inputs):
        due, self.due = self.due, []
        values = self.after(*inputs, *arrivals, *due)[: len(inputs) + len(arrivals)]
        result = step(*values[: len(inputs)])
        self.last = jax.tree.leaves(result)[0]
        return result, values[len(inputs) :]


def shards(
    inputs, out_grad, doc_lengths, w_qkv, b_qv, w_out, b_out, norm1_gain, norm1_bias,
    w_in, b_in, w_back, b_back, norm2_gain, norm2_bias, mask_logits, mask_noise,
):
    count, seq, width = inputs.shape
    docs = doc_lengths.shape[1]
    core, chip = lax.axis_index("core"), lax.axis_index("chip")
    odd = lax.axis_index("dp") % 2
    part = 2 * chip + core
    half = seq // 2
    head = w_out.shape[1]
    units = w_in.shape[2]
    assert lax.axis_size("pipe") == 2 and lax.axis_size("chip") == 2 and count == 2
    assert lax.axis_size("dp") % 2 == 0 and PARTS * head == width and seq % (2 * PARTS) == 0
    place = lax.axis_index("dp")
    line = lax.axis_size("dp") == 4
    middle = ((place == 1) | (place == 2)) if line else place >= 0
    info = jnp.stack([core, chip, odd, lax.axis_index("pipe"), middle]).astype(jnp.int32)
    order = Order()
    everyone = ("chip", "core")

    def diagonal(block):
        return lax.ppermute(block, everyone, [(i, i ^ 3) for i in range(PARTS)])

    low_rows = pltpu.VMEM((half, width), BF)
    low_columns = pltpu.VMEM((width, half), BF)
    up_scratch = [low_rows, low_rows, low_columns, low_columns]
    down_scratch = [pltpu.VMEM((width, half), F32), low_rows, low_rows, low_rows, pltpu.VMEM((half, half), F32)]
    flat = shape(half, width)
    flat32 = shape(half, width, dtype=F32)

    pack, half_pack, half_in = call(
        split_kernel,
        [shape(4 * head + 2 * PAD, width), shape(2 * head + PAD, width), shape(width // 2 + 2 * PAD, units)],
        [SMEM] + [HBM] * 5,
        (info, jnp.swapaxes(w_qkv[0], 1, 2).reshape(3 * head, width), w_out[0], w_in[0], b_in, b_qv[0]),
        [pltpu.VMEM((3 * head, width), BF), pltpu.VMEM((head, width), BF), pltpu.VMEM((width // 2, units), BF),
         pltpu.VMEM((1, units), BF), pltpu.VMEM((2, head), BF), pltpu.SemaphoreType.DMA((5,))],
        56 << 20,
    )
    got_pack = swap(half_pack, "chip")
    got_in = swap(half_in, "chip")
    near = [swap(v, "core") for v in (pack, w_in[0], w_back[0])]

    def prepare(*args):
        return call(
            functools.partial(prepare_kernel, docs),
            [flat, flat, shape(half, half, dtype=F32)],
            [SMEM, SMEM, VMEM, VMEM, VMEM, VMEM],
            args,
        )

    tokens0, top0, bias = order.run(prepare, info, doc_lengths, inputs, out_grad, mask_logits[0], mask_noise[0])
    (got_pack,) = order.after(got_pack)
    also_pack = swap(got_pack, "dp")
    w_back_own, got_pack = lax.optimization_barrier((w_back[0], got_pack))
    got_back = swap(w_back_own, "chip")
    cross_got_pack = swap(got_pack, "core")
    got_in, got_pack = lax.optimization_barrier((got_in, got_pack))
    also_in = swap(got_in, "dp")
    cross_got_in = swap(got_in, "core")
    also_pack, got_in = lax.optimization_barrier((also_pack, got_in))
    p1 = (pack, near[0], got_pack, also_pack, cross_got_pack, swap(also_pack, "core"))

    def attention(tokens, *p1):
        return call(
            attention_kernel,
            [flat32, shape(4, width, width), shape(2, width, dtype=F32), shape(PARTS, units, dtype=F32)],
            [SMEM] + [VMEM] * 11,
            (info, tokens, bias, b_out, norm1_gain, norm1_bias) + p1,
            up_scratch,
        )

    first, w4, both_b_qv, full_b_in = order.run(attention, tokens0, *p1)
    total = order.run(
        lambda *a: call(ffn_near_kernel, flat32, [VMEM] * 7, a),
        first, b_back, full_b_in, w_in[0], near[1], w_back[0], near[2],
    )
    (also_in,) = order.after(also_in)
    hidden_far, in_far = order.run(
        lambda *a: call(
            ffn_far_kernel, [shape(half, 2 * units), shape(2, width, units)], [SMEM] + [VMEM] * 6, (info,) + a
        ),
        first, full_b_in, got_in, also_in, cross_got_in, swap(also_in, "core"),
    )
    (got_back,) = order.after(got_back)
    backs = (w_back[0], near[2], got_back, swap(got_back, "core"))
    second = order.run(
        lambda *a: call(ffn_end_kernel, flat, [VMEM] * 6, a),
        total, hidden_far, norm2_gain, norm2_bias, backs[2], backs[3],
    )
    weights = (w4, both_b_qv, full_b_in, w_in[0], near[1], in_far) + backs
    passed = lax.ppermute(second, "pipe", [(0, 1)])

    tokens = order.run(
        lambda *a: call(choose_tokens_kernel, flat, [SMEM, VMEM, VMEM], (info,) + a), tokens0, passed
    )
    tokens_chip = swap(tokens, "chip")
    tokens_core = swap(tokens, "core")

    keep_width = units + head

    def layer(tokens):
        return call(
            layer_kernel,
            [flat, flat, shape(half, 2 * head)]
            + [shape(half, keep_width)] * 2 + [shape(half, units)] * 2
            + [flat, flat, flat, shape(width, half), shape(width // HEAD_DIM, half, half),
               flat32, shape(half, 128, dtype=F32), shape(half, PARTS * units),
               flat32, shape(half, 128, dtype=F32)],
            [VMEM] * (8 + WEIGHTS),
            (tokens, bias, b_out, norm1_gain, norm1_bias, b_back, norm2_gain, norm2_bias) + weights,
            up_scratch,
        )

    second, first_low, far_attended, *kept = order.run(layer, tokens)
    keeps, kept = kept[:PARTS], kept[PARTS:]
    q, k, v, kt, chance, unit1, scale1, slope, unit2, scale2 = kept
    keeps = [keeps[0], swap(keeps[1], "core"), swap(keeps[2], "chip"), diagonal(keeps[3])]
    far_chip = swap(first_low, "chip")

    def down(top):
        return call(
            down_kernel, flat, [VMEM] * (13 + WEIGHTS),
            (top, unit1, scale1, norm1_gain, unit2, scale2, norm2_gain, slope, q, k, v, kt, chance) + weights,
            down_scratch,
        )

    down_grad, (tokens_chip, tokens_core) = order.run_with((tokens_chip, tokens_core), down, top0)
    passed = lax.ppermute(down_grad, "pipe", [(1, 0)])
    tokens_all = [tokens, tokens_core, tokens_chip, swap(tokens_chip, "core")]

    def rows_of(column, own_rows, other_rows):
        return call(
            functools.partial(rows_kernel, docs, column),
            [shape(seq // PARTS, width)] * 2,
            [SMEM, SMEM, VMEM, VMEM],
            (info, doc_lengths, own_rows, other_rows),
            [pltpu.VMEM((seq, width), F32)],
        )

    def down_norm(top, passed):
        return call(
            down_norm_kernel, [flat, shape(half, 2 * width), flat32, shape(PAD, width, dtype=F32)], [SMEM] + [VMEM] * 6,
            (info, top, passed, unit2, scale2, norm2_gain, first_low),
        )

    (ffn_low, ffn_pack, sum_grad, sums), keeps[1:] = order.run_with(keeps[1:], down_norm, top0, passed)
    ffn_chip = swap(ffn_low, "chip")
    ffn_core = swap(ffn_pack, "core")

    def down_ffn(sum_grad):
        return call(
            down_ffn_kernel,
            [shape(half, units)] * 2 + [shape(half, 2 * units), flat32], [VMEM] * (2 + WEIGHTS),
            (sum_grad, slope) + weights,
        )

    *pres, first_grad = order.run(down_ffn, sum_grad)
    pre_core = swap(pres[1], "core")

    lanes = [dict(own=None, half=None, whole=None, end=None, middle=None, names=[]) for _ in range(2)]
    final = {}

    def slot(lane, name=None, new=None):
        if not line:
            if new is not None:
                final[name] = (lax.psum(new, "dp"),) * 2
            return
        if lane["whole"] is not None:
            final[lane["names"].pop(0)] = (lane["whole"], lane["end"])
        with_half, with_whole = lane["own"] is not None, lane["half"] is not None
        ins = [lane["own"], lane["end"]] if with_half else []
        if with_whole:
            ins += [lane["half"], lane["middle"]] + ([new] if new is not None else [])
        half_sum = whole = None
        going = new
        if ins:
            outs = with_half + with_whole + (with_whole and new is not None)
            results = order.run(
                lambda *a: call(
                    functools.partial(slot_kernel, with_half, with_whole, new is not None),
                    [shape(*a[0].shape)] * outs, [SMEM] + [VMEM] * len(a), (info,) + a,
                ),
                *ins,
            )
            if with_half:
                half_sum = results[0]
            if with_whole:
                whole = results[int(with_half)]
                going = results[-1] if new is not None else whole
        routes = ([(0, 1), (3, 2)] if new is not None else []) + ([(1, 0), (2, 3)] if whole is not None else [])
        lane["end"] = lax.ppermute(going, "dp", routes) if routes else None
        lane["middle"] = lax.ppermute(half_sum, "dp", [(1, 2), (2, 1)]) if half_sum is not None else None
        lane["own"], lane["half"], lane["whole"] = new, half_sum, whole
        if new is not None:
            lane["names"].append(name)

    def matrix(*names):
        sources = [v for name in names for v in final[name]]
        rows = sum(v.shape[0] for v in sources) // 2
        return order.run(
            lambda *a: call(
                whole_kernel, shape(rows, a[0].shape[1], dtype=F32), [SMEM] + [VMEM] * len(a), (info,) + a
            ),
            *sources,
        )

    def products_of(outs, lefts, left_starts, left_first, rights, right_starts, right_size):
        return order.run(
            lambda *a: call(
                functools.partial(products_kernel, half, left_starts, left_first, right_starts, right_size),
                [shape(n, right_size) for n in outs], [VMEM] * (2 * PARTS), a,
            ),
            *lefts, *rights,
        )

    chip_width = width + 8 * head

    def down_attention(first_grad, sums, *pres):
        return call(
            down_attention_kernel,
            [shape(half, chip_width), shape(half + PAD, -(-(2 * width + half + 3 * head) // 128) * 128)]
            + [shape(half, 3 * head)],
            [SMEM] + [VMEM] * (11 + PARTS),
            (info, first_grad, sums, unit1, scale1, norm1_gain, q, k, v, kt, chance) + pres + (far_attended, w4),
            [pltpu.VMEM((PAD, width), F32)] + down_scratch,
        )

    down_core_projected = 2 * width + half
    down_chip, down_pack, projected_zero = order.run(down_attention, first_grad, sums, *pres)
    ffn_chip, far_chip, pre_give = order.after(ffn_chip, far_chip, pres[2])
    ffns = [ffn_low, ffn_core, ffn_chip, swap(ffn_chip, "core")]
    far_cross = swap(far_chip, "core")
    pre_chip = swap(pre_give, "chip")
    none = (0, 0, 0, 0)
    quarter = units // 4
    one, two = lanes
    (far_cross,) = order.after(far_cross)
    back = products_of((quarter,) * 4, keeps, none, 0, ffns, none, width)
    slot(one, "back0", back[0])
    slot(two, "back1", back[1])
    (down_give,) = order.after(down_pack)
    down_other = swap(down_give, "core")

    def last_chunk(*args):
        return call(
            functools.partial(last_kernel, docs),
            shape(packed_rows(half) + PAD, width),
            [SMEM, SMEM] + [VMEM] * 2,
            (info, doc_lengths) + args,
            [pltpu.VMEM((seq, seq), F32)],
        )

    def split_columns(starts, sizes, packed):
        return order.run(
            lambda a: call(
                functools.partial(split_columns_kernel, starts), [shape(half, n) for n in sizes], [VMEM], (a,)
            ),
            packed,
        )

    order.arrived(down_other)
    slot(one, "back2", back[2])
    slot(two, "back3", back[3])
    (far_pre,) = split_columns((units,), (units,), pre_chip)
    far_pre = swap(far_pre, "core")
    (down_chip_give,) = order.after(down_chip)
    branch_chip = swap(down_chip_give, "chip")
    inner = products_of(
        (quarter,) * 4, [first_low, ffn_core, far_chip, far_cross], (0, width, 0, 0), 0,
        [pres[0], pre_core, pre_chip, far_pre], none, units,
    )
    slot(one, "in0", inner[0])
    slot(two, "in1", inner[1])
    last = order.run(last_chunk, down_pack, down_other)
    last_got = swap(last, "chip")
    slot(one, "in2", inner[2])
    far_branch, far_projected = split_columns((0, width + 4 * head), (width, 4 * head), branch_chip)
    far_branch, far_projected = swap(far_branch, "core"), swap(far_projected, "core")
    slot(two, "in3", inner[3])
    (w_out_low,) = products_of(
        (head,), [*keeps[:2], branch_chip, far_projected], (units, units, width + 3 * head, 3 * head), 0,
        [down_chip, down_other, branch_chip, far_branch], none, width,
    )
    w_qkv_low = products_of(
        (head,) * 3, [projected_zero, down_other, branch_chip, far_projected], (0, down_core_projected, width, 0), 0,
        tokens_all, none, width,
    )
    slot(one, "out", w_out_low)
    slot(two, "q", w_qkv_low[0])
    (second,) = order.after(second)
    second_other = swap(second, "core")
    grad_keep, grad_give = order.run(functools.partial(rows_of, width), down_pack, down_other)
    last = order.run(lambda a, b: call(add_kernel, shape(*a.shape), [VMEM] * 2, (a, b)), last, last_got)
    slot(one, "last", last)
    slot(two, "k", w_qkv_low[1])
    act_keep, act_give = order.run(functools.partial(rows_of, 0), second, second_other)
    act_give, grad_give = order.after(act_give, grad_give)
    act_got, grad_got = swap(act_give, "chip"), swap(grad_give, "chip")
    grad_w_back = matrix("back0", "back1", "back2", "back3")
    slot(one, "v", w_qkv_low[2])
    slot(two)
    activations = order.run(
        lambda a, b: call(stack_kernel, shape(2, seq // PARTS, width), [SMEM, VMEM, VMEM], (info, a, b)),
        act_keep, act_got,
    )
    input_grads = order.run(
        lambda a, b: call(stack_kernel, shape(2, seq // PARTS, width, dtype=F32), [SMEM, VMEM, VMEM], (info, a, b)),
        grad_keep, grad_got,
    )
    slot(one)
    grad_w_in = matrix("in0", "in1", "in2", "in3")
    slot(two)
    done = {}

    def choose(name):
        done[name] = order.run(
            lambda a, b: call(choose_kernel, shape(*a.shape), [SMEM, VMEM, VMEM], (info, a, b)), *final[name]
        )

    choose("out")
    choose("q")
    slot(one)
    choose("last")
    slot(two)
    choose("k")
    slot(one)
    choose("v")
    last = done["last"]
    grad_w_out, grad_w_qkv = order.run(
        lambda *a: call(
            float_kernel, [shape(head, width, dtype=F32), shape(3, head, width, dtype=F32)], [VMEM] * 4, a
        ),
        done["out"], done["q"], done["k"], done["v"],
    )
    grad_mask, *vectors, grad_b_in, grad_b_qv = call(
        last_out_kernel,
        [shape(seq, seq, dtype=F32)] + [shape(1, width, dtype=F32)] * 6
        + [shape(1, units, dtype=F32), shape(2, head, dtype=F32)],
        [SMEM] + [VMEM] * 4,
        (info, last, swap(last, "core"), mask_logits[0], mask_noise[0]),
    )
    results = (
        activations, input_grads, jnp.swapaxes(grad_w_qkv, 1, 2), grad_b_qv, grad_w_out,
        vectors[0][0], vectors[1][0], vectors[2][0],
        grad_w_in, grad_b_in[0], grad_w_back,
        vectors[3][0], vectors[4][0], vectors[5][0],
        grad_mask,
    )
    return tuple(item[None] for item in results)


def solution(mesh):
    pipe, dp, tensor = (mesh.shape[name] for name in ("pipe", "dp", "tensor"))
    split = Mesh(mesh.devices.reshape(pipe, dp, tensor // 2, 2), ("pipe", "dp", "chip", "core"))
    placed = (
        P("dp", None, None),
        P("dp", None, None),
        P("dp", None),
        P("pipe", None, None, TENSOR),
        P("pipe", None, TENSOR),
        P("pipe", TENSOR, None),
        P("pipe", None),
        P("pipe", None),
        P("pipe", None),
        P("pipe", None, TENSOR),
        P("pipe", TENSOR),
        P("pipe", TENSOR, None),
        P("pipe", None),
        P("pipe", None),
        P("pipe", None),
        P("pipe", None, None),
        P("pipe", None, None),
    )
    return jax.shard_map(
        shards,
        mesh=split,
        in_specs=placed,
        out_specs=(
            P("pipe", "dp", TENSOR, None),
            P("pipe", "dp", TENSOR, None),
            P("pipe", None, None, TENSOR),
            P("pipe", None, TENSOR),
            P("pipe", TENSOR, None),
            P("pipe", None),
            P("pipe", None),
            P("pipe", None),
            P("pipe", None, TENSOR),
            P("pipe", TENSOR),
            P("pipe", TENSOR, None),
            P("pipe", None),
            P("pipe", None),
            P("pipe", None),
            P("pipe", None, None),
        ),
        check_vma=False,
    )
```

```python
import functools
import math

import jax
import jax.numpy as jnp
from jax import lax
from jax.experimental import pallas as pl
from jax.experimental.pallas import tpu as pltpu
from jax.sharding import Mesh
from jax.sharding import PartitionSpec as P

HEAD_DIM = 64
EPSILON = 1e-12
MASKED = -1e30
BF = jnp.bfloat16
F32 = jnp.float32
NT = ((1,), (1,))
TN = ((0,), (0,))
NN = ((1,), (0,))
PARTS = 4
PAD = 16
TENSOR = ("chip", "core")
LIMIT = 8 << 20


def dot(left, right, dims=NN):
    return lax.dot_general(left, right, (dims, ((), ())), preferred_element_type=F32)


def swap(block, axis):
    return lax.ppermute(block, axis, [(i, i ^ 1) for i in range(lax.axis_size(axis))])


SMEM = pl.BlockSpec(memory_space=pltpu.SMEM)
VMEM = pl.BlockSpec(memory_space=pltpu.VMEM)
HBM = pl.BlockSpec(memory_space=pltpu.HBM)


def shape(*dims, dtype=BF):
    return jax.ShapeDtypeStruct(dims, dtype)


def call(kernel, out, ins, args, scratch=(), limit=LIMIT):
    return pl.pallas_call(
        kernel,
        out_shape=out,
        in_specs=ins,
        out_specs=jax.tree.map(lambda _: VMEM, out),
        scratch_shapes=list(scratch),
        compiler_params=pltpu.CompilerParams(vmem_limit_bytes=limit),
        cost_estimate=pl.CostEstimate(flops=0, bytes_accessed=0, transcendentals=0),
    )(*args)


def longest_start(info, lengths, docs):
    chip = info[1]
    sizes = [lengths[chip, i] for i in range(docs)]
    bounds, start, total = [], jnp.int32(0), jnp.int32(0)
    longest = sizes[0]
    for size in sizes[1:]:
        longest = jnp.maximum(longest, size)
    for size in sizes:
        start = jnp.where(size == longest, total, start)
        total = total + size
        bounds.append(total)
    return start, bounds


def prepare_kernel(docs, info, lengths, inputs, grads, logits, noise, tokens_out, top_out, bias_out):
    seq = logits.shape[0]
    half = seq // 2
    start, bounds = longest_start(info, lengths, docs)
    begin = lax.rem(start + half * info[0], seq)
    shift = lax.rem(seq - begin, seq)
    tokens_out[...] = pltpu.roll(inputs[info[1]].astype(F32), shift, 0)[:half].astype(BF)
    top_out[...] = pltpu.roll(grads[info[1]].astype(F32), shift, 0)[:half].astype(BF)
    table = logits[...] + noise[...]
    table = pltpu.roll(table, shift, 0)[:half]
    table = pltpu.roll(table, shift, 1)[:, :half]
    term = jnp.minimum(table, 0.0) - jnp.log1p(jnp.exp(-jnp.abs(table)))

    def owners(axis):
        place = begin + lax.broadcasted_iota(jnp.int32, (half, half), axis)
        place = jnp.where(place >= seq, place - seq, place)
        owner = jnp.zeros((half, half), jnp.int32)
        for bound in bounds:
            owner = owner + jnp.where(place >= bound, 1, 0)
        return owner

    bias_out[...] = jnp.where(owners(0) == owners(1), term, MASKED).T


def split_kernel(info, qkv, w_out, w_in, b_in, b_qv, pack, half_pack, half_in, qkv_scr, out_scr, in_scr, b_in_scr, b_qv_scr, sems):
    size = w_in.shape[0] // 2
    pairs = (
        (qkv, qkv_scr), (w_out, out_scr), (b_in, b_in_scr), (b_qv, b_qv_scr),
        (w_in.at[pl.ds(pl.multiple_of(info[2] * size, size), size)], in_scr),
    )
    copies = [pltpu.make_async_copy(src, dst, sems.at[i]) for i, (src, dst) in enumerate(pairs)]
    for copy in copies:
        copy.start()
    for copy in copies:
        copy.wait()
    head = out_scr.shape[0]
    step = 2 * head + PAD
    pack[: 2 * head] = qkv_scr[: 2 * head]
    pack[2 * head : step] = jnp.zeros((PAD, pack.shape[1]), BF)
    pack[2 * head : 2 * head + 1, : b_in.shape[1]] = b_in_scr[...]
    pack[step : step + head] = qkv_scr[2 * head :]
    pack[step + head : step + 2 * head] = out_scr[...]
    pack[step + 2 * head :] = jnp.zeros((PAD, pack.shape[1]), BF)
    pack[step + 2 * head : step + 2 * head + 1, :head] = b_qv_scr[0:1]
    pack[step + 2 * head : step + 2 * head + 1, head : 2 * head] = b_qv_scr[1:2]
    half_pack[...] = pack[pl.ds(pl.multiple_of(info[2] * step, PAD), step)]
    half_in[:size] = in_scr[...]
    half_in[size:] = jnp.zeros((half_in.shape[0] - size, half_in.shape[1]), BF)


def norm(values):
    average = jnp.mean(values, axis=-1, keepdims=True)
    centred = values - average
    variance = jnp.mean(centred * centred, axis=-1, keepdims=True)
    scale = lax.rsqrt(variance + EPSILON)
    return centred * scale, scale


def norm_back(grad, unit, scale, gain):
    direct = grad * gain
    return scale * (
        direct
        - jnp.mean(direct, axis=-1, keepdims=True)
        - unit * jnp.mean(direct * unit, axis=-1, keepdims=True)
    )


def assemble(info, pieces, w4, b_qv, b_in):
    head = w4.shape[1] // PARTS
    step = 2 * head + PAD
    even = info[2] == 0
    for part in range(PARTS):
        here = slice(part * head, (part + 1) * head)
        for which in range(2):
            if part < 2:
                block = pieces[part][which * step : (which + 1) * step]
            else:
                got, also = pieces[2 * part - 2], pieces[2 * part - 1]
                block = jnp.where(even, got[...], also[...]) if which == 0 else jnp.where(even, also[...], got[...])
            w4[2 * which, here] = block[:head]
            w4[2 * which + 1, here] = block[head : 2 * head]
            if which == 0:
                b_in[part : part + 1] = block[2 * head : 2 * head + 1, : b_in.shape[1]].astype(F32)
            else:
                row = block[2 * head : 2 * head + 1].astype(F32)
                b_qv[0:1, here] = row[:, :head]
                b_qv[1:2, here] = row[:, head : 2 * head]


class Weights:
    def __init__(self, refs):
        self.w4, self.b_qv, self.b_in, self.in_near, self.in_far, self.backs = (
            refs[0], refs[1], refs[2], refs[3:5], refs[5], refs[6:10]
        )
        self.units = self.in_far.shape[2]

    def w_in(self, part):
        return self.in_near[part][...] if part < 2 else self.in_far[part - 2]

    def w_back(self, part):
        return self.backs[part][...]


WEIGHTS = 10


def attention_forward(tokens, bias_ref, w4, b_qv, out_parts, scratch):
    width = tokens.shape[1]
    q_scr, k_scr, vt_scr, at_scr = scratch
    queries = (dot(tokens, w4[0], NT) + b_qv[0:1]).astype(BF)
    keys = dot(tokens, w4[1], NT).astype(BF)
    values = (dot(tokens, w4[2], NT) + b_qv[1:2]).astype(BF)
    values_t = values.T
    if out_parts is not None:
        q_out, k_out, v_out, kt_out, p_out = out_parts
        q_out[...], k_out[...], v_out[...] = queries, keys, values
        kt_out[...] = keys.T
    q_scr[...] = queries * jnp.asarray(1.0 / math.sqrt(HEAD_DIM), BF)
    k_scr[...] = keys
    vt_scr[...] = values_t
    pair = 2 * HEAD_DIM
    lane = lax.broadcasted_iota(jnp.int32, (tokens.shape[0], pair), 1)

    def heads(j):
        here = pl.ds(j * pair, pair)
        q_pair, k_pair = q_scr[:, here], k_scr[:, here]
        for s in range(2):
            mine = (lane >= HEAD_DIM) if s else (lane < HEAD_DIM)
            scores = dot(jnp.where(mine, k_pair, jnp.zeros_like(k_pair)), q_pair, NT) + bias_ref[...]
            exponent = jnp.exp(scores - jnp.max(scores, axis=0, keepdims=True))
            chance = (exponent * (1.0 / jnp.sum(exponent, axis=0, keepdims=True))).astype(BF)
            if out_parts is not None:
                p_out[2 * j + s] = chance
            rows = pl.ds(j * pair + s * HEAD_DIM, HEAD_DIM)
            at_scr[rows, :] = dot(vt_scr[rows, :], chance).astype(BF)

    for j in range(width // pair):
        heads(j)
    return at_scr[...].T


def gelu(values):
    cdf = 0.5 * (1.0 + lax.erf(values * math.sqrt(0.5)))
    return values * cdf, cdf


def attention_kernel(info, tokens, bias, b_out, gain, offset, *rest):
    pieces, (first_out, w4, b_qv, b_in, *scratch) = rest[:6], rest[6:]
    assemble(info, pieces, w4, b_qv, b_in)
    attended = attention_forward(tokens[...], bias, w4, b_qv, None, scratch)
    unit, _ = norm(tokens[...].astype(F32) + dot(attended, w4[3]) + b_out[...])
    first_out[...] = unit * gain[...] + offset[...]


def ffn_near_kernel(first, b_back, b_in, *rest):
    w_ins, w_backs, out = rest[:2], rest[2:4], rest[4]
    first_low = first[...].astype(BF)
    total = first[...] + b_back[...]
    for part in range(2):
        hidden, _ = gelu(dot(first_low, w_ins[part][...]) + b_in[part : part + 1])
        total = total + dot(hidden.astype(BF), w_backs[part][...])
    out[...] = total


def ffn_far_kernel(info, first, b_in, far_got, far_also, cross_got, cross_also, hidden_out, in_out):
    even = info[2] == 0
    units = in_out.shape[2]
    half = in_out.shape[1] // 2
    first_low = first[...].astype(BF)
    for part, (got, also) in enumerate(((far_got, far_also), (cross_got, cross_also))):
        in_out[part, :half] = jnp.where(even, got[:half], also[:half])
        in_out[part, half:] = jnp.where(even, also[:half], got[:half])
        hidden, _ = gelu(dot(first_low, in_out[part]) + b_in[part + 2 : part + 3])
        hidden_out[:, part * units : (part + 1) * units] = hidden.astype(BF)


def ffn_end_kernel(total, hidden, gain, offset, far, cross, out):
    units = far.shape[0]
    result = total[...] + dot(hidden[:, :units], far[...]) + dot(hidden[:, units:], cross[...])
    unit, _ = norm(result)
    out[...] = (unit * gain[...] + offset[...]).astype(BF)


def choose_tokens_kernel(info, first_tokens, passed, out):
    out[...] = jnp.where(info[3] == 0, first_tokens[...], passed[...])


def layer_kernel(tokens_ref, bias, b_out, gain_one, offset_one, b_back, gain_two, offset_two, *rest):
    weights, rest = Weights(rest[:WEIGHTS]), rest[WEIGHTS:]
    second_out, first_out, att_out, *rest = rest
    keep_outs, rest = rest[:PARTS], rest[PARTS:]
    (q_out, k_out, v_out, kt_out, p_out, unit1_out, scale1_out, slope_out, unit2_out, scale2_out, *scratch) = rest
    tokens = tokens_ref[...]
    width = tokens.shape[1]
    attended = attention_forward(
        tokens, bias, weights.w4, weights.b_qv, (q_out, k_out, v_out, kt_out, p_out), scratch
    )
    units, head = weights.units, width // PARTS
    for part in range(PARTS):
        out, base = (keep_outs[part], units) if part < 2 else (att_out, (part - 2) * head)
        out[:, base : base + head] = attended[:, part * head : (part + 1) * head]
    unit, scale = norm(tokens.astype(F32) + dot(attended, weights.w4[3]) + b_out[...])
    unit1_out[...] = unit
    scale1_out[...] = jnp.broadcast_to(scale, scale1_out.shape)
    first = unit * gain_one[...] + offset_one[...]
    first_low = first.astype(BF)
    first_out[...] = first_low
    total = first + b_back[...]
    for part in range(PARTS):
        pre = dot(first_low, weights.w_in(part)) + weights.b_in[part : part + 1]
        value, cdf = gelu(pre)
        hidden = value.astype(BF)
        keep_outs[part][:, :units] = hidden
        density = jnp.exp(-0.5 * pre * pre) * (1.0 / math.sqrt(2.0 * math.pi))
        slope_out[:, part * units : (part + 1) * units] = (cdf + pre * density).astype(BF)
        total = total + dot(hidden, weights.w_back(part))
    unit, scale = norm(total)
    unit2_out[...] = unit
    scale2_out[...] = jnp.broadcast_to(scale, scale2_out.shape)
    second_out[...] = (unit * gain_two[...] + offset_two[...]).astype(BF)


def rows_sum(values):
    return jnp.sum(values, axis=0, keepdims=True)


def ffn_backward(sum_grad, slope, weights, pre_outs):
    units = weights.units
    ffn_low = sum_grad.astype(BF)
    first_grad = sum_grad
    for part in range(PARTS):
        pre = dot(ffn_low, weights.w_back(part), NT) * slope[:, part * units : (part + 1) * units].astype(F32)
        pre = pre.astype(BF)
        if pre_outs is not None:
            pre_outs[part][...] = pre
        first_grad = first_grad + dot(pre, weights.w_in(part), NT)
    return first_grad


def attention_backward(first_grad, unit, scale, gain, refs, w_scr, scratch, outs):
    q_ref, k_ref, v_ref, kt_ref, p_ref = refs
    width = first_grad.shape[1]
    branch = norm_back(first_grad, unit, scale, gain)
    branch_low = branch.astype(BF)
    att_grad = dot(branch_low, w_scr[3], NT).astype(BF)
    pair = 2 * HEAD_DIM
    rows = first_grad.shape[0]
    lane = lax.broadcasted_iota(jnp.int32, (rows, pair), 1)
    root = 1.0 / math.sqrt(HEAD_DIM)
    dqt_scr, dk_scr, dv_scr, o_scr, term_scr = scratch
    o_scr[...] = att_grad
    term_scr[...] = jnp.zeros((rows, rows), F32)

    def heads(j, carry):
        here = pl.ds(pl.multiple_of(j * pair, pair), pair)
        q_pair, v_pair, o_pair = q_ref[:, here], v_ref[:, here], o_scr[:, here]
        dk, dv = [], []
        for s in range(2):
            mine = (lane >= HEAD_DIM) if s else (lane < HEAD_DIM)
            chance_low = p_ref[2 * j + s]
            chance = chance_low.astype(F32)
            chance_grad = dot(jnp.where(mine, v_pair, jnp.zeros_like(v_pair)), o_pair, NT)
            inner = jnp.sum(chance * chance_grad, axis=0, keepdims=True)
            score = chance * (chance_grad - inner)
            term_scr[...] += score
            low = score.astype(BF)
            dv.append(dot(chance_low, o_pair))
            dk.append(dot(low, q_pair))
            part = pl.ds(pl.multiple_of(j * pair + s * HEAD_DIM, HEAD_DIM), HEAD_DIM)
            dqt_scr[part, :] = dot(kt_ref[part, :], low) * root
        dk_scr[:, here] = (jnp.where(lane < HEAD_DIM, dk[0], dk[1]) * root).astype(BF)
        dv_scr[:, here] = jnp.where(lane < HEAD_DIM, dv[0], dv[1]).astype(BF)
        return carry

    lax.fori_loop(0, width // pair, heads, 0)
    dq = dqt_scr[...].T.astype(BF)
    dk, dv = dk_scr[...], dv_scr[...]
    term = term_scr[...]
    in_grad = branch + dot(dq, w_scr[0]) + dot(dk, w_scr[1]) + dot(dv, w_scr[2])
    if outs is not None:
        chip_out, core_out, projected_outs = outs
        chip_out[:, :width] = branch_low
        core_out[:rows, :width] = branch_low
        core_out[:rows, width : 2 * width] = in_grad.astype(BF)
        core_out[:rows, 2 * width : 2 * width + rows] = term.astype(BF)
        head = width // PARTS
        end = 2 * width + rows + 3 * head
        core_out[:rows, end:] = jnp.zeros((rows, core_out.shape[1] - end), BF)
        for part in range(PARTS):
            out, base = (core_out, 2 * width + rows) if part == 1 else (projected_outs[0], 0)
            out, base = (chip_out, width + (part - 2) * 4 * head) if part > 1 else (out, base)
            for i, grad in enumerate((dq, dk, dv)):
                out[:rows, base + i * head : base + (i + 1) * head] = grad[:, part * head : (part + 1) * head]
    return branch, in_grad, dq, dv


def down_kernel(top, unit1, scale1, gain_one, unit2, scale2, gain_two, slope, q_ref, k_ref, v_ref, kt_ref, p_ref, *rest):
    weights, (grad_out, *scratch) = Weights(rest[:WEIGHTS]), rest[WEIGHTS:]
    sum_grad = norm_back(top[...].astype(F32), unit2[...], scale2[:, :1], gain_two[...])
    first_grad = ffn_backward(sum_grad, slope, weights, None)
    _, in_grad, _, _ = attention_backward(
        first_grad, unit1[...], scale1[:, :1], gain_one[...], (q_ref, k_ref, v_ref, kt_ref, p_ref),
        weights.w4, scratch, None,
    )
    grad_out[...] = in_grad.astype(BF)


def down_norm_kernel(info, own_top, passed, unit2, scale2, gain_two, first, ffn_out, core_out, sum_grad_out, sums_out):
    top = jnp.where(info[3] == 0, passed[...], own_top[...]).astype(F32)
    unit = unit2[...]
    sum_grad = norm_back(top, unit, scale2[:, :1], gain_two[...])
    sum_grad_out[...] = sum_grad
    width = first.shape[1]
    ffn_out[...] = sum_grad.astype(BF)
    core_out[:, :width] = sum_grad.astype(BF)
    core_out[:, width:] = first[...]
    sums_out[...] = jnp.zeros_like(sums_out)
    sums_out[3:4] = rows_sum(sum_grad)
    sums_out[4:5] = rows_sum(top * unit)
    sums_out[5:6] = rows_sum(top)


def down_ffn_kernel(sum_grad, slope, *rest):
    weights, (*pre_outs, first_grad_out) = Weights(rest[:WEIGHTS]), rest[WEIGHTS:]
    first_grad_out[...] = ffn_backward(sum_grad[...], slope, weights, pre_outs)


def down_attention_kernel(info, first_grad, sums, unit1, scale1, gain_one, q_ref, k_ref, v_ref, kt_ref, p_ref, *rest):
    pres, attended, w4, rest = rest[:PARTS], rest[PARTS], rest[PARTS + 1], rest[PARTS + 2 :]
    chip_out, core_out, zero, sums_scr, *scratch = rest
    unit = unit1[...]
    grad = first_grad[...]
    rows, width = grad.shape
    branch, in_grad, dq, dv = attention_backward(
        grad, unit, scale1[:, :1], gain_one[...], (q_ref, k_ref, v_ref, kt_ref, p_ref),
        w4, scratch, (chip_out, core_out, (zero,)),
    )
    head = width // PARTS
    for i in range(2):
        end = width + (i + 1) * 4 * head
        chip_out[:, end - head : end] = attended[:, i * head : (i + 1) * head]
    sums_scr[...] = sums[...]
    sums_scr[0:1] = rows_sum(branch)
    sums_scr[1:2] = rows_sum(grad * unit)
    sums_scr[2:3] = rows_sum(grad)
    head = width // PARTS
    place = 2 * info[1] + info[0]
    dq_sum, dv_sum = rows_sum(dq.astype(F32)), rows_sum(dv.astype(F32))
    for part in range(PARTS):
        units = pres[0].shape[1]
        pre = pres[part][...]
        sums_scr[pl.ds(6 + jnp.bitwise_xor(place, part), 1), :units] = rows_sum(pre.astype(F32))
        here = slice(part * head, (part + 1) * head)
        row = jnp.concatenate(
            [dq_sum[:, here], dv_sum[:, here], jnp.zeros((1, width - 2 * head), F32)], axis=1
        )
        sums_scr[pl.ds(10 + jnp.bitwise_xor(place, part), 1)] = row
    core_out[rows:, :width] = sums_scr[...].astype(BF)
    core_out[rows:, width:] = jnp.zeros((PAD, core_out.shape[1] - width), BF)


def products(lefts, rights):
    total = None
    for left, right in zip(lefts, rights):
        value = dot(left, right, TN)
        total = value if total is None else total + value
    return total.astype(BF)


def products_kernel(rows, left_starts, left_first, right_starts, right_size, *refs):
    lefts, rights, outs = refs[:PARTS], refs[PARTS : 2 * PARTS], refs[2 * PARTS :]
    done = left_first
    for out in outs:
        size = out.shape[0]
        out[...] = products(
            [ref[:rows, start + done : start + done + size] for ref, start in zip(lefts, left_starts)],
            [ref[:rows, start : start + right_size] for ref, start in zip(rights, right_starts)],
        )
        done += size


def add_kernel(left, right, out):
    out[...] = (left[...].astype(F32) + right[...].astype(F32)).astype(BF)


def whole_kernel(info, *refs):
    *sources, out = refs
    row = 0
    for kept, got in zip(sources[::2], sources[1::2]):
        size = kept.shape[0]
        out[row : row + size] = jnp.where(info[4] == 1, kept[...], got[...]).astype(F32)
        row += size


def slot_kernel(with_half, with_whole, with_new, info, *refs):
    refs = list(refs)
    ins = refs[: 2 * with_half + 2 * with_whole + (with_new and with_whole)]
    outs = refs[len(ins) :]

    def add():
        left, right = ins.pop(0), ins.pop(0)
        return (left[...].astype(F32) + right[...].astype(F32)).astype(BF)

    if with_half:
        outs.pop(0)[...] = add()
    if with_whole:
        whole = add()
        outs.pop(0)[...] = whole
        if with_new:
            outs.pop(0)[...] = jnp.where(info[4] == 1, whole, ins.pop(0)[...])


def split_columns_kernel(starts, ref, *outs):
    for start, out in zip(starts, outs):
        out[...] = ref[:, start : start + out.shape[1]]


def float_kernel(out, query, key, value, w_out, w_qkv):
    w_out[...] = out[...].astype(F32)
    for i, low in enumerate((query, key, value)):
        w_qkv[i] = low[...].astype(F32)


def choose_kernel(info, kept, got, out):
    out[...] = jnp.where(info[4] == 1, kept[...], got[...])


def stack_kernel(info, keep, got, activations, input_grads):
    width = activations.shape[2]
    for i, source in ((info[1], keep), (1 - info[1], got)):
        activations[i] = source[:, :width]
        input_grads[i] = source[:, width:].astype(F32)


def last_kernel(docs, info, lengths, own_core, other_core, out, scr):
    seq = scr.shape[0]
    half = seq // 2
    width = out.shape[1]
    start, _ = longest_start(info, lengths, docs)
    here = slice(2 * width, 2 * width + half)
    mine, theirs = own_core[:half, here].astype(F32).T, other_core[:half, here].astype(F32).T
    zero = jnp.zeros_like(mine)
    low = info[0] == 0
    scr[:half, :half] = jnp.where(low, mine, theirs)
    scr[half:, half:] = jnp.where(low, theirs, mine)
    scr[:half, half:] = zero
    scr[half:, :half] = zero
    full = pltpu.roll(scr[...], lax.rem(start + half * (1 - info[0]) + half, seq), 0)[:half]
    full = pltpu.roll(full, start, 1).astype(BF)
    rows = packed_rows(half)
    out[:rows] = jnp.zeros((rows, out.shape[1]), BF)
    out[rows:] = (own_core[half:, :width].astype(F32) + other_core[half:, :width].astype(F32)).astype(BF)
    for row, column, source_row, source_column, count in packing(half):
        out[row : row + count, column : column + half] = full[
            source_row : source_row + count, source_column : source_column + half
        ]


def packing(half):
    rows = packed_rows(half)
    moves = []
    for piece in range(2):
        done = 0
        while done < half:
            place = piece * half + done
            count = min(half - done, rows - place % rows)
            moves.append((place % rows, place // rows * half, done, piece * half, count))
            done += count
    return moves


def packed_rows(half):
    return -(-2 * half // (3 * PAD)) * PAD


def last_out_kernel(info, own, other, logits, noise, mask_out, *outs):
    half = logits.shape[0] // 2
    low = info[0] == 0
    first = jnp.where(low, own[...], other[...])
    second = jnp.where(low, other[...], own[...])
    for base, block in ((0, first), (half, second)):
        for row, column, to_row, to_column, count in packing(half):
            here = (slice(base + to_row, base + to_row + count), slice(to_column, to_column + half))
            slope = 1.0 / (1.0 + jnp.exp(logits[here] + noise[here]))
            mask_out[here] = block[row : row + count, column : column + half].astype(F32) * slope
    sums = own[packed_rows(half) :].astype(F32)
    *vectors, b_in, b_qv = outs
    for i, out in enumerate(vectors):
        out[...] = sums[i : i + 1]
    place = 2 * info[1] + info[0]
    for part in range(PARTS):

        @pl.when(place == part)
        def _():
            b_in[...] = sums[6 + part : 7 + part, : b_in.shape[1]]
            head = b_qv.shape[1]
            b_qv[0:1] = sums[10 + part : 11 + part, :head]
            b_qv[1:2] = sums[10 + part : 11 + part, head : 2 * head]


def rows_kernel(docs, column, info, lengths, second, second_other, pack, pack_other, keep_out, give_out, scr):
    seq, width = scr.shape
    half = seq // 2
    rows = seq // PARTS
    start, _ = longest_start(info, lengths, docs)
    low = info[0] == 0
    place = 2 * info[1] + info[0]
    far = 2 * (1 - info[1]) + info[0]
    for i, (own, other, first) in enumerate(((second, second_other, 0), (pack, pack_other, column))):
        here = slice(first, first + width)
        mine, theirs = own[:half, here].astype(F32), other[:half, here].astype(F32)
        scr[:half] = jnp.where(low, mine, theirs)
        scr[half:] = jnp.where(low, theirs, mine)
        to = slice(i * width, (i + 1) * width)
        keep_out[:, to] = pltpu.roll(scr[...], lax.rem(start + seq - place * rows, seq), 0)[:rows].astype(BF)
        give_out[:, to] = pltpu.roll(scr[...], lax.rem(start + seq - far * rows, seq), 0)[:rows].astype(BF)


class Order:
    def __init__(self):
        self.last = None
        self.due = []

    def after(self, *values):
        if self.last is None:
            return values
        return lax.optimization_barrier((*values, self.last))[: len(values)]

    def arrived(self, *values):
        self.due += values

    def run(self, step, *inputs):
        return self.run_with((), step, *inputs)[0]

    def run_with(self, arrivals, step, *inputs):
        due, self.due = self.due, []
        values = self.after(*inputs, *arrivals, *due)[: len(inputs) + len(arrivals)]
        result = step(*values[: len(inputs)])
        self.last = jax.tree.leaves(result)[0]
        return result, values[len(inputs) :]


def shards(
    inputs, out_grad, doc_lengths, w_qkv, b_qv, w_out, b_out, norm1_gain, norm1_bias,
    w_in, b_in, w_back, b_back, norm2_gain, norm2_bias, mask_logits, mask_noise,
):
    count, seq, width = inputs.shape
    docs = doc_lengths.shape[1]
    core, chip = lax.axis_index("core"), lax.axis_index("chip")
    odd = lax.axis_index("dp") % 2
    part = 2 * chip + core
    half = seq // 2
    head = w_out.shape[1]
    units = w_in.shape[2]
    assert lax.axis_size("pipe") == 2 and lax.axis_size("chip") == 2 and count == 2
    assert lax.axis_size("dp") % 2 == 0 and PARTS * head == width and seq % (2 * PARTS) == 0
    place = lax.axis_index("dp")
    line = lax.axis_size("dp") == 4
    middle = ((place == 1) | (place == 2)) if line else place >= 0
    info = jnp.stack([core, chip, odd, lax.axis_index("pipe"), middle]).astype(jnp.int32)
    order = Order()
    everyone = ("chip", "core")

    def diagonal(block):
        return lax.ppermute(block, everyone, [(i, i ^ 3) for i in range(PARTS)])

    low_rows = pltpu.VMEM((half, width), BF)
    low_columns = pltpu.VMEM((width, half), BF)
    up_scratch = [low_rows, low_rows, low_columns, low_columns]
    down_scratch = [pltpu.VMEM((width, half), F32), low_rows, low_rows, low_rows, pltpu.VMEM((half, half), F32)]
    flat = shape(half, width)
    flat32 = shape(half, width, dtype=F32)

    pack, half_pack, half_in = call(
        split_kernel,
        [shape(4 * head + 2 * PAD, width), shape(2 * head + PAD, width), shape(width // 2 + 2 * PAD, units)],
        [SMEM] + [HBM] * 5,
        (info, jnp.swapaxes(w_qkv[0], 1, 2).reshape(3 * head, width), w_out[0], w_in[0], b_in, b_qv[0]),
        [pltpu.VMEM((3 * head, width), BF), pltpu.VMEM((head, width), BF), pltpu.VMEM((width // 2, units), BF),
         pltpu.VMEM((1, units), BF), pltpu.VMEM((2, head), BF), pltpu.SemaphoreType.DMA((5,))],
        56 << 20,
    )
    got_pack = swap(half_pack, "chip")
    got_in = swap(half_in, "chip")
    near = [swap(v, "core") for v in (pack, w_in[0], w_back[0])]

    def prepare(*args):
        return call(
            functools.partial(prepare_kernel, docs),
            [flat, flat, shape(half, half, dtype=F32)],
            [SMEM, SMEM, VMEM, VMEM, VMEM, VMEM],
            args,
        )

    tokens0, top0, bias = order.run(prepare, info, doc_lengths, inputs, out_grad, mask_logits[0], mask_noise[0])
    got_pack, *near = order.after(got_pack, *near)
    also_pack = swap(got_pack, "dp")
    w_back_own, got_pack = lax.optimization_barrier((w_back[0], got_pack))
    got_back = swap(w_back_own, "chip")
    cross_got_pack = swap(got_pack, "core")
    got_in, got_pack = lax.optimization_barrier((got_in, got_pack))
    also_in = swap(got_in, "dp")
    cross_got_in = swap(got_in, "core")
    also_pack, got_in = lax.optimization_barrier((also_pack, got_in))
    p1 = (pack, near[0], got_pack, also_pack, cross_got_pack, swap(also_pack, "core"))

    def attention(tokens, *p1):
        return call(
            attention_kernel,
            [flat32, shape(4, width, width), shape(2, width, dtype=F32), shape(PARTS, units, dtype=F32)],
            [SMEM] + [VMEM] * 11,
            (info, tokens, bias, b_out, norm1_gain, norm1_bias) + p1,
            up_scratch,
        )

    first, w4, both_b_qv, full_b_in = order.run(attention, tokens0, *p1)
    order.arrived(cross_got_in)
    total = order.run(
        lambda *a: call(ffn_near_kernel, flat32, [VMEM] * 7, a),
        first, b_back, full_b_in, w_in[0], near[1], w_back[0], near[2],
    )
    (also_in,) = order.after(also_in)
    cross_also_in = swap(also_in, "core")
    (got_back,) = order.after(got_back)
    backs = (w_back[0], near[2], got_back, swap(got_back, "core"))
    hidden_far, in_far = order.run(
        lambda *a: call(
            ffn_far_kernel, [shape(half, 2 * units), shape(2, width, units)], [SMEM] + [VMEM] * 6, (info,) + a
        ),
        first, full_b_in, got_in, also_in, cross_got_in, cross_also_in,
    )
    second = order.run(
        lambda *a: call(ffn_end_kernel, flat, [VMEM] * 6, a),
        total, hidden_far, norm2_gain, norm2_bias, backs[2], backs[3],
    )
    weights = (w4, both_b_qv, full_b_in, w_in[0], near[1], in_far) + backs
    passed = lax.ppermute(second, "pipe", [(0, 1)])

    tokens = order.run(
        lambda *a: call(choose_tokens_kernel, flat, [SMEM, VMEM, VMEM], (info,) + a), tokens0, passed
    )
    tokens_chip = swap(tokens, "chip")
    tokens_core = swap(tokens, "core")

    keep_width = units + head

    def layer(tokens):
        return call(
            layer_kernel,
            [flat, flat, shape(half, 2 * head)]
            + [shape(half, keep_width)] * 2 + [shape(half, units)] * 2
            + [flat, flat, flat, shape(width, half), shape(width // HEAD_DIM, half, half),
               flat32, shape(half, 128, dtype=F32), shape(half, PARTS * units),
               flat32, shape(half, 128, dtype=F32)],
            [VMEM] * (8 + WEIGHTS),
            (tokens, bias, b_out, norm1_gain, norm1_bias, b_back, norm2_gain, norm2_bias) + weights,
            up_scratch,
        )

    second, first_low, far_attended, *kept = order.run(layer, tokens)
    keeps, kept = kept[:PARTS], kept[PARTS:]
    q, k, v, kt, chance, unit1, scale1, slope, unit2, scale2 = kept
    keeps = [keeps[0], swap(keeps[1], "core"), swap(keeps[2], "chip"), diagonal(keeps[3])]
    far_chip = swap(first_low, "chip")

    def down(top):
        return call(
            down_kernel, flat, [VMEM] * (13 + WEIGHTS),
            (top, unit1, scale1, norm1_gain, unit2, scale2, norm2_gain, slope, q, k, v, kt, chance) + weights,
            down_scratch,
        )

    down_grad, (tokens_chip, tokens_core) = order.run_with((tokens_chip, tokens_core), down, top0)
    passed = lax.ppermute(down_grad, "pipe", [(1, 0)])
    tokens_all = [tokens, tokens_core, tokens_chip, swap(tokens_chip, "core")]

    def rows_of(*args):
        return call(
            functools.partial(rows_kernel, docs, width),
            [shape(seq // PARTS, 2 * width)] * 2,
            [SMEM, SMEM] + [VMEM] * 4,
            (info, doc_lengths) + args,
            [pltpu.VMEM((seq, width), F32)],
        )

    def down_norm(top, passed):
        return call(
            down_norm_kernel, [flat, shape(half, 2 * width), flat32, shape(PAD, width, dtype=F32)], [SMEM] + [VMEM] * 6,
            (info, top, passed, unit2, scale2, norm2_gain, first_low),
        )

    (ffn_low, ffn_pack, sum_grad, sums), keeps[1:] = order.run_with(keeps[1:], down_norm, top0, passed)
    ffn_chip = swap(ffn_low, "chip")
    ffn_core = swap(ffn_pack, "core")
    (second,) = order.after(second)
    second_other = swap(second, "core")

    def down_ffn(sum_grad):
        return call(
            down_ffn_kernel,
            [shape(half, units)] * PARTS + [flat32], [VMEM] * (2 + WEIGHTS), (sum_grad, slope) + weights,
        )

    *pres, first_grad = order.run(down_ffn, sum_grad)
    pre_core = swap(pres[1], "core")

    lanes = [dict(own=None, half=None, whole=None, end=None, middle=None, names=[]) for _ in range(2)]
    final = {}

    def slot(lane, name=None, new=None):
        if not line:
            if new is not None:
                final[name] = (lax.psum(new, "dp"),) * 2
            return
        if lane["whole"] is not None:
            final[lane["names"].pop(0)] = (lane["whole"], lane["end"])
        with_half, with_whole = lane["own"] is not None, lane["half"] is not None
        ins = [lane["own"], lane["end"]] if with_half else []
        if with_whole:
            ins += [lane["half"], lane["middle"]] + ([new] if new is not None else [])
        half_sum = whole = None
        going = new
        if ins:
            outs = with_half + with_whole + (with_whole and new is not None)
            results = order.run(
                lambda *a: call(
                    functools.partial(slot_kernel, with_half, with_whole, new is not None),
                    [shape(*a[0].shape)] * outs, [SMEM] + [VMEM] * len(a), (info,) + a,
                ),
                *ins,
            )
            if with_half:
                half_sum = results[0]
            if with_whole:
                whole = results[int(with_half)]
                going = results[-1] if new is not None else whole
        if new is not None and whole is None:
            (going,) = order.after(going)
        routes = ([(0, 1), (3, 2)] if new is not None else []) + ([(1, 0), (2, 3)] if whole is not None else [])
        lane["end"] = lax.ppermute(going, "dp", routes) if routes else None
        lane["middle"] = lax.ppermute(half_sum, "dp", [(1, 2), (2, 1)]) if half_sum is not None else None
        lane["own"], lane["half"], lane["whole"] = new, half_sum, whole
        if new is not None:
            lane["names"].append(name)

    def matrix(*names):
        sources = [v for name in names for v in final[name]]
        rows = sum(v.shape[0] for v in sources) // 2
        return order.run(
            lambda *a: call(
                whole_kernel, shape(rows, a[0].shape[1], dtype=F32), [SMEM] + [VMEM] * len(a), (info,) + a
            ),
            *sources,
        )

    def products_of(outs, lefts, left_starts, left_first, rights, right_starts, right_size):
        return order.run(
            lambda *a: call(
                functools.partial(products_kernel, half, left_starts, left_first, right_starts, right_size),
                [shape(n, right_size) for n in outs], [VMEM] * (2 * PARTS), a,
            ),
            *lefts, *rights,
        )

    chip_width = width + 8 * head

    def down_attention(first_grad, sums, *pres):
        return call(
            down_attention_kernel,
            [shape(half, chip_width), shape(half + PAD, -(-(2 * width + half + 3 * head) // 128) * 128)]
            + [shape(half, 3 * head)],
            [SMEM] + [VMEM] * (12 + PARTS),
            (info, first_grad, sums, unit1, scale1, norm1_gain, q, k, v, kt, chance) + pres + (far_attended, w4),
            [pltpu.VMEM((PAD, width), F32)] + down_scratch,
        )

    down_core_projected = 2 * width + half
    down_chip, down_pack, projected_zero = order.run(down_attention, first_grad, sums, *pres)
    ffn_chip, far_chip, pre_two, pre_three = order.after(ffn_chip, far_chip, pres[2], pres[3])
    ffns = [ffn_low, ffn_core, ffn_chip, swap(ffn_chip, "core")]
    far_cross = swap(far_chip, "core")
    pre_chip, pre_diagonal = swap(pre_two, "chip"), diagonal(pre_three)
    none = (0, 0, 0, 0)
    quarter = units // 4
    one, two = lanes
    (far_cross,) = order.after(far_cross)
    order.arrived(second_other)
    back = products_of((quarter,) * 4, keeps, none, 0, ffns, none, width)
    slot(one, "back0", back[0])
    slot(two, "back1", back[1])
    (down_give,) = order.after(down_pack)
    down_other = swap(down_give, "core")

    def last_chunk(*args):
        return call(
            functools.partial(last_kernel, docs),
            shape(packed_rows(half) + PAD, width),
            [SMEM, SMEM] + [VMEM] * 2,
            (info, doc_lengths) + args,
            [pltpu.VMEM((seq, seq), F32)],
        )

    def split_columns(starts, sizes, packed):
        return order.run(
            lambda a: call(
                functools.partial(split_columns_kernel, starts), [shape(half, n) for n in sizes], [VMEM], (a,)
            ),
            packed,
        )

    last = order.run(last_chunk, down_pack, down_other)
    rows_keep, rows_give = order.run(rows_of, second, second_other, down_pack, down_other)
    slot(one, "back2", back[2])
    order.arrived(pre_core, far_cross, pre_chip)
    slot(two, "back3", back[3])
    inner = products_of(
        (quarter,) * 4, [first_low, ffn_core, far_chip, far_cross], (0, width, 0, 0), 0,
        [pres[0], pre_core, pre_chip, pre_diagonal], none, units,
    )
    (down_chip_give,) = order.after(down_chip)
    branch_chip = swap(down_chip_give, "chip")
    slot(one, "in0", inner[0])
    slot(two, "in1", inner[1])
    slot(one, "in2", inner[2])
    far_branch, far_projected = split_columns((0, width + 4 * head), (width, 4 * head), branch_chip)
    far_branch, far_projected = swap(far_branch, "core"), swap(far_projected, "core")
    slot(two, "in3", inner[3])
    slot(one, "last", last)
    (w_out_low,) = products_of(
        (head,), [*keeps[:2], branch_chip, far_projected], (units, units, width + 3 * head, 3 * head), 0,
        [down_chip, down_other, branch_chip, far_branch], none, width,
    )
    w_qkv_low = products_of(
        (head,) * 3, [projected_zero, down_other, branch_chip, far_projected], (0, down_core_projected, width, 0), 0,
        tokens_all, none, width,
    )
    slot(two, "out", w_out_low)
    (rows_give,) = order.after(rows_give)
    rows_got = swap(rows_give, "chip")
    slot(one, "q", w_qkv_low[0])
    slot(two, "k", w_qkv_low[1])
    activations, input_grads = order.run(
        lambda a, b: call(
            stack_kernel, [shape(2, seq // PARTS, width), shape(2, seq // PARTS, width, dtype=F32)],
            [SMEM, VMEM, VMEM], (info, a, b),
        ),
        rows_keep, rows_got,
    )
    slot(one, "v", w_qkv_low[2])
    slot(two)
    done = {}

    def choose(name):
        done[name] = order.run(
            lambda a, b: call(choose_kernel, shape(*a.shape), [SMEM, VMEM, VMEM], (info, a, b)), *final[name]
        )

    slot(one)
    if line:
        order.arrived(two["end"])
    slot(two)
    choose("last")
    last_got = swap(done["last"], "chip")
    if line:
        order.arrived(one["end"])
    slot(one)
    choose("out")
    grad_w_back = matrix("back0", "back1", "back2", "back3")
    choose("q")
    last = order.run(lambda a, b: call(add_kernel, shape(*a.shape), [VMEM] * 2, (a, b)), done["last"], last_got)
    slot(two)
    choose("k")
    grad_w_in = matrix("in0", "in1", "in2", "in3")
    slot(one)
    choose("v")
    grad_w_out, grad_w_qkv = order.run(
        lambda *a: call(
            float_kernel, [shape(head, width, dtype=F32), shape(3, head, width, dtype=F32)], [VMEM] * 4, a
        ),
        done["out"], done["q"], done["k"], done["v"],
    )
    grad_mask, *vectors, grad_b_in, grad_b_qv = call(
        last_out_kernel,
        [shape(seq, seq, dtype=F32)] + [shape(1, width, dtype=F32)] * 6
        + [shape(1, units, dtype=F32), shape(2, head, dtype=F32)],
        [SMEM] + [VMEM] * 4,
        (info, last, swap(last, "core"), mask_logits[0], mask_noise[0]),
    )
    results = (
        activations, input_grads, jnp.swapaxes(grad_w_qkv, 1, 2), grad_b_qv, grad_w_out,
        vectors[0][0], vectors[1][0], vectors[2][0],
        grad_w_in, grad_b_in[0], grad_w_back,
        vectors[3][0], vectors[4][0], vectors[5][0],
        grad_mask,
    )
    return tuple(item[None] for item in results)


def solution(mesh):
    pipe, dp, tensor = (mesh.shape[name] for name in ("pipe", "dp", "tensor"))
    split = Mesh(mesh.devices.reshape(pipe, dp, tensor // 2, 2), ("pipe", "dp", "chip", "core"))
    placed = (
        P("dp", None, None),
        P("dp", None, None),
        P("dp", None),
        P("pipe", None, None, TENSOR),
        P("pipe", None, TENSOR),
        P("pipe", TENSOR, None),
        P("pipe", None),
        P("pipe", None),
        P("pipe", None),
        P("pipe", None, TENSOR),
        P("pipe", TENSOR),
        P("pipe", TENSOR, None),
        P("pipe", None),
        P("pipe", None),
        P("pipe", None),
        P("pipe", None, None),
        P("pipe", None, None),
    )
    return jax.shard_map(
        shards,
        mesh=split,
        in_specs=placed,
        out_specs=(
            P("pipe", "dp", TENSOR, None),
            P("pipe", "dp", TENSOR, None),
            P("pipe", None, None, TENSOR),
            P("pipe", None, TENSOR),
            P("pipe", TENSOR, None),
            P("pipe", None),
            P("pipe", None),
            P("pipe", None),
            P("pipe", None, TENSOR),
            P("pipe", TENSOR),
            P("pipe", TENSOR, None),
            P("pipe", None),
            P("pipe", None),
            P("pipe", None),
            P("pipe", None, None),
        ),
        check_vma=False,
    )
```

```python
import functools
import math

import jax
import jax.numpy as jnp
from jax import lax
from jax.experimental import pallas as pl
from jax.experimental.pallas import tpu as pltpu
from jax.sharding import Mesh
from jax.sharding import PartitionSpec as P

HEAD_DIM = 64
EPSILON = 1e-12
MASKED = -1e30
BF = jnp.bfloat16
F32 = jnp.float32
NT = ((1,), (1,))
TN = ((0,), (0,))
NN = ((1,), (0,))
PARTS = 4
PAD = 16
TENSOR = ("chip", "core")
LIMIT = 8 << 20


def dot(left, right, dims=NN):
    return lax.dot_general(left, right, (dims, ((), ())), preferred_element_type=F32)


def swap(block, axis):
    return lax.ppermute(block, axis, [(i, i ^ 1) for i in range(lax.axis_size(axis))])


SMEM = pl.BlockSpec(memory_space=pltpu.SMEM)
VMEM = pl.BlockSpec(memory_space=pltpu.VMEM)
HBM = pl.BlockSpec(memory_space=pltpu.HBM)


def shape(*dims, dtype=BF):
    return jax.ShapeDtypeStruct(dims, dtype)


def call(kernel, out, ins, args, scratch=(), limit=LIMIT):
    return pl.pallas_call(
        kernel,
        out_shape=out,
        in_specs=ins,
        out_specs=jax.tree.map(lambda _: VMEM, out),
        scratch_shapes=list(scratch),
        compiler_params=pltpu.CompilerParams(vmem_limit_bytes=limit),
        cost_estimate=pl.CostEstimate(flops=0, bytes_accessed=0, transcendentals=0),
    )(*args)


def longest_start(info, lengths, docs):
    chip = info[1]
    sizes = [lengths[chip, i] for i in range(docs)]
    bounds, start, total = [], jnp.int32(0), jnp.int32(0)
    longest = sizes[0]
    for size in sizes[1:]:
        longest = jnp.maximum(longest, size)
    for size in sizes:
        start = jnp.where(size == longest, total, start)
        total = total + size
        bounds.append(total)
    return start, bounds


def prepare_kernel(docs, info, lengths, inputs, grads, logits, noise, tokens_out, top_out, bias_out):
    seq = logits.shape[0]
    half = seq // 2
    start, bounds = longest_start(info, lengths, docs)
    begin = lax.rem(start + half * info[0], seq)
    shift = lax.rem(seq - begin, seq)
    tokens_out[...] = pltpu.roll(inputs[info[1]].astype(F32), shift, 0)[:half].astype(BF)
    top_out[...] = pltpu.roll(grads[info[1]].astype(F32), shift, 0)[:half].astype(BF)
    table = logits[...] + noise[...]
    table = pltpu.roll(table, shift, 0)[:half]
    table = pltpu.roll(table, shift, 1)[:, :half]
    term = jnp.minimum(table, 0.0) - jnp.log1p(jnp.exp(-jnp.abs(table)))

    def owners(axis):
        place = begin + lax.broadcasted_iota(jnp.int32, (half, half), axis)
        place = jnp.where(place >= seq, place - seq, place)
        owner = jnp.zeros((half, half), jnp.int32)
        for bound in bounds:
            owner = owner + jnp.where(place >= bound, 1, 0)
        return owner

    bias_out[...] = jnp.where(owners(0) == owners(1), term, MASKED).T


def split_kernel(info, qkv, w_out, w_in, b_in, b_qv, pack, half_pack, half_in, qkv_scr, out_scr, in_scr, b_in_scr, b_qv_scr, sems):
    size = w_in.shape[0] // 2
    pairs = (
        (qkv, qkv_scr), (w_out, out_scr), (b_in, b_in_scr), (b_qv, b_qv_scr),
        (w_in.at[pl.ds(pl.multiple_of(info[2] * size, size), size)], in_scr),
    )
    copies = [pltpu.make_async_copy(src, dst, sems.at[i]) for i, (src, dst) in enumerate(pairs)]
    for copy in copies:
        copy.start()
    for copy in copies:
        copy.wait()
    head = out_scr.shape[0]
    step = 2 * head + PAD
    pack[: 2 * head] = qkv_scr[: 2 * head]
    pack[2 * head : step] = jnp.zeros((PAD, pack.shape[1]), BF)
    pack[2 * head : 2 * head + 1, : b_in.shape[1]] = b_in_scr[...]
    pack[step : step + head] = qkv_scr[2 * head :]
    pack[step + head : step + 2 * head] = out_scr[...]
    pack[step + 2 * head :] = jnp.zeros((PAD, pack.shape[1]), BF)
    pack[step + 2 * head : step + 2 * head + 1, :head] = b_qv_scr[0:1]
    pack[step + 2 * head : step + 2 * head + 1, head : 2 * head] = b_qv_scr[1:2]
    half_pack[...] = pack[pl.ds(pl.multiple_of(info[2] * step, PAD), step)]
    half_in[:size] = in_scr[...]
    half_in[size:] = jnp.zeros((half_in.shape[0] - size, half_in.shape[1]), BF)


def norm(values):
    average = jnp.mean(values, axis=-1, keepdims=True)
    centred = values - average
    variance = jnp.mean(centred * centred, axis=-1, keepdims=True)
    scale = lax.rsqrt(variance + EPSILON)
    return centred * scale, scale


def norm_back(grad, unit, scale, gain):
    direct = grad * gain
    return scale * (
        direct
        - jnp.mean(direct, axis=-1, keepdims=True)
        - unit * jnp.mean(direct * unit, axis=-1, keepdims=True)
    )


def assemble(info, pieces, w4, b_qv, b_in):
    head = w4.shape[1] // PARTS
    step = 2 * head + PAD
    even = info[2] == 0
    for part in range(PARTS):
        here = slice(part * head, (part + 1) * head)
        for which in range(2):
            if part < 2:
                block = pieces[part][which * step : (which + 1) * step]
            else:
                got, also = pieces[2 * part - 2], pieces[2 * part - 1]
                block = jnp.where(even, got[...], also[...]) if which == 0 else jnp.where(even, also[...], got[...])
            w4[2 * which, here] = block[:head]
            w4[2 * which + 1, here] = block[head : 2 * head]
            if which == 0:
                b_in[part : part + 1] = block[2 * head : 2 * head + 1, : b_in.shape[1]].astype(F32)
            else:
                row = block[2 * head : 2 * head + 1].astype(F32)
                b_qv[0:1, here] = row[:, :head]
                b_qv[1:2, here] = row[:, head : 2 * head]


class Weights:
    def __init__(self, refs):
        self.w4, self.b_qv, self.b_in, self.in_near, self.in_far, self.backs = (
            refs[0], refs[1], refs[2], refs[3:5], refs[5], refs[6:10]
        )
        self.units = self.in_far.shape[2]

    def w_in(self, part):
        return self.in_near[part][...] if part < 2 else self.in_far[part - 2]

    def w_back(self, part):
        return self.backs[part][...]


WEIGHTS = 10


def attention_forward(tokens, bias_ref, w4, b_qv, out_parts, scratch):
    width = tokens.shape[1]
    q_scr, k_scr, vt_scr, at_scr = scratch
    queries = (dot(tokens, w4[0], NT) + b_qv[0:1]).astype(BF)
    keys = dot(tokens, w4[1], NT).astype(BF)
    values = (dot(tokens, w4[2], NT) + b_qv[1:2]).astype(BF)
    values_t = values.T
    if out_parts is not None:
        q_out, k_out, v_out, kt_out, p_out = out_parts
        q_out[...], k_out[...], v_out[...] = queries, keys, values
        kt_out[...] = keys.T
    q_scr[...] = queries * jnp.asarray(1.0 / math.sqrt(HEAD_DIM), BF)
    k_scr[...] = keys
    vt_scr[...] = values_t
    pair = 2 * HEAD_DIM
    lane = lax.broadcasted_iota(jnp.int32, (tokens.shape[0], pair), 1)

    def heads(j):
        here = pl.ds(j * pair, pair)
        q_pair, k_pair = q_scr[:, here], k_scr[:, here]
        for s in range(2):
            mine = (lane >= HEAD_DIM) if s else (lane < HEAD_DIM)
            scores = dot(jnp.where(mine, k_pair, jnp.zeros_like(k_pair)), q_pair, NT) + bias_ref[...]
            exponent = jnp.exp(scores - jnp.max(scores, axis=0, keepdims=True))
            chance = (exponent * (1.0 / jnp.sum(exponent, axis=0, keepdims=True))).astype(BF)
            if out_parts is not None:
                p_out[2 * j + s] = chance
            rows = pl.ds(j * pair + s * HEAD_DIM, HEAD_DIM)
            at_scr[rows, :] = dot(vt_scr[rows, :], chance).astype(BF)

    for j in range(width // pair):
        heads(j)
    return at_scr[...].T


def gelu(values):
    cdf = 0.5 * (1.0 + lax.erf(values * math.sqrt(0.5)))
    return values * cdf, cdf


def attention_kernel(info, tokens, bias, b_out, gain, offset, *rest):
    pieces, (first_out, w4, b_qv, b_in, *scratch) = rest[:6], rest[6:]
    assemble(info, pieces, w4, b_qv, b_in)
    attended = attention_forward(tokens[...], bias, w4, b_qv, None, scratch)
    unit, _ = norm(tokens[...].astype(F32) + dot(attended, w4[3]) + b_out[...])
    first_out[...] = unit * gain[...] + offset[...]


def ffn_near_kernel(first, b_back, b_in, *rest):
    w_ins, w_backs, out = rest[:2], rest[2:4], rest[4]
    first_low = first[...].astype(BF)
    total = first[...] + b_back[...]
    for part in range(2):
        hidden, _ = gelu(dot(first_low, w_ins[part][...]) + b_in[part : part + 1])
        total = total + dot(hidden.astype(BF), w_backs[part][...])
    out[...] = total


def ffn_far_kernel(info, first, b_in, far_got, far_also, cross_got, cross_also, hidden_out, in_out):
    even = info[2] == 0
    units = in_out.shape[2]
    half = in_out.shape[1] // 2
    first_low = first[...].astype(BF)
    for part, (got, also) in enumerate(((far_got, far_also), (cross_got, cross_also))):
        in_out[part, :half] = jnp.where(even, got[:half], also[:half])
        in_out[part, half:] = jnp.where(even, also[:half], got[:half])
        hidden, _ = gelu(dot(first_low, in_out[part]) + b_in[part + 2 : part + 3])
        hidden_out[:, part * units : (part + 1) * units] = hidden.astype(BF)


def ffn_end_kernel(total, hidden, gain, offset, far, cross, out):
    units = far.shape[0]
    result = total[...] + dot(hidden[:, :units], far[...]) + dot(hidden[:, units:], cross[...])
    unit, _ = norm(result)
    out[...] = (unit * gain[...] + offset[...]).astype(BF)


def choose_tokens_kernel(info, first_tokens, passed, out):
    out[...] = jnp.where(info[3] == 0, first_tokens[...], passed[...])


def layer_kernel(tokens_ref, bias, b_out, gain_one, offset_one, b_back, gain_two, offset_two, *rest):
    weights, rest = Weights(rest[:WEIGHTS]), rest[WEIGHTS:]
    second_out, first_out, att_out, *rest = rest
    keep_outs, rest = rest[:PARTS], rest[PARTS:]
    (q_out, k_out, v_out, kt_out, p_out, unit1_out, scale1_out, slope_out, unit2_out, scale2_out, *scratch) = rest
    tokens = tokens_ref[...]
    width = tokens.shape[1]
    attended = attention_forward(
        tokens, bias, weights.w4, weights.b_qv, (q_out, k_out, v_out, kt_out, p_out), scratch
    )
    units, head = weights.units, width // PARTS
    for part in range(PARTS):
        out, base = (keep_outs[part], units) if part < 2 else (att_out, (part - 2) * head)
        out[:, base : base + head] = attended[:, part * head : (part + 1) * head]
    unit, scale = norm(tokens.astype(F32) + dot(attended, weights.w4[3]) + b_out[...])
    unit1_out[...] = unit
    scale1_out[...] = jnp.broadcast_to(scale, scale1_out.shape)
    first = unit * gain_one[...] + offset_one[...]
    first_low = first.astype(BF)
    first_out[...] = first_low
    total = first + b_back[...]
    for part in range(PARTS):
        pre = dot(first_low, weights.w_in(part)) + weights.b_in[part : part + 1]
        value, cdf = gelu(pre)
        hidden = value.astype(BF)
        keep_outs[part][:, :units] = hidden
        density = jnp.exp(-0.5 * pre * pre) * (1.0 / math.sqrt(2.0 * math.pi))
        slope_out[:, part * units : (part + 1) * units] = (cdf + pre * density).astype(BF)
        total = total + dot(hidden, weights.w_back(part))
    unit, scale = norm(total)
    unit2_out[...] = unit
    scale2_out[...] = jnp.broadcast_to(scale, scale2_out.shape)
    second_out[...] = (unit * gain_two[...] + offset_two[...]).astype(BF)


def rows_sum(values):
    return jnp.sum(values, axis=0, keepdims=True)


def ffn_backward(sum_grad, slope, weights, pre_outs):
    units = weights.units
    ffn_low = sum_grad.astype(BF)
    first_grad = sum_grad
    for part in range(PARTS):
        pre = dot(ffn_low, weights.w_back(part), NT) * slope[:, part * units : (part + 1) * units].astype(F32)
        pre = pre.astype(BF)
        if pre_outs is not None:
            pre_outs[part][...] = pre
        first_grad = first_grad + dot(pre, weights.w_in(part), NT)
    return first_grad


def attention_backward(first_grad, unit, scale, gain, refs, w_scr, scratch, outs):
    q_ref, k_ref, v_ref, kt_ref, p_ref = refs
    width = first_grad.shape[1]
    branch = norm_back(first_grad, unit, scale, gain)
    branch_low = branch.astype(BF)
    att_grad = dot(branch_low, w_scr[3], NT).astype(BF)
    pair = 2 * HEAD_DIM
    rows = first_grad.shape[0]
    lane = lax.broadcasted_iota(jnp.int32, (rows, pair), 1)
    root = 1.0 / math.sqrt(HEAD_DIM)
    dqt_scr, dk_scr, dv_scr, o_scr, term_scr = scratch
    o_scr[...] = att_grad
    term_scr[...] = jnp.zeros((rows, rows), F32)

    def heads(j, carry):
        here = pl.ds(pl.multiple_of(j * pair, pair), pair)
        q_pair, v_pair, o_pair = q_ref[:, here], v_ref[:, here], o_scr[:, here]
        dk, dv = [], []
        for s in range(2):
            mine = (lane >= HEAD_DIM) if s else (lane < HEAD_DIM)
            chance_low = p_ref[2 * j + s]
            chance = chance_low.astype(F32)
            chance_grad = dot(jnp.where(mine, v_pair, jnp.zeros_like(v_pair)), o_pair, NT)
            inner = jnp.sum(chance * chance_grad, axis=0, keepdims=True)
            score = chance * (chance_grad - inner)
            term_scr[...] += score
            low = score.astype(BF)
            dv.append(dot(chance_low, o_pair))
            dk.append(dot(low, q_pair))
            part = pl.ds(pl.multiple_of(j * pair + s * HEAD_DIM, HEAD_DIM), HEAD_DIM)
            dqt_scr[part, :] = dot(kt_ref[part, :], low) * root
        dk_scr[:, here] = (jnp.where(lane < HEAD_DIM, dk[0], dk[1]) * root).astype(BF)
        dv_scr[:, here] = jnp.where(lane < HEAD_DIM, dv[0], dv[1]).astype(BF)
        return carry

    lax.fori_loop(0, width // pair, heads, 0)
    dq = dqt_scr[...].T.astype(BF)
    dk, dv = dk_scr[...], dv_scr[...]
    term = term_scr[...]
    in_grad = branch + dot(dq, w_scr[0]) + dot(dk, w_scr[1]) + dot(dv, w_scr[2])
    if outs is not None:
        chip_out, core_out, projected_outs = outs
        chip_out[:, :width] = branch_low
        core_out[:rows, :width] = branch_low
        core_out[:rows, width : 2 * width] = in_grad.astype(BF)
        core_out[:rows, 2 * width : 2 * width + rows] = term.astype(BF)
        head = width // PARTS
        end = 2 * width + rows + 3 * head
        core_out[:rows, end:] = jnp.zeros((rows, core_out.shape[1] - end), BF)
        for part in range(PARTS):
            out, base = (core_out, 2 * width + rows) if part == 1 else (projected_outs[0], 0)
            out, base = (chip_out, width + (part - 2) * 4 * head) if part > 1 else (out, base)
            for i, grad in enumerate((dq, dk, dv)):
                out[:rows, base + i * head : base + (i + 1) * head] = grad[:, part * head : (part + 1) * head]
    return branch, in_grad, dq, dv


def down_kernel(top, unit1, scale1, gain_one, unit2, scale2, gain_two, slope, q_ref, k_ref, v_ref, kt_ref, p_ref, *rest):
    weights, (grad_out, *scratch) = Weights(rest[:WEIGHTS]), rest[WEIGHTS:]
    sum_grad = norm_back(top[...].astype(F32), unit2[...], scale2[:, :1], gain_two[...])
    first_grad = ffn_backward(sum_grad, slope, weights, None)
    _, in_grad, _, _ = attention_backward(
        first_grad, unit1[...], scale1[:, :1], gain_one[...], (q_ref, k_ref, v_ref, kt_ref, p_ref),
        weights.w4, scratch, None,
    )
    grad_out[...] = in_grad.astype(BF)


def down_norm_kernel(info, own_top, passed, unit2, scale2, gain_two, first, ffn_out, core_out, sum_grad_out, sums_out):
    top = jnp.where(info[3] == 0, passed[...], own_top[...]).astype(F32)
    unit = unit2[...]
    sum_grad = norm_back(top, unit, scale2[:, :1], gain_two[...])
    sum_grad_out[...] = sum_grad
    width = first.shape[1]
    ffn_out[...] = sum_grad.astype(BF)
    core_out[:, :width] = sum_grad.astype(BF)
    core_out[:, width:] = first[...]
    sums_out[...] = jnp.zeros_like(sums_out)
    sums_out[3:4] = rows_sum(sum_grad)
    sums_out[4:5] = rows_sum(top * unit)
    sums_out[5:6] = rows_sum(top)


def down_ffn_kernel(sum_grad, slope, *rest):
    weights, (*pre_outs, first_grad_out) = Weights(rest[:WEIGHTS]), rest[WEIGHTS:]
    first_grad_out[...] = ffn_backward(sum_grad[...], slope, weights, pre_outs)


def down_attention_kernel(info, first_grad, sums, unit1, scale1, gain_one, q_ref, k_ref, v_ref, kt_ref, p_ref, *rest):
    pres, attended, w4, rest = rest[:PARTS], rest[PARTS], rest[PARTS + 1], rest[PARTS + 2 :]
    chip_out, core_out, zero, sums_scr, *scratch = rest
    unit = unit1[...]
    grad = first_grad[...]
    rows, width = grad.shape
    branch, in_grad, dq, dv = attention_backward(
        grad, unit, scale1[:, :1], gain_one[...], (q_ref, k_ref, v_ref, kt_ref, p_ref),
        w4, scratch, (chip_out, core_out, (zero,)),
    )
    head = width // PARTS
    for i in range(2):
        end = width + (i + 1) * 4 * head
        chip_out[:, end - head : end] = attended[:, i * head : (i + 1) * head]
    sums_scr[...] = sums[...]
    sums_scr[0:1] = rows_sum(branch)
    sums_scr[1:2] = rows_sum(grad * unit)
    sums_scr[2:3] = rows_sum(grad)
    head = width // PARTS
    place = 2 * info[1] + info[0]
    dq_sum, dv_sum = rows_sum(dq.astype(F32)), rows_sum(dv.astype(F32))
    for part in range(PARTS):
        units = pres[0].shape[1]
        pre = pres[part][...]
        sums_scr[pl.ds(6 + jnp.bitwise_xor(place, part), 1), :units] = rows_sum(pre.astype(F32))
        here = slice(part * head, (part + 1) * head)
        row = jnp.concatenate(
            [dq_sum[:, here], dv_sum[:, here], jnp.zeros((1, width - 2 * head), F32)], axis=1
        )
        sums_scr[pl.ds(10 + jnp.bitwise_xor(place, part), 1)] = row
    core_out[rows:, :width] = sums_scr[...].astype(BF)
    core_out[rows:, width:] = jnp.zeros((PAD, core_out.shape[1] - width), BF)


def products(lefts, rights):
    total = None
    for left, right in zip(lefts, rights):
        value = dot(left, right, TN)
        total = value if total is None else total + value
    return total.astype(BF)


def products_kernel(rows, left_starts, left_first, right_starts, right_size, *refs):
    lefts, rights, outs = refs[:PARTS], refs[PARTS : 2 * PARTS], refs[2 * PARTS :]
    done = left_first
    for out in outs:
        size = out.shape[0]
        out[...] = products(
            [ref[:rows, start + done : start + done + size] for ref, start in zip(lefts, left_starts)],
            [ref[:rows, start : start + right_size] for ref, start in zip(rights, right_starts)],
        )
        done += size


def add_kernel(left, right, out):
    out[...] = (left[...].astype(F32) + right[...].astype(F32)).astype(BF)


def whole_kernel(info, *refs):
    *sources, out = refs
    row = 0
    for kept, got in zip(sources[::2], sources[1::2]):
        size = kept.shape[0]
        out[row : row + size] = jnp.where(info[4] == 1, kept[...], got[...]).astype(F32)
        row += size


def slot_kernel(with_half, with_whole, with_new, info, *refs):
    refs = list(refs)
    ins = refs[: 2 * with_half + 2 * with_whole + (with_new and with_whole)]
    outs = refs[len(ins) :]

    def add():
        left, right = ins.pop(0), ins.pop(0)
        return (left[...].astype(F32) + right[...].astype(F32)).astype(BF)

    if with_half:
        outs.pop(0)[...] = add()
    if with_whole:
        whole = add()
        outs.pop(0)[...] = whole
        if with_new:
            outs.pop(0)[...] = jnp.where(info[4] == 1, whole, ins.pop(0)[...])


def split_columns_kernel(starts, ref, *outs):
    for start, out in zip(starts, outs):
        out[...] = ref[:, start : start + out.shape[1]]


def rest_out_kernel(info, *refs):
    *sources, w_out, w_qkv = refs
    outs = (w_out, w_qkv.at[0], w_qkv.at[1], w_qkv.at[2])
    for kept, got, out in zip(sources[::2], sources[1::2], outs):
        out[...] = jnp.where(info[4] == 1, kept[...], got[...]).astype(F32)


def choose_kernel(info, kept, got, out):
    out[...] = jnp.where(info[4] == 1, kept[...], got[...])


def stack_kernel(info, keep, got, activations, input_grads):
    width = activations.shape[2]
    for i, source in ((info[1], keep), (1 - info[1], got)):
        activations[i] = source[:, :width]
        input_grads[i] = source[:, width:].astype(F32)


def last_kernel(docs, info, lengths, own_core, other_core, out, scr):
    seq = scr.shape[0]
    half = seq // 2
    width = out.shape[1]
    start, _ = longest_start(info, lengths, docs)
    here = slice(2 * width, 2 * width + half)
    mine, theirs = own_core[:half, here].astype(F32).T, other_core[:half, here].astype(F32).T
    zero = jnp.zeros_like(mine)
    low = info[0] == 0
    scr[:half, :half] = jnp.where(low, mine, theirs)
    scr[half:, half:] = jnp.where(low, theirs, mine)
    scr[:half, half:] = zero
    scr[half:, :half] = zero
    full = pltpu.roll(scr[...], lax.rem(start + half * (1 - info[0]) + half, seq), 0)[:half]
    full = pltpu.roll(full, start, 1).astype(BF)
    rows = packed_rows(half)
    out[:rows] = jnp.zeros((rows, out.shape[1]), BF)
    out[rows:] = (own_core[half:, :width].astype(F32) + other_core[half:, :width].astype(F32)).astype(BF)
    for row, column, source_row, source_column, count in packing(half):
        out[row : row + count, column : column + half] = full[
            source_row : source_row + count, source_column : source_column + half
        ]


def packing(half):
    rows = packed_rows(half)
    moves = []
    for piece in range(2):
        done = 0
        while done < half:
            place = piece * half + done
            count = min(half - done, rows - place % rows)
            moves.append((place % rows, place // rows * half, done, piece * half, count))
            done += count
    return moves


def packed_rows(half):
    return -(-2 * half // (3 * PAD)) * PAD


def last_out_kernel(info, own, other, logits, noise, mask_out, *outs):
    half = logits.shape[0] // 2
    low = info[0] == 0
    first = jnp.where(low, own[...], other[...])
    second = jnp.where(low, other[...], own[...])
    for base, block in ((0, first), (half, second)):
        for row, column, to_row, to_column, count in packing(half):
            here = (slice(base + to_row, base + to_row + count), slice(to_column, to_column + half))
            slope = 1.0 / (1.0 + jnp.exp(logits[here] + noise[here]))
            mask_out[here] = block[row : row + count, column : column + half].astype(F32) * slope
    sums = own[packed_rows(half) :].astype(F32)
    *vectors, b_in, b_qv = outs
    for i, out in enumerate(vectors):
        out[...] = sums[i : i + 1]
    place = 2 * info[1] + info[0]
    for part in range(PARTS):

        @pl.when(place == part)
        def _():
            b_in[...] = sums[6 + part : 7 + part, : b_in.shape[1]]
            head = b_qv.shape[1]
            b_qv[0:1] = sums[10 + part : 11 + part, :head]
            b_qv[1:2] = sums[10 + part : 11 + part, head : 2 * head]


def rows_kernel(docs, column, info, lengths, second, second_other, pack, pack_other, keep_out, give_out, scr):
    seq, width = scr.shape
    half = seq // 2
    rows = seq // PARTS
    start, _ = longest_start(info, lengths, docs)
    low = info[0] == 0
    place = 2 * info[1] + info[0]
    far = 2 * (1 - info[1]) + info[0]
    for i, (own, other, first) in enumerate(((second, second_other, 0), (pack, pack_other, column))):
        here = slice(first, first + width)
        mine, theirs = own[:half, here].astype(F32), other[:half, here].astype(F32)
        scr[:half] = jnp.where(low, mine, theirs)
        scr[half:] = jnp.where(low, theirs, mine)
        to = slice(i * width, (i + 1) * width)
        keep_out[:, to] = pltpu.roll(scr[...], lax.rem(start + seq - place * rows, seq), 0)[:rows].astype(BF)
        give_out[:, to] = pltpu.roll(scr[...], lax.rem(start + seq - far * rows, seq), 0)[:rows].astype(BF)


class Order:
    def __init__(self):
        self.last = None
        self.due = []

    def after(self, *values):
        if self.last is None:
            return values
        return lax.optimization_barrier((*values, self.last))[: len(values)]

    def arrived(self, *values):
        self.due += values

    def run(self, step, *inputs):
        return self.run_with((), step, *inputs)[0]

    def run_with(self, arrivals, step, *inputs):
        due, self.due = self.due, []
        values = self.after(*inputs, *arrivals, *due)[: len(inputs) + len(arrivals)]
        result = step(*values[: len(inputs)])
        self.last = jax.tree.leaves(result)[0]
        return result, values[len(inputs) :]


def shards(
    inputs, out_grad, doc_lengths, w_qkv, b_qv, w_out, b_out, norm1_gain, norm1_bias,
    w_in, b_in, w_back, b_back, norm2_gain, norm2_bias, mask_logits, mask_noise,
):
    count, seq, width = inputs.shape
    docs = doc_lengths.shape[1]
    core, chip = lax.axis_index("core"), lax.axis_index("chip")
    odd = lax.axis_index("dp") % 2
    part = 2 * chip + core
    half = seq // 2
    head = w_out.shape[1]
    units = w_in.shape[2]
    assert lax.axis_size("pipe") == 2 and lax.axis_size("chip") == 2 and count == 2
    assert lax.axis_size("dp") % 2 == 0 and PARTS * head == width and seq % (2 * PARTS) == 0
    place = lax.axis_index("dp")
    line = lax.axis_size("dp") == 4
    middle = ((place == 1) | (place == 2)) if line else place >= 0
    info = jnp.stack([core, chip, odd, lax.axis_index("pipe"), middle]).astype(jnp.int32)
    order = Order()
    everyone = ("chip", "core")

    def diagonal(block):
        return lax.ppermute(block, everyone, [(i, i ^ 3) for i in range(PARTS)])

    low_rows = pltpu.VMEM((half, width), BF)
    low_columns = pltpu.VMEM((width, half), BF)
    up_scratch = [low_rows, low_rows, low_columns, low_columns]
    down_scratch = [pltpu.VMEM((width, half), F32), low_rows, low_rows, low_rows, pltpu.VMEM((half, half), F32)]
    flat = shape(half, width)
    flat32 = shape(half, width, dtype=F32)

    pack, half_pack, half_in = call(
        split_kernel,
        [shape(4 * head + 2 * PAD, width), shape(2 * head + PAD, width), shape(width // 2 + 2 * PAD, units)],
        [SMEM] + [HBM] * 5,
        (info, jnp.swapaxes(w_qkv[0], 1, 2).reshape(3 * head, width), w_out[0], w_in[0], b_in, b_qv[0]),
        [pltpu.VMEM((3 * head, width), BF), pltpu.VMEM((head, width), BF), pltpu.VMEM((width // 2, units), BF),
         pltpu.VMEM((1, units), BF), pltpu.VMEM((2, head), BF), pltpu.SemaphoreType.DMA((5,))],
        56 << 20,
    )
    got_pack = swap(half_pack, "chip")
    got_in = swap(half_in, "chip")
    near = [swap(v, "core") for v in (pack, w_in[0], w_back[0])]

    def prepare(*args):
        return call(
            functools.partial(prepare_kernel, docs),
            [flat, flat, shape(half, half, dtype=F32)],
            [SMEM, SMEM, VMEM, VMEM, VMEM, VMEM],
            args,
        )

    tokens0, top0, bias = order.run(prepare, info, doc_lengths, inputs, out_grad, mask_logits[0], mask_noise[0])
    got_pack, *near = order.after(got_pack, *near)
    also_pack = swap(got_pack, "dp")
    w_back_own, got_pack = lax.optimization_barrier((w_back[0], got_pack))
    got_back = swap(w_back_own, "chip")
    cross_got_pack = swap(got_pack, "core")
    got_in, got_pack = lax.optimization_barrier((got_in, got_pack))
    also_in = swap(got_in, "dp")
    cross_got_in = swap(got_in, "core")
    also_pack, got_in = lax.optimization_barrier((also_pack, got_in))
    p1 = (pack, near[0], got_pack, also_pack, cross_got_pack, swap(also_pack, "core"))

    def attention(tokens, *p1):
        return call(
            attention_kernel,
            [flat32, shape(4, width, width), shape(2, width, dtype=F32), shape(PARTS, units, dtype=F32)],
            [SMEM] + [VMEM] * 11,
            (info, tokens, bias, b_out, norm1_gain, norm1_bias) + p1,
            up_scratch,
        )

    first, w4, both_b_qv, full_b_in = order.run(attention, tokens0, *p1)
    order.arrived(cross_got_in)
    total = order.run(
        lambda *a: call(ffn_near_kernel, flat32, [VMEM] * 7, a),
        first, b_back, full_b_in, w_in[0], near[1], w_back[0], near[2],
    )
    (also_in,) = order.after(also_in)
    cross_also_in = swap(also_in, "core")
    (got_back,) = order.after(got_back)
    backs = (w_back[0], near[2], got_back, swap(got_back, "core"))
    hidden_far, in_far = order.run(
        lambda *a: call(
            ffn_far_kernel, [shape(half, 2 * units), shape(2, width, units)], [SMEM] + [VMEM] * 6, (info,) + a
        ),
        first, full_b_in, got_in, also_in, cross_got_in, cross_also_in,
    )
    second = order.run(
        lambda *a: call(ffn_end_kernel, flat, [VMEM] * 6, a),
        total, hidden_far, norm2_gain, norm2_bias, backs[2], backs[3],
    )
    weights = (w4, both_b_qv, full_b_in, w_in[0], near[1], in_far) + backs
    passed = lax.ppermute(second, "pipe", [(0, 1)])

    tokens = order.run(
        lambda *a: call(choose_tokens_kernel, flat, [SMEM, VMEM, VMEM], (info,) + a), tokens0, passed
    )
    tokens_chip = swap(tokens, "chip")
    tokens_core = swap(tokens, "core")

    keep_width = units + head

    def layer(tokens):
        return call(
            layer_kernel,
            [flat, flat, shape(half, 2 * head)]
            + [shape(half, keep_width)] * 2 + [shape(half, units)] * 2
            + [flat, flat, flat, shape(width, half), shape(width // HEAD_DIM, half, half),
               flat32, shape(half, 128, dtype=F32), shape(half, PARTS * units),
               flat32, shape(half, 128, dtype=F32)],
            [VMEM] * (8 + WEIGHTS),
            (tokens, bias, b_out, norm1_gain, norm1_bias, b_back, norm2_gain, norm2_bias) + weights,
            up_scratch,
        )

    second, first_low, far_attended, *kept = order.run(layer, tokens)
    keeps, kept = kept[:PARTS], kept[PARTS:]
    q, k, v, kt, chance, unit1, scale1, slope, unit2, scale2 = kept
    keeps = [keeps[0], swap(keeps[1], "core"), swap(keeps[2], "chip"), diagonal(keeps[3])]
    far_chip = swap(first_low, "chip")

    def down(top):
        return call(
            down_kernel, flat, [VMEM] * (13 + WEIGHTS),
            (top, unit1, scale1, norm1_gain, unit2, scale2, norm2_gain, slope, q, k, v, kt, chance) + weights,
            down_scratch,
        )

    down_grad, (tokens_chip, tokens_core) = order.run_with((tokens_chip, tokens_core), down, top0)
    passed = lax.ppermute(down_grad, "pipe", [(1, 0)])
    tokens_all = [tokens, tokens_core, tokens_chip, swap(tokens_chip, "core")]

    def rows_of(*args):
        return call(
            functools.partial(rows_kernel, docs, width),
            [shape(seq // PARTS, 2 * width)] * 2,
            [SMEM, SMEM] + [VMEM] * 4,
            (info, doc_lengths) + args,
            [pltpu.VMEM((seq, width), F32)],
        )

    def down_norm(top, passed):
        return call(
            down_norm_kernel, [flat, shape(half, 2 * width), flat32, shape(PAD, width, dtype=F32)], [SMEM] + [VMEM] * 6,
            (info, top, passed, unit2, scale2, norm2_gain, first_low),
        )

    (ffn_low, ffn_pack, sum_grad, sums), keeps[1:] = order.run_with(keeps[1:], down_norm, top0, passed)
    ffn_chip = swap(ffn_low, "chip")
    ffn_core = swap(ffn_pack, "core")
    (second,) = order.after(second)
    second_other = swap(second, "core")

    def down_ffn(sum_grad):
        return call(
            down_ffn_kernel,
            [shape(half, units)] * PARTS + [flat32], [VMEM] * (2 + WEIGHTS), (sum_grad, slope) + weights,
        )

    *pres, first_grad = order.run(down_ffn, sum_grad)
    pre_core = swap(pres[1], "core")

    lanes = [dict(own=None, half=None, whole=None, end=None, middle=None, names=[]) for _ in range(2)]
    final = {}

    def slot(lane, name=None, new=None):
        if not line:
            if new is not None:
                final[name] = (lax.psum(new, "dp"),) * 2
            return
        if lane["whole"] is not None:
            final[lane["names"].pop(0)] = (lane["whole"], lane["end"])
        with_half, with_whole = lane["own"] is not None, lane["half"] is not None
        ins = [lane["own"], lane["end"]] if with_half else []
        if with_whole:
            ins += [lane["half"], lane["middle"]] + ([new] if new is not None else [])
        half_sum = whole = None
        going = new
        if ins:
            outs = with_half + with_whole + (with_whole and new is not None)
            results = order.run(
                lambda *a: call(
                    functools.partial(slot_kernel, with_half, with_whole, new is not None),
                    [shape(*a[0].shape)] * outs, [SMEM] + [VMEM] * len(a), (info,) + a,
                ),
                *ins,
            )
            if with_half:
                half_sum = results[0]
            if with_whole:
                whole = results[int(with_half)]
                going = results[-1] if new is not None else whole
        if new is not None and whole is None:
            (going,) = order.after(going)
        routes = ([(0, 1), (3, 2)] if new is not None else []) + ([(1, 0), (2, 3)] if whole is not None else [])
        lane["end"] = lax.ppermute(going, "dp", routes) if routes else None
        lane["middle"] = lax.ppermute(half_sum, "dp", [(1, 2), (2, 1)]) if half_sum is not None else None
        lane["own"], lane["half"], lane["whole"] = new, half_sum, whole
        if new is not None:
            lane["names"].append(name)

    def matrix(*names):
        sources = [v for name in names for v in final[name]]
        rows = sum(v.shape[0] for v in sources) // 2
        return order.run(
            lambda *a: call(
                whole_kernel, shape(rows, a[0].shape[1], dtype=F32), [SMEM] + [VMEM] * len(a), (info,) + a
            ),
            *sources,
        )

    def products_of(outs, lefts, left_starts, left_first, rights, right_starts, right_size):
        return order.run(
            lambda *a: call(
                functools.partial(products_kernel, half, left_starts, left_first, right_starts, right_size),
                [shape(n, right_size) for n in outs], [VMEM] * (2 * PARTS), a,
            ),
            *lefts, *rights,
        )

    chip_width = width + 8 * head

    def down_attention(first_grad, sums, *pres):
        return call(
            down_attention_kernel,
            [shape(half, chip_width), shape(half + PAD, -(-(2 * width + half + 3 * head) // 128) * 128)]
            + [shape(half, 3 * head)],
            [SMEM] + [VMEM] * (12 + PARTS),
            (info, first_grad, sums, unit1, scale1, norm1_gain, q, k, v, kt, chance) + pres + (far_attended, w4),
            [pltpu.VMEM((PAD, width), F32)] + down_scratch,
        )

    down_core_projected = 2 * width + half
    down_chip, down_pack, projected_zero = order.run(down_attention, first_grad, sums, *pres)
    ffn_chip, far_chip = order.after(ffn_chip, far_chip)
    ffns = [ffn_low, ffn_core, ffn_chip, swap(ffn_chip, "core")]
    far_cross = swap(far_chip, "core")
    pre_chip, pre_diagonal = swap(pres[2], "chip"), diagonal(pres[3])
    none = (0, 0, 0, 0)
    quarter = units // 4
    one, two = lanes
    order.arrived(second_other)
    back = products_of((quarter,) * 4, keeps, none, 0, ffns, none, width)
    down_give, down_chip_give = order.after(down_pack, down_chip)
    down_other = swap(down_give, "core")
    branch_chip = swap(down_chip_give, "chip")
    slot(one, "back0", back[0])
    slot(two, "back1", back[1])

    def last_chunk(*args):
        return call(
            functools.partial(last_kernel, docs),
            shape(packed_rows(half) + PAD, width),
            [SMEM, SMEM] + [VMEM] * 2,
            (info, doc_lengths) + args,
            [pltpu.VMEM((seq, seq), F32)],
        )

    def split_columns(starts, sizes, packed):
        return order.run(
            lambda a: call(
                functools.partial(split_columns_kernel, starts), [shape(half, n) for n in sizes], [VMEM], (a,)
            ),
            packed,
        )

    last = order.run(last_chunk, down_pack, down_other)
    rows_keep, rows_give = order.run(rows_of, second, second_other, down_pack, down_other)
    order.arrived(far_cross, pre_core)
    slot(one, "back2", back[2])
    slot(two, "back3", back[3])
    slot(one, "last", last)
    if line:
        order.arrived(two["end"], two["middle"])
    far_branch, far_projected = split_columns((0, width + 4 * head), (width, 4 * head), branch_chip)
    far_branch, far_projected = swap(far_branch, "core"), swap(far_projected, "core")
    (w_out_low,) = products_of(
        (head,), [*keeps[:2], branch_chip, far_projected], (units, units, width + 3 * head, 3 * head), 0,
        [down_chip, down_other, branch_chip, far_branch], none, width,
    )
    w_qkv_low = products_of(
        (head,) * 3, [projected_zero, down_other, branch_chip, far_projected], (0, down_core_projected, width, 0), 0,
        tokens_all, none, width,
    )
    slot(two, "q", w_qkv_low[0])
    slot(one, "k", w_qkv_low[1])
    order.arrived(pre_chip)
    slot(two, "v", w_qkv_low[2])
    inner = products_of(
        (quarter,) * 4, [first_low, ffn_core, far_chip, far_cross], (0, width, 0, 0), 0,
        [pres[0], pre_core, pre_chip, pre_diagonal], none, units,
    )
    slot(one, "in0", inner[0])
    slot(two, "in1", inner[1])
    (rows_give,) = order.after(rows_give)
    rows_got = swap(rows_give, "chip")
    slot(one, "in2", inner[2])
    last = order.run(
        lambda a, b: call(choose_kernel, shape(*a.shape), [SMEM, VMEM, VMEM], (info, a, b)), *final["last"]
    )
    last_got = swap(last, "chip")
    slot(two, "in3", inner[3])
    slot(one, "out", w_out_low)
    grad_w_back = matrix("back0", "back1", "back2", "back3")
    slot(two)
    activations, input_grads = order.run(
        lambda a, b: call(
            stack_kernel, [shape(2, seq // PARTS, width), shape(2, seq // PARTS, width, dtype=F32)],
            [SMEM, VMEM, VMEM], (info, a, b),
        ),
        rows_keep, rows_got,
    )
    slot(one)
    last = order.run(lambda a, b: call(add_kernel, shape(*a.shape), [VMEM] * 2, (a, b)), last, last_got)
    last_other = swap(last, "core")
    if line:
        order.arrived(two["end"])
    slot(two)
    grad_mask, *vectors, grad_b_in, grad_b_qv = order.run(
        lambda *a: call(
            last_out_kernel,
            [shape(seq, seq, dtype=F32)] + [shape(1, width, dtype=F32)] * 6
            + [shape(1, units, dtype=F32), shape(2, head, dtype=F32)],
            [SMEM] + [VMEM] * 4, (info,) + a,
        ),
        last, last_other, mask_logits[0], mask_noise[0],
    )
    if line:
        order.arrived(one["end"])
    slot(one)
    slot(two)
    slot(one)
    grad_w_qkv = matrix("q", "k", "v").reshape(3, head, width)
    grad_w_in = matrix("in0", "in1", "in2", "in3")
    grad_w_out = matrix("out")
    results = (
        activations, input_grads, jnp.swapaxes(grad_w_qkv, 1, 2), grad_b_qv, grad_w_out,
        vectors[0][0], vectors[1][0], vectors[2][0],
        grad_w_in, grad_b_in[0], grad_w_back,
        vectors[3][0], vectors[4][0], vectors[5][0],
        grad_mask,
    )
    return tuple(item[None] for item in results)


def solution(mesh):
    pipe, dp, tensor = (mesh.shape[name] for name in ("pipe", "dp", "tensor"))
    split = Mesh(mesh.devices.reshape(pipe, dp, tensor // 2, 2), ("pipe", "dp", "chip", "core"))
    placed = (
        P("dp", None, None),
        P("dp", None, None),
        P("dp", None),
        P("pipe", None, None, TENSOR),
        P("pipe", None, TENSOR),
        P("pipe", TENSOR, None),
        P("pipe", None),
        P("pipe", None),
        P("pipe", None),
        P("pipe", None, TENSOR),
        P("pipe", TENSOR),
        P("pipe", TENSOR, None),
        P("pipe", None),
        P("pipe", None),
        P("pipe", None),
        P("pipe", None, None),
        P("pipe", None, None),
    )
    return jax.shard_map(
        shards,
        mesh=split,
        in_specs=placed,
        out_specs=(
            P("pipe", "dp", TENSOR, None),
            P("pipe", "dp", TENSOR, None),
            P("pipe", None, None, TENSOR),
            P("pipe", None, TENSOR),
            P("pipe", TENSOR, None),
            P("pipe", None),
            P("pipe", None),
            P("pipe", None),
            P("pipe", None, TENSOR),
            P("pipe", TENSOR),
            P("pipe", TENSOR, None),
            P("pipe", None),
            P("pipe", None),
            P("pipe", None),
            P("pipe", None, None),
        ),
        check_vma=False,
    )
```

```python
import functools
import math

import jax
import jax.numpy as jnp
from jax import lax
from jax.experimental import pallas as pl
from jax.experimental.pallas import tpu as pltpu
from jax.sharding import Mesh
from jax.sharding import PartitionSpec as P

HEAD_DIM = 64
EPSILON = 1e-12
MASKED = -1e30
BF = jnp.bfloat16
F32 = jnp.float32
NT = ((1,), (1,))
TN = ((0,), (0,))
NN = ((1,), (0,))
PARTS = 4
PAD = 16
TENSOR = ("chip", "core")
LIMIT = 8 << 20


def dot(left, right, dims=NN):
    return lax.dot_general(left, right, (dims, ((), ())), preferred_element_type=F32)


def swap(block, axis):
    return lax.ppermute(block, axis, [(i, i ^ 1) for i in range(lax.axis_size(axis))])


SMEM = pl.BlockSpec(memory_space=pltpu.SMEM)
VMEM = pl.BlockSpec(memory_space=pltpu.VMEM)
HBM = pl.BlockSpec(memory_space=pltpu.HBM)


def shape(*dims, dtype=BF):
    return jax.ShapeDtypeStruct(dims, dtype)


def call(kernel, out, ins, args, scratch=(), limit=LIMIT):
    return pl.pallas_call(
        kernel,
        out_shape=out,
        in_specs=ins,
        out_specs=jax.tree.map(lambda _: VMEM, out),
        scratch_shapes=list(scratch),
        compiler_params=pltpu.CompilerParams(vmem_limit_bytes=limit),
        cost_estimate=pl.CostEstimate(flops=0, bytes_accessed=0, transcendentals=0),
    )(*args)


def longest_start(info, lengths, docs):
    chip = info[1]
    sizes = [lengths[chip, i] for i in range(docs)]
    bounds, start, total = [], jnp.int32(0), jnp.int32(0)
    longest = sizes[0]
    for size in sizes[1:]:
        longest = jnp.maximum(longest, size)
    for size in sizes:
        start = jnp.where(size == longest, total, start)
        total = total + size
        bounds.append(total)
    return start, bounds


def prepare_kernel(docs, info, lengths, inputs, grads, logits, noise, tokens_out, top_out, bias_out):
    seq = logits.shape[0]
    half = seq // 2
    start, bounds = longest_start(info, lengths, docs)
    begin = lax.rem(start + half * info[0], seq)
    shift = lax.rem(seq - begin, seq)
    tokens_out[...] = pltpu.roll(inputs[info[1]].astype(F32), shift, 0)[:half].astype(BF)
    top_out[...] = pltpu.roll(grads[info[1]].astype(F32), shift, 0)[:half].astype(BF)
    table = logits[...] + noise[...]
    table = pltpu.roll(table, shift, 0)[:half]
    table = pltpu.roll(table, shift, 1)[:, :half]
    term = jnp.minimum(table, 0.0) - jnp.log1p(jnp.exp(-jnp.abs(table)))

    def owners(axis):
        place = begin + lax.broadcasted_iota(jnp.int32, (half, half), axis)
        place = jnp.where(place >= seq, place - seq, place)
        owner = jnp.zeros((half, half), jnp.int32)
        for bound in bounds:
            owner = owner + jnp.where(place >= bound, 1, 0)
        return owner

    bias_out[...] = jnp.where(owners(0) == owners(1), term, MASKED).T


def split_kernel(info, qkv, w_out, w_in, b_in, b_qv, pack, half_pack, half_in, qkv_scr, out_scr, in_scr, b_in_scr, b_qv_scr, sems):
    size = w_in.shape[0] // 2
    pairs = (
        (qkv, qkv_scr), (w_out, out_scr), (b_in, b_in_scr), (b_qv, b_qv_scr),
        (w_in.at[pl.ds(pl.multiple_of(info[2] * size, size), size)], in_scr),
    )
    copies = [pltpu.make_async_copy(src, dst, sems.at[i]) for i, (src, dst) in enumerate(pairs)]
    for copy in copies:
        copy.start()
    for copy in copies:
        copy.wait()
    head = out_scr.shape[0]
    step = 2 * head + PAD
    pack[: 2 * head] = qkv_scr[: 2 * head]
    pack[2 * head : step] = jnp.zeros((PAD, pack.shape[1]), BF)
    pack[2 * head : 2 * head + 1, : b_in.shape[1]] = b_in_scr[...]
    pack[step : step + head] = qkv_scr[2 * head :]
    pack[step + head : step + 2 * head] = out_scr[...]
    pack[step + 2 * head :] = jnp.zeros((PAD, pack.shape[1]), BF)
    pack[step + 2 * head : step + 2 * head + 1, :head] = b_qv_scr[0:1]
    pack[step + 2 * head : step + 2 * head + 1, head : 2 * head] = b_qv_scr[1:2]
    half_pack[...] = pack[pl.ds(pl.multiple_of(info[2] * step, PAD), step)]
    half_in[:size] = in_scr[...]
    half_in[size:] = jnp.zeros((half_in.shape[0] - size, half_in.shape[1]), BF)


def norm(values):
    average = jnp.mean(values, axis=-1, keepdims=True)
    centred = values - average
    variance = jnp.mean(centred * centred, axis=-1, keepdims=True)
    scale = lax.rsqrt(variance + EPSILON)
    return centred * scale, scale


def norm_back(grad, unit, scale, gain):
    direct = grad * gain
    return scale * (
        direct
        - jnp.mean(direct, axis=-1, keepdims=True)
        - unit * jnp.mean(direct * unit, axis=-1, keepdims=True)
    )


def assemble(info, pieces, w4, b_qv, b_in):
    head = w4.shape[1] // PARTS
    step = 2 * head + PAD
    even = info[2] == 0
    for part in range(PARTS):
        here = slice(part * head, (part + 1) * head)
        for which in range(2):
            if part < 2:
                block = pieces[part][which * step : (which + 1) * step]
            else:
                got, also = pieces[2 * part - 2], pieces[2 * part - 1]
                block = jnp.where(even, got[...], also[...]) if which == 0 else jnp.where(even, also[...], got[...])
            w4[2 * which, here] = block[:head]
            w4[2 * which + 1, here] = block[head : 2 * head]
            if which == 0:
                b_in[part : part + 1] = block[2 * head : 2 * head + 1, : b_in.shape[1]].astype(F32)
            else:
                row = block[2 * head : 2 * head + 1].astype(F32)
                b_qv[0:1, here] = row[:, :head]
                b_qv[1:2, here] = row[:, head : 2 * head]


class Weights:
    def __init__(self, refs):
        self.w4, self.b_qv, self.b_in, self.in_near, self.in_far, self.backs = (
            refs[0], refs[1], refs[2], refs[3:5], refs[5], refs[6:10]
        )
        self.units = self.in_far.shape[2]

    def w_in(self, part):
        return self.in_near[part][...] if part < 2 else self.in_far[part - 2]

    def w_back(self, part):
        return self.backs[part][...]


WEIGHTS = 10


def attention_forward(tokens, bias_ref, w4, b_qv, out_parts, scratch):
    width = tokens.shape[1]
    q_scr, k_scr, vt_scr, at_scr = scratch
    queries = (dot(tokens, w4[0], NT) + b_qv[0:1]).astype(BF)
    keys = dot(tokens, w4[1], NT).astype(BF)
    values = (dot(tokens, w4[2], NT) + b_qv[1:2]).astype(BF)
    values_t = values.T
    if out_parts is not None:
        q_out, k_out, v_out, kt_out, p_out = out_parts
        q_out[...], k_out[...], v_out[...] = queries, keys, values
        kt_out[...] = keys.T
    q_scr[...] = queries * jnp.asarray(1.0 / math.sqrt(HEAD_DIM), BF)
    k_scr[...] = keys
    vt_scr[...] = values_t
    pair = 2 * HEAD_DIM
    lane = lax.broadcasted_iota(jnp.int32, (tokens.shape[0], pair), 1)

    def heads(j):
        here = pl.ds(j * pair, pair)
        q_pair, k_pair = q_scr[:, here], k_scr[:, here]
        for s in range(2):
            mine = (lane >= HEAD_DIM) if s else (lane < HEAD_DIM)
            scores = dot(jnp.where(mine, k_pair, jnp.zeros_like(k_pair)), q_pair, NT) + bias_ref[...]
            exponent = jnp.exp(scores - jnp.max(scores, axis=0, keepdims=True))
            chance = (exponent * (1.0 / jnp.sum(exponent, axis=0, keepdims=True))).astype(BF)
            if out_parts is not None:
                p_out[2 * j + s] = chance
            rows = pl.ds(j * pair + s * HEAD_DIM, HEAD_DIM)
            at_scr[rows, :] = dot(vt_scr[rows, :], chance).astype(BF)

    for j in range(width // pair):
        heads(j)
    return at_scr[...].T


def gelu(values):
    cdf = 0.5 * (1.0 + lax.erf(values * math.sqrt(0.5)))
    return values * cdf, cdf


def attention_kernel(info, tokens, bias, b_out, gain, offset, *rest):
    pieces, (first_out, w4, b_qv, b_in, *scratch) = rest[:6], rest[6:]
    assemble(info, pieces, w4, b_qv, b_in)
    attended = attention_forward(tokens[...], bias, w4, b_qv, None, scratch)
    unit, _ = norm(tokens[...].astype(F32) + dot(attended, w4[3]) + b_out[...])
    first_out[...] = unit * gain[...] + offset[...]


def ffn_near_kernel(first, b_back, b_in, *rest):
    w_ins, w_backs, out = rest[:2], rest[2:4], rest[4]
    first_low = first[...].astype(BF)
    total = first[...] + b_back[...]
    for part in range(2):
        hidden, _ = gelu(dot(first_low, w_ins[part][...]) + b_in[part : part + 1])
        total = total + dot(hidden.astype(BF), w_backs[part][...])
    out[...] = total


def ffn_far_kernel(info, first, b_in, far_got, far_also, cross_got, cross_also, hidden_out, in_out):
    even = info[2] == 0
    units = in_out.shape[2]
    half = in_out.shape[1] // 2
    first_low = first[...].astype(BF)
    for part, (got, also) in enumerate(((far_got, far_also), (cross_got, cross_also))):
        in_out[part, :half] = jnp.where(even, got[:half], also[:half])
        in_out[part, half:] = jnp.where(even, also[:half], got[:half])
        hidden, _ = gelu(dot(first_low, in_out[part]) + b_in[part + 2 : part + 3])
        hidden_out[:, part * units : (part + 1) * units] = hidden.astype(BF)


def ffn_end_kernel(total, hidden, gain, offset, far, cross, out):
    units = far.shape[0]
    result = total[...] + dot(hidden[:, :units], far[...]) + dot(hidden[:, units:], cross[...])
    unit, _ = norm(result)
    out[...] = (unit * gain[...] + offset[...]).astype(BF)


def choose_tokens_kernel(info, first_tokens, passed, out):
    out[...] = jnp.where(info[3] == 0, first_tokens[...], passed[...])


def layer_kernel(tokens_ref, bias, b_out, gain_one, offset_one, b_back, gain_two, offset_two, *rest):
    weights, rest = Weights(rest[:WEIGHTS]), rest[WEIGHTS:]
    second_out, first_out, att_out, *rest = rest
    keep_outs, rest = rest[:PARTS], rest[PARTS:]
    (q_out, k_out, v_out, kt_out, p_out, unit1_out, scale1_out, slope_out, unit2_out, scale2_out, *scratch) = rest
    tokens = tokens_ref[...]
    width = tokens.shape[1]
    attended = attention_forward(
        tokens, bias, weights.w4, weights.b_qv, (q_out, k_out, v_out, kt_out, p_out), scratch
    )
    units, head = weights.units, width // PARTS
    for part in range(PARTS):
        out, base = (keep_outs[part], units) if part < 2 else (att_out, (part - 2) * head)
        out[:, base : base + head] = attended[:, part * head : (part + 1) * head]
    unit, scale = norm(tokens.astype(F32) + dot(attended, weights.w4[3]) + b_out[...])
    unit1_out[...] = unit
    scale1_out[...] = jnp.broadcast_to(scale, scale1_out.shape)
    first = unit * gain_one[...] + offset_one[...]
    first_low = first.astype(BF)
    first_out[...] = first_low
    total = first + b_back[...]
    for part in range(PARTS):
        pre = dot(first_low, weights.w_in(part)) + weights.b_in[part : part + 1]
        value, cdf = gelu(pre)
        hidden = value.astype(BF)
        keep_outs[part][:, :units] = hidden
        density = jnp.exp(-0.5 * pre * pre) * (1.0 / math.sqrt(2.0 * math.pi))
        slope_out[:, part * units : (part + 1) * units] = (cdf + pre * density).astype(BF)
        total = total + dot(hidden, weights.w_back(part))
    unit, scale = norm(total)
    unit2_out[...] = unit
    scale2_out[...] = jnp.broadcast_to(scale, scale2_out.shape)
    second_out[...] = (unit * gain_two[...] + offset_two[...]).astype(BF)


def rows_sum(values):
    return jnp.sum(values, axis=0, keepdims=True)


def ffn_backward(sum_grad, slope, weights, pre_outs):
    units = weights.units
    ffn_low = sum_grad.astype(BF)
    first_grad = sum_grad
    for part in range(PARTS):
        pre = dot(ffn_low, weights.w_back(part), NT) * slope[:, part * units : (part + 1) * units].astype(F32)
        pre = pre.astype(BF)
        if pre_outs is not None:
            pre_outs[part][...] = pre
        first_grad = first_grad + dot(pre, weights.w_in(part), NT)
    return first_grad


def attention_backward(first_grad, unit, scale, gain, refs, w_scr, scratch, outs):
    q_ref, k_ref, v_ref, kt_ref, p_ref = refs
    width = first_grad.shape[1]
    branch = norm_back(first_grad, unit, scale, gain)
    branch_low = branch.astype(BF)
    att_grad = dot(branch_low, w_scr[3], NT).astype(BF)
    pair = 2 * HEAD_DIM
    rows = first_grad.shape[0]
    lane = lax.broadcasted_iota(jnp.int32, (rows, pair), 1)
    root = 1.0 / math.sqrt(HEAD_DIM)
    dqt_scr, dk_scr, dv_scr, o_scr, term_scr = scratch
    o_scr[...] = att_grad
    term_scr[...] = jnp.zeros((rows, rows), F32)

    def heads(j, carry):
        here = pl.ds(pl.multiple_of(j * pair, pair), pair)
        q_pair, v_pair, o_pair = q_ref[:, here], v_ref[:, here], o_scr[:, here]
        dk, dv = [], []
        for s in range(2):
            mine = (lane >= HEAD_DIM) if s else (lane < HEAD_DIM)
            chance_low = p_ref[2 * j + s]
            chance = chance_low.astype(F32)
            chance_grad = dot(jnp.where(mine, v_pair, jnp.zeros_like(v_pair)), o_pair, NT)
            inner = jnp.sum(chance * chance_grad, axis=0, keepdims=True)
            score = chance * (chance_grad - inner)
            term_scr[...] += score
            low = score.astype(BF)
            dv.append(dot(chance_low, o_pair))
            dk.append(dot(low, q_pair))
            part = pl.ds(pl.multiple_of(j * pair + s * HEAD_DIM, HEAD_DIM), HEAD_DIM)
            dqt_scr[part, :] = dot(kt_ref[part, :], low) * root
        dk_scr[:, here] = (jnp.where(lane < HEAD_DIM, dk[0], dk[1]) * root).astype(BF)
        dv_scr[:, here] = jnp.where(lane < HEAD_DIM, dv[0], dv[1]).astype(BF)
        return carry

    lax.fori_loop(0, width // pair, heads, 0)
    dq = dqt_scr[...].T.astype(BF)
    dk, dv = dk_scr[...], dv_scr[...]
    term = term_scr[...]
    in_grad = branch + dot(dq, w_scr[0]) + dot(dk, w_scr[1]) + dot(dv, w_scr[2])
    if outs is not None:
        chip_out, diagonal_out, core_out, projected_outs = outs
        chip_out[:, :width] = branch_low
        core_out[:rows, :width] = branch_low
        core_out[:rows, width : 2 * width] = in_grad.astype(BF)
        core_out[:rows, 2 * width : 2 * width + rows] = term.astype(BF)
        head = width // PARTS
        end = 2 * width + rows + 3 * head
        core_out[:rows, end:] = jnp.zeros((rows, core_out.shape[1] - end), BF)
        for part in range(PARTS):
            out, base = (core_out, 2 * width + rows) if part == 1 else (projected_outs[0], 0)
            out, base = ((chip_out, width), (diagonal_out, 0))[part - 2] if part > 1 else (out, base)
            for i, grad in enumerate((dq, dk, dv)):
                out[:rows, base + i * head : base + (i + 1) * head] = grad[:, part * head : (part + 1) * head]
    return branch, in_grad, dq, dv


def down_kernel(top, unit1, scale1, gain_one, unit2, scale2, gain_two, slope, q_ref, k_ref, v_ref, kt_ref, p_ref, *rest):
    weights, (grad_out, *scratch) = Weights(rest[:WEIGHTS]), rest[WEIGHTS:]
    sum_grad = norm_back(top[...].astype(F32), unit2[...], scale2[:, :1], gain_two[...])
    first_grad = ffn_backward(sum_grad, slope, weights, None)
    _, in_grad, _, _ = attention_backward(
        first_grad, unit1[...], scale1[:, :1], gain_one[...], (q_ref, k_ref, v_ref, kt_ref, p_ref),
        weights.w4, scratch, None,
    )
    grad_out[...] = in_grad.astype(BF)


def down_norm_kernel(info, own_top, passed, unit2, scale2, gain_two, first, ffn_out, core_out, sum_grad_out, sums_out):
    top = jnp.where(info[3] == 0, passed[...], own_top[...]).astype(F32)
    unit = unit2[...]
    sum_grad = norm_back(top, unit, scale2[:, :1], gain_two[...])
    sum_grad_out[...] = sum_grad
    width = first.shape[1]
    ffn_out[...] = sum_grad.astype(BF)
    core_out[:, :width] = sum_grad.astype(BF)
    core_out[:, width:] = first[...]
    sums_out[...] = jnp.zeros_like(sums_out)
    sums_out[3:4] = rows_sum(sum_grad)
    sums_out[4:5] = rows_sum(top * unit)
    sums_out[5:6] = rows_sum(top)


def down_ffn_kernel(sum_grad, slope, *rest):
    weights, (*pre_outs, first_grad_out) = Weights(rest[:WEIGHTS]), rest[WEIGHTS:]
    first_grad_out[...] = ffn_backward(sum_grad[...], slope, weights, pre_outs)


def down_attention_kernel(info, first_grad, sums, unit1, scale1, gain_one, q_ref, k_ref, v_ref, kt_ref, p_ref, *rest):
    pres, attended, w4, rest = rest[:PARTS], rest[PARTS], rest[PARTS + 1], rest[PARTS + 2 :]
    chip_out, diagonal_out, core_out, zero, sums_scr, *scratch = rest
    unit = unit1[...]
    grad = first_grad[...]
    rows, width = grad.shape
    branch, in_grad, dq, dv = attention_backward(
        grad, unit, scale1[:, :1], gain_one[...], (q_ref, k_ref, v_ref, kt_ref, p_ref),
        w4, scratch, (chip_out, diagonal_out, core_out, (zero,)),
    )
    head = width // PARTS
    chip_out[:, width + 3 * head :] = attended[:, :head]
    diagonal_out[:, 3 * head :] = attended[:, head:]
    sums_scr[...] = sums[...]
    sums_scr[0:1] = rows_sum(branch)
    sums_scr[1:2] = rows_sum(grad * unit)
    sums_scr[2:3] = rows_sum(grad)
    head = width // PARTS
    place = 2 * info[1] + info[0]
    dq_sum, dv_sum = rows_sum(dq.astype(F32)), rows_sum(dv.astype(F32))
    for part in range(PARTS):
        units = pres[0].shape[1]
        pre = pres[part][...]
        sums_scr[pl.ds(6 + jnp.bitwise_xor(place, part), 1), :units] = rows_sum(pre.astype(F32))
        here = slice(part * head, (part + 1) * head)
        row = jnp.concatenate(
            [dq_sum[:, here], dv_sum[:, here], jnp.zeros((1, width - 2 * head), F32)], axis=1
        )
        sums_scr[pl.ds(10 + jnp.bitwise_xor(place, part), 1)] = row
    core_out[rows:, :width] = sums_scr[...].astype(BF)
    core_out[rows:, width:] = jnp.zeros((PAD, core_out.shape[1] - width), BF)


def products(lefts, rights):
    total = None
    for left, right in zip(lefts, rights):
        value = dot(left, right, TN)
        total = value if total is None else total + value
    return total.astype(BF)


def products_kernel(rows, left_starts, left_first, right_starts, right_size, *refs):
    lefts, rights, outs = refs[:PARTS], refs[PARTS : 2 * PARTS], refs[2 * PARTS :]
    done = left_first
    for out in outs:
        size = out.shape[0]
        out[...] = products(
            [ref[:rows, start + done : start + done + size] for ref, start in zip(lefts, left_starts)],
            [ref[:rows, start : start + right_size] for ref, start in zip(rights, right_starts)],
        )
        done += size


def add_kernel(left, right, out):
    out[...] = (left[...].astype(F32) + right[...].astype(F32)).astype(BF)


def whole_kernel(info, *refs):
    *sources, out = refs
    row = 0
    for kept, got in zip(sources[::2], sources[1::2]):
        size = kept.shape[0]
        out[row : row + size] = jnp.where(info[4] == 1, kept[...], got[...]).astype(F32)
        row += size


def slot_kernel(with_half, with_whole, with_new, info, *refs):
    refs = list(refs)
    ins = refs[: 2 * with_half + 2 * with_whole + (with_new and with_whole)]
    outs = refs[len(ins) :]

    def add():
        left, right = ins.pop(0), ins.pop(0)
        return (left[...].astype(F32) + right[...].astype(F32)).astype(BF)

    if with_half:
        outs.pop(0)[...] = add()
    if with_whole:
        whole = add()
        outs.pop(0)[...] = whole
        if with_new:
            outs.pop(0)[...] = jnp.where(info[4] == 1, whole, ins.pop(0)[...])


def split_rows_kernel(ref, upper, lower):
    rows, width = upper.shape
    upper[...] = ref[:rows, :width]
    lower[...] = ref[rows:, :width]


def w_out_products_kernel(starts, own_keep, core_keep, chip_keep, far_keep, own, core, chip, upper, lower, out):
    head, width = out.shape
    rows = own.shape[0]
    keeps = (own_keep, core_keep, chip_keep, far_keep)
    out[...] = products(
        [ref[:rows, start : start + head] for ref, start in zip(keeps, starts)],
        [own[:, :width], core[:rows, :width], chip[:, :width], jnp.concatenate([upper[...], lower[...]])],
    )


def rest_out_kernel(info, *refs):
    *sources, w_out, w_qkv = refs
    outs = (w_out, w_qkv.at[0], w_qkv.at[1], w_qkv.at[2])
    for kept, got, out in zip(sources[::2], sources[1::2], outs):
        out[...] = jnp.where(info[4] == 1, kept[...], got[...]).astype(F32)


def choose_kernel(info, kept, got, out):
    out[...] = jnp.where(info[4] == 1, kept[...], got[...])


def stack_kernel(info, keep, got, activations, input_grads):
    width = activations.shape[2]
    for i, source in ((info[1], keep), (1 - info[1], got)):
        activations[i] = source[:, :width]
        input_grads[i] = source[:, width:].astype(F32)


def last_kernel(docs, info, lengths, own_core, other_core, out, scr):
    seq = scr.shape[0]
    half = seq // 2
    width = out.shape[1]
    start, _ = longest_start(info, lengths, docs)
    here = slice(2 * width, 2 * width + half)
    mine, theirs = own_core[:half, here].astype(F32).T, other_core[:half, here].astype(F32).T
    zero = jnp.zeros_like(mine)
    low = info[0] == 0
    scr[:half, :half] = jnp.where(low, mine, theirs)
    scr[half:, half:] = jnp.where(low, theirs, mine)
    scr[:half, half:] = zero
    scr[half:, :half] = zero
    full = pltpu.roll(scr[...], lax.rem(start + half * (1 - info[0]) + half, seq), 0)[:half]
    full = pltpu.roll(full, start, 1).astype(BF)
    rows = packed_rows(half)
    out[:rows] = jnp.zeros((rows, out.shape[1]), BF)
    out[rows:] = (own_core[half:, :width].astype(F32) + other_core[half:, :width].astype(F32)).astype(BF)
    for row, column, source_row, source_column, count in packing(half):
        out[row : row + count, column : column + half] = full[
            source_row : source_row + count, source_column : source_column + half
        ]


def packing(half):
    rows = packed_rows(half)
    moves = []
    for piece in range(2):
        done = 0
        while done < half:
            place = piece * half + done
            count = min(half - done, rows - place % rows)
            moves.append((place % rows, place // rows * half, done, piece * half, count))
            done += count
    return moves


def packed_rows(half):
    return -(-2 * half // (3 * PAD)) * PAD


def last_out_kernel(info, own, other, logits, noise, mask_out, *outs):
    half = logits.shape[0] // 2
    low = info[0] == 0
    first = jnp.where(low, own[...], other[...])
    second = jnp.where(low, other[...], own[...])
    for base, block in ((0, first), (half, second)):
        for row, column, to_row, to_column, count in packing(half):
            here = (slice(base + to_row, base + to_row + count), slice(to_column, to_column + half))
            slope = 1.0 / (1.0 + jnp.exp(logits[here] + noise[here]))
            mask_out[here] = block[row : row + count, column : column + half].astype(F32) * slope
    sums = own[packed_rows(half) :].astype(F32)
    *vectors, b_in, b_qv = outs
    for i, out in enumerate(vectors):
        out[...] = sums[i : i + 1]
    place = 2 * info[1] + info[0]
    for part in range(PARTS):

        @pl.when(place == part)
        def _():
            b_in[...] = sums[6 + part : 7 + part, : b_in.shape[1]]
            head = b_qv.shape[1]
            b_qv[0:1] = sums[10 + part : 11 + part, :head]
            b_qv[1:2] = sums[10 + part : 11 + part, head : 2 * head]


def rows_kernel(docs, column, info, lengths, second, second_other, pack, pack_other, keep_out, give_out, scr):
    seq, width = scr.shape
    half = seq // 2
    rows = seq // PARTS
    start, _ = longest_start(info, lengths, docs)
    low = info[0] == 0
    place = 2 * info[1] + info[0]
    far = 2 * (1 - info[1]) + info[0]
    for i, (own, other, first) in enumerate(((second, second_other, 0), (pack, pack_other, column))):
        here = slice(first, first + width)
        mine, theirs = own[:half, here].astype(F32), other[:half, here].astype(F32)
        scr[:half] = jnp.where(low, mine, theirs)
        scr[half:] = jnp.where(low, theirs, mine)
        to = slice(i * width, (i + 1) * width)
        keep_out[:, to] = pltpu.roll(scr[...], lax.rem(start + seq - place * rows, seq), 0)[:rows].astype(BF)
        give_out[:, to] = pltpu.roll(scr[...], lax.rem(start + seq - far * rows, seq), 0)[:rows].astype(BF)


class Order:
    def __init__(self):
        self.last = None
        self.due = []

    def after(self, *values):
        if self.last is None:
            return values
        return lax.optimization_barrier((*values, self.last))[: len(values)]

    def arrived(self, *values):
        self.due += values

    def run(self, step, *inputs):
        return self.run_with((), step, *inputs)[0]

    def run_with(self, arrivals, step, *inputs):
        due, self.due = self.due, []
        values = self.after(*inputs, *arrivals, *due)[: len(inputs) + len(arrivals)]
        result = step(*values[: len(inputs)])
        self.last = jax.tree.leaves(result)[0]
        return result, values[len(inputs) :]


def shards(
    inputs, out_grad, doc_lengths, w_qkv, b_qv, w_out, b_out, norm1_gain, norm1_bias,
    w_in, b_in, w_back, b_back, norm2_gain, norm2_bias, mask_logits, mask_noise,
):
    count, seq, width = inputs.shape
    docs = doc_lengths.shape[1]
    core, chip = lax.axis_index("core"), lax.axis_index("chip")
    odd = lax.axis_index("dp") % 2
    part = 2 * chip + core
    half = seq // 2
    head = w_out.shape[1]
    units = w_in.shape[2]
    assert lax.axis_size("pipe") == 2 and lax.axis_size("chip") == 2 and count == 2
    assert lax.axis_size("dp") % 2 == 0 and PARTS * head == width and seq % (2 * PARTS) == 0
    place = lax.axis_index("dp")
    line = lax.axis_size("dp") == 4
    middle = ((place == 1) | (place == 2)) if line else place >= 0
    info = jnp.stack([core, chip, odd, lax.axis_index("pipe"), middle]).astype(jnp.int32)
    order = Order()
    everyone = ("chip", "core")

    def diagonal(block):
        return lax.ppermute(block, everyone, [(i, i ^ 3) for i in range(PARTS)])

    low_rows = pltpu.VMEM((half, width), BF)
    low_columns = pltpu.VMEM((width, half), BF)
    up_scratch = [low_rows, low_rows, low_columns, low_columns]
    down_scratch = [pltpu.VMEM((width, half), F32), low_rows, low_rows, low_rows, pltpu.VMEM((half, half), F32)]
    flat = shape(half, width)
    flat32 = shape(half, width, dtype=F32)

    pack, half_pack, half_in = call(
        split_kernel,
        [shape(4 * head + 2 * PAD, width), shape(2 * head + PAD, width), shape(width // 2 + 2 * PAD, units)],
        [SMEM] + [HBM] * 5,
        (info, jnp.swapaxes(w_qkv[0], 1, 2).reshape(3 * head, width), w_out[0], w_in[0], b_in, b_qv[0]),
        [pltpu.VMEM((3 * head, width), BF), pltpu.VMEM((head, width), BF), pltpu.VMEM((width // 2, units), BF),
         pltpu.VMEM((1, units), BF), pltpu.VMEM((2, head), BF), pltpu.SemaphoreType.DMA((5,))],
        56 << 20,
    )
    got_pack = swap(half_pack, "chip")
    got_in = swap(half_in, "chip")
    near = [swap(v, "core") for v in (pack, w_in[0], w_back[0])]

    def prepare(*args):
        return call(
            functools.partial(prepare_kernel, docs),
            [flat, flat, shape(half, half, dtype=F32)],
            [SMEM, SMEM, VMEM, VMEM, VMEM, VMEM],
            args,
        )

    tokens0, top0, bias = order.run(prepare, info, doc_lengths, inputs, out_grad, mask_logits[0], mask_noise[0])
    got_pack, *near = order.after(got_pack, *near)
    also_pack = swap(got_pack, "dp")
    w_back_own, got_pack = lax.optimization_barrier((w_back[0], got_pack))
    got_back = swap(w_back_own, "chip")
    cross_got_pack = swap(got_pack, "core")
    got_in, got_pack = lax.optimization_barrier((got_in, got_pack))
    also_in = swap(got_in, "dp")
    cross_got_in = swap(got_in, "core")
    also_pack, got_in = lax.optimization_barrier((also_pack, got_in))
    p1 = (pack, near[0], got_pack, also_pack, cross_got_pack, swap(also_pack, "core"))

    def attention(tokens, *p1):
        return call(
            attention_kernel,
            [flat32, shape(4, width, width), shape(2, width, dtype=F32), shape(PARTS, units, dtype=F32)],
            [SMEM] + [VMEM] * 11,
            (info, tokens, bias, b_out, norm1_gain, norm1_bias) + p1,
            up_scratch,
        )

    first, w4, both_b_qv, full_b_in = order.run(attention, tokens0, *p1)
    order.arrived(cross_got_in)
    total = order.run(
        lambda *a: call(ffn_near_kernel, flat32, [VMEM] * 7, a),
        first, b_back, full_b_in, w_in[0], near[1], w_back[0], near[2],
    )
    (also_in,) = order.after(also_in)
    cross_also_in = swap(also_in, "core")
    (got_back,) = order.after(got_back)
    backs = (w_back[0], near[2], got_back, swap(got_back, "core"))
    hidden_far, in_far = order.run(
        lambda *a: call(
            ffn_far_kernel, [shape(half, 2 * units), shape(2, width, units)], [SMEM] + [VMEM] * 6, (info,) + a
        ),
        first, full_b_in, got_in, also_in, cross_got_in, cross_also_in,
    )
    second = order.run(
        lambda *a: call(ffn_end_kernel, flat, [VMEM] * 6, a),
        total, hidden_far, norm2_gain, norm2_bias, backs[2], backs[3],
    )
    weights = (w4, both_b_qv, full_b_in, w_in[0], near[1], in_far) + backs
    passed = lax.ppermute(second, "pipe", [(0, 1)])

    tokens = order.run(
        lambda *a: call(choose_tokens_kernel, flat, [SMEM, VMEM, VMEM], (info,) + a), tokens0, passed
    )
    tokens_chip = swap(tokens, "chip")
    tokens_core = swap(tokens, "core")

    keep_width = units + head

    def layer(tokens):
        return call(
            layer_kernel,
            [flat, flat, shape(half, 2 * head)]
            + [shape(half, keep_width)] * 2 + [shape(half, units)] * 2
            + [flat, flat, flat, shape(width, half), shape(width // HEAD_DIM, half, half),
               flat32, shape(half, 128, dtype=F32), shape(half, PARTS * units),
               flat32, shape(half, 128, dtype=F32)],
            [VMEM] * (8 + WEIGHTS),
            (tokens, bias, b_out, norm1_gain, norm1_bias, b_back, norm2_gain, norm2_bias) + weights,
            up_scratch,
        )

    second, first_low, far_attended, *kept = order.run(layer, tokens)
    keeps, kept = kept[:PARTS], kept[PARTS:]
    q, k, v, kt, chance, unit1, scale1, slope, unit2, scale2 = kept
    keeps = [keeps[0], swap(keeps[1], "core"), swap(keeps[2], "chip"), diagonal(keeps[3])]
    far_chip = swap(first_low, "chip")

    def down(top):
        return call(
            down_kernel, flat, [VMEM] * (13 + WEIGHTS),
            (top, unit1, scale1, norm1_gain, unit2, scale2, norm2_gain, slope, q, k, v, kt, chance) + weights,
            down_scratch,
        )

    down_grad, (tokens_chip, tokens_core) = order.run_with((tokens_chip, tokens_core), down, top0)
    passed = lax.ppermute(down_grad, "pipe", [(1, 0)])
    tokens_all = [tokens, tokens_core, tokens_chip, swap(tokens_chip, "core")]

    def rows_of(*args):
        return call(
            functools.partial(rows_kernel, docs, width),
            [shape(seq // PARTS, 2 * width)] * 2,
            [SMEM, SMEM] + [VMEM] * 4,
            (info, doc_lengths) + args,
            [pltpu.VMEM((seq, width), F32)],
        )

    def down_norm(top, passed):
        return call(
            down_norm_kernel, [flat, shape(half, 2 * width), flat32, shape(PAD, width, dtype=F32)], [SMEM] + [VMEM] * 6,
            (info, top, passed, unit2, scale2, norm2_gain, first_low),
        )

    (ffn_low, ffn_pack, sum_grad, sums), keeps[1:] = order.run_with(keeps[1:], down_norm, top0, passed)
    ffn_chip = swap(ffn_low, "chip")
    ffn_core = swap(ffn_pack, "core")
    (second,) = order.after(second)
    second_other = swap(second, "core")

    def down_ffn(sum_grad):
        return call(
            down_ffn_kernel,
            [shape(half, units)] * PARTS + [flat32], [VMEM] * (2 + WEIGHTS), (sum_grad, slope) + weights,
        )

    *pres, first_grad = order.run(down_ffn, sum_grad)
    pre_core = swap(pres[1], "core")

    lanes = [dict(own=None, half=None, whole=None, end=None, middle=None, names=[]) for _ in range(2)]
    final = {}

    def slot(lane, name=None, new=None):
        if not line:
            if new is not None:
                final[name] = (lax.psum(new, "dp"),) * 2
            return
        if lane["whole"] is not None:
            final[lane["names"].pop(0)] = (lane["whole"], lane["end"])
        with_half, with_whole = lane["own"] is not None, lane["half"] is not None
        ins = [lane["own"], lane["end"]] if with_half else []
        if with_whole:
            ins += [lane["half"], lane["middle"]] + ([new] if new is not None else [])
        half_sum = whole = None
        going = new
        if new is not None and not with_whole:
            (going,) = order.after(going)
        if ins:
            outs = with_half + with_whole + (with_whole and new is not None)
            results = order.run(
                lambda *a: call(
                    functools.partial(slot_kernel, with_half, with_whole, new is not None),
                    [shape(*a[0].shape)] * outs, [SMEM] + [VMEM] * len(a), (info,) + a,
                ),
                *ins,
            )
            if with_half:
                half_sum = results[0]
            if with_whole:
                whole = results[int(with_half)]
                going = results[-1] if new is not None else whole
        routes = ([(0, 1), (3, 2)] if new is not None else []) + ([(1, 0), (2, 3)] if whole is not None else [])
        lane["end"] = lax.ppermute(going, "dp", routes) if routes else None
        lane["middle"] = lax.ppermute(half_sum, "dp", [(1, 2), (2, 1)]) if half_sum is not None else None
        lane["own"], lane["half"], lane["whole"] = new, half_sum, whole
        if new is not None:
            lane["names"].append(name)

    def matrix(*names):
        sources = [v for name in names for v in final[name]]
        rows = sum(v.shape[0] for v in sources) // 2
        return order.run(
            lambda *a: call(
                whole_kernel, shape(rows, a[0].shape[1], dtype=F32), [SMEM] + [VMEM] * len(a), (info,) + a
            ),
            *sources,
        )

    def products_of(outs, lefts, left_starts, left_first, rights, right_starts, right_size):
        return order.run(
            lambda *a: call(
                functools.partial(products_kernel, half, left_starts, left_first, right_starts, right_size),
                [shape(n, right_size) for n in outs], [VMEM] * (2 * PARTS), a,
            ),
            *lefts, *rights,
        )


    def down_attention(first_grad, sums, *pres):
        return call(
            down_attention_kernel,
            [shape(half, 2 * width), shape(half, width), shape(half + PAD, -(-(2 * width + half + 3 * head) // 128) * 128)]
            + [shape(half, 3 * head)],
            [SMEM] + [VMEM] * (12 + PARTS),
            (info, first_grad, sums, unit1, scale1, norm1_gain, q, k, v, kt, chance) + pres + (far_attended, w4),
            [pltpu.VMEM((PAD, width), F32)] + down_scratch,
        )

    down_core_projected = 2 * width + half
    down_chip, down_diagonal, down_pack, projected_zero = order.run(down_attention, first_grad, sums, *pres)
    ffn_chip, far_chip = order.after(ffn_chip, far_chip)
    ffns = [ffn_low, ffn_core, ffn_chip, swap(ffn_chip, "core")]
    far_cross = swap(far_chip, "core")
    pre_chip, pre_diagonal = swap(pres[2], "chip"), diagonal(pres[3])
    none = (0, 0, 0, 0)
    quarter = units // 4
    one, two = lanes
    order.arrived(second_other, tokens_all[3])
    back = products_of((quarter,) * 2, keeps, none, 0, ffns, none, width)
    down_give, chip_give, diagonal_give = order.after(down_pack, down_chip, down_diagonal)
    down_other = swap(down_give, "core")
    branch_chip = swap(chip_give, "chip")
    far_projected = diagonal(diagonal_give)
    slot(one, "back0", back[0])
    slot(two, "back1", back[1])

    def last_chunk(*args):
        return call(
            functools.partial(last_kernel, docs),
            shape(packed_rows(half) + PAD, width),
            [SMEM, SMEM] + [VMEM] * 2,
            (info, doc_lengths) + args,
            [pltpu.VMEM((seq, seq), F32)],
        )

    back += products_of((quarter,) * 2, keeps, none, 2 * quarter, ffns, none, width)
    last = order.run(last_chunk, down_pack, down_other)
    rows_keep, rows_give = order.run(rows_of, second, second_other, down_pack, down_other)
    order.arrived(far_cross, pre_core)
    slot(one, "back2", back[2])
    slot(two, "back3", back[3])
    upper, lower = order.run(
        lambda a: call(split_rows_kernel, [shape(half // 2, width)] * 2, [VMEM], (a,)), branch_chip
    )
    upper, lower = swap(upper, "core"), swap(lower, "core")
    slot(one, "last", last)
    w_out_low = order.run(
        lambda *a: call(
            functools.partial(w_out_products_kernel, (units, units, width + 3 * head, 3 * head)),
            shape(head, width), [VMEM] * 9, a,
        ),
        *keeps[:2], branch_chip, far_projected, down_chip, down_other, branch_chip, upper, lower,
    )
    w_qkv_low = products_of(
        (head,) * 3, [projected_zero, down_other, branch_chip, far_projected], (0, down_core_projected, width, 0), 0,
        tokens_all, none, width,
    )
    slot(two, "q", w_qkv_low[0])
    slot(one, "k", w_qkv_low[1])
    order.arrived(pre_chip)
    slot(two, "v", w_qkv_low[2])
    inner = products_of(
        (quarter,) * 4, [first_low, ffn_core, far_chip, far_cross], (0, width, 0, 0), 0,
        [pres[0], pre_core, pre_chip, pre_diagonal], none, units,
    )
    slot(one, "in0", inner[0])
    slot(two, "in1", inner[1])
    (rows_give,) = order.after(rows_give)
    rows_got = swap(rows_give, "chip")
    slot(one, "in2", inner[2])
    last = order.run(
        lambda a, b: call(choose_kernel, shape(*a.shape), [SMEM, VMEM, VMEM], (info, a, b)), *final["last"]
    )
    last_got = swap(last, "chip")
    slot(two, "in3", inner[3])
    slot(one, "out", w_out_low)
    slot(two)
    activations, input_grads = order.run(
        lambda a, b: call(
            stack_kernel, [shape(2, seq // PARTS, width), shape(2, seq // PARTS, width, dtype=F32)],
            [SMEM, VMEM, VMEM], (info, a, b),
        ),
        rows_keep, rows_got,
    )
    slot(one)
    last = order.run(lambda a, b: call(add_kernel, shape(*a.shape), [VMEM] * 2, (a, b)), last, last_got)
    last_other = swap(last, "core")
    if line:
        order.arrived(two["end"])
    slot(two)
    grad_mask, *vectors, grad_b_in, grad_b_qv = order.run(
        lambda *a: call(
            last_out_kernel,
            [shape(seq, seq, dtype=F32)] + [shape(1, width, dtype=F32)] * 6
            + [shape(1, units, dtype=F32), shape(2, head, dtype=F32)],
            [SMEM] + [VMEM] * 4, (info,) + a,
        ),
        last, last_other, mask_logits[0], mask_noise[0],
    )
    if line:
        order.arrived(one["end"])
    slot(one)
    slot(two)
    slot(one)
    grad_w_qkv = matrix("q", "k", "v").reshape(3, head, width)
    grad_w_in = matrix("in0", "in1", "in2", "in3")
    grad_w_back = matrix("back0", "back1", "back2", "back3")
    grad_w_out = matrix("out")
    results = (
        activations, input_grads, jnp.swapaxes(grad_w_qkv, 1, 2), grad_b_qv, grad_w_out,
        vectors[0][0], vectors[1][0], vectors[2][0],
        grad_w_in, grad_b_in[0], grad_w_back,
        vectors[3][0], vectors[4][0], vectors[5][0],
        grad_mask,
    )
    return tuple(item[None] for item in results)


def solution(mesh):
    pipe, dp, tensor = (mesh.shape[name] for name in ("pipe", "dp", "tensor"))
    split = Mesh(mesh.devices.reshape(pipe, dp, tensor // 2, 2), ("pipe", "dp", "chip", "core"))
    placed = (
        P("dp", None, None),
        P("dp", None, None),
        P("dp", None),
        P("pipe", None, None, TENSOR),
        P("pipe", None, TENSOR),
        P("pipe", TENSOR, None),
        P("pipe", None),
        P("pipe", None),
        P("pipe", None),
        P("pipe", None, TENSOR),
        P("pipe", TENSOR),
        P("pipe", TENSOR, None),
        P("pipe", None),
        P("pipe", None),
        P("pipe", None),
        P("pipe", None, None),
        P("pipe", None, None),
    )
    return jax.shard_map(
        shards,
        mesh=split,
        in_specs=placed,
        out_specs=(
            P("pipe", "dp", TENSOR, None),
            P("pipe", "dp", TENSOR, None),
            P("pipe", None, None, TENSOR),
            P("pipe", None, TENSOR),
            P("pipe", TENSOR, None),
            P("pipe", None),
            P("pipe", None),
            P("pipe", None),
            P("pipe", None, TENSOR),
            P("pipe", TENSOR),
            P("pipe", TENSOR, None),
            P("pipe", None),
            P("pipe", None),
            P("pipe", None),
            P("pipe", None, None),
        ),
        check_vma=False,
    )
```

```python
import functools
import math

import jax
import jax.numpy as jnp
from jax import lax
from jax.experimental import pallas as pl
from jax.experimental.pallas import tpu as pltpu
from jax.sharding import Mesh
from jax.sharding import PartitionSpec as P

HEAD_DIM = 64
EPSILON = 1e-12
MASKED = -1e30
BF = jnp.bfloat16
F32 = jnp.float32
NT = ((1,), (1,))
TN = ((0,), (0,))
NN = ((1,), (0,))
PARTS = 4
PAD = 16
TENSOR = ("chip", "core")
LIMIT = 8 << 20


def dot(left, right, dims=NN):
    return lax.dot_general(left, right, (dims, ((), ())), preferred_element_type=F32)


def swap(block, axis):
    return lax.ppermute(block, axis, [(i, i ^ 1) for i in range(lax.axis_size(axis))])


SMEM = pl.BlockSpec(memory_space=pltpu.SMEM)
VMEM = pl.BlockSpec(memory_space=pltpu.VMEM)
HBM = pl.BlockSpec(memory_space=pltpu.HBM)


def shape(*dims, dtype=BF):
    return jax.ShapeDtypeStruct(dims, dtype)


def call(kernel, out, ins, args, scratch=(), limit=LIMIT):
    return pl.pallas_call(
        kernel,
        out_shape=out,
        in_specs=ins,
        out_specs=jax.tree.map(lambda _: VMEM, out),
        scratch_shapes=list(scratch),
        compiler_params=pltpu.CompilerParams(vmem_limit_bytes=limit),
        cost_estimate=pl.CostEstimate(flops=0, bytes_accessed=0, transcendentals=0),
    )(*args)


def longest_start(info, lengths, docs):
    chip = info[1]
    sizes = [lengths[chip, i] for i in range(docs)]
    bounds, start, total = [], jnp.int32(0), jnp.int32(0)
    longest = sizes[0]
    for size in sizes[1:]:
        longest = jnp.maximum(longest, size)
    for size in sizes:
        start = jnp.where(size == longest, total, start)
        total = total + size
        bounds.append(total)
    return start, bounds


def prepare_kernel(docs, info, lengths, inputs, grads, logits, noise, tokens_out, top_out, bias_out):
    seq = logits.shape[0]
    half = seq // 2
    start, bounds = longest_start(info, lengths, docs)
    begin = lax.rem(start + half * info[0], seq)
    shift = lax.rem(seq - begin, seq)
    tokens_out[...] = pltpu.roll(inputs[info[1]].astype(F32), shift, 0)[:half].astype(BF)
    top_out[...] = pltpu.roll(grads[info[1]].astype(F32), shift, 0)[:half].astype(BF)
    table = logits[...] + noise[...]
    table = pltpu.roll(table, shift, 0)[:half]
    table = pltpu.roll(table, shift, 1)[:, :half]
    term = jnp.minimum(table, 0.0) - jnp.log1p(jnp.exp(-jnp.abs(table)))

    def owners(axis):
        place = begin + lax.broadcasted_iota(jnp.int32, (half, half), axis)
        place = jnp.where(place >= seq, place - seq, place)
        owner = jnp.zeros((half, half), jnp.int32)
        for bound in bounds:
            owner = owner + jnp.where(place >= bound, 1, 0)
        return owner

    bias_out[...] = jnp.where(owners(0) == owners(1), term, MASKED).T


def split_kernel(info, qkv, w_out, w_in, b_in, b_qv, pack, half_pack, half_in, qkv_scr, out_scr, in_scr, b_in_scr, b_qv_scr, sems):
    size = w_in.shape[0] // 2
    pairs = (
        (qkv, qkv_scr), (w_out, out_scr), (b_in, b_in_scr), (b_qv, b_qv_scr),
        (w_in.at[pl.ds(pl.multiple_of(info[2] * size, size), size)], in_scr),
    )
    copies = [pltpu.make_async_copy(src, dst, sems.at[i]) for i, (src, dst) in enumerate(pairs)]
    for copy in copies:
        copy.start()
    for copy in copies:
        copy.wait()
    head = out_scr.shape[0]
    step = 2 * head + PAD
    pack[: 2 * head] = qkv_scr[: 2 * head]
    pack[2 * head : step] = jnp.zeros((PAD, pack.shape[1]), BF)
    pack[2 * head : 2 * head + 1, : b_in.shape[1]] = b_in_scr[...]
    pack[step : step + head] = qkv_scr[2 * head :]
    pack[step + head : step + 2 * head] = out_scr[...]
    pack[step + 2 * head :] = jnp.zeros((PAD, pack.shape[1]), BF)
    pack[step + 2 * head : step + 2 * head + 1, :head] = b_qv_scr[0:1]
    pack[step + 2 * head : step + 2 * head + 1, head : 2 * head] = b_qv_scr[1:2]
    half_pack[...] = pack[pl.ds(pl.multiple_of(info[2] * step, PAD), step)]
    half_in[:size] = in_scr[...]
    half_in[size:] = jnp.zeros((half_in.shape[0] - size, half_in.shape[1]), BF)


def norm(values):
    average = jnp.mean(values, axis=-1, keepdims=True)
    centred = values - average
    variance = jnp.mean(centred * centred, axis=-1, keepdims=True)
    scale = lax.rsqrt(variance + EPSILON)
    return centred * scale, scale


def norm_back(grad, unit, scale, gain):
    direct = grad * gain
    return scale * (
        direct
        - jnp.mean(direct, axis=-1, keepdims=True)
        - unit * jnp.mean(direct * unit, axis=-1, keepdims=True)
    )


def assemble(info, pieces, w4, b_qv, b_in):
    head = w4.shape[1] // PARTS
    step = 2 * head + PAD
    even = info[2] == 0
    for part in range(PARTS):
        here = slice(part * head, (part + 1) * head)
        for which in range(2):
            if part < 2:
                block = pieces[part][which * step : (which + 1) * step]
            else:
                got, also = pieces[2 * part - 2], pieces[2 * part - 1]
                block = jnp.where(even, got[...], also[...]) if which == 0 else jnp.where(even, also[...], got[...])
            w4[2 * which, here] = block[:head]
            w4[2 * which + 1, here] = block[head : 2 * head]
            if which == 0:
                b_in[part : part + 1] = block[2 * head : 2 * head + 1, : b_in.shape[1]].astype(F32)
            else:
                row = block[2 * head : 2 * head + 1].astype(F32)
                b_qv[0:1, here] = row[:, :head]
                b_qv[1:2, here] = row[:, head : 2 * head]


class Weights:
    def __init__(self, refs):
        self.w4, self.b_qv, self.b_in, self.in_near, self.in_far, self.backs = (
            refs[0], refs[1], refs[2], refs[3:5], refs[5], refs[6:10]
        )
        self.units = self.in_far.shape[2]

    def w_in(self, part):
        return self.in_near[part][...] if part < 2 else self.in_far[part - 2]

    def w_back(self, part):
        return self.backs[part][...]


WEIGHTS = 10


def attention_forward(tokens, bias_ref, w4, b_qv, out_parts, scratch):
    width = tokens.shape[1]
    q_scr, k_scr, vt_scr, at_scr = scratch
    queries = (dot(tokens, w4[0], NT) + b_qv[0:1]).astype(BF)
    keys = dot(tokens, w4[1], NT).astype(BF)
    values = (dot(tokens, w4[2], NT) + b_qv[1:2]).astype(BF)
    values_t = values.T
    if out_parts is not None:
        q_out, k_out, v_out, kt_out, p_out = out_parts
        q_out[...], k_out[...], v_out[...] = queries, keys, values
        kt_out[...] = keys.T
    q_scr[...] = queries * jnp.asarray(1.0 / math.sqrt(HEAD_DIM), BF)
    k_scr[...] = keys
    vt_scr[...] = values_t
    pair = 2 * HEAD_DIM
    lane = lax.broadcasted_iota(jnp.int32, (tokens.shape[0], pair), 1)

    def heads(j):
        here = pl.ds(j * pair, pair)
        q_pair, k_pair = q_scr[:, here], k_scr[:, here]
        for s in range(2):
            mine = (lane >= HEAD_DIM) if s else (lane < HEAD_DIM)
            scores = dot(jnp.where(mine, k_pair, jnp.zeros_like(k_pair)), q_pair, NT) + bias_ref[...]
            exponent = jnp.exp(scores - jnp.max(scores, axis=0, keepdims=True))
            chance = (exponent * (1.0 / jnp.sum(exponent, axis=0, keepdims=True))).astype(BF)
            if out_parts is not None:
                p_out[2 * j + s] = chance
            rows = pl.ds(j * pair + s * HEAD_DIM, HEAD_DIM)
            at_scr[rows, :] = dot(vt_scr[rows, :], chance).astype(BF)

    for j in range(width // pair):
        heads(j)
    return at_scr[...].T


def gelu(values):
    cdf = 0.5 * (1.0 + lax.erf(values * math.sqrt(0.5)))
    return values * cdf, cdf


def attention_kernel(info, tokens, bias, b_out, gain, offset, *rest):
    pieces, (first_out, w4, b_qv, b_in, *scratch) = rest[:6], rest[6:]
    assemble(info, pieces, w4, b_qv, b_in)
    attended = attention_forward(tokens[...], bias, w4, b_qv, None, scratch)
    unit, _ = norm(tokens[...].astype(F32) + dot(attended, w4[3]) + b_out[...])
    first_out[...] = unit * gain[...] + offset[...]


def ffn_near_kernel(first, b_back, b_in, *rest):
    w_ins, w_backs, out = rest[:2], rest[2:4], rest[4]
    first_low = first[...].astype(BF)
    total = first[...] + b_back[...]
    for part in range(2):
        hidden, _ = gelu(dot(first_low, w_ins[part][...]) + b_in[part : part + 1])
        total = total + dot(hidden.astype(BF), w_backs[part][...])
    out[...] = total


def ffn_far_kernel(info, first, b_in, far_got, far_also, cross, hidden_out, in_out):
    even = info[2] == 0
    units = in_out.shape[2]
    half = in_out.shape[1] // 2
    first_low = first[...].astype(BF)
    size = far_got.shape[0]
    pairs = ((far_got[:half], far_also[:half]), (cross[size : size + half], cross[:half]))
    for part, (got, also) in enumerate(pairs):
        in_out[part, :half] = jnp.where(even, got, also)
        in_out[part, half:] = jnp.where(even, also, got)
        hidden, _ = gelu(dot(first_low, in_out[part]) + b_in[part + 2 : part + 3])
        hidden_out[:, part * units : (part + 1) * units] = hidden.astype(BF)


def ffn_end_kernel(total, hidden, gain, offset, far, cross, out):
    units = far.shape[0]
    result = total[...] + dot(hidden[:, :units], far[...]) + dot(hidden[:, units:], cross[...])
    unit, _ = norm(result)
    out[...] = (unit * gain[...] + offset[...]).astype(BF)


def choose_tokens_kernel(info, first_tokens, passed, out):
    out[...] = jnp.where(info[3] == 0, first_tokens[...], passed[...])


def layer_kernel(tokens_ref, bias, b_out, gain_one, offset_one, b_back, gain_two, offset_two, *rest):
    weights, rest = Weights(rest[:WEIGHTS]), rest[WEIGHTS:]
    second_out, first_out, att_out, *rest = rest
    keep_outs, rest = rest[:PARTS], rest[PARTS:]
    (q_out, k_out, v_out, kt_out, p_out, unit1_out, scale1_out, slope_out, unit2_out, scale2_out, *scratch) = rest
    tokens = tokens_ref[...]
    width = tokens.shape[1]
    attended = attention_forward(
        tokens, bias, weights.w4, weights.b_qv, (q_out, k_out, v_out, kt_out, p_out), scratch
    )
    units, head = weights.units, width // PARTS
    for part in range(PARTS):
        out, base = (keep_outs[part], units) if part < 2 else (att_out, (part - 2) * head)
        out[:, base : base + head] = attended[:, part * head : (part + 1) * head]
    unit, scale = norm(tokens.astype(F32) + dot(attended, weights.w4[3]) + b_out[...])
    unit1_out[...] = unit
    scale1_out[...] = jnp.broadcast_to(scale, scale1_out.shape)
    first = unit * gain_one[...] + offset_one[...]
    first_low = first.astype(BF)
    first_out[...] = first_low
    total = first + b_back[...]
    for part in range(PARTS):
        pre = dot(first_low, weights.w_in(part)) + weights.b_in[part : part + 1]
        value, cdf = gelu(pre)
        hidden = value.astype(BF)
        keep_outs[part][:, :units] = hidden
        density = jnp.exp(-0.5 * pre * pre) * (1.0 / math.sqrt(2.0 * math.pi))
        slope_out[:, part * units : (part + 1) * units] = (cdf + pre * density).astype(BF)
        total = total + dot(hidden, weights.w_back(part))
    unit, scale = norm(total)
    unit2_out[...] = unit
    scale2_out[...] = jnp.broadcast_to(scale, scale2_out.shape)
    second_out[...] = (unit * gain_two[...] + offset_two[...]).astype(BF)


def rows_sum(values):
    return jnp.sum(values, axis=0, keepdims=True)


def ffn_backward(sum_grad, slope, weights, pre_outs):
    units = weights.units
    ffn_low = sum_grad.astype(BF)
    first_grad = sum_grad
    for part in range(PARTS):
        pre = dot(ffn_low, weights.w_back(part), NT) * slope[:, part * units : (part + 1) * units].astype(F32)
        pre = pre.astype(BF)
        if pre_outs is not None:
            pre_outs[part][...] = pre
        first_grad = first_grad + dot(pre, weights.w_in(part), NT)
    return first_grad


def attention_backward(first_grad, unit, scale, gain, refs, w_scr, scratch, outs):
    q_ref, k_ref, v_ref, kt_ref, p_ref = refs
    width = first_grad.shape[1]
    branch = norm_back(first_grad, unit, scale, gain)
    branch_low = branch.astype(BF)
    att_grad = dot(branch_low, w_scr[3], NT).astype(BF)
    pair = 2 * HEAD_DIM
    rows = first_grad.shape[0]
    lane = lax.broadcasted_iota(jnp.int32, (rows, pair), 1)
    root = 1.0 / math.sqrt(HEAD_DIM)
    dqt_scr, dk_scr, dv_scr, o_scr, term_scr = scratch
    o_scr[...] = att_grad
    term_scr[...] = jnp.zeros((rows, rows), F32)

    def heads(j, carry):
        here = pl.ds(pl.multiple_of(j * pair, pair), pair)
        q_pair, v_pair, o_pair = q_ref[:, here], v_ref[:, here], o_scr[:, here]
        dk, dv = [], []
        for s in range(2):
            mine = (lane >= HEAD_DIM) if s else (lane < HEAD_DIM)
            chance_low = p_ref[2 * j + s]
            chance = chance_low.astype(F32)
            chance_grad = dot(jnp.where(mine, v_pair, jnp.zeros_like(v_pair)), o_pair, NT)
            inner = jnp.sum(chance * chance_grad, axis=0, keepdims=True)
            score = chance * (chance_grad - inner)
            term_scr[...] += score
            low = score.astype(BF)
            dv.append(dot(chance_low, o_pair))
            dk.append(dot(low, q_pair))
            part = pl.ds(pl.multiple_of(j * pair + s * HEAD_DIM, HEAD_DIM), HEAD_DIM)
            dqt_scr[part, :] = dot(kt_ref[part, :], low) * root
        dk_scr[:, here] = (jnp.where(lane < HEAD_DIM, dk[0], dk[1]) * root).astype(BF)
        dv_scr[:, here] = jnp.where(lane < HEAD_DIM, dv[0], dv[1]).astype(BF)
        return carry

    lax.fori_loop(0, width // pair, heads, 0)
    dq = dqt_scr[...].T.astype(BF)
    dk, dv = dk_scr[...], dv_scr[...]
    term = term_scr[...]
    in_grad = branch + dot(dq, w_scr[0]) + dot(dk, w_scr[1]) + dot(dv, w_scr[2])
    if outs is not None:
        chip_out, diagonal_out, core_out, projected_outs = outs
        chip_out[:, :width] = branch_low
        core_out[:rows, :width] = branch_low
        core_out[:rows, width : 2 * width] = in_grad.astype(BF)
        core_out[:rows, 2 * width : 2 * width + rows] = term.astype(BF)
        head = width // PARTS
        end = 2 * width + rows + 3 * head
        core_out[:rows, end:] = jnp.zeros((rows, core_out.shape[1] - end), BF)
        for part in range(PARTS):
            out, base = (core_out, 2 * width + rows) if part == 1 else (projected_outs[0], 0)
            out, base = ((chip_out, width), (diagonal_out, 0))[part - 2] if part > 1 else (out, base)
            for i, grad in enumerate((dq, dk, dv)):
                out[:rows, base + i * head : base + (i + 1) * head] = grad[:, part * head : (part + 1) * head]
    return branch, in_grad, dq, dv


def down_kernel(top, unit1, scale1, gain_one, unit2, scale2, gain_two, slope, q_ref, k_ref, v_ref, kt_ref, p_ref, *rest):
    weights, (grad_out, *scratch) = Weights(rest[:WEIGHTS]), rest[WEIGHTS:]
    sum_grad = norm_back(top[...].astype(F32), unit2[...], scale2[:, :1], gain_two[...])
    first_grad = ffn_backward(sum_grad, slope, weights, None)
    _, in_grad, _, _ = attention_backward(
        first_grad, unit1[...], scale1[:, :1], gain_one[...], (q_ref, k_ref, v_ref, kt_ref, p_ref),
        weights.w4, scratch, None,
    )
    grad_out[...] = in_grad.astype(BF)


def down_norm_kernel(info, own_top, passed, unit2, scale2, gain_two, first, ffn_out, core_out, sum_grad_out, sums_out):
    top = jnp.where(info[3] == 0, passed[...], own_top[...]).astype(F32)
    unit = unit2[...]
    sum_grad = norm_back(top, unit, scale2[:, :1], gain_two[...])
    sum_grad_out[...] = sum_grad
    width = first.shape[1]
    ffn_out[...] = sum_grad.astype(BF)
    core_out[:, :width] = sum_grad.astype(BF)
    core_out[:, width:] = first[...]
    sums_out[...] = jnp.zeros_like(sums_out)
    sums_out[3:4] = rows_sum(sum_grad)
    sums_out[4:5] = rows_sum(top * unit)
    sums_out[5:6] = rows_sum(top)


def down_ffn_kernel(sum_grad, slope, *rest):
    weights, (*pre_outs, first_grad_out) = Weights(rest[:WEIGHTS]), rest[WEIGHTS:]
    first_grad_out[...] = ffn_backward(sum_grad[...], slope, weights, pre_outs)


def down_attention_kernel(info, first_grad, sums, unit1, scale1, gain_one, q_ref, k_ref, v_ref, kt_ref, p_ref, *rest):
    pres, attended, w4, rest = rest[:PARTS], rest[PARTS], rest[PARTS + 1], rest[PARTS + 2 :]
    chip_out, diagonal_out, core_out, zero, sums_scr, *scratch = rest
    unit = unit1[...]
    grad = first_grad[...]
    rows, width = grad.shape
    branch, in_grad, dq, dv = attention_backward(
        grad, unit, scale1[:, :1], gain_one[...], (q_ref, k_ref, v_ref, kt_ref, p_ref),
        w4, scratch, (chip_out, diagonal_out, core_out, (zero,)),
    )
    head = width // PARTS
    chip_out[:, width + 3 * head :] = attended[:, :head]
    diagonal_out[:, 3 * head :] = attended[:, head:]
    sums_scr[...] = sums[...]
    sums_scr[0:1] = rows_sum(branch)
    sums_scr[1:2] = rows_sum(grad * unit)
    sums_scr[2:3] = rows_sum(grad)
    head = width // PARTS
    place = 2 * info[1] + info[0]
    dq_sum, dv_sum = rows_sum(dq.astype(F32)), rows_sum(dv.astype(F32))
    for part in range(PARTS):
        units = pres[0].shape[1]
        pre = pres[part][...]
        sums_scr[pl.ds(6 + jnp.bitwise_xor(place, part), 1), :units] = rows_sum(pre.astype(F32))
        here = slice(part * head, (part + 1) * head)
        row = jnp.concatenate(
            [dq_sum[:, here], dv_sum[:, here], jnp.zeros((1, width - 2 * head), F32)], axis=1
        )
        sums_scr[pl.ds(10 + jnp.bitwise_xor(place, part), 1)] = row
    core_out[rows:, :width] = sums_scr[...].astype(BF)
    core_out[rows:, width:] = jnp.zeros((PAD, core_out.shape[1] - width), BF)


def products(lefts, rights):
    total = None
    for left, right in zip(lefts, rights):
        value = dot(left, right, TN)
        total = value if total is None else total + value
    return total.astype(BF)


def products_kernel(rows, left_starts, left_first, right_starts, right_size, *refs):
    lefts, rights, outs = refs[:PARTS], refs[PARTS : 2 * PARTS], refs[2 * PARTS :]
    done = left_first
    for out in outs:
        size = out.shape[0]
        out[...] = products(
            [ref[:rows, start + done : start + done + size] for ref, start in zip(lefts, left_starts)],
            [ref[:rows, start : start + right_size] for ref, start in zip(rights, right_starts)],
        )
        done += size


def add_kernel(left, right, out):
    out[...] = (left[...].astype(F32) + right[...].astype(F32)).astype(BF)


def whole_kernel(info, *refs):
    *sources, out = refs
    row = 0
    for kept, got in zip(sources[::2], sources[1::2]):
        size = kept.shape[0]
        out[row : row + size] = jnp.where(info[4] == 1, kept[...], got[...]).astype(F32)
        row += size


def slot_kernel(with_half, with_whole, with_new, info, *refs):
    refs = list(refs)
    ins = refs[: 2 * with_half + 2 * with_whole + (with_new and with_whole)]
    outs = refs[len(ins) :]

    def add():
        left, right = ins.pop(0), ins.pop(0)
        return (left[...].astype(F32) + right[...].astype(F32)).astype(BF)

    if with_half:
        outs.pop(0)[...] = add()
    if with_whole:
        whole = add()
        outs.pop(0)[...] = whole
        if with_new:
            outs.pop(0)[...] = jnp.where(info[4] == 1, whole, ins.pop(0)[...])


def split_rows_kernel(ref, upper, lower):
    rows, width = upper.shape
    upper[...] = ref[:rows, :width]
    lower[...] = ref[rows:, :width]


def w_out_products_kernel(starts, own_keep, core_keep, chip_keep, far_keep, own, core, chip, upper, lower, out):
    head, width = out.shape
    rows = own.shape[0]
    keeps = (own_keep, core_keep, chip_keep, far_keep)
    out[...] = products(
        [ref[:rows, start : start + head] for ref, start in zip(keeps, starts)],
        [own[:, :width], core[:rows, :width], chip[:, :width], jnp.concatenate([upper[...], lower[...]])],
    )


def rest_out_kernel(info, *refs):
    *sources, w_out, w_qkv = refs
    outs = (w_out, w_qkv.at[0], w_qkv.at[1], w_qkv.at[2])
    for kept, got, out in zip(sources[::2], sources[1::2], outs):
        out[...] = jnp.where(info[4] == 1, kept[...], got[...]).astype(F32)


def choose_kernel(info, kept, got, out):
    out[...] = jnp.where(info[4] == 1, kept[...], got[...])


def stack_kernel(info, keep, got, activations, input_grads):
    width = activations.shape[2]
    for i, source in ((info[1], keep), (1 - info[1], got)):
        activations[i] = source[:, :width]
        input_grads[i] = source[:, width:].astype(F32)


def last_kernel(docs, info, lengths, own_core, other_core, out, scr):
    seq = scr.shape[0]
    half = seq // 2
    width = out.shape[1]
    start, _ = longest_start(info, lengths, docs)
    here = slice(2 * width, 2 * width + half)
    mine, theirs = own_core[:half, here].astype(F32).T, other_core[:half, here].astype(F32).T
    zero = jnp.zeros_like(mine)
    low = info[0] == 0
    scr[:half, :half] = jnp.where(low, mine, theirs)
    scr[half:, half:] = jnp.where(low, theirs, mine)
    scr[:half, half:] = zero
    scr[half:, :half] = zero
    full = pltpu.roll(scr[...], lax.rem(start + half * (1 - info[0]) + half, seq), 0)[:half]
    full = pltpu.roll(full, start, 1).astype(BF)
    rows = packed_rows(half)
    out[:rows] = jnp.zeros((rows, out.shape[1]), BF)
    out[rows:] = (own_core[half:, :width].astype(F32) + other_core[half:, :width].astype(F32)).astype(BF)
    for row, column, source_row, source_column, count in packing(half):
        out[row : row + count, column : column + half] = full[
            source_row : source_row + count, source_column : source_column + half
        ]


def packing(half):
    rows = packed_rows(half)
    moves = []
    for piece in range(2):
        done = 0
        while done < half:
            place = piece * half + done
            count = min(half - done, rows - place % rows)
            moves.append((place % rows, place // rows * half, done, piece * half, count))
            done += count
    return moves


def packed_rows(half):
    return -(-2 * half // (3 * PAD)) * PAD


def last_out_kernel(info, own, other, logits, noise, mask_out, *outs):
    half = logits.shape[0] // 2
    low = info[0] == 0
    first = jnp.where(low, own[...], other[...])
    second = jnp.where(low, other[...], own[...])
    for base, block in ((0, first), (half, second)):
        for row, column, to_row, to_column, count in packing(half):
            here = (slice(base + to_row, base + to_row + count), slice(to_column, to_column + half))
            slope = 1.0 / (1.0 + jnp.exp(logits[here] + noise[here]))
            mask_out[here] = block[row : row + count, column : column + half].astype(F32) * slope
    sums = own[packed_rows(half) :].astype(F32)
    *vectors, b_in, b_qv = outs
    for i, out in enumerate(vectors):
        out[...] = sums[i : i + 1]
    place = 2 * info[1] + info[0]
    for part in range(PARTS):

        @pl.when(place == part)
        def _():
            b_in[...] = sums[6 + part : 7 + part, : b_in.shape[1]]
            head = b_qv.shape[1]
            b_qv[0:1] = sums[10 + part : 11 + part, :head]
            b_qv[1:2] = sums[10 + part : 11 + part, head : 2 * head]


def rows_kernel(docs, column, info, lengths, second, second_other, pack, pack_other, keep_out, give_out, scr):
    seq, width = scr.shape
    half = seq // 2
    rows = seq // PARTS
    start, _ = longest_start(info, lengths, docs)
    low = info[0] == 0
    place = 2 * info[1] + info[0]
    far = 2 * (1 - info[1]) + info[0]
    for i, (own, other, first) in enumerate(((second, second_other, 0), (pack, pack_other, column))):
        here = slice(first, first + width)
        mine, theirs = own[:half, here].astype(F32), other[:half, here].astype(F32)
        scr[:half] = jnp.where(low, mine, theirs)
        scr[half:] = jnp.where(low, theirs, mine)
        to = slice(i * width, (i + 1) * width)
        keep_out[:, to] = pltpu.roll(scr[...], lax.rem(start + seq - place * rows, seq), 0)[:rows].astype(BF)
        give_out[:, to] = pltpu.roll(scr[...], lax.rem(start + seq - far * rows, seq), 0)[:rows].astype(BF)


class Order:
    def __init__(self):
        self.last = None
        self.due = []

    def after(self, *values):
        if self.last is None:
            return values
        return lax.optimization_barrier((*values, self.last))[: len(values)]

    def arrived(self, *values):
        self.due += values

    def run(self, step, *inputs):
        return self.run_with((), step, *inputs)[0]

    def run_with(self, arrivals, step, *inputs):
        due, self.due = self.due, []
        values = self.after(*inputs, *arrivals, *due)[: len(inputs) + len(arrivals)]
        result = step(*values[: len(inputs)])
        self.last = jax.tree.leaves(result)[0]
        return result, values[len(inputs) :]


def shards(
    inputs, out_grad, doc_lengths, w_qkv, b_qv, w_out, b_out, norm1_gain, norm1_bias,
    w_in, b_in, w_back, b_back, norm2_gain, norm2_bias, mask_logits, mask_noise,
):
    count, seq, width = inputs.shape
    docs = doc_lengths.shape[1]
    core, chip = lax.axis_index("core"), lax.axis_index("chip")
    odd = lax.axis_index("dp") % 2
    part = 2 * chip + core
    half = seq // 2
    head = w_out.shape[1]
    units = w_in.shape[2]
    assert lax.axis_size("pipe") == 2 and lax.axis_size("chip") == 2 and count == 2
    assert lax.axis_size("dp") % 2 == 0 and PARTS * head == width and seq % (2 * PARTS) == 0
    place = lax.axis_index("dp")
    line = lax.axis_size("dp") == 4
    middle = ((place == 1) | (place == 2)) if line else place >= 0
    info = jnp.stack([core, chip, odd, lax.axis_index("pipe"), middle]).astype(jnp.int32)
    order = Order()
    everyone = ("chip", "core")

    def diagonal(block):
        return lax.ppermute(block, everyone, [(i, i ^ 3) for i in range(PARTS)])

    low_rows = pltpu.VMEM((half, width), BF)
    low_columns = pltpu.VMEM((width, half), BF)
    up_scratch = [low_rows, low_rows, low_columns, low_columns]
    down_scratch = [pltpu.VMEM((width, half), F32), low_rows, low_rows, low_rows, pltpu.VMEM((half, half), F32)]
    flat = shape(half, width)
    flat32 = shape(half, width, dtype=F32)

    pack, half_pack, half_in = call(
        split_kernel,
        [shape(4 * head + 2 * PAD, width), shape(2 * head + PAD, width), shape(width // 2 + 2 * PAD, units)],
        [SMEM] + [HBM] * 5,
        (info, jnp.swapaxes(w_qkv[0], 1, 2).reshape(3 * head, width), w_out[0], w_in[0], b_in, b_qv[0]),
        [pltpu.VMEM((3 * head, width), BF), pltpu.VMEM((head, width), BF), pltpu.VMEM((width // 2, units), BF),
         pltpu.VMEM((1, units), BF), pltpu.VMEM((2, head), BF), pltpu.SemaphoreType.DMA((5,))],
        56 << 20,
    )
    got_pack = swap(half_pack, "chip")
    got_in = swap(half_in, "chip")
    near = [swap(v, "core") for v in (pack, w_in[0], w_back[0])]

    def prepare(*args):
        return call(
            functools.partial(prepare_kernel, docs),
            [flat, flat, shape(half, half, dtype=F32)],
            [SMEM, SMEM, VMEM, VMEM, VMEM, VMEM],
            args,
        )

    tokens0, top0, bias = order.run(prepare, info, doc_lengths, inputs, out_grad, mask_logits[0], mask_noise[0])
    got_pack, *near = order.after(got_pack, *near)
    also_pack = swap(got_pack, "dp")
    w_back_own, got_pack = lax.optimization_barrier((w_back[0], got_pack))
    got_back = swap(w_back_own, "chip")
    cross_got_pack = swap(got_pack, "core")
    got_in, got_pack = lax.optimization_barrier((got_in, got_pack))
    also_in = swap(got_in, "dp")
    also_pack, got_in = lax.optimization_barrier((also_pack, got_in))
    p1 = (pack, near[0], got_pack, also_pack, cross_got_pack, swap(also_pack, "core"))

    def attention(tokens, *p1):
        return call(
            attention_kernel,
            [flat32, shape(4, width, width), shape(2, width, dtype=F32), shape(PARTS, units, dtype=F32)],
            [SMEM] + [VMEM] * 11,
            (info, tokens, bias, b_out, norm1_gain, norm1_bias) + p1,
            up_scratch,
        )

    first, w4, both_b_qv, full_b_in = order.run(attention, tokens0, *p1)
    total = order.run(
        lambda *a: call(ffn_near_kernel, flat32, [VMEM] * 7, a),
        first, b_back, full_b_in, w_in[0], near[1], w_back[0], near[2],
    )
    (also_in,) = order.after(also_in)
    cross_in = swap(jnp.concatenate([also_in, got_in]), "core")
    (got_back,) = order.after(got_back)
    backs = (w_back[0], near[2], got_back, swap(got_back, "core"))
    hidden_far, in_far = order.run(
        lambda *a: call(
            ffn_far_kernel, [shape(half, 2 * units), shape(2, width, units)], [SMEM] + [VMEM] * 5, (info,) + a
        ),
        first, full_b_in, got_in, also_in, cross_in,
    )
    second = order.run(
        lambda *a: call(ffn_end_kernel, flat, [VMEM] * 6, a),
        total, hidden_far, norm2_gain, norm2_bias, backs[2], backs[3],
    )
    weights = (w4, both_b_qv, full_b_in, w_in[0], near[1], in_far) + backs
    passed = lax.ppermute(second, "pipe", [(0, 1)])

    tokens = order.run(
        lambda *a: call(choose_tokens_kernel, flat, [SMEM, VMEM, VMEM], (info,) + a), tokens0, passed
    )
    tokens_chip = swap(tokens, "chip")
    tokens_core = swap(tokens, "core")

    keep_width = units + head

    def layer(tokens):
        return call(
            layer_kernel,
            [flat, flat, shape(half, 2 * head)]
            + [shape(half, keep_width)] * 2 + [shape(half, units)] * 2
            + [flat, flat, flat, shape(width, half), shape(width // HEAD_DIM, half, half),
               flat32, shape(half, 128, dtype=F32), shape(half, PARTS * units),
               flat32, shape(half, 128, dtype=F32)],
            [VMEM] * (8 + WEIGHTS),
            (tokens, bias, b_out, norm1_gain, norm1_bias, b_back, norm2_gain, norm2_bias) + weights,
            up_scratch,
        )

    second, first_low, far_attended, *kept = order.run(layer, tokens)
    keeps, kept = kept[:PARTS], kept[PARTS:]
    q, k, v, kt, chance, unit1, scale1, slope, unit2, scale2 = kept
    keeps = [keeps[0], swap(keeps[1], "core"), swap(keeps[2], "chip"), diagonal(keeps[3])]
    far_chip = swap(first_low, "chip")

    def down(top):
        return call(
            down_kernel, flat, [VMEM] * (13 + WEIGHTS),
            (top, unit1, scale1, norm1_gain, unit2, scale2, norm2_gain, slope, q, k, v, kt, chance) + weights,
            down_scratch,
        )

    down_grad, (tokens_chip, tokens_core) = order.run_with((tokens_chip, tokens_core), down, top0)
    passed = lax.ppermute(down_grad, "pipe", [(1, 0)])
    tokens_all = [tokens, tokens_core, tokens_chip, swap(tokens_chip, "core")]

    def rows_of(*args):
        return call(
            functools.partial(rows_kernel, docs, width),
            [shape(seq // PARTS, 2 * width)] * 2,
            [SMEM, SMEM] + [VMEM] * 4,
            (info, doc_lengths) + args,
            [pltpu.VMEM((seq, width), F32)],
        )

    def down_norm(top, passed):
        return call(
            down_norm_kernel, [flat, shape(half, 2 * width), flat32, shape(PAD, width, dtype=F32)], [SMEM] + [VMEM] * 6,
            (info, top, passed, unit2, scale2, norm2_gain, first_low),
        )

    (ffn_low, ffn_pack, sum_grad, sums), keeps[1:] = order.run_with(keeps[1:], down_norm, top0, passed)
    ffn_chip = swap(ffn_low, "chip")
    ffn_core = swap(ffn_pack, "core")
    (second,) = order.after(second)
    second_other = swap(second, "core")

    def down_ffn(sum_grad):
        return call(
            down_ffn_kernel,
            [shape(half, units)] * PARTS + [flat32], [VMEM] * (2 + WEIGHTS), (sum_grad, slope) + weights,
        )

    *pres, first_grad = order.run(down_ffn, sum_grad)
    pre_core = swap(pres[1], "core")

    lanes = [dict(own=None, half=None, whole=None, end=None, middle=None, names=[]) for _ in range(2)]
    final = {}

    def slot(lane, name=None, new=None):
        if not line:
            if new is not None:
                final[name] = (lax.psum(new, "dp"),) * 2
            return
        if lane["whole"] is not None:
            final[lane["names"].pop(0)] = (lane["whole"], lane["end"])
        with_half, with_whole = lane["own"] is not None, lane["half"] is not None
        ins = [lane["own"], lane["end"]] if with_half else []
        if with_whole:
            ins += [lane["half"], lane["middle"]] + ([new] if new is not None else [])
        half_sum = whole = None
        going = new
        if new is not None and not with_whole:
            (going,) = order.after(going)
        if ins:
            outs = with_half + with_whole + (with_whole and new is not None)
            results = order.run(
                lambda *a: call(
                    functools.partial(slot_kernel, with_half, with_whole, new is not None),
                    [shape(*a[0].shape)] * outs, [SMEM] + [VMEM] * len(a), (info,) + a,
                ),
                *ins,
            )
            if with_half:
                half_sum = results[0]
            if with_whole:
                whole = results[int(with_half)]
                going = results[-1] if new is not None else whole
        routes = ([(0, 1), (3, 2)] if new is not None else []) + ([(1, 0), (2, 3)] if whole is not None else [])
        lane["end"] = lax.ppermute(going, "dp", routes) if routes else None
        lane["middle"] = lax.ppermute(half_sum, "dp", [(1, 2), (2, 1)]) if half_sum is not None else None
        lane["own"], lane["half"], lane["whole"] = new, half_sum, whole
        if new is not None:
            lane["names"].append(name)

    def matrix(*names):
        sources = [v for name in names for v in final[name]]
        rows = sum(v.shape[0] for v in sources) // 2
        return order.run(
            lambda *a: call(
                whole_kernel, shape(rows, a[0].shape[1], dtype=F32), [SMEM] + [VMEM] * len(a), (info,) + a
            ),
            *sources,
        )

    def products_of(outs, lefts, left_starts, left_first, rights, right_starts, right_size):
        return order.run(
            lambda *a: call(
                functools.partial(products_kernel, half, left_starts, left_first, right_starts, right_size),
                [shape(n, right_size) for n in outs], [VMEM] * (2 * PARTS), a,
            ),
            *lefts, *rights,
        )


    def down_attention(first_grad, sums, *pres):
        return call(
            down_attention_kernel,
            [shape(half, 2 * width), shape(half, width), shape(half + PAD, -(-(2 * width + half + 3 * head) // 128) * 128)]
            + [shape(half, 3 * head)],
            [SMEM] + [VMEM] * (12 + PARTS),
            (info, first_grad, sums, unit1, scale1, norm1_gain, q, k, v, kt, chance) + pres + (far_attended, w4),
            [pltpu.VMEM((PAD, width), F32)] + down_scratch,
        )

    down_core_projected = 2 * width + half
    down_chip, down_diagonal, down_pack, projected_zero = order.run(down_attention, first_grad, sums, *pres)
    ffn_chip, far_chip = order.after(ffn_chip, far_chip)
    ffns = [ffn_low, ffn_core, ffn_chip, swap(ffn_chip, "core")]
    far_cross = swap(far_chip, "core")
    pre_chip, pre_diagonal = swap(pres[2], "chip"), diagonal(pres[3])
    none = (0, 0, 0, 0)
    quarter = units // 4
    one, two = lanes
    order.arrived(second_other, tokens_all[3])
    back = products_of((quarter,) * 2, keeps, none, 0, ffns, none, width)
    down_give, chip_give, diagonal_give = order.after(down_pack, down_chip, down_diagonal)
    down_other = swap(down_give, "core")
    branch_chip = swap(chip_give, "chip")
    far_projected = diagonal(diagonal_give)
    slot(one, "back0", back[0])
    slot(two, "back1", back[1])

    def last_chunk(*args):
        return call(
            functools.partial(last_kernel, docs),
            shape(packed_rows(half) + PAD, width),
            [SMEM, SMEM] + [VMEM] * 2,
            (info, doc_lengths) + args,
            [pltpu.VMEM((seq, seq), F32)],
        )

    back += products_of((quarter,) * 2, keeps, none, 2 * quarter, ffns, none, width)
    last = order.run(last_chunk, down_pack, down_other)
    rows_keep, rows_give = order.run(rows_of, second, second_other, down_pack, down_other)
    order.arrived(far_cross, pre_core)
    slot(one, "back2", back[2])
    slot(two, "back3", back[3])
    upper, lower = order.run(
        lambda a: call(split_rows_kernel, [shape(half // 2, width)] * 2, [VMEM], (a,)), branch_chip
    )
    upper, lower = swap(upper, "core"), swap(lower, "core")
    slot(one, "last", last)
    w_out_low = order.run(
        lambda *a: call(
            functools.partial(w_out_products_kernel, (units, units, width + 3 * head, 3 * head)),
            shape(head, width), [VMEM] * 9, a,
        ),
        *keeps[:2], branch_chip, far_projected, down_chip, down_other, branch_chip, upper, lower,
    )
    w_qkv_low = products_of(
        (head,) * 3, [projected_zero, down_other, branch_chip, far_projected], (0, down_core_projected, width, 0), 0,
        tokens_all, none, width,
    )
    slot(two, "q", w_qkv_low[0])
    slot(one, "k", w_qkv_low[1])
    order.arrived(pre_chip)
    slot(two, "v", w_qkv_low[2])
    inner = products_of(
        (quarter,) * 4, [first_low, ffn_core, far_chip, far_cross], (0, width, 0, 0), 0,
        [pres[0], pre_core, pre_chip, pre_diagonal], none, units,
    )
    slot(one, "in0", inner[0])
    slot(two, "in1", inner[1])
    (rows_give,) = order.after(rows_give)
    rows_got = swap(rows_give, "chip")
    slot(one, "in2", inner[2])
    last = order.run(
        lambda a, b: call(choose_kernel, shape(*a.shape), [SMEM, VMEM, VMEM], (info, a, b)), *final["last"]
    )
    last_got = swap(last, "chip")
    slot(two, "in3", inner[3])
    slot(one, "out", w_out_low)
    slot(two)
    activations, input_grads = order.run(
        lambda a, b: call(
            stack_kernel, [shape(2, seq // PARTS, width), shape(2, seq // PARTS, width, dtype=F32)],
            [SMEM, VMEM, VMEM], (info, a, b),
        ),
        rows_keep, rows_got,
    )
    slot(one)
    last = order.run(lambda a, b: call(add_kernel, shape(*a.shape), [VMEM] * 2, (a, b)), last, last_got)
    last_other = swap(last, "core")
    if line:
        order.arrived(two["end"])
    slot(two)
    grad_mask, *vectors, grad_b_in, grad_b_qv = order.run(
        lambda *a: call(
            last_out_kernel,
            [shape(seq, seq, dtype=F32)] + [shape(1, width, dtype=F32)] * 6
            + [shape(1, units, dtype=F32), shape(2, head, dtype=F32)],
            [SMEM] + [VMEM] * 4, (info,) + a,
        ),
        last, last_other, mask_logits[0], mask_noise[0],
    )
    if line:
        order.arrived(one["end"])
    slot(one)
    slot(two)
    slot(one)
    grad_w_qkv = matrix("q", "k", "v").reshape(3, head, width)
    grad_w_in = matrix("in0", "in1", "in2", "in3")
    grad_w_back = matrix("back0", "back1", "back2", "back3")
    grad_w_out = matrix("out")
    results = (
        activations, input_grads, jnp.swapaxes(grad_w_qkv, 1, 2), grad_b_qv, grad_w_out,
        vectors[0][0], vectors[1][0], vectors[2][0],
        grad_w_in, grad_b_in[0], grad_w_back,
        vectors[3][0], vectors[4][0], vectors[5][0],
        grad_mask,
    )
    return tuple(item[None] for item in results)


def solution(mesh):
    pipe, dp, tensor = (mesh.shape[name] for name in ("pipe", "dp", "tensor"))
    split = Mesh(mesh.devices.reshape(pipe, dp, tensor // 2, 2), ("pipe", "dp", "chip", "core"))
    placed = (
        P("dp", None, None),
        P("dp", None, None),
        P("dp", None),
        P("pipe", None, None, TENSOR),
        P("pipe", None, TENSOR),
        P("pipe", TENSOR, None),
        P("pipe", None),
        P("pipe", None),
        P("pipe", None),
        P("pipe", None, TENSOR),
        P("pipe", TENSOR),
        P("pipe", TENSOR, None),
        P("pipe", None),
        P("pipe", None),
        P("pipe", None),
        P("pipe", None, None),
        P("pipe", None, None),
    )
    return jax.shard_map(
        shards,
        mesh=split,
        in_specs=placed,
        out_specs=(
            P("pipe", "dp", TENSOR, None),
            P("pipe", "dp", TENSOR, None),
            P("pipe", None, None, TENSOR),
            P("pipe", None, TENSOR),
            P("pipe", TENSOR, None),
            P("pipe", None),
            P("pipe", None),
            P("pipe", None),
            P("pipe", None, TENSOR),
            P("pipe", TENSOR),
            P("pipe", TENSOR, None),
            P("pipe", None),
            P("pipe", None),
            P("pipe", None),
            P("pipe", None, None),
        ),
        check_vma=False,
    )
```

```python
import functools
import math

import jax
import jax.numpy as jnp
from jax import lax
from jax.experimental import pallas as pl
from jax.experimental.pallas import tpu as pltpu
from jax.sharding import Mesh
from jax.sharding import PartitionSpec as P

HEAD_DIM = 64
EPSILON = 1e-12
MASKED = -1e30
BF = jnp.bfloat16
F32 = jnp.float32
NT = ((1,), (1,))
TN = ((0,), (0,))
NN = ((1,), (0,))
PARTS = 4
PAD = 16
TENSOR = ("chip", "core")
LIMIT = 8 << 20


def dot(left, right, dims=NN):
    return lax.dot_general(left, right, (dims, ((), ())), preferred_element_type=F32)


def swap(block, axis):
    return lax.ppermute(block, axis, [(i, i ^ 1) for i in range(lax.axis_size(axis))])


SMEM = pl.BlockSpec(memory_space=pltpu.SMEM)
VMEM = pl.BlockSpec(memory_space=pltpu.VMEM)
HBM = pl.BlockSpec(memory_space=pltpu.HBM)


def shape(*dims, dtype=BF):
    return jax.ShapeDtypeStruct(dims, dtype)


def call(kernel, out, ins, args, scratch=(), limit=LIMIT):
    return pl.pallas_call(
        kernel,
        out_shape=out,
        in_specs=ins,
        out_specs=jax.tree.map(lambda _: VMEM, out),
        scratch_shapes=list(scratch),
        compiler_params=pltpu.CompilerParams(vmem_limit_bytes=limit),
        cost_estimate=pl.CostEstimate(flops=0, bytes_accessed=0, transcendentals=0),
    )(*args)


def longest_start(info, lengths, docs):
    chip = info[1]
    sizes = [lengths[chip, i] for i in range(docs)]
    bounds, start, total = [], jnp.int32(0), jnp.int32(0)
    longest = sizes[0]
    for size in sizes[1:]:
        longest = jnp.maximum(longest, size)
    for size in sizes:
        start = jnp.where(size == longest, total, start)
        total = total + size
        bounds.append(total)
    return start, bounds


def prepare_kernel(docs, info, lengths, inputs, grads, logits, noise, tokens_out, top_out, bias_out):
    seq = logits.shape[0]
    half = seq // 2
    start, bounds = longest_start(info, lengths, docs)
    begin = lax.rem(start + half * info[0], seq)
    shift = lax.rem(seq - begin, seq)
    tokens_out[...] = pltpu.roll(inputs[info[1]].astype(F32), shift, 0)[:half].astype(BF)
    top_out[...] = pltpu.roll(grads[info[1]].astype(F32), shift, 0)[:half].astype(BF)
    table = logits[...] + noise[...]
    table = pltpu.roll(table, shift, 0)[:half]
    table = pltpu.roll(table, shift, 1)[:, :half]
    term = jnp.minimum(table, 0.0) - jnp.log1p(jnp.exp(-jnp.abs(table)))

    def owners(axis):
        place = begin + lax.broadcasted_iota(jnp.int32, (half, half), axis)
        place = jnp.where(place >= seq, place - seq, place)
        owner = jnp.zeros((half, half), jnp.int32)
        for bound in bounds:
            owner = owner + jnp.where(place >= bound, 1, 0)
        return owner

    bias_out[...] = jnp.where(owners(0) == owners(1), term, MASKED).T


def split_kernel(info, qkv, w_out, w_in, b_in, b_qv, pack, half_pack, half_in, qkv_scr, out_scr, in_scr, b_in_scr, b_qv_scr, sems):
    size = w_in.shape[0] // 2
    pairs = (
        (qkv, qkv_scr), (w_out, out_scr), (b_in, b_in_scr), (b_qv, b_qv_scr),
        (w_in.at[pl.ds(pl.multiple_of(info[2] * size, size), size)], in_scr),
    )
    copies = [pltpu.make_async_copy(src, dst, sems.at[i]) for i, (src, dst) in enumerate(pairs)]
    for copy in copies:
        copy.start()
    for copy in copies:
        copy.wait()
    head = out_scr.shape[0]
    step = 2 * head + PAD
    pack[: 2 * head] = qkv_scr[: 2 * head]
    pack[2 * head : step] = jnp.zeros((PAD, pack.shape[1]), BF)
    pack[2 * head : 2 * head + 1, : b_in.shape[1]] = b_in_scr[...]
    pack[step : step + head] = qkv_scr[2 * head :]
    pack[step + head : step + 2 * head] = out_scr[...]
    pack[step + 2 * head :] = jnp.zeros((PAD, pack.shape[1]), BF)
    pack[step + 2 * head : step + 2 * head + 1, :head] = b_qv_scr[0:1]
    pack[step + 2 * head : step + 2 * head + 1, head : 2 * head] = b_qv_scr[1:2]
    half_pack[...] = pack[pl.ds(pl.multiple_of(info[2] * step, PAD), step)]
    half_in[:size] = in_scr[...]
    half_in[size:] = jnp.zeros((half_in.shape[0] - size, half_in.shape[1]), BF)


def norm(values):
    average = jnp.mean(values, axis=-1, keepdims=True)
    centred = values - average
    variance = jnp.mean(centred * centred, axis=-1, keepdims=True)
    scale = lax.rsqrt(variance + EPSILON)
    return centred * scale, scale


def norm_back(grad, unit, scale, gain):
    direct = grad * gain
    return scale * (
        direct
        - jnp.mean(direct, axis=-1, keepdims=True)
        - unit * jnp.mean(direct * unit, axis=-1, keepdims=True)
    )


def assemble(info, pieces, w4, b_qv, b_in):
    head = w4.shape[1] // PARTS
    step = 2 * head + PAD
    even = info[2] == 0
    for part in range(PARTS):
        here = slice(part * head, (part + 1) * head)
        for which in range(2):
            if part < 2:
                block = pieces[part][which * step : (which + 1) * step]
            else:
                got, also = pieces[2 * part - 2], pieces[2 * part - 1]
                block = jnp.where(even, got[...], also[...]) if which == 0 else jnp.where(even, also[...], got[...])
            w4[2 * which, here] = block[:head]
            w4[2 * which + 1, here] = block[head : 2 * head]
            if which == 0:
                b_in[part : part + 1] = block[2 * head : 2 * head + 1, : b_in.shape[1]].astype(F32)
            else:
                row = block[2 * head : 2 * head + 1].astype(F32)
                b_qv[0:1, here] = row[:, :head]
                b_qv[1:2, here] = row[:, head : 2 * head]


class Weights:
    def __init__(self, refs):
        self.w4, self.b_qv, self.b_in, self.in_near, self.in_far, self.backs = (
            refs[0], refs[1], refs[2], refs[3:5], refs[5], refs[6:10]
        )
        self.units = self.in_far.shape[2]

    def w_in(self, part):
        return self.in_near[part][...] if part < 2 else self.in_far[part - 2]

    def w_back(self, part):
        return self.backs[part][...]


WEIGHTS = 10


def attention_forward(tokens, bias_ref, w4, b_qv, out_parts, scratch):
    width = tokens.shape[1]
    q_scr, k_scr, vt_scr, at_scr = scratch
    queries = (dot(tokens, w4[0], NT) + b_qv[0:1]).astype(BF)
    keys = dot(tokens, w4[1], NT).astype(BF)
    values = (dot(tokens, w4[2], NT) + b_qv[1:2]).astype(BF)
    values_t = values.T
    if out_parts is not None:
        q_out, k_out, v_out, kt_out, p_out = out_parts
        q_out[...], k_out[...], v_out[...] = queries, keys, values
        kt_out[...] = keys.T
    q_scr[...] = queries * jnp.asarray(1.0 / math.sqrt(HEAD_DIM), BF)
    k_scr[...] = keys
    vt_scr[...] = values_t
    pair = 2 * HEAD_DIM
    lane = lax.broadcasted_iota(jnp.int32, (tokens.shape[0], pair), 1)

    def heads(j):
        here = pl.ds(j * pair, pair)
        q_pair, k_pair = q_scr[:, here], k_scr[:, here]
        for s in range(2):
            mine = (lane >= HEAD_DIM) if s else (lane < HEAD_DIM)
            scores = dot(jnp.where(mine, k_pair, jnp.zeros_like(k_pair)), q_pair, NT) + bias_ref[...]
            exponent = jnp.exp(scores - jnp.max(scores, axis=0, keepdims=True))
            chance = (exponent * (1.0 / jnp.sum(exponent, axis=0, keepdims=True))).astype(BF)
            if out_parts is not None:
                p_out[2 * j + s] = chance
            rows = pl.ds(j * pair + s * HEAD_DIM, HEAD_DIM)
            at_scr[rows, :] = dot(vt_scr[rows, :], chance).astype(BF)

    for j in range(width // pair):
        heads(j)
    return at_scr[...].T


def gelu(values):
    cdf = 0.5 * (1.0 + lax.erf(values * math.sqrt(0.5)))
    return values * cdf, cdf


def attention_kernel(info, tokens, bias, b_out, gain, offset, *rest):
    pieces, (first_out, w4, b_qv, b_in, *scratch) = rest[:6], rest[6:]
    assemble(info, pieces, w4, b_qv, b_in)
    attended = attention_forward(tokens[...], bias, w4, b_qv, None, scratch)
    unit, _ = norm(tokens[...].astype(F32) + dot(attended, w4[3]) + b_out[...])
    first_out[...] = unit * gain[...] + offset[...]


def ffn_near_kernel(first, b_back, b_in, *rest):
    w_ins, w_backs, out = rest[:2], rest[2:4], rest[4]
    first_low = first[...].astype(BF)
    total = first[...] + b_back[...]
    for part in range(2):
        hidden, _ = gelu(dot(first_low, w_ins[part][...]) + b_in[part : part + 1])
        total = total + dot(hidden.astype(BF), w_backs[part][...])
    out[...] = total


def ffn_far_kernel(info, first, b_in, far_got, far_also, cross, hidden_out, in_out):
    even = info[2] == 0
    units = in_out.shape[2]
    half = in_out.shape[1] // 2
    first_low = first[...].astype(BF)
    size = far_got.shape[0]
    pairs = ((far_got[:half], far_also[:half]), (cross[size : size + half], cross[:half]))
    for part, (got, also) in enumerate(pairs):
        in_out[part, :half] = jnp.where(even, got, also)
        in_out[part, half:] = jnp.where(even, also, got)
        hidden, _ = gelu(dot(first_low, in_out[part]) + b_in[part + 2 : part + 3])
        hidden_out[:, part * units : (part + 1) * units] = hidden.astype(BF)


def ffn_end_kernel(total, hidden, gain, offset, far, cross, out):
    units = far.shape[0]
    result = total[...] + dot(hidden[:, :units], far[...]) + dot(hidden[:, units:], cross[...])
    unit, _ = norm(result)
    out[...] = (unit * gain[...] + offset[...]).astype(BF)


def choose_tokens_kernel(info, first_tokens, passed, out):
    out[...] = jnp.where(info[3] == 0, first_tokens[...], passed[...])


def layer_kernel(tokens_ref, bias, b_out, gain_one, offset_one, b_back, gain_two, offset_two, *rest):
    weights, rest = Weights(rest[:WEIGHTS]), rest[WEIGHTS:]
    second_out, first_out, att_out, *rest = rest
    keep_outs, rest = rest[:PARTS], rest[PARTS:]
    (q_out, k_out, v_out, kt_out, p_out, unit1_out, scale1_out, slope_out, unit2_out, scale2_out, *scratch) = rest
    tokens = tokens_ref[...]
    width = tokens.shape[1]
    attended = attention_forward(
        tokens, bias, weights.w4, weights.b_qv, (q_out, k_out, v_out, kt_out, p_out), scratch
    )
    units, head = weights.units, width // PARTS
    for part in range(PARTS):
        out, base = (keep_outs[part], units) if part < 2 else (att_out, (part - 2) * head)
        out[:, base : base + head] = attended[:, part * head : (part + 1) * head]
    unit, scale = norm(tokens.astype(F32) + dot(attended, weights.w4[3]) + b_out[...])
    unit1_out[...] = unit
    scale1_out[...] = jnp.broadcast_to(scale, scale1_out.shape)
    first = unit * gain_one[...] + offset_one[...]
    first_low = first.astype(BF)
    first_out[...] = first_low
    total = first + b_back[...]
    for part in range(PARTS):
        pre = dot(first_low, weights.w_in(part)) + weights.b_in[part : part + 1]
        value, cdf = gelu(pre)
        hidden = value.astype(BF)
        keep_outs[part][:, :units] = hidden
        density = jnp.exp(-0.5 * pre * pre) * (1.0 / math.sqrt(2.0 * math.pi))
        slope_out[:, part * units : (part + 1) * units] = (cdf + pre * density).astype(BF)
        total = total + dot(hidden, weights.w_back(part))
    unit, scale = norm(total)
    unit2_out[...] = unit
    scale2_out[...] = jnp.broadcast_to(scale, scale2_out.shape)
    second_out[...] = (unit * gain_two[...] + offset_two[...]).astype(BF)


def rows_sum(values):
    return jnp.sum(values, axis=0, keepdims=True)


def ffn_backward(sum_grad, slope, weights, pre_outs):
    units = weights.units
    ffn_low = sum_grad.astype(BF)
    first_grad = sum_grad
    for part in range(PARTS):
        pre = dot(ffn_low, weights.w_back(part), NT) * slope[:, part * units : (part + 1) * units].astype(F32)
        pre = pre.astype(BF)
        if pre_outs is not None:
            pre_outs[part][...] = pre
        first_grad = first_grad + dot(pre, weights.w_in(part), NT)
    return first_grad


def attention_backward(first_grad, unit, scale, gain, refs, w_scr, scratch, outs):
    q_ref, k_ref, v_ref, kt_ref, p_ref = refs
    width = first_grad.shape[1]
    branch = norm_back(first_grad, unit, scale, gain)
    branch_low = branch.astype(BF)
    att_grad = dot(branch_low, w_scr[3], NT).astype(BF)
    pair = 2 * HEAD_DIM
    rows = first_grad.shape[0]
    lane = lax.broadcasted_iota(jnp.int32, (rows, pair), 1)
    root = 1.0 / math.sqrt(HEAD_DIM)
    dqt_scr, dk_scr, dv_scr, o_scr, term_scr = scratch
    o_scr[...] = att_grad
    term_scr[...] = jnp.zeros((rows, rows), F32)

    def heads(j, carry):
        here = pl.ds(pl.multiple_of(j * pair, pair), pair)
        q_pair, v_pair, o_pair = q_ref[:, here], v_ref[:, here], o_scr[:, here]
        dk, dv = [], []
        for s in range(2):
            mine = (lane >= HEAD_DIM) if s else (lane < HEAD_DIM)
            chance_low = p_ref[2 * j + s]
            chance = chance_low.astype(F32)
            chance_grad = dot(jnp.where(mine, v_pair, jnp.zeros_like(v_pair)), o_pair, NT)
            inner = jnp.sum(chance * chance_grad, axis=0, keepdims=True)
            score = chance * (chance_grad - inner)
            term_scr[...] += score
            low = score.astype(BF)
            dv.append(dot(chance_low, o_pair))
            dk.append(dot(low, q_pair))
            part = pl.ds(pl.multiple_of(j * pair + s * HEAD_DIM, HEAD_DIM), HEAD_DIM)
            dqt_scr[part, :] = dot(kt_ref[part, :], low) * root
        dk_scr[:, here] = (jnp.where(lane < HEAD_DIM, dk[0], dk[1]) * root).astype(BF)
        dv_scr[:, here] = jnp.where(lane < HEAD_DIM, dv[0], dv[1]).astype(BF)
        return carry

    lax.fori_loop(0, width // pair, heads, 0)
    dq = dqt_scr[...].T.astype(BF)
    dk, dv = dk_scr[...], dv_scr[...]
    term = term_scr[...]
    in_grad = branch + dot(dq, w_scr[0]) + dot(dk, w_scr[1]) + dot(dv, w_scr[2])
    if outs is not None:
        chip_out, diagonal_out, core_out, projected_outs = outs
        chip_out[:, :width] = branch_low
        core_out[:rows, :width] = branch_low
        core_out[:rows, width : 2 * width] = in_grad.astype(BF)
        core_out[:rows, 2 * width : 2 * width + rows] = term.astype(BF)
        head = width // PARTS
        end = 2 * width + rows + 3 * head
        core_out[:rows, end:] = jnp.zeros((rows, core_out.shape[1] - end), BF)
        for part in range(PARTS):
            out, base = (core_out, 2 * width + rows) if part == 1 else (projected_outs[0], 0)
            out, base = ((chip_out, width), (diagonal_out, 0))[part - 2] if part > 1 else (out, base)
            for i, grad in enumerate((dq, dk, dv)):
                out[:rows, base + i * head : base + (i + 1) * head] = grad[:, part * head : (part + 1) * head]
    return branch, in_grad, dq, dv


def down_kernel(top, unit1, scale1, gain_one, unit2, scale2, gain_two, slope, q_ref, k_ref, v_ref, kt_ref, p_ref, *rest):
    weights, (grad_out, *scratch) = Weights(rest[:WEIGHTS]), rest[WEIGHTS:]
    sum_grad = norm_back(top[...].astype(F32), unit2[...], scale2[:, :1], gain_two[...])
    first_grad = ffn_backward(sum_grad, slope, weights, None)
    _, in_grad, _, _ = attention_backward(
        first_grad, unit1[...], scale1[:, :1], gain_one[...], (q_ref, k_ref, v_ref, kt_ref, p_ref),
        weights.w4, scratch, None,
    )
    grad_out[...] = in_grad.astype(BF)


def down_norm_kernel(info, own_top, passed, unit2, scale2, gain_two, first, ffn_out, core_out, sum_grad_out, sums_out):
    top = jnp.where(info[3] == 0, passed[...], own_top[...]).astype(F32)
    unit = unit2[...]
    sum_grad = norm_back(top, unit, scale2[:, :1], gain_two[...])
    sum_grad_out[...] = sum_grad
    width = first.shape[1]
    ffn_out[...] = sum_grad.astype(BF)
    core_out[:, :width] = sum_grad.astype(BF)
    core_out[:, width:] = first[...]
    sums_out[...] = jnp.zeros_like(sums_out)
    sums_out[3:4] = rows_sum(sum_grad)
    sums_out[4:5] = rows_sum(top * unit)
    sums_out[5:6] = rows_sum(top)


def down_ffn_kernel(sum_grad, slope, *rest):
    weights, (*pre_outs, first_grad_out) = Weights(rest[:WEIGHTS]), rest[WEIGHTS:]
    first_grad_out[...] = ffn_backward(sum_grad[...], slope, weights, pre_outs)


def down_attention_kernel(info, first_grad, sums, unit1, scale1, gain_one, q_ref, k_ref, v_ref, kt_ref, p_ref, *rest):
    pres, attended, w4, rest = rest[:PARTS], rest[PARTS], rest[PARTS + 1], rest[PARTS + 2 :]
    chip_out, diagonal_out, core_out, zero, sums_scr, *scratch = rest
    unit = unit1[...]
    grad = first_grad[...]
    rows, width = grad.shape
    branch, in_grad, dq, dv = attention_backward(
        grad, unit, scale1[:, :1], gain_one[...], (q_ref, k_ref, v_ref, kt_ref, p_ref),
        w4, scratch, (chip_out, diagonal_out, core_out, (zero,)),
    )
    head = width // PARTS
    chip_out[:, width + 3 * head :] = attended[:, :head]
    diagonal_out[:, 3 * head :] = attended[:, head:]
    sums_scr[...] = sums[...]
    sums_scr[0:1] = rows_sum(branch)
    sums_scr[1:2] = rows_sum(grad * unit)
    sums_scr[2:3] = rows_sum(grad)
    head = width // PARTS
    place = 2 * info[1] + info[0]
    dq_sum, dv_sum = rows_sum(dq.astype(F32)), rows_sum(dv.astype(F32))
    for part in range(PARTS):
        units = pres[0].shape[1]
        pre = pres[part][...]
        sums_scr[pl.ds(6 + jnp.bitwise_xor(place, part), 1), :units] = rows_sum(pre.astype(F32))
        here = slice(part * head, (part + 1) * head)
        row = jnp.concatenate(
            [dq_sum[:, here], dv_sum[:, here], jnp.zeros((1, width - 2 * head), F32)], axis=1
        )
        sums_scr[pl.ds(10 + jnp.bitwise_xor(place, part), 1)] = row
    core_out[rows:, :width] = sums_scr[...].astype(BF)
    core_out[rows:, width:] = jnp.zeros((PAD, core_out.shape[1] - width), BF)


def products(lefts, rights):
    total = None
    for left, right in zip(lefts, rights):
        value = dot(left, right, TN)
        total = value if total is None else total + value
    return total.astype(BF)


def products_kernel(rows, left_starts, left_first, right_starts, right_size, *refs):
    lefts, rights, outs = refs[:PARTS], refs[PARTS : 2 * PARTS], refs[2 * PARTS :]
    done = left_first
    for out in outs:
        size = out.shape[0]
        out[...] = products(
            [ref[:rows, start + done : start + done + size] for ref, start in zip(lefts, left_starts)],
            [ref[:rows, start : start + right_size] for ref, start in zip(rights, right_starts)],
        )
        done += size


def add_kernel(left, right, out):
    out[...] = (left[...].astype(F32) + right[...].astype(F32)).astype(BF)


def whole_kernel(info, *refs):
    *sources, out = refs
    row = 0
    for kept, got in zip(sources[::2], sources[1::2]):
        size = kept.shape[0]
        out[row : row + size] = jnp.where(info[4] == 1, kept[...], got[...]).astype(F32)
        row += size


def slot_kernel(with_half, with_whole, with_new, info, *refs):
    refs = list(refs)
    ins = refs[: 2 * with_half + 2 * with_whole + (with_new and with_whole)]
    outs = refs[len(ins) :]

    def add():
        left, right = ins.pop(0), ins.pop(0)
        return (left[...].astype(F32) + right[...].astype(F32)).astype(BF)

    if with_half:
        outs.pop(0)[...] = add()
    if with_whole:
        whole = add()
        outs.pop(0)[...] = whole
        if with_new:
            outs.pop(0)[...] = jnp.where(info[4] == 1, whole, ins.pop(0)[...])


def split_rows_kernel(ref, upper, lower):
    rows, width = upper.shape
    upper[...] = ref[:rows, :width]
    lower[...] = ref[rows:, :width]


def w_out_products_kernel(starts, own_keep, core_keep, chip_keep, far_keep, own, core, chip, upper, lower, out):
    head, width = out.shape
    rows = own.shape[0]
    keeps = (own_keep, core_keep, chip_keep, far_keep)
    out[...] = products(
        [ref[:rows, start : start + head] for ref, start in zip(keeps, starts)],
        [own[:, :width], core[:rows, :width], chip[:, :width], jnp.concatenate([upper[...], lower[...]])],
    )


def rest_out_kernel(info, *refs):
    *sources, w_out, w_qkv = refs
    outs = (w_out, w_qkv.at[0], w_qkv.at[1], w_qkv.at[2])
    for kept, got, out in zip(sources[::2], sources[1::2], outs):
        out[...] = jnp.where(info[4] == 1, kept[...], got[...]).astype(F32)


def choose_kernel(info, kept, got, out):
    out[...] = jnp.where(info[4] == 1, kept[...], got[...])


def stack_kernel(info, keep, got, activations, input_grads):
    width = activations.shape[2]
    for i, source in ((info[1], keep), (1 - info[1], got)):
        activations[i] = source[:, :width]
        input_grads[i] = source[:, width:].astype(F32)


def last_kernel(docs, info, lengths, own_core, other_core, out, scr):
    seq = scr.shape[0]
    half = seq // 2
    width = out.shape[1]
    start, _ = longest_start(info, lengths, docs)
    here = slice(2 * width, 2 * width + half)
    mine, theirs = own_core[:half, here].astype(F32).T, other_core[:half, here].astype(F32).T
    zero = jnp.zeros_like(mine)
    low = info[0] == 0
    scr[:half, :half] = jnp.where(low, mine, theirs)
    scr[half:, half:] = jnp.where(low, theirs, mine)
    scr[:half, half:] = zero
    scr[half:, :half] = zero
    full = pltpu.roll(scr[...], lax.rem(start + half * (1 - info[0]) + half, seq), 0)[:half]
    full = pltpu.roll(full, start, 1).astype(BF)
    rows = packed_rows(half)
    out[:rows] = jnp.zeros((rows, out.shape[1]), BF)
    out[rows:] = (own_core[half:, :width].astype(F32) + other_core[half:, :width].astype(F32)).astype(BF)
    for row, column, source_row, source_column, count in packing(half):
        out[row : row + count, column : column + half] = full[
            source_row : source_row + count, source_column : source_column + half
        ]


def packing(half):
    rows = packed_rows(half)
    moves = []
    for piece in range(2):
        done = 0
        while done < half:
            place = piece * half + done
            count = min(half - done, rows - place % rows)
            moves.append((place % rows, place // rows * half, done, piece * half, count))
            done += count
    return moves


def packed_rows(half):
    return -(-2 * half // (3 * PAD)) * PAD


def last_out_kernel(info, own, other, logits, noise, mask_out, *outs):
    half = logits.shape[0] // 2
    low = info[0] == 0
    first = jnp.where(low, own[...], other[...])
    second = jnp.where(low, other[...], own[...])
    for base, block in ((0, first), (half, second)):
        for row, column, to_row, to_column, count in packing(half):
            here = (slice(base + to_row, base + to_row + count), slice(to_column, to_column + half))
            slope = 1.0 / (1.0 + jnp.exp(logits[here] + noise[here]))
            mask_out[here] = block[row : row + count, column : column + half].astype(F32) * slope
    sums = own[packed_rows(half) :].astype(F32)
    *vectors, b_in, b_qv = outs
    for i, out in enumerate(vectors):
        out[...] = sums[i : i + 1]
    place = 2 * info[1] + info[0]
    for part in range(PARTS):

        @pl.when(place == part)
        def _():
            b_in[...] = sums[6 + part : 7 + part, : b_in.shape[1]]
            head = b_qv.shape[1]
            b_qv[0:1] = sums[10 + part : 11 + part, :head]
            b_qv[1:2] = sums[10 + part : 11 + part, head : 2 * head]


def rows_kernel(docs, column, info, lengths, second, second_other, pack, pack_other, keep_out, give_out, scr):
    seq, width = scr.shape
    half = seq // 2
    rows = seq // PARTS
    start, _ = longest_start(info, lengths, docs)
    low = info[0] == 0
    place = 2 * info[1] + info[0]
    far = 2 * (1 - info[1]) + info[0]
    for i, (own, other, first) in enumerate(((second, second_other, 0), (pack, pack_other, column))):
        here = slice(first, first + width)
        mine, theirs = own[:half, here].astype(F32), other[:half, here].astype(F32)
        scr[:half] = jnp.where(low, mine, theirs)
        scr[half:] = jnp.where(low, theirs, mine)
        to = slice(i * width, (i + 1) * width)
        keep_out[:, to] = pltpu.roll(scr[...], lax.rem(start + seq - place * rows, seq), 0)[:rows].astype(BF)
        give_out[:, to] = pltpu.roll(scr[...], lax.rem(start + seq - far * rows, seq), 0)[:rows].astype(BF)


class Order:
    def __init__(self):
        self.last = None
        self.due = []

    def after(self, *values):
        if self.last is None:
            return values
        return lax.optimization_barrier((*values, self.last))[: len(values)]

    def arrived(self, *values):
        self.due += values

    def run(self, step, *inputs):
        return self.run_with((), step, *inputs)[0]

    def run_with(self, arrivals, step, *inputs):
        due, self.due = self.due, []
        values = self.after(*due, *inputs, *arrivals)[len(due) :]
        result = step(*values[: len(inputs)])
        self.last = jax.tree.leaves(result)[0]
        return result, values[len(inputs) :]


def shards(
    inputs, out_grad, doc_lengths, w_qkv, b_qv, w_out, b_out, norm1_gain, norm1_bias,
    w_in, b_in, w_back, b_back, norm2_gain, norm2_bias, mask_logits, mask_noise,
):
    count, seq, width = inputs.shape
    docs = doc_lengths.shape[1]
    core, chip = lax.axis_index("core"), lax.axis_index("chip")
    odd = lax.axis_index("dp") % 2
    part = 2 * chip + core
    half = seq // 2
    head = w_out.shape[1]
    units = w_in.shape[2]
    assert lax.axis_size("pipe") == 2 and lax.axis_size("chip") == 2 and count == 2
    assert lax.axis_size("dp") % 2 == 0 and PARTS * head == width and seq % (2 * PARTS) == 0
    place = lax.axis_index("dp")
    line = lax.axis_size("dp") == 4
    middle = ((place == 1) | (place == 2)) if line else place >= 0
    info = jnp.stack([core, chip, odd, lax.axis_index("pipe"), middle]).astype(jnp.int32)
    order = Order()
    everyone = ("chip", "core")

    def diagonal(block):
        return lax.ppermute(block, everyone, [(i, i ^ 3) for i in range(PARTS)])

    low_rows = pltpu.VMEM((half, width), BF)
    low_columns = pltpu.VMEM((width, half), BF)
    up_scratch = [low_rows, low_rows, low_columns, low_columns]
    down_scratch = [pltpu.VMEM((width, half), F32), low_rows, low_rows, low_rows, pltpu.VMEM((half, half), F32)]
    flat = shape(half, width)
    flat32 = shape(half, width, dtype=F32)

    pack, half_pack, half_in = call(
        split_kernel,
        [shape(4 * head + 2 * PAD, width), shape(2 * head + PAD, width), shape(width // 2 + 2 * PAD, units)],
        [SMEM] + [HBM] * 5,
        (info, jnp.swapaxes(w_qkv[0], 1, 2).reshape(3 * head, width), w_out[0], w_in[0], b_in, b_qv[0]),
        [pltpu.VMEM((3 * head, width), BF), pltpu.VMEM((head, width), BF), pltpu.VMEM((width // 2, units), BF),
         pltpu.VMEM((1, units), BF), pltpu.VMEM((2, head), BF), pltpu.SemaphoreType.DMA((5,))],
        56 << 20,
    )
    got_pack = swap(half_pack, "chip")
    got_in = swap(half_in, "chip")
    near = [swap(v, "core") for v in (pack, w_in[0], w_back[0])]

    def prepare(*args):
        return call(
            functools.partial(prepare_kernel, docs),
            [flat, flat, shape(half, half, dtype=F32)],
            [SMEM, SMEM, VMEM, VMEM, VMEM, VMEM],
            args,
        )

    tokens0, top0, bias = order.run(prepare, info, doc_lengths, inputs, out_grad, mask_logits[0], mask_noise[0])
    got_pack, *near = order.after(got_pack, *near)
    also_pack = swap(got_pack, "dp")
    w_back_own, got_pack = lax.optimization_barrier((w_back[0], got_pack))
    got_back = swap(w_back_own, "chip")
    cross_got_pack = swap(got_pack, "core")
    got_in, got_pack = lax.optimization_barrier((got_in, got_pack))
    also_in = swap(got_in, "dp")
    also_pack, got_in = lax.optimization_barrier((also_pack, got_in))
    p1 = (pack, near[0], got_pack, also_pack, cross_got_pack, swap(also_pack, "core"))

    def attention(tokens, *p1):
        return call(
            attention_kernel,
            [flat32, shape(4, width, width), shape(2, width, dtype=F32), shape(PARTS, units, dtype=F32)],
            [SMEM] + [VMEM] * 11,
            (info, tokens, bias, b_out, norm1_gain, norm1_bias) + p1,
            up_scratch,
        )

    first, w4, both_b_qv, full_b_in = order.run(attention, tokens0, *p1)
    total = order.run(
        lambda *a: call(ffn_near_kernel, flat32, [VMEM] * 7, a),
        first, b_back, full_b_in, w_in[0], near[1], w_back[0], near[2],
    )
    (also_in,) = order.after(also_in)
    cross_in = swap(jnp.concatenate([also_in, got_in]), "core")
    (got_back,) = order.after(got_back)
    backs = (w_back[0], near[2], got_back, swap(got_back, "core"))
    hidden_far, in_far = order.run(
        lambda *a: call(
            ffn_far_kernel, [shape(half, 2 * units), shape(2, width, units)], [SMEM] + [VMEM] * 5, (info,) + a
        ),
        first, full_b_in, got_in, also_in, cross_in,
    )
    second = order.run(
        lambda *a: call(ffn_end_kernel, flat, [VMEM] * 6, a),
        total, hidden_far, norm2_gain, norm2_bias, backs[2], backs[3],
    )
    weights = (w4, both_b_qv, full_b_in, w_in[0], near[1], in_far) + backs
    passed = lax.ppermute(second, "pipe", [(0, 1)])

    tokens = order.run(
        lambda *a: call(choose_tokens_kernel, flat, [SMEM, VMEM, VMEM], (info,) + a), tokens0, passed
    )
    tokens_chip = swap(tokens, "chip")
    tokens_core = swap(tokens, "core")

    keep_width = units + head

    def layer(tokens):
        return call(
            layer_kernel,
            [flat, flat, shape(half, 2 * head)]
            + [shape(half, keep_width)] * 2 + [shape(half, units)] * 2
            + [flat, flat, flat, shape(width, half), shape(width // HEAD_DIM, half, half),
               flat32, shape(half, 128, dtype=F32), shape(half, PARTS * units),
               flat32, shape(half, 128, dtype=F32)],
            [VMEM] * (8 + WEIGHTS),
            (tokens, bias, b_out, norm1_gain, norm1_bias, b_back, norm2_gain, norm2_bias) + weights,
            up_scratch,
        )

    second, first_low, far_attended, *kept = order.run(layer, tokens)
    keeps, kept = kept[:PARTS], kept[PARTS:]
    q, k, v, kt, chance, unit1, scale1, slope, unit2, scale2 = kept
    keeps = [keeps[0], swap(keeps[1], "core"), swap(keeps[2], "chip"), diagonal(keeps[3])]
    far_chip = swap(first_low, "chip")

    def down(top):
        return call(
            down_kernel, flat, [VMEM] * (13 + WEIGHTS),
            (top, unit1, scale1, norm1_gain, unit2, scale2, norm2_gain, slope, q, k, v, kt, chance) + weights,
            down_scratch,
        )

    down_grad, (tokens_chip, tokens_core) = order.run_with((tokens_chip, tokens_core), down, top0)
    passed = lax.ppermute(down_grad, "pipe", [(1, 0)])
    tokens_all = [tokens, tokens_core, tokens_chip, swap(tokens_chip, "core")]

    def rows_of(*args):
        return call(
            functools.partial(rows_kernel, docs, width),
            [shape(seq // PARTS, 2 * width)] * 2,
            [SMEM, SMEM] + [VMEM] * 4,
            (info, doc_lengths) + args,
            [pltpu.VMEM((seq, width), F32)],
        )

    def down_norm(top, passed):
        return call(
            down_norm_kernel, [flat, shape(half, 2 * width), flat32, shape(PAD, width, dtype=F32)], [SMEM] + [VMEM] * 6,
            (info, top, passed, unit2, scale2, norm2_gain, first_low),
        )

    (ffn_low, ffn_pack, sum_grad, sums), keeps[1:] = order.run_with(keeps[1:], down_norm, top0, passed)
    ffn_chip = swap(ffn_low, "chip")
    ffn_core = swap(ffn_pack, "core")
    (second,) = order.after(second)
    second_other = swap(second, "core")

    def down_ffn(sum_grad):
        return call(
            down_ffn_kernel,
            [shape(half, units)] * PARTS + [flat32], [VMEM] * (2 + WEIGHTS), (sum_grad, slope) + weights,
        )

    *pres, first_grad = order.run(down_ffn, sum_grad)
    pre_core = swap(pres[1], "core")

    lanes = [dict(own=None, half=None, whole=None, end=None, middle=None, names=[]) for _ in range(2)]
    final = {}

    def slot(lane, name=None, new=None):
        if not line:
            if new is not None:
                final[name] = (lax.psum(new, "dp"),) * 2
            return
        if lane["whole"] is not None:
            final[lane["names"].pop(0)] = (lane["whole"], lane["end"])
        with_half, with_whole = lane["own"] is not None, lane["half"] is not None
        ins = [lane["own"], lane["end"]] if with_half else []
        if with_whole:
            ins += [lane["half"], lane["middle"]] + ([new] if new is not None else [])
        half_sum = whole = None
        going = new
        if new is not None and not with_whole:
            (going,) = order.after(going)
        if ins:
            outs = with_half + with_whole + (with_whole and new is not None)
            results = order.run(
                lambda *a: call(
                    functools.partial(slot_kernel, with_half, with_whole, new is not None),
                    [shape(*a[0].shape)] * outs, [SMEM] + [VMEM] * len(a), (info,) + a,
                ),
                *ins,
            )
            if with_half:
                half_sum = results[0]
            if with_whole:
                whole = results[int(with_half)]
                going = results[-1] if new is not None else whole
        routes = ([(0, 1), (3, 2)] if new is not None else []) + ([(1, 0), (2, 3)] if whole is not None else [])
        lane["end"] = lax.ppermute(going, "dp", routes) if routes else None
        lane["middle"] = lax.ppermute(half_sum, "dp", [(1, 2), (2, 1)]) if half_sum is not None else None
        lane["own"], lane["half"], lane["whole"] = new, half_sum, whole
        if new is not None:
            lane["names"].append(name)

    def matrix(*names):
        sources = [v for name in names for v in final[name]]
        rows = sum(v.shape[0] for v in sources) // 2
        return order.run(
            lambda *a: call(
                whole_kernel, shape(rows, a[0].shape[1], dtype=F32), [SMEM] + [VMEM] * len(a), (info,) + a
            ),
            *sources,
        )

    def products_of(outs, lefts, left_starts, left_first, rights, right_starts, right_size):
        return order.run(
            lambda *a: call(
                functools.partial(products_kernel, half, left_starts, left_first, right_starts, right_size),
                [shape(n, right_size) for n in outs], [VMEM] * (2 * PARTS), a,
            ),
            *lefts, *rights,
        )


    def down_attention(first_grad, sums, *pres):
        return call(
            down_attention_kernel,
            [shape(half, 2 * width), shape(half, width), shape(half + PAD, -(-(2 * width + half + 3 * head) // 128) * 128)]
            + [shape(half, 3 * head)],
            [SMEM] + [VMEM] * (12 + PARTS),
            (info, first_grad, sums, unit1, scale1, norm1_gain, q, k, v, kt, chance) + pres + (far_attended, w4),
            [pltpu.VMEM((PAD, width), F32)] + down_scratch,
        )

    down_core_projected = 2 * width + half
    down_chip, down_diagonal, down_pack, projected_zero = order.run(down_attention, first_grad, sums, *pres)
    ffn_chip, far_chip = order.after(ffn_chip, far_chip)
    ffns = [ffn_low, ffn_core, ffn_chip, swap(ffn_chip, "core")]
    far_cross = swap(far_chip, "core")
    pre_chip, pre_diagonal = swap(pres[2], "chip"), diagonal(pres[3])
    none = (0, 0, 0, 0)
    quarter = units // 4
    one, two = lanes
    order.arrived(second_other, tokens_all[3])
    back = products_of((quarter,) * 2, keeps, none, 0, ffns, none, width)
    down_give, chip_give, diagonal_give = order.after(down_pack, down_chip, down_diagonal)
    down_other = swap(down_give, "core")
    branch_chip = swap(chip_give, "chip")
    far_projected = diagonal(diagonal_give)
    slot(one, "back0", back[0])
    slot(two, "back1", back[1])

    def last_chunk(*args):
        return call(
            functools.partial(last_kernel, docs),
            shape(packed_rows(half) + PAD, width),
            [SMEM, SMEM] + [VMEM] * 2,
            (info, doc_lengths) + args,
            [pltpu.VMEM((seq, seq), F32)],
        )

    back += products_of((quarter,) * 2, keeps, none, 2 * quarter, ffns, none, width)
    last = order.run(last_chunk, down_pack, down_other)
    rows_keep, rows_give = order.run(rows_of, second, second_other, down_pack, down_other)
    order.arrived(far_cross, pre_core)
    slot(one, "back2", back[2])
    slot(two, "back3", back[3])
    upper, lower = order.run(
        lambda a: call(split_rows_kernel, [shape(half // 2, width)] * 2, [VMEM], (a,)), branch_chip
    )
    upper, lower = swap(upper, "core"), swap(lower, "core")
    slot(one, "last", last)
    w_out_low = order.run(
        lambda *a: call(
            functools.partial(w_out_products_kernel, (units, units, width + 3 * head, 3 * head)),
            shape(head, width), [VMEM] * 9, a,
        ),
        *keeps[:2], branch_chip, far_projected, down_chip, down_other, branch_chip, upper, lower,
    )
    w_qkv_low = products_of(
        (head,) * 3, [projected_zero, down_other, branch_chip, far_projected], (0, down_core_projected, width, 0), 0,
        tokens_all, none, width,
    )
    slot(two, "q", w_qkv_low[0])
    slot(one, "k", w_qkv_low[1])
    order.arrived(pre_chip)
    slot(two, "v", w_qkv_low[2])
    inner = products_of(
        (quarter,) * 4, [first_low, ffn_core, far_chip, far_cross], (0, width, 0, 0), 0,
        [pres[0], pre_core, pre_chip, pre_diagonal], none, units,
    )
    slot(one, "in0", inner[0])
    slot(two, "in1", inner[1])
    (rows_give,) = order.after(rows_give)
    rows_got = swap(rows_give, "chip")
    slot(one, "in2", inner[2])
    last = order.run(
        lambda a, b: call(choose_kernel, shape(*a.shape), [SMEM, VMEM, VMEM], (info, a, b)), *final["last"]
    )
    last_got = swap(last, "chip")
    slot(two, "in3", inner[3])
    slot(one, "out", w_out_low)
    slot(two)
    activations, input_grads = order.run(
        lambda a, b: call(
            stack_kernel, [shape(2, seq // PARTS, width), shape(2, seq // PARTS, width, dtype=F32)],
            [SMEM, VMEM, VMEM], (info, a, b),
        ),
        rows_keep, rows_got,
    )
    slot(one)
    last = order.run(lambda a, b: call(add_kernel, shape(*a.shape), [VMEM] * 2, (a, b)), last, last_got)
    last_other = swap(last, "core")
    if line:
        order.arrived(two["end"])
    slot(two)
    grad_mask, *vectors, grad_b_in, grad_b_qv = order.run(
        lambda *a: call(
            last_out_kernel,
            [shape(seq, seq, dtype=F32)] + [shape(1, width, dtype=F32)] * 6
            + [shape(1, units, dtype=F32), shape(2, head, dtype=F32)],
            [SMEM] + [VMEM] * 4, (info,) + a,
        ),
        last, last_other, mask_logits[0], mask_noise[0],
    )
    if line:
        order.arrived(one["end"])
    slot(one)
    slot(two)
    slot(one)
    grad_w_qkv = matrix("q", "k", "v").reshape(3, head, width)
    grad_w_in = matrix("in0", "in1", "in2", "in3")
    grad_w_back = matrix("back0", "back1", "back2", "back3")
    grad_w_out = matrix("out")
    results = (
        activations, input_grads, jnp.swapaxes(grad_w_qkv, 1, 2), grad_b_qv, grad_w_out,
        vectors[0][0], vectors[1][0], vectors[2][0],
        grad_w_in, grad_b_in[0], grad_w_back,
        vectors[3][0], vectors[4][0], vectors[5][0],
        grad_mask,
    )
    return tuple(item[None] for item in results)


def solution(mesh):
    pipe, dp, tensor = (mesh.shape[name] for name in ("pipe", "dp", "tensor"))
    split = Mesh(mesh.devices.reshape(pipe, dp, tensor // 2, 2), ("pipe", "dp", "chip", "core"))
    placed = (
        P("dp", None, None),
        P("dp", None, None),
        P("dp", None),
        P("pipe", None, None, TENSOR),
        P("pipe", None, TENSOR),
        P("pipe", TENSOR, None),
        P("pipe", None),
        P("pipe", None),
        P("pipe", None),
        P("pipe", None, TENSOR),
        P("pipe", TENSOR),
        P("pipe", TENSOR, None),
        P("pipe", None),
        P("pipe", None),
        P("pipe", None),
        P("pipe", None, None),
        P("pipe", None, None),
    )
    return jax.shard_map(
        shards,
        mesh=split,
        in_specs=placed,
        out_specs=(
            P("pipe", "dp", TENSOR, None),
            P("pipe", "dp", TENSOR, None),
            P("pipe", None, None, TENSOR),
            P("pipe", None, TENSOR),
            P("pipe", TENSOR, None),
            P("pipe", None),
            P("pipe", None),
            P("pipe", None),
            P("pipe", None, TENSOR),
            P("pipe", TENSOR),
            P("pipe", TENSOR, None),
            P("pipe", None),
            P("pipe", None),
            P("pipe", None),
            P("pipe", None, None),
        ),
        check_vma=False,
    )
```

```python
import functools
import math

import jax
import jax.numpy as jnp
from jax import lax
from jax.experimental import pallas as pl
from jax.experimental.pallas import tpu as pltpu
from jax.sharding import Mesh
from jax.sharding import PartitionSpec as P

HEAD_DIM = 64
EPSILON = 1e-12
MASKED = -1e30
BF = jnp.bfloat16
F32 = jnp.float32
NT = ((1,), (1,))
TN = ((0,), (0,))
NN = ((1,), (0,))
PARTS = 4
PAD = 16
TENSOR = ("chip", "core")
LIMIT = 8 << 20


def dot(left, right, dims=NN):
    return lax.dot_general(left, right, (dims, ((), ())), preferred_element_type=F32)


def swap(block, axis):
    return lax.ppermute(block, axis, [(i, i ^ 1) for i in range(lax.axis_size(axis))])


SMEM = pl.BlockSpec(memory_space=pltpu.SMEM)
VMEM = pl.BlockSpec(memory_space=pltpu.VMEM)
HBM = pl.BlockSpec(memory_space=pltpu.HBM)


def shape(*dims, dtype=BF):
    return jax.ShapeDtypeStruct(dims, dtype)


def call(kernel, out, ins, args, scratch=(), limit=LIMIT):
    return pl.pallas_call(
        kernel,
        out_shape=out,
        in_specs=ins,
        out_specs=jax.tree.map(lambda _: VMEM, out),
        scratch_shapes=list(scratch),
        compiler_params=pltpu.CompilerParams(vmem_limit_bytes=limit),
        cost_estimate=pl.CostEstimate(flops=0, bytes_accessed=0, transcendentals=0),
    )(*args)


def longest_start(info, lengths, docs):
    chip = info[1]
    sizes = [lengths[chip, i] for i in range(docs)]
    bounds, start, total = [], jnp.int32(0), jnp.int32(0)
    longest = sizes[0]
    for size in sizes[1:]:
        longest = jnp.maximum(longest, size)
    for size in sizes:
        start = jnp.where(size == longest, total, start)
        total = total + size
        bounds.append(total)
    return start, bounds


def prepare_kernel(docs, info, lengths, inputs, grads, logits, noise, tokens_out, top_out, bias_out):
    seq = logits.shape[0]
    half = seq // 2
    start, bounds = longest_start(info, lengths, docs)
    begin = lax.rem(start + half * info[0], seq)
    shift = lax.rem(seq - begin, seq)
    tokens_out[...] = pltpu.roll(inputs[info[1]].astype(F32), shift, 0)[:half].astype(BF)
    top_out[...] = pltpu.roll(grads[info[1]].astype(F32), shift, 0)[:half].astype(BF)
    table = logits[...] + noise[...]
    table = pltpu.roll(table, shift, 0)[:half]
    table = pltpu.roll(table, shift, 1)[:, :half]
    term = jnp.minimum(table, 0.0) - jnp.log1p(jnp.exp(-jnp.abs(table)))

    def owners(axis):
        place = begin + lax.broadcasted_iota(jnp.int32, (half, half), axis)
        place = jnp.where(place >= seq, place - seq, place)
        owner = jnp.zeros((half, half), jnp.int32)
        for bound in bounds:
            owner = owner + jnp.where(place >= bound, 1, 0)
        return owner

    bias_out[...] = jnp.where(owners(0) == owners(1), term, MASKED).T


def split_kernel(info, qkv, w_out, w_in, b_in, b_qv, pack, half_pack, half_in, qkv_scr, out_scr, in_scr, b_in_scr, b_qv_scr, sems):
    size = w_in.shape[0] // 2
    pairs = (
        (qkv, qkv_scr), (w_out, out_scr), (b_in, b_in_scr), (b_qv, b_qv_scr),
        (w_in.at[pl.ds(pl.multiple_of(info[2] * size, size), size)], in_scr),
    )
    copies = [pltpu.make_async_copy(src, dst, sems.at[i]) for i, (src, dst) in enumerate(pairs)]
    for copy in copies:
        copy.start()
    for copy in copies:
        copy.wait()
    head = out_scr.shape[0]
    step = 2 * head + PAD
    pack[: 2 * head] = qkv_scr[: 2 * head]
    pack[2 * head : step] = jnp.zeros((PAD, pack.shape[1]), BF)
    pack[2 * head : 2 * head + 1, : b_in.shape[1]] = b_in_scr[...]
    pack[step : step + head] = qkv_scr[2 * head :]
    pack[step + head : step + 2 * head] = out_scr[...]
    pack[step + 2 * head :] = jnp.zeros((PAD, pack.shape[1]), BF)
    pack[step + 2 * head : step + 2 * head + 1, :head] = b_qv_scr[0:1]
    pack[step + 2 * head : step + 2 * head + 1, head : 2 * head] = b_qv_scr[1:2]
    half_pack[...] = pack[pl.ds(pl.multiple_of(info[2] * step, PAD), step)]
    half_in[:size] = in_scr[...]
    half_in[size:] = jnp.zeros((half_in.shape[0] - size, half_in.shape[1]), BF)


def norm(values):
    average = jnp.mean(values, axis=-1, keepdims=True)
    centred = values - average
    variance = jnp.mean(centred * centred, axis=-1, keepdims=True)
    scale = lax.rsqrt(variance + EPSILON)
    return centred * scale, scale


def norm_back(grad, unit, scale, gain):
    direct = grad * gain
    return scale * (
        direct
        - jnp.mean(direct, axis=-1, keepdims=True)
        - unit * jnp.mean(direct * unit, axis=-1, keepdims=True)
    )


def assemble(info, pieces, w4, b_qv, b_in):
    head = w4.shape[1] // PARTS
    step = 2 * head + PAD
    even = info[2] == 0
    for part in range(PARTS):
        here = slice(part * head, (part + 1) * head)
        for which in range(2):
            if part < 2:
                block = pieces[part][which * step : (which + 1) * step]
            else:
                got, also = pieces[2 * part - 2], pieces[2 * part - 1]
                block = jnp.where(even, got[...], also[...]) if which == 0 else jnp.where(even, also[...], got[...])
            w4[2 * which, here] = block[:head]
            w4[2 * which + 1, here] = block[head : 2 * head]
            if which == 0:
                b_in[part : part + 1] = block[2 * head : 2 * head + 1, : b_in.shape[1]].astype(F32)
            else:
                row = block[2 * head : 2 * head + 1].astype(F32)
                b_qv[0:1, here] = row[:, :head]
                b_qv[1:2, here] = row[:, head : 2 * head]


class Weights:
    def __init__(self, refs):
        self.w4, self.b_qv, self.b_in, self.in_near, self.in_far, self.backs = (
            refs[0], refs[1], refs[2], refs[3:5], refs[5], refs[6:10]
        )
        self.units = self.in_far.shape[2]

    def w_in(self, part):
        return self.in_near[part][...] if part < 2 else self.in_far[part - 2]

    def w_back(self, part):
        return self.backs[part][...]


WEIGHTS = 10


def attention_forward(tokens, bias_ref, w4, b_qv, out_parts, scratch):
    width = tokens.shape[1]
    q_scr, k_scr, vt_scr, at_scr = scratch
    queries = (dot(tokens, w4[0], NT) + b_qv[0:1]).astype(BF)
    keys = dot(tokens, w4[1], NT).astype(BF)
    values = (dot(tokens, w4[2], NT) + b_qv[1:2]).astype(BF)
    values_t = values.T
    if out_parts is not None:
        q_out, k_out, v_out, kt_out, p_out = out_parts
        q_out[...], k_out[...], v_out[...] = queries, keys, values
        kt_out[...] = keys.T
    q_scr[...] = queries * jnp.asarray(1.0 / math.sqrt(HEAD_DIM), BF)
    k_scr[...] = keys
    vt_scr[...] = values_t
    pair = 2 * HEAD_DIM
    lane = lax.broadcasted_iota(jnp.int32, (tokens.shape[0], pair), 1)

    def heads(j):
        here = pl.ds(j * pair, pair)
        q_pair, k_pair = q_scr[:, here], k_scr[:, here]
        for s in range(2):
            mine = (lane >= HEAD_DIM) if s else (lane < HEAD_DIM)
            scores = dot(jnp.where(mine, k_pair, jnp.zeros_like(k_pair)), q_pair, NT) + bias_ref[...]
            exponent = jnp.exp(scores - jnp.max(scores, axis=0, keepdims=True))
            chance = (exponent * (1.0 / jnp.sum(exponent, axis=0, keepdims=True))).astype(BF)
            if out_parts is not None:
                p_out[2 * j + s] = chance
            rows = pl.ds(j * pair + s * HEAD_DIM, HEAD_DIM)
            at_scr[rows, :] = dot(vt_scr[rows, :], chance).astype(BF)

    for j in range(width // pair):
        heads(j)
    return at_scr[...].T


def gelu(values):
    cdf = 0.5 * (1.0 + lax.erf(values * math.sqrt(0.5)))
    return values * cdf, cdf


def attention_kernel(info, tokens, bias, b_out, gain, offset, *rest):
    pieces, (first_out, w4, b_qv, b_in, *scratch) = rest[:6], rest[6:]
    assemble(info, pieces, w4, b_qv, b_in)
    attended = attention_forward(tokens[...], bias, w4, b_qv, None, scratch)
    unit, _ = norm(tokens[...].astype(F32) + dot(attended, w4[3]) + b_out[...])
    first_out[...] = unit * gain[...] + offset[...]


def ffn_near_kernel(first, b_back, b_in, *rest):
    w_ins, w_backs, out = rest[:2], rest[2:4], rest[4]
    first_low = first[...].astype(BF)
    total = first[...] + b_back[...]
    for part in range(2):
        hidden, _ = gelu(dot(first_low, w_ins[part][...]) + b_in[part : part + 1])
        total = total + dot(hidden.astype(BF), w_backs[part][...])
    out[...] = total


def ffn_far_kernel(info, first, b_in, far_got, far_also, cross, hidden_out, in_out):
    even = info[2] == 0
    units = in_out.shape[2]
    half = in_out.shape[1] // 2
    first_low = first[...].astype(BF)
    size = far_got.shape[0]
    pairs = ((far_got[:half], far_also[:half]), (cross[size : size + half], cross[:half]))
    for part, (got, also) in enumerate(pairs):
        in_out[part, :half] = jnp.where(even, got, also)
        in_out[part, half:] = jnp.where(even, also, got)
        hidden, _ = gelu(dot(first_low, in_out[part]) + b_in[part + 2 : part + 3])
        hidden_out[:, part * units : (part + 1) * units] = hidden.astype(BF)


def ffn_end_kernel(total, hidden, gain, offset, far, cross, out):
    units = far.shape[0]
    result = total[...] + dot(hidden[:, :units], far[...]) + dot(hidden[:, units:], cross[...])
    unit, _ = norm(result)
    out[...] = (unit * gain[...] + offset[...]).astype(BF)


def choose_tokens_kernel(info, first_tokens, passed, out):
    out[...] = jnp.where(info[3] == 0, first_tokens[...], passed[...])


def layer_kernel(tokens_ref, bias, b_out, gain_one, offset_one, b_back, gain_two, offset_two, *rest):
    weights, rest = Weights(rest[:WEIGHTS]), rest[WEIGHTS:]
    second_out, first_out, att_out, *rest = rest
    keep_outs, rest = rest[:PARTS], rest[PARTS:]
    (q_out, k_out, v_out, kt_out, p_out, unit1_out, scale1_out, slope_out, unit2_out, scale2_out, *scratch) = rest
    tokens = tokens_ref[...]
    width = tokens.shape[1]
    attended = attention_forward(
        tokens, bias, weights.w4, weights.b_qv, (q_out, k_out, v_out, kt_out, p_out), scratch
    )
    units, head = weights.units, width // PARTS
    for part in range(PARTS):
        out, base = (keep_outs[part], units) if part < 2 else (att_out, (part - 2) * head)
        out[:, base : base + head] = attended[:, part * head : (part + 1) * head]
    unit, scale = norm(tokens.astype(F32) + dot(attended, weights.w4[3]) + b_out[...])
    unit1_out[...] = unit
    scale1_out[...] = jnp.broadcast_to(scale, scale1_out.shape)
    first = unit * gain_one[...] + offset_one[...]
    first_low = first.astype(BF)
    first_out[...] = first_low
    total = first + b_back[...]
    for part in range(PARTS):
        pre = dot(first_low, weights.w_in(part)) + weights.b_in[part : part + 1]
        value, cdf = gelu(pre)
        hidden = value.astype(BF)
        keep_outs[part][:, :units] = hidden
        density = jnp.exp(-0.5 * pre * pre) * (1.0 / math.sqrt(2.0 * math.pi))
        slope_out[:, part * units : (part + 1) * units] = (cdf + pre * density).astype(BF)
        total = total + dot(hidden, weights.w_back(part))
    unit, scale = norm(total)
    unit2_out[...] = unit
    scale2_out[...] = jnp.broadcast_to(scale, scale2_out.shape)
    second_out[...] = (unit * gain_two[...] + offset_two[...]).astype(BF)


def rows_sum(values):
    return jnp.sum(values, axis=0, keepdims=True)


def ffn_backward(sum_grad, slope, weights, pre_outs):
    units = weights.units
    ffn_low = sum_grad.astype(BF)
    first_grad = sum_grad
    for part in range(PARTS):
        pre = dot(ffn_low, weights.w_back(part), NT) * slope[:, part * units : (part + 1) * units].astype(F32)
        pre = pre.astype(BF)
        if pre_outs is not None:
            pre_outs[part][...] = pre
        first_grad = first_grad + dot(pre, weights.w_in(part), NT)
    return first_grad


def attention_backward(first_grad, unit, scale, gain, refs, w_scr, scratch, outs):
    q_ref, k_ref, v_ref, kt_ref, p_ref = refs
    width = first_grad.shape[1]
    branch = norm_back(first_grad, unit, scale, gain)
    branch_low = branch.astype(BF)
    att_grad = dot(branch_low, w_scr[3], NT).astype(BF)
    pair = 2 * HEAD_DIM
    rows = first_grad.shape[0]
    lane = lax.broadcasted_iota(jnp.int32, (rows, pair), 1)
    root = 1.0 / math.sqrt(HEAD_DIM)
    dqt_scr, dk_scr, dv_scr, o_scr, term_scr = scratch
    o_scr[...] = att_grad
    term_scr[...] = jnp.zeros((rows, rows), F32)

    def heads(j, carry):
        here = pl.ds(pl.multiple_of(j * pair, pair), pair)
        q_pair, v_pair, o_pair = q_ref[:, here], v_ref[:, here], o_scr[:, here]
        dk, dv = [], []
        for s in range(2):
            mine = (lane >= HEAD_DIM) if s else (lane < HEAD_DIM)
            chance_low = p_ref[2 * j + s]
            chance = chance_low.astype(F32)
            chance_grad = dot(jnp.where(mine, v_pair, jnp.zeros_like(v_pair)), o_pair, NT)
            inner = jnp.sum(chance * chance_grad, axis=0, keepdims=True)
            score = chance * (chance_grad - inner)
            term_scr[...] += score
            low = score.astype(BF)
            dv.append(dot(chance_low, o_pair))
            dk.append(dot(low, q_pair))
            part = pl.ds(pl.multiple_of(j * pair + s * HEAD_DIM, HEAD_DIM), HEAD_DIM)
            dqt_scr[part, :] = dot(kt_ref[part, :], low) * root
        dk_scr[:, here] = (jnp.where(lane < HEAD_DIM, dk[0], dk[1]) * root).astype(BF)
        dv_scr[:, here] = jnp.where(lane < HEAD_DIM, dv[0], dv[1]).astype(BF)
        return carry

    lax.fori_loop(0, width // pair, heads, 0)
    dq = dqt_scr[...].T.astype(BF)
    dk, dv = dk_scr[...], dv_scr[...]
    term = term_scr[...]
    in_grad = branch + dot(dq, w_scr[0]) + dot(dk, w_scr[1]) + dot(dv, w_scr[2])
    if outs is not None:
        chip_out, diagonal_out, core_out, projected_outs = outs
        chip_out[:, :width] = branch_low
        core_out[:rows, :width] = branch_low
        core_out[:rows, width : 2 * width] = in_grad.astype(BF)
        core_out[:rows, 2 * width : 2 * width + rows] = term.astype(BF)
        head = width // PARTS
        end = 2 * width + rows + 3 * head
        core_out[:rows, end:] = jnp.zeros((rows, core_out.shape[1] - end), BF)
        for part in range(PARTS):
            out, base = (core_out, 2 * width + rows) if part == 1 else (projected_outs[0], 0)
            out, base = ((chip_out, width), (diagonal_out, 0))[part - 2] if part > 1 else (out, base)
            for i, grad in enumerate((dq, dk, dv)):
                out[:rows, base + i * head : base + (i + 1) * head] = grad[:, part * head : (part + 1) * head]
    return branch, in_grad, dq, dv


def down_kernel(top, unit1, scale1, gain_one, unit2, scale2, gain_two, slope, q_ref, k_ref, v_ref, kt_ref, p_ref, *rest):
    weights, (grad_out, *scratch) = Weights(rest[:WEIGHTS]), rest[WEIGHTS:]
    sum_grad = norm_back(top[...].astype(F32), unit2[...], scale2[:, :1], gain_two[...])
    first_grad = ffn_backward(sum_grad, slope, weights, None)
    _, in_grad, _, _ = attention_backward(
        first_grad, unit1[...], scale1[:, :1], gain_one[...], (q_ref, k_ref, v_ref, kt_ref, p_ref),
        weights.w4, scratch, None,
    )
    grad_out[...] = in_grad.astype(BF)


def down_norm_kernel(info, own_top, passed, unit2, scale2, gain_two, first, ffn_out, core_out, sum_grad_out, sums_out):
    top = jnp.where(info[3] == 0, passed[...], own_top[...]).astype(F32)
    unit = unit2[...]
    sum_grad = norm_back(top, unit, scale2[:, :1], gain_two[...])
    sum_grad_out[...] = sum_grad
    width = first.shape[1]
    ffn_out[...] = sum_grad.astype(BF)
    core_out[:, :width] = sum_grad.astype(BF)
    core_out[:, width:] = first[...]
    sums_out[...] = jnp.zeros_like(sums_out)
    sums_out[3:4] = rows_sum(sum_grad)
    sums_out[4:5] = rows_sum(top * unit)
    sums_out[5:6] = rows_sum(top)


def down_ffn_kernel(sum_grad, slope, *rest):
    weights, (*pre_outs, first_grad_out) = Weights(rest[:WEIGHTS]), rest[WEIGHTS:]
    first_grad_out[...] = ffn_backward(sum_grad[...], slope, weights, pre_outs)


def down_attention_kernel(info, first_grad, sums, unit1, scale1, gain_one, q_ref, k_ref, v_ref, kt_ref, p_ref, *rest):
    pres, attended, w4, rest = rest[:PARTS], rest[PARTS], rest[PARTS + 1], rest[PARTS + 2 :]
    chip_out, diagonal_out, core_out, zero, sums_scr, *scratch = rest
    unit = unit1[...]
    grad = first_grad[...]
    rows, width = grad.shape
    branch, in_grad, dq, dv = attention_backward(
        grad, unit, scale1[:, :1], gain_one[...], (q_ref, k_ref, v_ref, kt_ref, p_ref),
        w4, scratch, (chip_out, diagonal_out, core_out, (zero,)),
    )
    head = width // PARTS
    chip_out[:, width + 3 * head :] = attended[:, :head]
    diagonal_out[:, 3 * head :] = attended[:, head:]
    sums_scr[...] = sums[...]
    sums_scr[0:1] = rows_sum(branch)
    sums_scr[1:2] = rows_sum(grad * unit)
    sums_scr[2:3] = rows_sum(grad)
    head = width // PARTS
    place = 2 * info[1] + info[0]
    dq_sum, dv_sum = rows_sum(dq.astype(F32)), rows_sum(dv.astype(F32))
    for part in range(PARTS):
        units = pres[0].shape[1]
        pre = pres[part][...]
        sums_scr[pl.ds(6 + jnp.bitwise_xor(place, part), 1), :units] = rows_sum(pre.astype(F32))
        here = slice(part * head, (part + 1) * head)
        row = jnp.concatenate(
            [dq_sum[:, here], dv_sum[:, here], jnp.zeros((1, width - 2 * head), F32)], axis=1
        )
        sums_scr[pl.ds(10 + jnp.bitwise_xor(place, part), 1)] = row
    core_out[rows:, :width] = sums_scr[...].astype(BF)
    core_out[rows:, width:] = jnp.zeros((PAD, core_out.shape[1] - width), BF)


def products(lefts, rights):
    total = None
    for left, right in zip(lefts, rights):
        value = dot(left, right, TN)
        total = value if total is None else total + value
    return total.astype(BF)


def products_kernel(rows, left_starts, left_first, right_starts, right_size, *refs):
    lefts, rights, outs = refs[:PARTS], refs[PARTS : 2 * PARTS], refs[2 * PARTS :]
    done = left_first
    for out in outs:
        size = out.shape[0]
        out[...] = products(
            [ref[:rows, start + done : start + done + size] for ref, start in zip(lefts, left_starts)],
            [ref[:rows, start : start + right_size] for ref, start in zip(rights, right_starts)],
        )
        done += size


def add_kernel(left, right, out):
    out[...] = (left[...].astype(F32) + right[...].astype(F32)).astype(BF)


def whole_kernel(info, *refs):
    *sources, out = refs
    row = 0
    for kept, got in zip(sources[::2], sources[1::2]):
        size = kept.shape[0]
        out[row : row + size] = jnp.where(info[4] == 1, kept[...], got[...]).astype(F32)
        row += size


def slot_kernel(with_half, with_whole, with_new, info, *refs):
    refs = list(refs)
    ins = refs[: 2 * with_half + 2 * with_whole + (with_new and with_whole)]
    outs = refs[len(ins) :]

    def add():
        left, right = ins.pop(0), ins.pop(0)
        return (left[...].astype(F32) + right[...].astype(F32)).astype(BF)

    if with_half:
        outs.pop(0)[...] = add()
    if with_whole:
        whole = add()
        outs.pop(0)[...] = whole
        if with_new:
            outs.pop(0)[...] = jnp.where(info[4] == 1, whole, ins.pop(0)[...])


def split_rows_kernel(ref, upper, lower):
    rows, width = upper.shape
    upper[...] = ref[:rows, :width]
    lower[...] = ref[rows:, :width]


def w_out_products_kernel(starts, own_keep, core_keep, chip_keep, far_keep, own, core, chip, upper, lower, out):
    head, width = out.shape
    rows = own.shape[0]
    keeps = (own_keep, core_keep, chip_keep, far_keep)
    out[...] = products(
        [ref[:rows, start : start + head] for ref, start in zip(keeps, starts)],
        [own[:, :width], core[:rows, :width], chip[:, :width], jnp.concatenate([upper[...], lower[...]])],
    )


def rest_out_kernel(info, *refs):
    *sources, w_out, w_qkv = refs
    outs = (w_out, w_qkv.at[0], w_qkv.at[1], w_qkv.at[2])
    for kept, got, out in zip(sources[::2], sources[1::2], outs):
        out[...] = jnp.where(info[4] == 1, kept[...], got[...]).astype(F32)


def choose_kernel(info, kept, got, out):
    out[...] = jnp.where(info[4] == 1, kept[...], got[...])


def stack_kernel(info, keep, got, activations, input_grads):
    width = activations.shape[2]
    for i, source in ((info[1], keep), (1 - info[1], got)):
        activations[i] = source[:, :width]
        input_grads[i] = source[:, width:].astype(F32)


def last_kernel(docs, info, lengths, own_core, other_core, out, scr):
    seq = scr.shape[0]
    half = seq // 2
    width = out.shape[1]
    start, _ = longest_start(info, lengths, docs)
    here = slice(2 * width, 2 * width + half)
    mine, theirs = own_core[:half, here].astype(F32).T, other_core[:half, here].astype(F32).T
    zero = jnp.zeros_like(mine)
    low = info[0] == 0
    scr[:half, :half] = jnp.where(low, mine, theirs)
    scr[half:, half:] = jnp.where(low, theirs, mine)
    scr[:half, half:] = zero
    scr[half:, :half] = zero
    full = pltpu.roll(scr[...], lax.rem(start + half * (1 - info[0]) + half, seq), 0)[:half]
    full = pltpu.roll(full, start, 1).astype(BF)
    rows = packed_rows(half)
    out[:rows] = jnp.zeros((rows, out.shape[1]), BF)
    out[rows:] = (own_core[half:, :width].astype(F32) + other_core[half:, :width].astype(F32)).astype(BF)
    for row, column, source_row, source_column, count in packing(half):
        out[row : row + count, column : column + half] = full[
            source_row : source_row + count, source_column : source_column + half
        ]


def packing(half):
    rows = packed_rows(half)
    moves = []
    for piece in range(2):
        done = 0
        while done < half:
            place = piece * half + done
            count = min(half - done, rows - place % rows)
            moves.append((place % rows, place // rows * half, done, piece * half, count))
            done += count
    return moves


def packed_rows(half):
    return -(-2 * half // (3 * PAD)) * PAD


def last_out_kernel(info, own, other, logits, noise, mask_out, *outs):
    half = logits.shape[0] // 2
    low = info[0] == 0
    first = jnp.where(low, own[...], other[...])
    second = jnp.where(low, other[...], own[...])
    for base, block in ((0, first), (half, second)):
        for row, column, to_row, to_column, count in packing(half):
            here = (slice(base + to_row, base + to_row + count), slice(to_column, to_column + half))
            slope = 1.0 / (1.0 + jnp.exp(logits[here] + noise[here]))
            mask_out[here] = block[row : row + count, column : column + half].astype(F32) * slope
    sums = own[packed_rows(half) :].astype(F32)
    *vectors, b_in, b_qv = outs
    for i, out in enumerate(vectors):
        out[...] = sums[i : i + 1]
    place = 2 * info[1] + info[0]
    for part in range(PARTS):

        @pl.when(place == part)
        def _():
            b_in[...] = sums[6 + part : 7 + part, : b_in.shape[1]]
            head = b_qv.shape[1]
            b_qv[0:1] = sums[10 + part : 11 + part, :head]
            b_qv[1:2] = sums[10 + part : 11 + part, head : 2 * head]


def rows_kernel(docs, column, info, lengths, second, second_other, pack, pack_other, keep_out, give_out, scr):
    seq, width = scr.shape
    half = seq // 2
    rows = seq // PARTS
    start, _ = longest_start(info, lengths, docs)
    low = info[0] == 0
    place = 2 * info[1] + info[0]
    far = 2 * (1 - info[1]) + info[0]
    for i, (own, other, first) in enumerate(((second, second_other, 0), (pack, pack_other, column))):
        here = slice(first, first + width)
        mine, theirs = own[:half, here].astype(F32), other[:half, here].astype(F32)
        scr[:half] = jnp.where(low, mine, theirs)
        scr[half:] = jnp.where(low, theirs, mine)
        to = slice(i * width, (i + 1) * width)
        keep_out[:, to] = pltpu.roll(scr[...], lax.rem(start + seq - place * rows, seq), 0)[:rows].astype(BF)
        give_out[:, to] = pltpu.roll(scr[...], lax.rem(start + seq - far * rows, seq), 0)[:rows].astype(BF)


class Order:
    def __init__(self):
        self.last = None
        self.due = []

    def after(self, *values):
        if self.last is None:
            return values
        return lax.optimization_barrier((*values, self.last))[: len(values)]

    def arrived(self, *values):
        self.due += values

    def run(self, step, *inputs):
        return self.run_with((), step, *inputs)[0]

    def run_with(self, arrivals, step, *inputs):
        due, self.due = self.due, []
        values = self.after(*due, *inputs, *arrivals)[len(due) :]
        result = step(*values[: len(inputs)])
        self.last = jax.tree.leaves(result)[0]
        return result, values[len(inputs) :]


def shards(
    inputs, out_grad, doc_lengths, w_qkv, b_qv, w_out, b_out, norm1_gain, norm1_bias,
    w_in, b_in, w_back, b_back, norm2_gain, norm2_bias, mask_logits, mask_noise,
):
    count, seq, width = inputs.shape
    docs = doc_lengths.shape[1]
    core, chip = lax.axis_index("core"), lax.axis_index("chip")
    odd = lax.axis_index("dp") % 2
    part = 2 * chip + core
    half = seq // 2
    head = w_out.shape[1]
    units = w_in.shape[2]
    assert lax.axis_size("pipe") == 2 and lax.axis_size("chip") == 2 and count == 2
    assert lax.axis_size("dp") % 2 == 0 and PARTS * head == width and seq % (2 * PARTS) == 0
    place = lax.axis_index("dp")
    line = lax.axis_size("dp") == 4
    middle = ((place == 1) | (place == 2)) if line else place >= 0
    info = jnp.stack([core, chip, odd, lax.axis_index("pipe"), middle]).astype(jnp.int32)
    order = Order()
    everyone = ("chip", "core")

    def diagonal(block):
        return lax.ppermute(block, everyone, [(i, i ^ 3) for i in range(PARTS)])

    low_rows = pltpu.VMEM((half, width), BF)
    low_columns = pltpu.VMEM((width, half), BF)
    up_scratch = [low_rows, low_rows, low_columns, low_columns]
    down_scratch = [pltpu.VMEM((width, half), F32), low_rows, low_rows, low_rows, pltpu.VMEM((half, half), F32)]
    flat = shape(half, width)
    flat32 = shape(half, width, dtype=F32)

    pack, half_pack, half_in = call(
        split_kernel,
        [shape(4 * head + 2 * PAD, width), shape(2 * head + PAD, width), shape(width // 2 + 2 * PAD, units)],
        [SMEM] + [HBM] * 5,
        (info, jnp.swapaxes(w_qkv[0], 1, 2).reshape(3 * head, width), w_out[0], w_in[0], b_in, b_qv[0]),
        [pltpu.VMEM((3 * head, width), BF), pltpu.VMEM((head, width), BF), pltpu.VMEM((width // 2, units), BF),
         pltpu.VMEM((1, units), BF), pltpu.VMEM((2, head), BF), pltpu.SemaphoreType.DMA((5,))],
        56 << 20,
    )
    got_pack = swap(half_pack, "chip")
    got_in = swap(half_in, "chip")
    near = [swap(v, "core") for v in (pack, w_in[0], w_back[0])]

    def prepare(*args):
        return call(
            functools.partial(prepare_kernel, docs),
            [flat, flat, shape(half, half, dtype=F32)],
            [SMEM, SMEM, VMEM, VMEM, VMEM, VMEM],
            args,
        )

    tokens0, top0, bias = order.run(prepare, info, doc_lengths, inputs, out_grad, mask_logits[0], mask_noise[0])
    got_pack, *near = order.after(got_pack, *near)
    also_pack = swap(got_pack, "dp")
    w_back_own, got_pack = lax.optimization_barrier((w_back[0], got_pack))
    got_back = swap(w_back_own, "chip")
    cross_got_pack = swap(got_pack, "core")
    got_in, got_pack = lax.optimization_barrier((got_in, got_pack))
    also_in = swap(got_in, "dp")
    also_pack, got_in = lax.optimization_barrier((also_pack, got_in))
    p1 = (pack, near[0], got_pack, also_pack, cross_got_pack, swap(also_pack, "core"))

    def attention(tokens, *p1):
        return call(
            attention_kernel,
            [flat32, shape(4, width, width), shape(2, width, dtype=F32), shape(PARTS, units, dtype=F32)],
            [SMEM] + [VMEM] * 11,
            (info, tokens, bias, b_out, norm1_gain, norm1_bias) + p1,
            up_scratch,
        )

    first, w4, both_b_qv, full_b_in = order.run(attention, tokens0, *p1)
    total = order.run(
        lambda *a: call(ffn_near_kernel, flat32, [VMEM] * 7, a),
        first, b_back, full_b_in, w_in[0], near[1], w_back[0], near[2],
    )
    (also_in,) = order.after(also_in)
    cross_in = swap(jnp.concatenate([also_in, got_in]), "core")
    (got_back,) = order.after(got_back)
    backs = (w_back[0], near[2], got_back, swap(got_back, "core"))
    hidden_far, in_far = order.run(
        lambda *a: call(
            ffn_far_kernel, [shape(half, 2 * units), shape(2, width, units)], [SMEM] + [VMEM] * 5, (info,) + a
        ),
        first, full_b_in, got_in, also_in, cross_in,
    )
    second = order.run(
        lambda *a: call(ffn_end_kernel, flat, [VMEM] * 6, a),
        total, hidden_far, norm2_gain, norm2_bias, backs[2], backs[3],
    )
    weights = (w4, both_b_qv, full_b_in, w_in[0], near[1], in_far) + backs
    passed = lax.ppermute(second, "pipe", [(0, 1)])

    tokens = order.run(
        lambda *a: call(choose_tokens_kernel, flat, [SMEM, VMEM, VMEM], (info,) + a), tokens0, passed
    )
    tokens_chip = swap(tokens, "chip")
    tokens_core = swap(tokens, "core")

    keep_width = units + head

    def layer(tokens):
        return call(
            layer_kernel,
            [flat, flat, shape(half, 2 * head)]
            + [shape(half, keep_width)] * 2 + [shape(half, units)] * 2
            + [flat, flat, flat, shape(width, half), shape(width // HEAD_DIM, half, half),
               flat32, shape(half, 128, dtype=F32), shape(half, PARTS * units),
               flat32, shape(half, 128, dtype=F32)],
            [VMEM] * (8 + WEIGHTS),
            (tokens, bias, b_out, norm1_gain, norm1_bias, b_back, norm2_gain, norm2_bias) + weights,
            up_scratch,
        )

    second, first_low, far_attended, *kept = order.run(layer, tokens)
    keeps, kept = kept[:PARTS], kept[PARTS:]
    q, k, v, kt, chance, unit1, scale1, slope, unit2, scale2 = kept
    keeps = [keeps[0], swap(keeps[1], "core"), swap(keeps[2], "chip"), diagonal(keeps[3])]
    far_chip = swap(first_low, "chip")

    def down(top):
        return call(
            down_kernel, flat, [VMEM] * (13 + WEIGHTS),
            (top, unit1, scale1, norm1_gain, unit2, scale2, norm2_gain, slope, q, k, v, kt, chance) + weights,
            down_scratch,
        )

    down_grad, (tokens_chip, tokens_core) = order.run_with((tokens_chip, tokens_core), down, top0)
    passed = lax.ppermute(down_grad, "pipe", [(1, 0)])
    tokens_all = [tokens, tokens_core, tokens_chip, swap(tokens_chip, "core")]

    def rows_of(*args):
        return call(
            functools.partial(rows_kernel, docs, width),
            [shape(seq // PARTS, 2 * width)] * 2,
            [SMEM, SMEM] + [VMEM] * 4,
            (info, doc_lengths) + args,
            [pltpu.VMEM((seq, width), F32)],
        )

    def down_norm(top, passed):
        return call(
            down_norm_kernel, [flat, shape(half, 2 * width), flat32, shape(PAD, width, dtype=F32)], [SMEM] + [VMEM] * 6,
            (info, top, passed, unit2, scale2, norm2_gain, first_low),
        )

    (ffn_low, ffn_pack, sum_grad, sums), keeps[1:] = order.run_with(keeps[1:], down_norm, top0, passed)
    ffn_chip = swap(ffn_low, "chip")
    ffn_core = swap(ffn_pack, "core")
    (second,) = order.after(second)
    second_other = swap(second, "core")

    def down_ffn(sum_grad):
        return call(
            down_ffn_kernel,
            [shape(half, units)] * PARTS + [flat32], [VMEM] * (2 + WEIGHTS), (sum_grad, slope) + weights,
        )

    *pres, first_grad = order.run(down_ffn, sum_grad)
    pre_core = swap(pres[1], "core")

    lanes = [dict(own=None, half=None, whole=None, end=None, middle=None, names=[]) for _ in range(2)]
    final = {}

    def slot(lane, name=None, new=None):
        if not line:
            if new is not None:
                final[name] = (lax.psum(new, "dp"),) * 2
            return
        if lane["whole"] is not None:
            final[lane["names"].pop(0)] = (lane["whole"], lane["end"])
        with_half, with_whole = lane["own"] is not None, lane["half"] is not None
        ins = [lane["own"], lane["end"]] if with_half else []
        if with_whole:
            ins += [lane["half"], lane["middle"]] + ([new] if new is not None else [])
        half_sum = whole = None
        going = new
        if new is not None and not with_whole:
            (going,) = order.after(going)
        if ins:
            outs = with_half + with_whole + (with_whole and new is not None)
            results = order.run(
                lambda *a: call(
                    functools.partial(slot_kernel, with_half, with_whole, new is not None),
                    [shape(*a[0].shape)] * outs, [SMEM] + [VMEM] * len(a), (info,) + a,
                ),
                *ins,
            )
            if with_half:
                half_sum = results[0]
            if with_whole:
                whole = results[int(with_half)]
                going = results[-1] if new is not None else whole
        routes = ([(0, 1), (3, 2)] if new is not None else []) + ([(1, 0), (2, 3)] if whole is not None else [])
        lane["end"] = lax.ppermute(going, "dp", routes) if routes else None
        lane["middle"] = lax.ppermute(half_sum, "dp", [(1, 2), (2, 1)]) if half_sum is not None else None
        lane["own"], lane["half"], lane["whole"] = new, half_sum, whole
        if new is not None:
            lane["names"].append(name)

    def matrix(*names):
        sources = [v for name in names for v in final[name]]
        rows = sum(v.shape[0] for v in sources) // 2
        return order.run(
            lambda *a: call(
                whole_kernel, shape(rows, a[0].shape[1], dtype=F32), [SMEM] + [VMEM] * len(a), (info,) + a
            ),
            *sources,
        )

    def products_of(outs, lefts, left_starts, left_first, rights, right_starts, right_size):
        return order.run(
            lambda *a: call(
                functools.partial(products_kernel, half, left_starts, left_first, right_starts, right_size),
                [shape(n, right_size) for n in outs], [VMEM] * (2 * PARTS), a,
            ),
            *lefts, *rights,
        )


    def down_attention(first_grad, sums, *pres):
        return call(
            down_attention_kernel,
            [shape(half, 2 * width), shape(half, width), shape(half + PAD, -(-(2 * width + half + 3 * head) // 128) * 128)]
            + [shape(half, 3 * head)],
            [SMEM] + [VMEM] * (12 + PARTS),
            (info, first_grad, sums, unit1, scale1, norm1_gain, q, k, v, kt, chance) + pres + (far_attended, w4),
            [pltpu.VMEM((PAD, width), F32)] + down_scratch,
        )

    down_core_projected = 2 * width + half
    down_chip, down_diagonal, down_pack, projected_zero = order.run(down_attention, first_grad, sums, *pres)
    ffn_chip, far_chip = order.after(ffn_chip, far_chip)
    ffns = [ffn_low, ffn_core, ffn_chip, swap(ffn_chip, "core")]
    far_cross = swap(far_chip, "core")
    pre_chip, pre_diagonal = swap(pres[2], "chip"), diagonal(pres[3])
    none = (0, 0, 0, 0)
    quarter = units // 4
    one, two = lanes
    order.arrived(second_other, tokens_all[3])
    back = products_of((quarter,) * 2, keeps, none, 0, ffns, none, width)
    down_give, chip_give, diagonal_give = order.after(down_pack, down_chip, down_diagonal)
    down_other = swap(down_give, "core")
    branch_chip = swap(chip_give, "chip")
    far_projected = diagonal(diagonal_give)
    slot(one, "back0", back[0])
    slot(two, "back1", back[1])

    def last_chunk(*args):
        return call(
            functools.partial(last_kernel, docs),
            shape(packed_rows(half) + PAD, width),
            [SMEM, SMEM] + [VMEM] * 2,
            (info, doc_lengths) + args,
            [pltpu.VMEM((seq, seq), F32)],
        )

    back += products_of((quarter,) * 2, keeps, none, 2 * quarter, ffns, none, width)
    last = order.run(last_chunk, down_pack, down_other)
    rows_keep, rows_give = order.run(rows_of, second, second_other, down_pack, down_other)
    order.arrived(far_cross, pre_core)
    slot(one, "back2", back[2])
    slot(two, "back3", back[3])
    upper, lower = order.run(
        lambda a: call(split_rows_kernel, [shape(half // 2, width)] * 2, [VMEM], (a,)), branch_chip
    )
    upper, lower = swap(upper, "core"), swap(lower, "core")
    slot(one, "last", last)
    w_out_low = order.run(
        lambda *a: call(
            functools.partial(w_out_products_kernel, (units, units, width + 3 * head, 3 * head)),
            shape(head, width), [VMEM] * 9, a,
        ),
        *keeps[:2], branch_chip, far_projected, down_chip, down_other, branch_chip, upper, lower,
    )
    w_qkv_low = products_of(
        (head,) * 3, [projected_zero, down_other, branch_chip, far_projected], (0, down_core_projected, width, 0), 0,
        tokens_all, none, width,
    )
    slot(two, "q", w_qkv_low[0])
    slot(one, "k", w_qkv_low[1])
    order.arrived(pre_chip)
    slot(two, "v", w_qkv_low[2])
    inner = products_of(
        (quarter,) * 4, [first_low, ffn_core, far_chip, far_cross], (0, width, 0, 0), 0,
        [pres[0], pre_core, pre_chip, pre_diagonal], none, units,
    )
    slot(one, "in0", inner[0])
    slot(two, "in1", inner[1])
    (rows_give,) = order.after(rows_give)
    rows_got = swap(rows_give, "chip")
    slot(one, "in2", inner[2])
    last = order.run(
        lambda a, b: call(choose_kernel, shape(*a.shape), [SMEM, VMEM, VMEM], (info, a, b)), *final["last"]
    )
    last_got = swap(last, "chip")
    slot(two, "in3", inner[3])
    slot(one, "out", w_out_low)
    slot(two)
    slot(one)
    last = order.run(lambda a, b: call(add_kernel, shape(*a.shape), [VMEM] * 2, (a, b)), last, last_got)
    last_other = swap(last, "core")
    if line:
        order.arrived(two["end"])
    slot(two)
    grad_mask, *vectors, grad_b_in, grad_b_qv = order.run(
        lambda *a: call(
            last_out_kernel,
            [shape(seq, seq, dtype=F32)] + [shape(1, width, dtype=F32)] * 6
            + [shape(1, units, dtype=F32), shape(2, head, dtype=F32)],
            [SMEM] + [VMEM] * 4, (info,) + a,
        ),
        last, last_other, mask_logits[0], mask_noise[0],
    )
    activations, input_grads = order.run(
        lambda a, b: call(
            stack_kernel, [shape(2, seq // PARTS, width), shape(2, seq // PARTS, width, dtype=F32)],
            [SMEM, VMEM, VMEM], (info, a, b),
        ),
        rows_keep, rows_got,
    )
    if line:
        order.arrived(one["end"])
    slot(one)
    slot(two)
    slot(one)
    grad_w_qkv = matrix("q", "k", "v").reshape(3, head, width)
    grad_w_in = matrix("in0", "in1", "in2", "in3")
    grad_w_back = matrix("back0", "back1", "back2", "back3")
    grad_w_out = matrix("out")
    results = (
        activations, input_grads, jnp.swapaxes(grad_w_qkv, 1, 2), grad_b_qv, grad_w_out,
        vectors[0][0], vectors[1][0], vectors[2][0],
        grad_w_in, grad_b_in[0], grad_w_back,
        vectors[3][0], vectors[4][0], vectors[5][0],
        grad_mask,
    )
    return tuple(item[None] for item in results)


def solution(mesh):
    pipe, dp, tensor = (mesh.shape[name] for name in ("pipe", "dp", "tensor"))
    split = Mesh(mesh.devices.reshape(pipe, dp, tensor // 2, 2), ("pipe", "dp", "chip", "core"))
    placed = (
        P("dp", None, None),
        P("dp", None, None),
        P("dp", None),
        P("pipe", None, None, TENSOR),
        P("pipe", None, TENSOR),
        P("pipe", TENSOR, None),
        P("pipe", None),
        P("pipe", None),
        P("pipe", None),
        P("pipe", None, TENSOR),
        P("pipe", TENSOR),
        P("pipe", TENSOR, None),
        P("pipe", None),
        P("pipe", None),
        P("pipe", None),
        P("pipe", None, None),
        P("pipe", None, None),
    )
    return jax.shard_map(
        shards,
        mesh=split,
        in_specs=placed,
        out_specs=(
            P("pipe", "dp", TENSOR, None),
            P("pipe", "dp", TENSOR, None),
            P("pipe", None, None, TENSOR),
            P("pipe", None, TENSOR),
            P("pipe", TENSOR, None),
            P("pipe", None),
            P("pipe", None),
            P("pipe", None),
            P("pipe", None, TENSOR),
            P("pipe", TENSOR),
            P("pipe", TENSOR, None),
            P("pipe", None),
            P("pipe", None),
            P("pipe", None),
            P("pipe", None, None),
        ),
        check_vma=False,
    )
```
